32 devices in a mesh: replica: 4 (over y, core), section: 2 (over x), tensor: 4 (over z).
Axes of the slice: x: 2, y: 2, z: 4, core: 2. Of those that a mesh axis runs over, the one named last changes fastest.
Arguments:
- inputs: bfloat16 [4, 4, 128, 12288], P('replica', None, 'tensor'), may hold values from -0.375 to 0.375
- cotangent: bfloat16 [4, 4, 128, 12288], P('replica', None, 'tensor'), may hold values from -36 to 36
- micro_counts: int32 [4], replicated, may hold values from 1 to 4
- bounds: int32 [4, 3], replicated, may hold values from 0 to 2, as said below
- holder_down: bfloat16 [4, 2, 2, 64, 12288], P('replica', 'section'), may hold values from -0.25 to 0.25, as said below
- holder_up: bfloat16 [4, 2, 2, 64, 12288], P('replica', 'section'), may hold values from -0.25 to 0.25, as said below
- master_down: float32 [2, 64, 12288], P('section', None, ('replica', 'tensor')), may hold values from -0.25 to 0.25
- master_up: float32 [2, 64, 12288], P('section', None, ('replica', 'tensor')), may hold values from -0.25 to 0.25
- moment_down: float32 [2, 64, 12288], P('section', None, ('replica', 'tensor')), may hold values from -4 to 4
- moment_up: float32 [2, 64, 12288], P('section', None, ('replica', 'tensor')), may hold values from -4 to 4
- second_down: float32 [2, 64, 12288], P('section', None, ('replica', 'tensor')), may hold values from 0.01 to 1
- second_up: float32 [2, 64, 12288], P('section', None, ('replica', 'tensor')), may hold values from 0.01 to 1
Outputs:
- new_holder_down: bfloat16 [4, 2, 2, 64, 12288], P('replica', 'section')
- new_holder_up: bfloat16 [4, 2, 2, 64, 12288], P('replica', 'section')
- new_master_down: float32 [2, 64, 12288], P('section', None, ('replica', 'tensor'))
- new_master_up: float32 [2, 64, 12288], P('section', None, ('replica', 'tensor'))
- new_moment_down: float32 [2, 64, 12288], P('section', None, ('replica', 'tensor'))
- new_moment_up: float32 [2, 64, 12288], P('section', None, ('replica', 'tensor'))
- new_second_down: float32 [2, 64, 12288], P('section', None, ('replica', 'tensor'))
- new_second_up: float32 [2, 64, 12288], P('section', None, ('replica', 'tensor'))
The draws below stay inside these ranges and needn't reach their ends.
Inputs may be any that keep to these rules, and one draw needn't show every extreme that they name: `bounds`: each row starts at 0, never falls and ends at 2; the sections that hold layers come first, 1 to 2 of them and at least one, and their layer counts differ by at most one; a layer l held by section s satisfies s <= l <= s + 1; a section holds at most 2 layers, and some section of replica 0 holds exactly 2. `holder_down`: each used slot holds master_down's layer that lives there by bounds, rounded to bfloat16; unused slots are zeros. `holder_up`: each used slot holds master_up's layer that lives there by bounds, rounded to bfloat16; unused slots are zeros.
All inputs are finite; a program needn't handle non-finite values.
Results may differ from the reference program's by a relative error of at most 0.006.
Values may be sent and summed in bfloat16 or wider, within the bound.
No kernel may reach another device: no remote copies, remote signals or barrier semaphores. Data moves between devices by JAX's collectives and lax.ppermute only.
A program may use at most 192 MiB of HBM per device.

```python
import math
import jax
import jax.numpy as jnp
from jax import lax

D = 12288
R = 64
MICRO = 4
LAYERS = 2
MAXL = 2
TOKMB = 128
N_REPLICA = 4
N_SECTION = 2


def layer_bounds(key):
    key = jax.random.fold_in(key, 101)
    first_key, second_key = jax.random.split(key)
    lowest = max(1, N_SECTION - 1)
    dropped = jax.random.randint(first_key, (N_REPLICA,), 0, N_SECTION - lowest + 1)
    used_count = (N_SECTION - dropped).at[0].set(lowest).astype(jnp.int32)
    per_base = LAYERS // used_count
    spare_count = LAYERS - per_base * used_count
    column = jnp.arange(N_SECTION, dtype=jnp.int32)[None, :]
    scores = jax.random.randint(second_key, (N_REPLICA, N_SECTION), 0, 1000) * N_SECTION + column
    scores = scores.at[0, 0].set(-1)
    scores = jnp.where(column < used_count[:, None], scores, 1000 * N_SECTION + N_SECTION)
    ranking = jnp.argsort(jnp.argsort(scores, axis=1, stable=True), axis=1, stable=True)
    extra = (ranking < spare_count[:, None]).astype(jnp.int32)
    per_section = jnp.where(column < used_count[:, None], per_base[:, None] + extra, 0)
    ends = jnp.cumsum(per_section, axis=1).astype(jnp.int32)
    return jnp.concatenate([jnp.zeros((N_REPLICA, 1), jnp.int32), ends], axis=1)


def master_values(key, member):
    key = jax.random.fold_in(key, 200 + member)
    first_key = jax.random.fold_in(key, 0)
    gaussian = jnp.clip(jax.random.normal(first_key, (LAYERS, R, D), jnp.float32), -5.0, 5.0)
    return gaussian * 0.05


def holder_values(key, member):
    master = master_values(key, member)
    bounds = layer_bounds(key)
    slot_ids = jnp.arange(MAXL, dtype=jnp.int32)
    layer_index = bounds[:, :N_SECTION, None] + slot_ids[None, None, :]
    present = layer_index < bounds[:, 1:, None]
    picked = jnp.take(master, jnp.clip(layer_index, 0, LAYERS - 1), axis=0)
    return jnp.where(present[..., None, None], picked, 0.0)


def draw_bounds(key, part):
    return layer_bounds(key)


def draw_master_down(key, part):
    return master_values(key, 1)


def draw_master_up(key, part):
    return master_values(key, 2)


def draw_holder_down(key, part):
    return holder_values(key, 1).astype(jnp.bfloat16)


def draw_holder_up(key, part):
    return holder_values(key, 2).astype(jnp.bfloat16)


def draw_inputs(key, part):
    key = jax.random.fold_in(key, 7)
    subkeys = jax.random.split(key, 3)
    extent = (N_REPLICA, MICRO, TOKMB, D)
    row_scale = jnp.exp(jax.random.uniform(subkeys[1], (N_REPLICA, MICRO, TOKMB, 1), jnp.float32, 0.0, 2.3026))
    column = jnp.exp(jax.random.uniform(subkeys[2], (1, 1, 1, D), jnp.float32, 0.0, 2.3026))
    values_base = jnp.clip(jax.random.normal(subkeys[0], extent, jnp.float32), -6.0, 6.0)
    return (values_base * row_scale * column / 1600.0).astype(jnp.bfloat16)


def touch_ends(array, key, least, high):
    longest = array.shape.index(max(array.shape))
    spots = []
    for shift in (0, 1):
        where = [jax.random.randint(jax.random.fold_in(key, axis), (), 0, length) for axis, length in enumerate(array.shape)]
        where[longest] = (where[longest] + shift) % array.shape[longest]
        spots.append(tuple(where))
    return array.at[spots[0]].set(least).at[spots[1]].set(high)


def block_levels(rng, shape, shards, smallest, top_value):
    def one(position, blocks):
        heights = jax.random.uniform(jax.random.fold_in(jax.random.fold_in(rng, 6), position), (blocks,), jnp.float32, smallest / len(shards), top_value / len(shards))
        return jnp.repeat(jnp.exp(heights), shape[position] // blocks).reshape((-1,) + (1,) * (len(shape) - position - 1))

    factor_of = one(*shards[0])
    for cut in shards[1:]:
        factor_of = factor_of * one(*cut)
    return factor_of


def scatter_about(key, shape, scale, limit, cuts=(), kind=jnp.bfloat16):
    array = scale * jax.random.normal(key, shape, jnp.float32)
    if cuts:
        array = array * block_levels(key, shape, cuts, -0.22, 0.18)
    return jnp.clip(array, -limit, limit).astype(kind)


def setup_inputs(seed: int = 0) -> dict:
    seeds = jax.random.split(jax.random.key(seed), 13)
    inputs = draw_inputs(jax.random.fold_in(seeds[12], 71), 0)
    cotangent = scatter_about(seeds[1], (N_REPLICA, MICRO, TOKMB, D), 6.0, 36.0, ((0, 4), (2, 4)))
    micro_counts = touch_ends(jax.random.randint(seeds[2], (N_REPLICA,), 1, MICRO + 1), jax.random.fold_in(seeds[2], 1), 1, MICRO).astype(jnp.int32)
    bounds = draw_bounds(jax.random.fold_in(seeds[12], 71), 0)
    holder_down = draw_holder_down(jax.random.fold_in(seeds[12], 71), 0)
    holder_up = draw_holder_up(jax.random.fold_in(seeds[12], 71), 0)
    master_down = draw_master_down(jax.random.fold_in(seeds[12], 71), 0)
    master_up = draw_master_up(jax.random.fold_in(seeds[12], 71), 0)
    moment_down = scatter_about(seeds[8], (LAYERS, R, D), 0.3, 4.0, ((0, 2), (2, 16)), jnp.float32)
    moment_up = scatter_about(seeds[9], (LAYERS, R, D), 0.3, 4.0, ((0, 2), (2, 16)), jnp.float32)
    second_down = jnp.clip(jnp.exp(math.log(1.0) - 4.6051702 * jax.random.uniform(seeds[10], (LAYERS, R, D), jnp.float32) ** block_levels(seeds[10], (LAYERS, R, D), ((0, 2), (2, 16)), -0.2, 0.2)), 0.01, 1.0)
    second_up = jnp.clip(jnp.exp(math.log(1.0) - 4.6051702 * jax.random.uniform(seeds[11], (LAYERS, R, D), jnp.float32) ** block_levels(seeds[11], (LAYERS, R, D), ((0, 2), (2, 16)), -0.2, 0.2)), 0.01, 1.0)
    return dict(inputs=inputs, cotangent=cotangent, micro_counts=micro_counts, bounds=bounds, holder_down=holder_down, holder_up=holder_up, master_down=master_down, master_up=master_up, moment_down=moment_down, moment_up=moment_up, second_down=second_down, second_up=second_up)


norm_eps = 1e-06
learn_rate = 0.01
beta_one = 0.9
beta_two = 0.95
decay_rate = 0.1
adam_eps = 1e-08
first_fix = 0.9999734386011124
second_fix = 0.9940794707796659

def layer_forward(hidden, down_w, up_w):
    features = hidden.shape[-1]
    ranks = down_w.shape[0]
    widened = hidden.astype(jnp.float32)
    inverse = lax.rsqrt(lax.optimization_barrier(jnp.mean(widened * widened, axis=-1, keepdims=True)) + norm_eps)
    normed = (widened * inverse).astype(jnp.bfloat16)
    projected = lax.dot_general(normed, down_w, (((1,), (1,)), ((), ())), preferred_element_type=jnp.float32) / math.sqrt(features)
    active = jax.nn.silu(projected).astype(jnp.bfloat16)
    branch = jnp.dot(active, up_w, preferred_element_type=jnp.float32) / math.sqrt(ranks)
    return (widened + branch).astype(jnp.bfloat16)

def layer_backward(hidden, down_w, up_w, incoming):
    features = hidden.shape[-1]
    ranks = down_w.shape[0]
    widened = hidden.astype(jnp.float32)
    inverse = lax.rsqrt(lax.optimization_barrier(jnp.mean(widened * widened, axis=-1, keepdims=True)) + norm_eps)
    normed = (widened * inverse).astype(jnp.bfloat16)
    projected = lax.dot_general(normed, down_w, (((1,), (1,)), ((), ())), preferred_element_type=jnp.float32) / math.sqrt(features)
    active = jax.nn.silu(projected).astype(jnp.bfloat16)
    sigmoid_u = jax.nn.sigmoid(projected)
    d_active = lax.dot_general(incoming, up_w, (((1,), (1,)), ((), ())), preferred_element_type=jnp.float32) / math.sqrt(ranks)
    d_inner = (d_active * sigmoid_u * (1.0 + projected * (1.0 - sigmoid_u))).astype(jnp.bfloat16)
    grad_up = lax.dot_general(active, incoming, (((0,), (0,)), ((), ())), preferred_element_type=jnp.float32) / math.sqrt(ranks)
    grad_down = lax.dot_general(d_inner, normed, (((0,), (0,)), ((), ())), preferred_element_type=jnp.float32) / math.sqrt(features)
    d_normed = jnp.dot(d_inner, down_w, preferred_element_type=jnp.float32) / math.sqrt(features)
    mixed = lax.optimization_barrier(jnp.mean(d_normed * widened, axis=-1, keepdims=True))
    d_wide = incoming.astype(jnp.float32) + inverse * (d_normed - widened * inverse * inverse * mixed)
    return (d_wide.astype(jnp.bfloat16), grad_down, grad_up)

def adam_update(params, moments, seconds, gradient):
    new_moments = beta_one * moments + (1.0 - beta_one) * gradient
    new_seconds = beta_two * seconds + (1.0 - beta_two) * gradient * gradient
    new_params = params - learn_rate * (new_moments / first_fix / (jnp.sqrt(new_seconds / second_fix) + adam_eps) + decay_rate * params)
    return (new_params, new_moments, new_seconds)

def to_holders(params, bounds):
    slot_ids = jnp.arange(MAXL, dtype=jnp.int32)
    layer_at = (bounds[:, :N_SECTION, None] + slot_ids[None, None, :]).astype(jnp.int32)
    present = layer_at < bounds[:, 1:, None]
    picked = params.astype(jnp.bfloat16)[jnp.clip(layer_at, 0, LAYERS - 1)]
    return jnp.where(present[..., None, None], picked, jnp.zeros_like(picked))

def reference(inputs, cotangent, micro_counts, bounds, holder_down, holder_up, master_down, master_up, moment_down, moment_up, second_down, second_up):
    layer_ids = jnp.arange(LAYERS, dtype=jnp.int32)
    grad_down = jnp.zeros((LAYERS, R, D), jnp.float32)
    grad_up = jnp.zeros((LAYERS, R, D), jnp.float32)
    for replica_at in range(N_REPLICA):
        row_bounds = bounds[replica_at]
        section_of = lax.optimization_barrier(jnp.sum((row_bounds[None, 1:] <= layer_ids[:, None]).astype(jnp.int32), axis=1)).astype(jnp.int32)
        slot_of = (layer_ids - row_bounds[section_of]).astype(jnp.int32)
        downs = holder_down[replica_at][section_of, slot_of]
        ups = holder_up[replica_at][section_of, slot_of]
        counted = micro_counts[replica_at]

        def one_micro(carry, item):
            block_in, cot_block, micro_index = item

            def forward_layer(hidden, weights):
                return (layer_forward(hidden, weights[0], weights[1]), hidden)
            _, stored = lax.scan(forward_layer, block_in, (downs, ups))
            starting = jnp.where(micro_index < counted, cot_block, jnp.zeros_like(cot_block))

            def backward_layer(incoming, pieces):
                d_hidden, g_down, g_up = layer_backward(pieces[0], pieces[1], pieces[2], incoming)
                return (d_hidden, (g_down, g_up))
            _, (g_down, g_up) = lax.scan(backward_layer, starting, (stored, downs, ups), reverse=True)
            return ((carry[0] + g_down, carry[1] + g_up), None)
        (grad_down, grad_up), _ = lax.scan(one_micro, (grad_down, grad_up), (inputs[replica_at], cotangent[replica_at], jnp.arange(MICRO, dtype=jnp.int32)))
    new_master_down, new_moment_down, new_second_down = adam_update(master_down, moment_down, second_down, grad_down)
    new_master_up, new_moment_up, new_second_up = adam_update(master_up, moment_up, second_up, grad_up)
    new_holder_down = to_holders(new_master_down, bounds)
    new_holder_up = to_holders(new_master_up, bounds)
    return (new_holder_down, new_holder_up, new_master_down, new_master_up, new_moment_down, new_moment_up, new_second_down, new_second_up)
```

```python
import functools
import math

import jax
import jax.numpy as jnp
from jax import lax
from jax.experimental import pallas as pl
from jax.experimental.pallas import tpu as pltpu
from jax.sharding import PartitionSpec as P

norm_eps = 1e-06
learn_rate = 0.01
beta_one = 0.9
beta_two = 0.95
decay_rate = 0.1
adam_eps = 1e-08
first_fix = 0.9999734386011124
second_fix = 0.9940794707796659

f32 = jnp.float32
bf16 = jnp.bfloat16
exact = lax.Precision.HIGHEST
vmem_bytes = 40 * 1024 * 1024


def params(**kw):
    return pltpu.CompilerParams(vmem_limit_bytes=vmem_bytes, **kw)


def dot_last(x, y, precision=None):
    return lax.dot_general(
        x, y, (((1,), (1,)), ((), ())), preferred_element_type=f32, precision=precision
    )


def dot_first(x, y, precision=None):
    return lax.dot_general(
        x, y, (((0,), (0,)), ((), ())), preferred_element_type=f32, precision=precision
    )


def row_sum(x):
    return jnp.sum(x, axis=-1, keepdims=True)


def project_kernel(layers, per_micro, at, h_ref, g_ref, down_ref, up_ref, out_ref, sq_ref, acc_h, acc_g):
    step = pl.program_id(0)
    slots, ranks, width = down_ref.shape

    @pl.when(step == 0)
    def _():
        acc_h[...] = jnp.zeros_like(acc_h)
        acc_g[...] = jnp.zeros_like(acc_g)
        sq_ref[...] = jnp.zeros_like(sq_ref)

    h = h_ref[...]
    ups = up_ref[...].reshape(slots * ranks, width)
    both = jnp.concatenate([down_ref[...].reshape(slots * ranks, width), ups], axis=0)
    acc_h[...] += dot_last(h, both)
    acc_g[...] += dot_last(g_ref[...], ups)
    wide = h.astype(f32)
    sq_ref[...] += row_sum(wide * wide)

    @pl.when(step == pl.num_programs(0) - 1)
    def _():
        first, after, counted = at[0], at[1], at[2]
        tokens = h_ref.shape[0]
        rows = lax.broadcasted_iota(jnp.int32, (tokens, 1), 0)
        counts = rows < counted * per_micro
        ph = acc_h[...]
        pg = jnp.where(counts, acc_g[...], 0.0)
        pieces = []
        for slot in range(slots):
            lo, hi = slot * ranks, (slot + 1) * ranks
            pieces.append(
                jnp.concatenate(
                    [ph[:, lo:hi], ph[:, slots * ranks + lo : slots * ranks + hi], pg[:, lo:hi]],
                    axis=1,
                )
            )
        for layer in range(layers):
            total = jnp.zeros_like(pieces[0])
            for slot in range(slots):
                here = (first + slot == layer) & (layer < after)
                total = jnp.where(here, pieces[slot], total)
            out_ref[:, layer * 3 * ranks : (layer + 1) * 3 * ranks] = total


def project(at, hidden, cot, downs, ups, layers, per_micro):
    tokens, features = hidden.shape
    slots, ranks, _ = downs.shape
    width = features // 8
    kernel = functools.partial(project_kernel, layers, per_micro)
    return pl.pallas_call(
        kernel,
        grid_spec=pltpu.PrefetchScalarGridSpec(
            num_scalar_prefetch=1,
            grid=(features // width,),
            in_specs=[
                pl.BlockSpec((tokens, width), lambda i, at: (0, i)),
                pl.BlockSpec((tokens, width), lambda i, at: (0, i)),
                pl.BlockSpec((slots, ranks, width), lambda i, at: (0, 0, i)),
                pl.BlockSpec((slots, ranks, width), lambda i, at: (0, 0, i)),
            ],
            out_specs=[
                pl.BlockSpec((tokens, layers * 3 * ranks), lambda i, at: (0, 0)),
                pl.BlockSpec((tokens, 128), lambda i, at: (0, 0)),
            ],
            scratch_shapes=[
                pltpu.VMEM((tokens, 2 * slots * ranks), f32),
                pltpu.VMEM((tokens, slots * ranks), f32),
            ],
        ),
        out_shape=[
            jax.ShapeDtypeStruct((tokens, layers * 3 * ranks), f32),
            jax.ShapeDtypeStruct((tokens, 128), f32),
        ],
        compiler_params=params(),
        cost_estimate=pl.CostEstimate(
            flops=6 * tokens * slots * ranks * features,
            bytes_accessed=4 * (tokens + slots * ranks) * features,
            transcendentals=0,
        ),
        name="project",
    )(at, hidden, cot, downs, ups)


def gram_kernel(sections, at, *refs):
    around = refs[:sections]
    gram_ref, right_ref = refs[sections:]
    section_at = at[4]
    ranks = around[0].shape[0] // 2
    layers = []
    for layer in range(sections):
        distance = lax.rem(layer - section_at + sections, sections)
        chosen = around[0][...]
        for step in range(1, sections):
            chosen = jnp.where(distance == step, around[step][...], chosen)
        layers.append(chosen)
    lefts = [chosen[ranks:] for chosen in layers[:-1]]
    right = jnp.concatenate([chosen[:ranks] for chosen in layers[1:]] + lefts, axis=0)
    right_ref[...] = right
    gram_ref[...] = dot_last(jnp.concatenate(lefts, axis=0), right)


def gram(at, around):
    sections = len(around)
    ranks = around[0].shape[0] // 2
    columns = around[0].shape[1]
    before = (sections - 1) * ranks
    return pl.pallas_call(
        functools.partial(gram_kernel, sections),
        in_specs=[pl.BlockSpec(memory_space=pltpu.SMEM)]
        + [pl.BlockSpec(memory_space=pltpu.VMEM)] * sections,
        out_specs=[pl.BlockSpec(memory_space=pltpu.VMEM)] * 2,
        out_shape=[
            jax.ShapeDtypeStruct((before, 2 * before), f32),
            jax.ShapeDtypeStruct((2 * before, columns), bf16),
        ],
        compiler_params=params(),
        name="gram",
    )(at, *around)


def chain_kernel(sections, parts, features, per_micro, at, *refs):
    projections = refs[:sections]
    sq_ref = refs[sections]
    grams = refs[sections + 1 : sections + 1 + parts]
    factor_ref, mixed_ref = refs[sections + 1 + parts :]
    layers = sections
    section_at, counted = at[4], at[2]
    tokens = sq_ref.shape[0]
    total = projections[0][...]
    for other in projections[1:]:
        total = total + other[...]
    table = grams[0][...]
    for other in grams[1:]:
        table = table + other[...]
    ranks = total.shape[1] // (3 * layers)
    scale_d = 1.0 / math.sqrt(features)
    scale_r = 1.0 / math.sqrt(ranks)

    def part(layer, which):
        at_column = (3 * layer + which) * ranks
        return total[:, at_column : at_column + ranks]

    def up_down(i, layer):
        return table[i * ranks : (i + 1) * ranks, (layer - 1) * ranks : layer * ranks]

    def up_up(i, j):
        at_column = (layers - 1 + j) * ranks
        return table[i * ranks : (i + 1) * ranks, at_column : at_column + ranks]

    def times(x, y):
        return jnp.dot(x, y, preferred_element_type=f32, precision=exact)

    square = sq_ref[:, 0:1]
    inverses, inners, actives, sigmoids = [], [], [], []
    on_up = [[part(l, 1) for l in range(layers - 1)]]
    for layer in range(layers):
        inverse = lax.rsqrt(jnp.maximum(square, 0.0) * (1.0 / features) + norm_eps)
        on_down = part(layer, 0)
        for i in range(layer):
            on_down = on_down + scale_r * times(actives[i], up_down(i, layer))
        inner = on_down * (inverse * scale_d)
        sigmoid = jax.nn.sigmoid(inner)
        active = (inner * sigmoid).astype(bf16).astype(f32)
        inverses.append(inverse)
        inners.append(inner)
        sigmoids.append(sigmoid)
        actives.append(active)
        if layer < layers - 1:
            now = on_up[-1]
            grown = [now[l] + scale_r * times(active, up_up(layer, l)) for l in range(layers - 1)]
            square = square + scale_r * row_sum(active * (now[layer] + grown[layer]))
            on_up.append(grown)
    scaled = [None] * layers
    kappas = [None] * layers
    for layer in reversed(range(layers)):
        incoming = part(layer, 2)
        for k in range(layer + 1, layers):
            incoming = incoming + scale_d * dot_last(scaled[k], up_down(layer, k), exact)
            incoming = incoming - kappas[k] * on_up[k][layer]
        sigmoid, inner = sigmoids[layer], inners[layer]
        slope = sigmoid * (1.0 + inner * (1.0 - sigmoid))
        error = incoming * scale_r * slope
        scaled[layer] = error * inverses[layer]
        kappas[layer] = (
            inverses[layer] * inverses[layer] * (row_sum(error * inner) * (1.0 / features))
        )

    def owned(values):
        chosen = values[0]
        for layer in range(1, layers):
            chosen = jnp.where(section_at == layer, values[layer], chosen)
        return chosen

    own_error = owned(scaled)
    own_active = owned(actives)
    rows = lax.broadcasted_iota(jnp.int32, (tokens, 1), 0)
    counts = rows < counted * per_micro
    later = jnp.zeros_like(square)
    for k in range(1, layers):
        later = later + jnp.where(k > section_at, kappas[k], 0.0)
    on_hidden = jnp.concatenate([own_error * scale_d, -scale_r * later * own_active], axis=1)
    on_cot = jnp.concatenate(
        [jnp.zeros_like(own_active), jnp.where(counts, own_active * scale_r, 0.0)], axis=1
    )
    factor_ref[...] = jnp.concatenate([on_hidden.T, on_cot.T], axis=1).astype(bf16)
    both = scale_d * scale_r
    for k in range(1, layers):
        lo = (k - 1) * ranks
        across = dot_first(own_active, scaled[k], exact) * both
        mixed_ref[:ranks, lo : lo + ranks] = jnp.zeros_like(across)
        mixed_ref[ranks:, lo : lo + ranks] = jnp.where(k > section_at, across, 0.0)
    for i in range(layers - 1):
        lo = (layers - 1 + i) * ranks
        after = jnp.zeros_like(square)
        for k in range(i + 1, layers):
            after = after + jnp.where(k > section_at, kappas[k], 0.0)
        across = dot_first(own_error, actives[i], exact) * both
        mixed_ref[:ranks, lo : lo + ranks] = jnp.where(i < section_at, across, 0.0)
        mixed_ref[ranks:, lo : lo + ranks] = (
            dot_first(own_active, after * actives[i], exact) * (-scale_r * scale_r)
        )


def chain(at, projections, square, grams, features, per_micro):
    sections = len(projections)
    tokens, wide = projections[0].shape
    ranks = wide // (3 * sections)
    inputs = [*projections, square, *grams]
    kernel = functools.partial(chain_kernel, sections, len(grams), features, per_micro)
    return pl.pallas_call(
        kernel,
        in_specs=[pl.BlockSpec(memory_space=pltpu.SMEM)]
        + [pl.BlockSpec(memory_space=pltpu.VMEM)] * len(inputs),
        out_specs=[pl.BlockSpec(memory_space=pltpu.VMEM)] * 2,
        out_shape=[
            jax.ShapeDtypeStruct((2 * ranks, 2 * tokens), bf16),
            jax.ShapeDtypeStruct((2 * ranks, 2 * (sections - 1) * ranks), f32),
        ],
        compiler_params=params(),
        name="chain",
    )(at, *inputs)


def gradient_kernel(tensors, at, factor_ref, h_ref, g_ref, out_ref):
    columns = h_ref.shape[1] // tensors
    for owner in range(tensors):
        cut = pl.ds(owner * columns, columns)
        stacked = jnp.concatenate([h_ref[:, cut], g_ref[:, cut]], axis=0)
        block = jnp.dot(factor_ref[...], stacked, preferred_element_type=f32)
        out_ref[0, at[5] ^ owner] = block.astype(bf16)


def gradient(at, factors, hidden, cot, first, replicas, tensors):
    tokens, features = hidden.shape
    width = features // replicas
    rows = factors.shape[0]

    def chosen(i, at):
        return (0, at[3] ^ (first + 2 * i))

    return pl.pallas_call(
        functools.partial(gradient_kernel, tensors),
        grid_spec=pltpu.PrefetchScalarGridSpec(
            num_scalar_prefetch=1,
            grid=(replicas // 2,),
            in_specs=[
                pl.BlockSpec(factors.shape, lambda i, at: (0, 0)),
                pl.BlockSpec((tokens, width), chosen),
                pl.BlockSpec((tokens, width), chosen),
            ],
            out_specs=pl.BlockSpec(
                (1, tensors, rows, width // tensors), lambda i, at: (i, 0, 0, 0)
            ),
        ),
        out_shape=jax.ShapeDtypeStruct((replicas // 2, tensors, rows, width // tensors), bf16),
        compiler_params=params(),
        cost_estimate=pl.CostEstimate(
            flops=2 * rows * tokens * features,
            bytes_accessed=(2 * tokens + rows) * features,
            transcendentals=0,
        ),
        name="gradient",
    )(at, factors, hidden, cot)


def update_kernel(
    count, *refs
):
    pieces = refs[:count]
    mixed_ref, right_ref = refs[count : count + 2]
    state = refs[count + 2 : count + 8]
    outs = refs[count + 8 : count + 14]
    share_ref = refs[count + 14]
    grad = jnp.dot(
        mixed_ref[...], right_ref[...].astype(f32), preferred_element_type=f32, precision=exact
    )
    for piece in pieces:
        grad = grad + piece[...].reshape(grad.shape).astype(f32)
    ranks = grad.shape[0] // 2
    for which in range(2):
        own = grad[which * ranks : (which + 1) * ranks]
        master, moment, second = (state[2 * kind + which][0] for kind in range(3))
        moment = beta_one * moment + (1.0 - beta_one) * own
        second = beta_two * second + (1.0 - beta_two) * own * own
        master = master - learn_rate * (
            moment / first_fix / (jnp.sqrt(second / second_fix) + adam_eps) + decay_rate * master
        )
        outs[which][0] = master
        outs[2 + which][0] = moment
        outs[4 + which][0] = second
        share_ref[which * ranks : (which + 1) * ranks] = master.astype(bf16)


def update(pieces, mixed, right, state):
    _, ranks, columns = state[0].shape
    width = columns // 2

    def leading(piece):
        lead = piece.ndim - 2
        return pl.BlockSpec(
            (1,) * lead + (2 * ranks, width), lambda i: (0,) * lead + (0, i)
        )

    own = pl.BlockSpec((1, ranks, width), lambda i: (0, 0, i))
    return pl.pallas_call(
        functools.partial(update_kernel, len(pieces)),
        grid=(columns // width,),
        in_specs=[leading(piece) for piece in pieces]
        + [
            pl.BlockSpec(mixed.shape, lambda i: (0, 0)),
            pl.BlockSpec((right.shape[0], width), lambda i: (0, i)),
        ]
        + [own] * 6,
        out_specs=[own] * 6 + [pl.BlockSpec((2 * ranks, width), lambda i: (0, i))],
        out_shape=[jax.ShapeDtypeStruct(state[0].shape, f32)] * 6
        + [jax.ShapeDtypeStruct((2 * ranks, columns), bf16)],
        compiler_params=params(),
        name="update",
    )(*pieces, mixed, right, *state)


def place_kernel(orders, at, *refs):
    groups = len(orders)
    window = (refs[:groups], refs[groups : 2 * groups])
    down_ref, up_ref, zeros, sem = refs[2 * groups :]
    slots, ranks, features = down_ref.shape
    tensors, _, columns = window[0][0].shape
    first, after, replica_at, section_at, tensor_at = at[0], at[1], at[3], at[4], at[5]
    zeros[...] = jnp.zeros_like(zeros)

    def move(slot, distance, go):
        for group, order in enumerate(orders):
            for hop in range(tensors):
                owner = (replica_at ^ order) * tensors + (tensor_at ^ hop)
                cut = pl.ds(pl.multiple_of(owner * columns, columns), columns)
                for which, out in enumerate((down_ref, up_ref)):
                    target = out.at[slot, :, cut]
                    if distance is None:
                        source = zeros
                    else:
                        rows = pl.ds(which * ranks, ranks)
                        source = window[distance][group].at[hop, rows, :]
                    go(pltpu.make_async_copy(source, target, sem))

    for act in (lambda copy: copy.start(), lambda copy: copy.wait()):
        for slot in range(slots):
            layer = first + slot
            present = layer < after
            for distance in range(2):

                @pl.when(present & (layer - section_at == distance))
                def _():
                    move(slot, distance, act)

            @pl.when(jnp.logical_not(present))
            def _():
                move(slot, None, act)


def place(at, own, following, orders, slots, features):
    _, rows, columns = own[0].shape
    ranks = rows // 2
    anywhere = pl.BlockSpec(memory_space=pl.ANY)
    shape = jax.ShapeDtypeStruct((slots, ranks, features), bf16)
    return pl.pallas_call(
        functools.partial(place_kernel, orders),
        in_specs=[pl.BlockSpec(memory_space=pltpu.SMEM)]
        + [anywhere] * (len(own) + len(following)),
        out_specs=[anywhere] * 2,
        out_shape=[shape] * 2,
        scratch_shapes=[pltpu.VMEM((ranks, columns), bf16), pltpu.SemaphoreType.DMA],
        compiler_params=params(),
        name="place",
    )(at, *own, *following)


def swapped(block, axis, distance):
    route = [(i, i ^ distance) for i in range(lax.axis_size(axis))]
    return lax.ppermute(block, axis, route)


def from_next(block, distance=1):
    size = lax.axis_size("section")
    route = [((i + distance) % size, i) for i in range(size)]
    return lax.ppermute(block, "section", route)


def following_layer(block):
    size = lax.axis_size("section")
    return lax.ppermute(block, "section", [(i + 1, i) for i in range(size - 1)])


def summed(*blocks):
    total = blocks[0].astype(f32)
    for block in blocks[1:]:
        total = total + block.astype(f32)
    return total.astype(bf16)


def on_device(
    inputs,
    cotangent,
    micro_counts,
    bounds,
    holder_down,
    holder_up,
    master_down,
    master_up,
    moment_down,
    moment_up,
    second_down,
    second_up,
):
    replica_at = lax.axis_index("replica")
    section_at = lax.axis_index("section")
    tensor_at = lax.axis_index("tensor")
    sections = lax.axis_size("section")
    replicas = lax.axis_size("replica")
    tensors = lax.axis_size("tensor")
    assert replicas == 4 and tensors == 4
    _, micros, per_micro, features = inputs.shape
    slots, ranks = holder_down.shape[2:4]
    at = jnp.stack(
        [
            bounds[replica_at, section_at],
            bounds[replica_at, section_at + 1],
            micro_counts[replica_at],
            replica_at,
            section_at,
            tensor_at,
        ]
    ).astype(jnp.int32)
    hidden = inputs.reshape(micros * per_micro, features)
    cot = cotangent.reshape(micros * per_micro, features)

    owned = jnp.concatenate([master_down[0], master_up[0]], axis=0).astype(bf16)
    around = [owned] + [from_next(owned, d) for d in range(1, sections)]
    table, right = gram(at, around)
    table = table + sum(swapped(table, "replica", k) for k in range(1, replicas))
    tables = [table] + [swapped(table, "tensor", k) for k in range(1, tensors)]

    projected, square = project(
        at, hidden, cot, holder_down[0, 0], holder_up[0, 0], sections, per_micro
    )
    projections = [projected] + [from_next(projected, d) for d in range(1, sections)]
    factors, mixed = chain(at, projections, square, tables, features, per_micro)

    sent = gradient(at, factors, hidden, cot, 1, replicas, tensors)
    kept = gradient(at, factors, hidden, cot, 0, replicas, tensors)
    mixed = lax.psum(mixed, ("replica", "tensor"))
    near = swapped(sent, "replica", 1)
    across = swapped(summed(kept[1], near[1]), "replica", 2)
    along = [
        swapped(summed(kept[0, k], near[0, k], across[k]), "tensor", k) for k in range(1, tensors)
    ]
    state = [master_down, master_up, moment_down, moment_up, second_down, second_up]
    updated = update([kept, near, across, *along], mixed, right, state)
    share = updated[6]

    own_line = jnp.stack([share] + [swapped(share, "tensor", k) for k in range(1, tensors)])
    next_line = following_layer(own_line)
    own_far = swapped(own_line, "replica", 2)
    half = tensors // 2
    next_far = jnp.concatenate(
        [following_layer(own_far[:half]), swapped(next_line[half:], "replica", 2)], axis=0
    )
    own = [own_line, own_far, swapped(own_line, "replica", 1), swapped(own_far, "replica", 1)]
    following = [
        next_line,
        next_far,
        swapped(next_line, "replica", 1),
        swapped(next_far, "replica", 1),
    ]
    placed = place(at, own, following, (0, 2, 1, 3), slots, features)
    return (placed[0][None, None], placed[1][None, None], *updated[:6])


def solution(mesh):
    held = P("replica", "section", None, None, None)
    owned = P("section", None, ("replica", "tensor"))
    tokens = P("replica", None, "tensor", None)
    return jax.shard_map(
        on_device,
        mesh=mesh,
        in_specs=(tokens, tokens, P(), P(), held, held) + (owned,) * 6,
        out_specs=(held, held) + (owned,) * 6,
        check_vma=False,
    )
```

```python
import functools
import math

import jax
import jax.numpy as jnp
from jax import lax
from jax.experimental import pallas as pl
from jax.experimental.pallas import tpu as pltpu
from jax.sharding import PartitionSpec as P

norm_eps = 1e-06
learn_rate = 0.01
beta_one = 0.9
beta_two = 0.95
decay_rate = 0.1
adam_eps = 1e-08
first_fix = 0.9999734386011124
second_fix = 0.9940794707796659

f32 = jnp.float32
bf16 = jnp.bfloat16
exact = lax.Precision.HIGHEST
in_smem = pl.BlockSpec(memory_space=pltpu.SMEM)
in_vmem = pl.BlockSpec(memory_space=pltpu.VMEM)
anywhere = pl.BlockSpec(memory_space=pl.ANY)


def held_layers(bounds):
    at_row = lax.axis_index("replica")
    at_column = lax.axis_index("section")
    return bounds[at_row, at_column], bounds[at_row, at_column + 1]


def counted_rows(counts, tokens, per_micro):
    rows = lax.broadcasted_iota(jnp.int32, (tokens, 1), 0)
    return rows < counts[lax.axis_index("replica")] * per_micro


def dot_last(x, y, precision=None):
    return lax.dot_general(
        x, y, (((1,), (1,)), ((), ())), preferred_element_type=f32, precision=precision
    )


def dot_first(x, y, precision=None):
    return lax.dot_general(
        x, y, (((0,), (0,)), ((), ())), preferred_element_type=f32, precision=precision
    )


def row_sum(x):
    return jnp.sum(x, axis=-1, keepdims=True)


def project_kernel(layers, per_micro, bounds, counts, h_ref, g_ref, down_ref, up_ref, out_ref, sq_ref, acc_h, acc_g):
    step = pl.program_id(0)
    slots, ranks, width = down_ref.shape

    @pl.when(step == 0)
    def _():
        acc_h[...] = jnp.zeros_like(acc_h)
        acc_g[...] = jnp.zeros_like(acc_g)
        sq_ref[...] = jnp.zeros_like(sq_ref)

    h = h_ref[...]
    ups = up_ref[...].reshape(slots * ranks, width)
    both = jnp.concatenate([down_ref[...].reshape(slots * ranks, width), ups], axis=0)
    acc_h[...] += dot_last(h, both)
    acc_g[...] += dot_last(g_ref[...], ups)
    wide = h.astype(f32)
    sq_ref[...] += row_sum(wide * wide)

    @pl.when(step == pl.num_programs(0) - 1)
    def _():
        first, after = held_layers(bounds)
        ph = acc_h[...]
        pg = jnp.where(counted_rows(counts, h_ref.shape[0], per_micro), acc_g[...], 0.0)
        pieces = []
        for slot in range(slots):
            lo, hi = slot * ranks, (slot + 1) * ranks
            pieces.append(
                jnp.concatenate(
                    [ph[:, lo:hi], ph[:, slots * ranks + lo : slots * ranks + hi], pg[:, lo:hi]],
                    axis=1,
                )
            )
        for layer in range(layers):
            total = jnp.zeros_like(pieces[0])
            for slot in range(slots):
                here = (first + slot == layer) & (layer < after)
                total = jnp.where(here, pieces[slot], total)
            out_ref[:, layer * 3 * ranks : (layer + 1) * 3 * ranks] = total


def project(bounds, counts, hidden, cot, downs, ups, layers, per_micro):
    tokens, features = hidden.shape
    slots, ranks, _ = downs.shape
    width = features // 8
    kernel = functools.partial(project_kernel, layers, per_micro)
    return pl.pallas_call(
        kernel,
        grid_spec=pltpu.PrefetchScalarGridSpec(
            num_scalar_prefetch=2,
            grid=(features // width,),
            in_specs=[
                pl.BlockSpec((tokens, width), lambda i, *_: (0, i)),
                pl.BlockSpec((tokens, width), lambda i, *_: (0, i)),
                pl.BlockSpec((slots, ranks, width), lambda i, *_: (0, 0, i)),
                pl.BlockSpec((slots, ranks, width), lambda i, *_: (0, 0, i)),
            ],
            out_specs=[
                pl.BlockSpec((tokens, layers * 3 * ranks), lambda i, *_: (0, 0)),
                pl.BlockSpec((tokens, 128), lambda i, *_: (0, 0)),
            ],
            scratch_shapes=[
                pltpu.VMEM((tokens, 2 * slots * ranks), f32),
                pltpu.VMEM((tokens, slots * ranks), f32),
            ],
        ),
        out_shape=[
            jax.ShapeDtypeStruct((tokens, layers * 3 * ranks), f32),
            jax.ShapeDtypeStruct((tokens, 128), f32),
        ],
        cost_estimate=pl.CostEstimate(
            flops=6 * tokens * slots * ranks * features,
            bytes_accessed=4 * (tokens + slots * ranks) * features,
            transcendentals=0,
        ),
        name="project",
    )(bounds, counts, hidden, cot, downs, ups)


def gram_kernel(sections, *refs):
    around = refs[:sections]
    gram_ref, right_ref = refs[sections:]
    section_at = lax.axis_index("section")
    ranks = around[0].shape[0] // 2
    layers = []
    for layer in range(sections):
        distance = lax.rem(layer - section_at + sections, sections)
        chosen = around[0][...]
        for step in range(1, sections):
            chosen = jnp.where(distance == step, around[step][...], chosen)
        layers.append(chosen)
    lefts = [chosen[ranks:] for chosen in layers[:-1]]
    right = jnp.concatenate([chosen[:ranks] for chosen in layers[1:]] + lefts, axis=0)
    right_ref[...] = right
    gram_ref[...] = dot_last(jnp.concatenate(lefts, axis=0), right)


def gram(around):
    sections = len(around)
    ranks = around[0].shape[0] // 2
    columns = around[0].shape[1]
    before = (sections - 1) * ranks
    return pl.pallas_call(
        functools.partial(gram_kernel, sections),
        in_specs=[in_vmem] * sections,
        out_specs=[in_vmem] * 2,
        out_shape=[
            jax.ShapeDtypeStruct((before, 2 * before), f32),
            jax.ShapeDtypeStruct((2 * before, columns), bf16),
        ],
        name="gram",
    )(*around)


def chain_kernel(sections, parts, features, per_micro, counts, *refs):
    projections = refs[:sections]
    sq_ref = refs[sections]
    grams = refs[sections + 1 : sections + 1 + parts]
    down_ref, up_ref, mixed_ref = refs[sections + 1 + parts :]
    layers = sections
    section_at = lax.axis_index("section")
    tokens = sq_ref.shape[0]
    total = projections[0][...]
    for other in projections[1:]:
        total = total + other[...]
    table = grams[0][...]
    for other in grams[1:]:
        table = table + other[...]
    ranks = total.shape[1] // (3 * layers)
    scale_d = 1.0 / math.sqrt(features)
    scale_r = 1.0 / math.sqrt(ranks)

    def part(layer, which):
        at_column = (3 * layer + which) * ranks
        return total[:, at_column : at_column + ranks]

    def up_down(i, layer):
        return table[i * ranks : (i + 1) * ranks, (layer - 1) * ranks : layer * ranks]

    def up_up(i, j):
        at_column = (layers - 1 + j) * ranks
        return table[i * ranks : (i + 1) * ranks, at_column : at_column + ranks]

    def times(x, y):
        return jnp.dot(x, y, preferred_element_type=f32, precision=exact)

    square = sq_ref[:, 0:1]
    inverses, inners, actives, sigmoids = [], [], [], []
    on_up = [[part(l, 1) for l in range(layers - 1)]]
    for layer in range(layers):
        inverse = lax.rsqrt(jnp.maximum(square, 0.0) * (1.0 / features) + norm_eps)
        on_down = part(layer, 0)
        for i in range(layer):
            on_down = on_down + scale_r * times(actives[i], up_down(i, layer))
        inner = on_down * (inverse * scale_d)
        sigmoid = jax.nn.sigmoid(inner)
        active = (inner * sigmoid).astype(bf16).astype(f32)
        inverses.append(inverse)
        inners.append(inner)
        sigmoids.append(sigmoid)
        actives.append(active)
        if layer < layers - 1:
            now = on_up[-1]
            grown = [now[l] + scale_r * times(active, up_up(layer, l)) for l in range(layers - 1)]
            square = square + scale_r * row_sum(active * (now[layer] + grown[layer]))
            on_up.append(grown)
    scaled = [None] * layers
    kappas = [None] * layers
    for layer in reversed(range(layers)):
        incoming = part(layer, 2)
        for k in range(layer + 1, layers):
            incoming = incoming + scale_d * dot_last(scaled[k], up_down(layer, k), exact)
            incoming = incoming - kappas[k] * on_up[k][layer]
        sigmoid, inner = sigmoids[layer], inners[layer]
        slope = sigmoid * (1.0 + inner * (1.0 - sigmoid))
        error = incoming * scale_r * slope
        scaled[layer] = error * inverses[layer]
        kappas[layer] = (
            inverses[layer] * inverses[layer] * (row_sum(error * inner) * (1.0 / features))
        )

    def owned(values):
        chosen = values[0]
        for layer in range(1, layers):
            chosen = jnp.where(section_at == layer, values[layer], chosen)
        return chosen

    own_error = owned(scaled)
    own_active = owned(actives)
    counted = counted_rows(counts, tokens, per_micro)
    later = jnp.zeros_like(square)
    for k in range(1, layers):
        later = later + jnp.where(k > section_at, kappas[k], 0.0)
    down_ref[...] = (own_error * scale_d).T.astype(bf16)
    on_hidden = -scale_r * later * own_active
    on_cot = jnp.where(counted, own_active * scale_r, 0.0)
    up_ref[...] = jnp.concatenate([on_hidden.T, on_cot.T], axis=1).astype(bf16)
    both = scale_d * scale_r
    for k in range(1, layers):
        cut = slice((k - 1) * ranks, k * ranks)
        across = dot_first(own_active, scaled[k], exact) * both
        mixed_ref[:ranks, cut] = jnp.zeros_like(across)
        mixed_ref[ranks:, cut] = jnp.where(k > section_at, across, 0.0)
    for i in range(layers - 1):
        cut = slice((layers - 1 + i) * ranks, (layers + i) * ranks)
        after = jnp.zeros_like(square)
        for k in range(i + 1, layers):
            after = after + jnp.where(k > section_at, kappas[k], 0.0)
        across = dot_first(own_error, actives[i], exact) * both
        mixed_ref[:ranks, cut] = jnp.where(i < section_at, across, 0.0)
        across = dot_first(own_active, after * actives[i], exact)
        mixed_ref[ranks:, cut] = across * (-scale_r * scale_r)


def chain(counts, projections, square, grams, features, per_micro):
    sections = len(projections)
    tokens, wide = projections[0].shape
    ranks = wide // (3 * sections)
    inputs = [*projections, square, *grams]
    kernel = functools.partial(chain_kernel, sections, len(grams), features, per_micro)
    return pl.pallas_call(
        kernel,
        in_specs=[in_smem] + [in_vmem] * len(inputs),
        out_specs=[in_vmem] * 3,
        out_shape=[
            jax.ShapeDtypeStruct((ranks, tokens), bf16),
            jax.ShapeDtypeStruct((ranks, 2 * tokens), bf16),
            jax.ShapeDtypeStruct((2 * ranks, 2 * (sections - 1) * ranks), f32),
        ],
        name="chain",
    )(counts, *inputs)


def gradient_kernel(tensors, factor_ref, *refs):
    tokens, out_ref = refs[:-1], refs[-1]
    columns = tokens[0].shape[1] // tensors
    tensor_at = lax.axis_index("tensor")
    for owner in range(tensors):
        cut = pl.ds(owner * columns, columns)
        stacked = jnp.concatenate([ref[:, cut] for ref in tokens], axis=0)
        block = jnp.dot(factor_ref[...], stacked, preferred_element_type=f32)
        out_ref[0, tensor_at ^ owner] = block.astype(bf16)


def gradient(factors, sources, first, replicas, tensors):
    tokens, features = sources[0].shape
    width = features // replicas
    rows, depth = factors.shape

    def chosen(i):
        return (0, lax.axis_index("replica") ^ (first + 2 * i))

    return pl.pallas_call(
        functools.partial(gradient_kernel, tensors),
        grid=(replicas // 2,),
        in_specs=[pl.BlockSpec(factors.shape, lambda i: (0, 0))]
        + [pl.BlockSpec((tokens, width), chosen)] * len(sources),
        out_specs=pl.BlockSpec((1, tensors, rows, width // tensors), lambda i: (i, 0, 0, 0)),
        out_shape=jax.ShapeDtypeStruct((replicas // 2, tensors, rows, width // tensors), bf16),
        cost_estimate=pl.CostEstimate(
            flops=rows * depth * features,
            bytes_accessed=(depth + rows) * features,
            transcendentals=0,
        ),
        name="gradient",
    )(factors, *sources)


def update_kernel(count, *refs):
    pieces = refs[:count]
    mixes = refs[count : -8]
    right_ref, master_ref, moment_ref, second_ref = refs[-8:-4]
    new_master, new_moment, new_second, share_ref = refs[-4:]
    mixed = mixes[0][...]
    for other in mixes[1:]:
        mixed = mixed + other[...]
    grad = jnp.dot(mixed, right_ref[...].astype(f32), preferred_element_type=f32, precision=exact)
    for piece in pieces:
        grad = grad + piece[...].reshape(grad.shape).astype(f32)
    moment = beta_one * moment_ref[0] + (1.0 - beta_one) * grad
    second = beta_two * second_ref[0] + (1.0 - beta_two) * grad * grad
    master = master_ref[0]
    master = master - learn_rate * (
        moment / first_fix / (jnp.sqrt(second / second_fix) + adam_eps) + decay_rate * master
    )
    new_master[0] = master
    new_moment[0] = moment
    new_second[0] = second
    share_ref[...] = master.astype(bf16)


def update(pieces, mixes, which, right, state):
    _, ranks, columns = state[0].shape
    width = columns // 2

    def leading(piece):
        lead = piece.ndim - 2
        return pl.BlockSpec((1,) * lead + (ranks, width), lambda i: (0,) * lead + (0, i))

    own = pl.BlockSpec((1, ranks, width), lambda i: (0, 0, i))
    return pl.pallas_call(
        functools.partial(update_kernel, len(pieces)),
        grid=(columns // width,),
        in_specs=[leading(piece) for piece in pieces]
        + [pl.BlockSpec((ranks, mixed.shape[1]), lambda i: (which, 0)) for mixed in mixes]
        + [pl.BlockSpec((right.shape[0], width), lambda i: (0, i))]
        + [own] * 3,
        out_specs=[own] * 3 + [pl.BlockSpec((ranks, width), lambda i: (0, i))],
        out_shape=[jax.ShapeDtypeStruct(state[0].shape, f32)] * 3
        + [jax.ShapeDtypeStruct((ranks, columns), bf16)],
        name="update",
    )(*pieces, *mixes, right, *state)


def place_kernel(orders, bounds, *refs):
    groups = len(orders)
    window = (refs[:groups], refs[groups : 2 * groups])
    out_ref, zeros, sem = refs[2 * groups :]
    slots = out_ref.shape[0]
    tensors, _, columns = window[0][0].shape
    first, after = held_layers(bounds)
    replica_at = lax.axis_index("replica")
    section_at = lax.axis_index("section")
    tensor_at = lax.axis_index("tensor")
    zeros[...] = jnp.zeros_like(zeros)

    def move(slot, distance, go):
        for group, order in enumerate(orders):
            for hop in range(tensors):
                owner = (replica_at ^ order) * tensors + (tensor_at ^ hop)
                cut = pl.ds(pl.multiple_of(owner * columns, columns), columns)
                source = zeros if distance is None else window[distance][group].at[hop]
                go(pltpu.make_async_copy(source, out_ref.at[slot, :, cut], sem))

    for act in (lambda copy: copy.start(), lambda copy: copy.wait()):
        for slot in range(slots):
            layer = first + slot
            present = layer < after
            for distance in range(2):

                @pl.when(present & (layer - section_at == distance))
                def _():
                    move(slot, distance, act)

            @pl.when(jnp.logical_not(present))
            def _():
                move(slot, None, act)


def place(bounds, own, following, orders, slots, features):
    _, ranks, columns = own[0].shape
    return pl.pallas_call(
        functools.partial(place_kernel, orders),
        in_specs=[in_smem] + [anywhere] * (len(own) + len(following)),
        out_specs=anywhere,
        out_shape=jax.ShapeDtypeStruct((slots, ranks, features), bf16),
        scratch_shapes=[pltpu.VMEM((ranks, columns), bf16), pltpu.SemaphoreType.DMA],
        name="place",
    )(bounds, *own, *following)


def swapped(block, axis, distance):
    route = [(i, i ^ distance) for i in range(lax.axis_size(axis))]
    return lax.ppermute(block, axis, route)


def swaps(block, axis):
    return [swapped(block, axis, k) for k in range(1, lax.axis_size(axis))]


def from_next(block, distance=1):
    size = lax.axis_size("section")
    route = [((i + distance) % size, i) for i in range(size)]
    return lax.ppermute(block, "section", route)


def following_layer(block):
    size = lax.axis_size("section")
    return lax.ppermute(block, "section", [(i + 1, i) for i in range(size - 1)])


def summed(*blocks):
    total = blocks[0].astype(f32)
    for block in blocks[1:]:
        total = total + block.astype(f32)
    return total.astype(bf16)


def reduced(factors, sources, replicas, tensors):
    sent = gradient(factors, sources, 1, replicas, tensors)
    near = swapped(sent, "replica", 1)
    kept = gradient(factors, sources, 0, replicas, tensors)
    across = swapped(summed(kept[1], near[1]), "replica", 2)
    along = [
        swapped(summed(kept[0, k], near[0, k], across[k]), "tensor", k) for k in range(1, tensors)
    ]
    return [kept, near, across, *along]


def gathered(share):
    own_line = jnp.stack([share] + swaps(share, "tensor"))
    half = own_line.shape[0] // 2
    next_line = following_layer(own_line)
    own_far = swapped(own_line, "replica", 2)
    next_far = jnp.concatenate(
        [following_layer(own_far[:half]), swapped(next_line[half:], "replica", 2)], axis=0
    )
    return [
        [own_line, own_far, swapped(own_line, "replica", 1), swapped(own_far, "replica", 1)],
        [next_line, next_far, swapped(next_line, "replica", 1), swapped(next_far, "replica", 1)],
    ]


def on_device(
    inputs,
    cotangent,
    micro_counts,
    bounds,
    holder_down,
    holder_up,
    master_down,
    master_up,
    moment_down,
    moment_up,
    second_down,
    second_up,
):
    sections = lax.axis_size("section")
    replicas = lax.axis_size("replica")
    tensors = lax.axis_size("tensor")
    assert replicas == 4 and tensors == 4
    _, micros, per_micro, features = inputs.shape
    slots = holder_down.shape[2]
    hidden = inputs.reshape(micros * per_micro, features)
    cot = cotangent.reshape(micros * per_micro, features)

    owned = jnp.concatenate([master_down[0], master_up[0]], axis=0).astype(bf16)
    around = [owned] + [from_next(owned, d) for d in range(1, sections)]
    table, right = gram(around)
    table = table + sum(swaps(table, "replica"))
    tables = [table] + swaps(table, "tensor")

    projected, square = project(
        bounds, micro_counts, hidden, cot, holder_down[0, 0], holder_up[0, 0], sections, per_micro
    )
    projections = [projected] + [from_next(projected, d) for d in range(1, sections)]
    factors_down, factors_up, mixed = chain(
        micro_counts, projections, square, tables, features, per_micro
    )

    pieces_down = reduced(factors_down, [hidden], replicas, tensors)
    pieces_up = reduced(factors_up, [hidden, cot], replicas, tensors)
    mixed = mixed + sum(swaps(mixed, "replica"))
    mixes = [mixed] + swaps(mixed, "tensor")
    down = update(pieces_down, mixes, 0, right, [master_down, moment_down, second_down])
    up = update(pieces_up, mixes, 1, right, [master_up, moment_up, second_up])
    new_down, new_up = (
        place(bounds, *gathered(made[3]), (0, 2, 1, 3), slots, features)[None, None]
        for made in (down, up)
    )
    return (new_down, new_up, down[0], up[0], down[1], up[1], down[2], up[2])


def solution(mesh):
    held = P("replica", "section", None, None, None)
    owned = P("section", None, ("replica", "tensor"))
    tokens = P("replica", None, "tensor", None)
    return jax.shard_map(
        on_device,
        mesh=mesh,
        in_specs=(tokens, tokens, P(), P(), held, held) + (owned,) * 6,
        out_specs=(held, held) + (owned,) * 6,
        check_vma=False,
    )
```

```python
import functools
import math

import jax
import jax.numpy as jnp
from jax import lax
from jax.experimental import pallas as pl
from jax.experimental.pallas import tpu as pltpu
from jax.sharding import PartitionSpec as P

norm_eps = 1e-06
learn_rate = 0.01
beta_one = 0.9
beta_two = 0.95
decay_rate = 0.1
adam_eps = 1e-08
first_fix = 0.9999734386011124
second_fix = 0.9940794707796659

f32 = jnp.float32
bf16 = jnp.bfloat16
exact = lax.Precision.HIGHEST
in_smem = pl.BlockSpec(memory_space=pltpu.SMEM)
in_vmem = pl.BlockSpec(memory_space=pltpu.VMEM)
in_hbm = pl.BlockSpec(memory_space=pltpu.HBM)
limited = pltpu.CompilerParams(vmem_limit_bytes=16 * 1024 * 1024)


def held_layers(bounds):
    at_row = lax.axis_index("replica")
    at_column = lax.axis_index("section")
    return bounds[at_row, at_column], bounds[at_row, at_column + 1]


def counted_rows(counts, tokens, per_micro):
    rows = lax.broadcasted_iota(jnp.int32, (tokens, 1), 0)
    return rows < counts[lax.axis_index("replica")] * per_micro


def dot_last(x, y, precision=None):
    return lax.dot_general(
        x, y, (((1,), (1,)), ((), ())), preferred_element_type=f32, precision=precision
    )


def dot_first(x, y, precision=None):
    return lax.dot_general(
        x, y, (((0,), (0,)), ((), ())), preferred_element_type=f32, precision=precision
    )


def row_sum(x):
    return jnp.sum(x, axis=-1, keepdims=True)


def project_kernel(layers, per_micro, steps, bounds, counts, h_in, g_in, down_in, up_in, *refs):
    out_ref, sq_ref, h_ref, g_ref, weights, sems = refs
    slots, ranks, features = down_in.shape
    tokens = h_ref.shape[0]
    width = features // steps
    copies = []
    for step in range(steps):
        cut = pl.ds(step * width, width)
        moves = [
            (h_in.at[:, cut], h_ref.at[:, cut]),
            (g_in.at[:, cut], g_ref.at[:, cut]),
        ]
        for slot in range(slots):
            for which, source in enumerate((down_in, up_in)):
                rows = pl.ds((which * slots + slot) * ranks, ranks)
                moves.append((source.at[slot, :, cut], weights.at[rows, cut]))
        copies.append(
            [
                pltpu.make_async_copy(source, target, sems.at[step, i])
                for i, (source, target) in enumerate(moves)
            ]
        )
        for copy in copies[-1]:
            copy.start()
    ph = jnp.zeros((tokens, 2 * slots * ranks), f32)
    pg = jnp.zeros((tokens, slots * ranks), f32)
    square = jnp.zeros((tokens, 128), f32)
    for step in range(steps):
        for copy in copies[step]:
            copy.wait()
        cut = pl.ds(step * width, width)
        h = h_ref[:, cut]
        w = weights[:, cut]
        ph = ph + dot_last(h, w)
        pg = pg + dot_last(g_ref[:, cut], w[slots * ranks :])
        wide = h.astype(f32)
        wide = wide * wide
        for lane in range(0, width, 128):
            square = square + wide[:, lane : lane + 128]
    sq_ref[...] = jnp.broadcast_to(row_sum(square), square.shape)
    first, after = held_layers(bounds)
    pg = jnp.where(counted_rows(counts, tokens, per_micro), pg, 0.0)
    pieces = []
    for slot in range(slots):
        lo, hi = slot * ranks, (slot + 1) * ranks
        pieces.append(
            jnp.concatenate(
                [ph[:, lo:hi], ph[:, slots * ranks + lo : slots * ranks + hi], pg[:, lo:hi]],
                axis=1,
            )
        )
    for layer in range(layers):
        total = jnp.zeros_like(pieces[0])
        for slot in range(slots):
            here = (first + slot == layer) & (layer < after)
            total = jnp.where(here, pieces[slot], total)
        out_ref[:, layer * 3 * ranks : (layer + 1) * 3 * ranks] = total


def project(bounds, counts, hidden, cot, downs, ups, layers, per_micro):
    tokens, features = hidden.shape
    slots, ranks, _ = downs.shape
    steps = 8
    kernel = functools.partial(project_kernel, layers, per_micro, steps)
    return pl.pallas_call(
        kernel,
        in_specs=[in_smem] * 2 + [in_hbm] * 4,
        out_specs=[in_vmem] * 4,
        out_shape=[
            jax.ShapeDtypeStruct((tokens, layers * 3 * ranks), f32),
            jax.ShapeDtypeStruct((tokens, 128), f32),
            jax.ShapeDtypeStruct((tokens, features), bf16),
            jax.ShapeDtypeStruct((tokens, features), bf16),
        ],
        scratch_shapes=[
            pltpu.VMEM((2 * slots * ranks, features), bf16),
            pltpu.SemaphoreType.DMA((steps, 2 + 2 * slots)),
        ],
        compiler_params=limited,
        cost_estimate=pl.CostEstimate(
            flops=6 * tokens * slots * ranks * features,
            bytes_accessed=4 * (tokens + slots * ranks) * features,
            transcendentals=0,
        ),
        name="project",
    )(bounds, counts, hidden, cot, downs, ups)


def gram_kernel(sections, *refs):
    around = refs[:sections]
    gram_ref, right_ref = refs[sections:]
    section_at = lax.axis_index("section")
    ranks = around[0].shape[0] // 2
    layers = []
    for layer in range(sections):
        distance = lax.rem(layer - section_at + sections, sections)
        chosen = around[0][...]
        for step in range(1, sections):
            chosen = jnp.where(distance == step, around[step][...], chosen)
        layers.append(chosen)
    lefts = [chosen[ranks:] for chosen in layers[:-1]]
    right = jnp.concatenate([chosen[:ranks] for chosen in layers[1:]] + lefts, axis=0)
    right_ref[...] = right
    gram_ref[...] = dot_last(jnp.concatenate(lefts, axis=0), right)


def gram(around):
    sections = len(around)
    ranks = around[0].shape[0] // 2
    columns = around[0].shape[1]
    before = (sections - 1) * ranks
    return pl.pallas_call(
        functools.partial(gram_kernel, sections),
        in_specs=[in_vmem] * sections,
        out_specs=[in_vmem] * 2,
        out_shape=[
            jax.ShapeDtypeStruct((before, 2 * before), f32),
            jax.ShapeDtypeStruct((2 * before, columns), bf16),
        ],
        compiler_params=limited,
        name="gram",
    )(*around)


def chain_kernel(sections, parts, features, per_micro, counts, *refs):
    projections = refs[:sections]
    sq_ref = refs[sections]
    grams = refs[sections + 1 : sections + 1 + parts]
    factor_ref, mixed_ref = refs[sections + 1 + parts :]
    layers = sections
    section_at = lax.axis_index("section")
    tokens = sq_ref.shape[0]
    total = projections[0][...]
    for other in projections[1:]:
        total = total + other[...]
    table = grams[0][...]
    for other in grams[1:]:
        table = table + other[...]
    ranks = total.shape[1] // (3 * layers)
    scale_d = 1.0 / math.sqrt(features)
    scale_r = 1.0 / math.sqrt(ranks)

    def part(layer, which):
        at_column = (3 * layer + which) * ranks
        return total[:, at_column : at_column + ranks]

    def up_down(i, layer):
        return table[i * ranks : (i + 1) * ranks, (layer - 1) * ranks : layer * ranks]

    def up_up(i, j):
        at_column = (layers - 1 + j) * ranks
        return table[i * ranks : (i + 1) * ranks, at_column : at_column + ranks]

    def times(x, y):
        return jnp.dot(x, y, preferred_element_type=f32, precision=exact)

    square = sq_ref[:, 0:1]
    inverses, inners, actives, sigmoids = [], [], [], []
    on_up = [[part(l, 1) for l in range(layers - 1)]]
    for layer in range(layers):
        inverse = lax.rsqrt(jnp.maximum(square, 0.0) * (1.0 / features) + norm_eps)
        on_down = part(layer, 0)
        for i in range(layer):
            on_down = on_down + scale_r * times(actives[i], up_down(i, layer))
        inner = on_down * (inverse * scale_d)
        sigmoid = jax.nn.sigmoid(inner)
        active = (inner * sigmoid).astype(bf16).astype(f32)
        inverses.append(inverse)
        inners.append(inner)
        sigmoids.append(sigmoid)
        actives.append(active)
        if layer < layers - 1:
            now = on_up[-1]
            grown = [now[l] + scale_r * times(active, up_up(layer, l)) for l in range(layers - 1)]
            square = square + scale_r * row_sum(active * (now[layer] + grown[layer]))
            on_up.append(grown)
    scaled = [None] * layers
    kappas = [None] * layers
    for layer in reversed(range(layers)):
        incoming = part(layer, 2)
        for k in range(layer + 1, layers):
            incoming = incoming + scale_d * dot_last(scaled[k], up_down(layer, k), exact)
            incoming = incoming - kappas[k] * on_up[k][layer]
        sigmoid, inner = sigmoids[layer], inners[layer]
        slope = sigmoid * (1.0 + inner * (1.0 - sigmoid))
        error = incoming * scale_r * slope
        scaled[layer] = error * inverses[layer]
        kappas[layer] = (
            inverses[layer] * inverses[layer] * (row_sum(error * inner) * (1.0 / features))
        )

    def owned(values):
        chosen = values[0]
        for layer in range(1, layers):
            chosen = jnp.where(section_at == layer, values[layer], chosen)
        return chosen

    own_error = owned(scaled)
    own_active = owned(actives)
    counted = counted_rows(counts, tokens, per_micro)
    later = jnp.zeros_like(square)
    for k in range(1, layers):
        later = later + jnp.where(k > section_at, kappas[k], 0.0)
    on_hidden = jnp.concatenate([own_error * scale_d, -scale_r * later * own_active], axis=1)
    on_cot = jnp.concatenate(
        [jnp.zeros_like(own_active), jnp.where(counted, own_active * scale_r, 0.0)], axis=1
    )
    factor_ref[...] = jnp.concatenate([on_hidden.T, on_cot.T], axis=1).astype(bf16)
    both = scale_d * scale_r
    for k in range(1, layers):
        cut = slice((k - 1) * ranks, k * ranks)
        across = dot_first(own_active, scaled[k], exact) * both
        mixed_ref[:ranks, cut] = jnp.zeros_like(across)
        mixed_ref[ranks:, cut] = jnp.where(k > section_at, across, 0.0)
    for i in range(layers - 1):
        cut = slice((layers - 1 + i) * ranks, (layers + i) * ranks)
        after = jnp.zeros_like(square)
        for k in range(i + 1, layers):
            after = after + jnp.where(k > section_at, kappas[k], 0.0)
        across = dot_first(own_error, actives[i], exact) * both
        mixed_ref[:ranks, cut] = jnp.where(i < section_at, across, 0.0)
        across = dot_first(own_active, after * actives[i], exact)
        mixed_ref[ranks:, cut] = across * (-scale_r * scale_r)


def chain(counts, projections, square, grams, features, per_micro):
    sections = len(projections)
    tokens, wide = projections[0].shape
    ranks = wide // (3 * sections)
    inputs = [*projections, square, *grams]
    kernel = functools.partial(chain_kernel, sections, len(grams), features, per_micro)
    return pl.pallas_call(
        kernel,
        in_specs=[in_smem] + [in_vmem] * len(inputs),
        out_specs=[in_vmem] * 2,
        out_shape=[
            jax.ShapeDtypeStruct((2 * ranks, 2 * tokens), bf16),
            jax.ShapeDtypeStruct((2 * ranks, 2 * (sections - 1) * ranks), f32),
        ],
        compiler_params=limited,
        name="chain",
    )(counts, *inputs)


def gradient_kernel(first, factor_ref, h_ref, g_ref, out_ref):
    groups, tensors, _, columns = out_ref.shape
    replica_at = lax.axis_index("replica")
    tensor_at = lax.axis_index("tensor")
    factors = factor_ref[...]
    for group in range(groups):
        for hop in range(tensors):
            owner = (replica_at ^ (first + 2 * group)) * tensors + (tensor_at ^ hop)
            cut = pl.ds(pl.multiple_of(owner * columns, columns), columns)
            stacked = jnp.concatenate([h_ref[:, cut], g_ref[:, cut]], axis=0)
            block = jnp.dot(factors, stacked, preferred_element_type=f32)
            out_ref[group, hop] = block.astype(bf16)


def gradient(factors, hidden, cot, first, replicas, tensors):
    tokens, features = hidden.shape
    rows = factors.shape[0]
    shape = (replicas // 2, tensors, rows, features // (replicas * tensors))
    return pl.pallas_call(
        functools.partial(gradient_kernel, first),
        in_specs=[in_vmem] * 3,
        out_specs=in_vmem,
        out_shape=jax.ShapeDtypeStruct(shape, bf16),
        compiler_params=limited,
        cost_estimate=pl.CostEstimate(
            flops=2 * rows * tokens * features,
            bytes_accessed=(2 * tokens + rows) * features,
            transcendentals=0,
        ),
        name="gradient",
    )(factors, hidden, cot)


def update_kernel(count, *refs):
    pieces = refs[:count]
    mixed_ref, other_ref, right_ref = refs[count : count + 3]
    state_in = refs[count + 3 : count + 9]
    outs = refs[count + 9 : count + 15]
    share_ref, state, sems = refs[count + 15 :]
    copies = [
        pltpu.make_async_copy(source.at[0], state.at[i], sems.at[i])
        for i, source in enumerate(state_in)
    ]
    for copy in copies:
        copy.start()
    mixed = mixed_ref[...] + other_ref[...]
    grad = jnp.dot(mixed, right_ref[...].astype(f32), preferred_element_type=f32, precision=exact)
    for piece in pieces:
        grad = grad + piece[...].reshape(grad.shape).astype(f32)
    for copy in copies:
        copy.wait()
    ranks = grad.shape[0] // 2
    for which in range(2):
        rows = slice(which * ranks, (which + 1) * ranks)
        own = grad[rows]
        master, moment, second = (state[2 * kind + which] for kind in range(3))
        moment = beta_one * moment + (1.0 - beta_one) * own
        second = beta_two * second + (1.0 - beta_two) * own * own
        master = master - learn_rate * (
            moment / first_fix / (jnp.sqrt(second / second_fix) + adam_eps) + decay_rate * master
        )
        share_ref[rows] = master.astype(bf16)
        outs[which][0] = master
        outs[2 + which][0] = moment
        outs[4 + which][0] = second


def update(pieces, mixed, other, right, state):
    _, ranks, columns = state[0].shape

    def leading(piece):
        lead = piece.ndim - 2
        return pl.BlockSpec((1,) * lead + piece.shape[-2:], lambda i: (0,) * piece.ndim)

    whole = [leading(array) for array in (*pieces, mixed, other, right)]
    return pl.pallas_call(
        functools.partial(update_kernel, len(pieces)),
        grid=(1,),
        in_specs=whole + [in_hbm] * 6,
        out_specs=[leading(array) for array in state]
        + [pl.BlockSpec((2 * ranks, columns), lambda i: (0, 0))],
        out_shape=[jax.ShapeDtypeStruct(array.shape, f32) for array in state]
        + [jax.ShapeDtypeStruct((2 * ranks, columns), bf16)],
        scratch_shapes=[
            pltpu.VMEM((6, ranks, columns), f32),
            pltpu.SemaphoreType.DMA((6,)),
        ],
        compiler_params=limited,
        name="update",
    )(*pieces, mixed, other, right, *state)


def place_kernel(layout, bounds, *refs):
    sources = refs[: len(layout)]
    outs = refs[len(layout) : len(layout) + 2]
    zeros, sem = refs[len(layout) + 2 :]
    slots, ranks, features = outs[0].shape
    columns = zeros.shape[1]
    tensors = lax.axis_size("tensor")
    first, after = held_layers(bounds)
    replica_at = lax.axis_index("replica")
    section_at = lax.axis_index("section")
    tensor_at = lax.axis_index("tensor")
    zeros[...] = jnp.zeros_like(zeros)

    def fill(slot, distance, go):
        for (window, rows, owners), source in zip(layout, sources):
            if window != distance:
                continue
            for i, (order, hop) in enumerate(owners):
                owner = (replica_at ^ order) * tensors + (tensor_at ^ hop)
                cut = pl.ds(pl.multiple_of(owner * columns, columns), columns)
                for at, which in enumerate(rows):
                    block = source.at[i, pl.ds(at * ranks, ranks), :]
                    go(pltpu.make_async_copy(block, outs[which].at[slot, :, cut], sem))

    def clear(slot, go):
        for out in outs:
            for block in range(features // columns):
                cut = pl.ds(block * columns, columns)
                go(pltpu.make_async_copy(zeros, out.at[slot, :, cut], sem))

    for act in (lambda copy: copy.start(), lambda copy: copy.wait()):
        for slot in range(slots):
            layer = first + slot
            present = layer < after
            for distance in range(2):

                @pl.when(present & (layer - section_at == distance))
                def _():
                    fill(slot, distance, act)

            @pl.when(jnp.logical_not(present))
            def _():
                clear(slot, act)


def place(bounds, pieces, slots, ranks, features):
    layout = [piece[:3] for piece in pieces]
    arrays = [piece[3] for piece in pieces]
    columns = arrays[0].shape[-1]
    return pl.pallas_call(
        functools.partial(place_kernel, layout),
        in_specs=[in_smem] + [in_vmem] * len(arrays),
        out_specs=[in_hbm] * 2,
        out_shape=[jax.ShapeDtypeStruct((slots, ranks, features), bf16)] * 2,
        scratch_shapes=[pltpu.VMEM((ranks, columns), bf16), pltpu.SemaphoreType.DMA],
        compiler_params=limited,
        name="place",
    )(bounds, *arrays)


def swapped(block, axis, distance):
    route = [(i, i ^ distance) for i in range(lax.axis_size(axis))]
    return lax.ppermute(block, axis, route)


def swaps(block, axis):
    return [swapped(block, axis, k) for k in range(1, lax.axis_size(axis))]


def from_next(block, distance=1):
    size = lax.axis_size("section")
    route = [((i + distance) % size, i) for i in range(size)]
    return lax.ppermute(block, "section", route)


def following_layer(block):
    size = lax.axis_size("section")
    return lax.ppermute(block, "section", [(i + 1, i) for i in range(size - 1)])


def summed(*blocks):
    total = blocks[0].astype(f32)
    for block in blocks[1:]:
        total = total + block.astype(f32)
    return total.astype(bf16)


def reduced(factors, hidden, cot, replicas, tensors):
    sent = gradient(factors, hidden, cot, 1, replicas, tensors)
    near = swapped(sent, "replica", 1)
    kept = gradient(factors, hidden, cot, 0, replicas, tensors)
    across = swapped(summed(kept[1, 1:], near[1, 1:]), "replica", 2)
    last = swapped(summed(kept[1, 0], near[1, 0]), "replica", 2)
    along = [
        swapped(summed(kept[0, k], near[0, k], across[k - 1]), "tensor", k)
        for k in range(1, tensors)
    ]
    return [kept, near, last, *along]


def gathered(share):
    ranks = share.shape[0] // 2
    far_one = swapped(share, "replica", 2)
    next_one = following_layer(share)
    line = jnp.stack(swaps(share, "tensor"))
    next_far_one = following_layer(far_one)
    far_line = swapped(line, "replica", 2)
    next_line = following_layer(line)
    near = jnp.concatenate([share[None], far_one[None], line])
    next_near = jnp.concatenate([next_one[None], next_far_one[None], next_line])
    next_far_down = following_layer(far_line[:, :ranks])
    next_far_up = swapped(next_line[:, ranks:], "replica", 2)
    hops = range(1, lax.axis_size("tensor"))
    near_owners = [(0, 0), (2, 0)] + [(0, hop) for hop in hops]
    far_owners = [(2, hop) for hop in hops]
    pieces = []
    for window, rows, owners, block in (
        (0, (0, 1), near_owners, near),
        (1, (0, 1), near_owners, next_near),
        (0, (0, 1), far_owners, far_line),
        (1, (0,), far_owners, next_far_down),
        (1, (1,), far_owners, next_far_up),
    ):
        other = [(order ^ 1, hop) for order, hop in owners]
        pieces.append((window, rows, owners, block))
        pieces.append((window, rows, other, swapped(block, "replica", 1)))
    return pieces


def on_device(
    inputs,
    cotangent,
    micro_counts,
    bounds,
    holder_down,
    holder_up,
    master_down,
    master_up,
    moment_down,
    moment_up,
    second_down,
    second_up,
):
    sections = lax.axis_size("section")
    replicas = lax.axis_size("replica")
    tensors = lax.axis_size("tensor")
    assert replicas == 4 and tensors == 4
    _, micros, per_micro, features = inputs.shape
    slots = holder_down.shape[2]
    hidden = inputs.reshape(micros * per_micro, features)
    cot = cotangent.reshape(micros * per_micro, features)

    projected, square, hidden, cot = project(
        bounds, micro_counts, hidden, cot, holder_down[0, 0], holder_up[0, 0], sections, per_micro
    )
    owned = jnp.concatenate([master_down[0], master_up[0]], axis=0).astype(bf16)
    around = [from_next(owned, d) for d in range(1, sections)]
    around, projected = lax.optimization_barrier((around, projected))
    table, right = gram([owned, *around])
    projections = [projected] + [from_next(projected, d) for d in range(1, sections)]
    table = table + sum(swaps(table, "replica"))
    tables = [table] + swaps(table, "tensor")
    factors, mixed = chain(micro_counts, projections, square, tables, features, per_micro)

    pieces = reduced(factors, hidden, cot, replicas, tensors)
    for axis, distance in (("tensor", 1), ("tensor", 2), ("replica", 1)):
        mixed = mixed + swapped(mixed, axis, distance)
    other = swapped(mixed, "replica", 2)
    state = [master_down, master_up, moment_down, moment_up, second_down, second_up]
    updated = update(pieces, mixed, other, right, state)
    placed = place(bounds, gathered(updated[6]), slots, holder_down.shape[3], features)
    return (placed[0][None, None], placed[1][None, None], *updated[:6])


def solution(mesh):
    held = P("replica", "section", None, None, None)
    owned = P("section", None, ("replica", "tensor"))
    tokens = P("replica", None, "tensor", None)
    return jax.shard_map(
        on_device,
        mesh=mesh,
        in_specs=(tokens, tokens, P(), P(), held, held) + (owned,) * 6,
        out_specs=(held, held) + (owned,) * 6,
        check_vma=False,
    )
```

```python
import functools
import math

import jax
import jax.numpy as jnp
from jax import lax
from jax.experimental import pallas as pl
from jax.experimental.pallas import tpu as pltpu
from jax.sharding import PartitionSpec as P

norm_eps = 1e-06
learn_rate = 0.01
beta_one = 0.9
beta_two = 0.95
decay_rate = 0.1
adam_eps = 1e-08
first_fix = 0.9999734386011124
second_fix = 0.9940794707796659

f32 = jnp.float32
bf16 = jnp.bfloat16
exact = lax.Precision.HIGHEST
in_smem = pl.BlockSpec(memory_space=pltpu.SMEM)
in_vmem = pl.BlockSpec(memory_space=pltpu.VMEM)
in_hbm = pl.BlockSpec(memory_space=pltpu.HBM)
limited = pltpu.CompilerParams(vmem_limit_bytes=16 * 1024 * 1024)


def held_layers(bounds):
    at_row = lax.axis_index("replica")
    at_column = lax.axis_index("section")
    return bounds[at_row, at_column], bounds[at_row, at_column + 1]


def counted_rows(counts, tokens, per_micro):
    rows = lax.broadcasted_iota(jnp.int32, (tokens, 1), 0)
    return rows < counts[lax.axis_index("replica")] * per_micro


def dot_last(x, y, precision=None):
    return lax.dot_general(
        x, y, (((1,), (1,)), ((), ())), preferred_element_type=f32, precision=precision
    )


def dot_first(x, y, precision=None):
    return lax.dot_general(
        x, y, (((0,), (0,)), ((), ())), preferred_element_type=f32, precision=precision
    )


def row_sum(x):
    return jnp.sum(x, axis=-1, keepdims=True)


def store_by_layer(out_ref, bounds, layers, pieces):
    first, after = held_layers(bounds)
    columns = pieces[0].shape[1]
    for layer in range(layers):
        total = jnp.zeros_like(pieces[0])
        for slot, piece in enumerate(pieces):
            here = (first + slot == layer) & (layer < after)
            total = jnp.where(here, piece, total)
        out_ref[:, layer * columns : (layer + 1) * columns] = total


def project_kernel(layers, steps, bounds, h_in, down_in, up_in, *refs):
    out_ref, sq_ref, h_ref, up_ref, down_ref, sems = refs
    slots, ranks, features = down_in.shape
    tokens = h_ref.shape[0]
    width = features // steps
    copies = []
    for step in range(steps):
        cut = pl.ds(step * width, width)
        moves = [(h_in.at[:, cut], h_ref.at[:, cut])]
        for slot in range(slots):
            rows = pl.ds(slot * ranks, ranks)
            moves.append((down_in.at[slot, :, cut], down_ref.at[rows, cut]))
            moves.append((up_in.at[slot, :, cut], up_ref.at[rows, cut]))
        copies.append(
            [
                pltpu.make_async_copy(source, target, sems.at[step, i])
                for i, (source, target) in enumerate(moves)
            ]
        )
        for copy in copies[-1]:
            copy.start()
    ph = jnp.zeros((tokens, 2 * slots * ranks), f32)
    square = jnp.zeros((tokens, 128), f32)
    for step in range(steps):
        for copy in copies[step]:
            copy.wait()
        cut = pl.ds(step * width, width)
        h = h_ref[:, cut]
        ph = ph + dot_last(h, jnp.concatenate([down_ref[:, cut], up_ref[:, cut]], axis=0))
        wide = h.astype(f32)
        wide = wide * wide
        for lane in range(0, width, 128):
            square = square + wide[:, lane : lane + 128]
    sq_ref[...] = jnp.broadcast_to(row_sum(square), square.shape)
    pieces = []
    for slot in range(slots):
        lo, hi = slot * ranks, (slot + 1) * ranks
        up = slots * ranks
        pieces.append(jnp.concatenate([ph[:, lo:hi], ph[:, up + lo : up + hi]], axis=1))
    store_by_layer(out_ref, bounds, layers, pieces)


def project(bounds, hidden, downs, ups, layers):
    tokens, features = hidden.shape
    slots, ranks, _ = downs.shape
    steps = 8
    sources = [pltpu.with_memory_space_constraint(x, pltpu.HBM) for x in (hidden, downs, ups)]
    return pl.pallas_call(
        functools.partial(project_kernel, layers, steps),
        in_specs=[in_smem] + [in_hbm] * 3,
        out_specs=[in_vmem] * 4,
        out_shape=[
            jax.ShapeDtypeStruct((tokens, layers * 2 * ranks), f32),
            jax.ShapeDtypeStruct((tokens, 128), f32),
            jax.ShapeDtypeStruct((tokens, features), bf16),
            jax.ShapeDtypeStruct((slots * ranks, features), bf16),
        ],
        scratch_shapes=[
            pltpu.VMEM((slots * ranks, features), bf16),
            pltpu.SemaphoreType.DMA((steps, 1 + 2 * slots)),
        ],
        compiler_params=limited,
        cost_estimate=pl.CostEstimate(
            flops=4 * tokens * slots * ranks * features,
            bytes_accessed=2 * (tokens + 2 * slots * ranks) * features,
            transcendentals=0,
        ),
        name="project",
    )(bounds, *sources)


def project_back_kernel(layers, ranks, per_micro, bounds, counts, g_ref, up_ref, out_ref):
    pg = dot_last(g_ref[...], up_ref[...])
    pg = jnp.where(counted_rows(counts, pg.shape[0], per_micro), pg, 0.0)
    slots = pg.shape[1] // ranks
    pieces = [pg[:, slot * ranks : (slot + 1) * ranks] for slot in range(slots)]
    store_by_layer(out_ref, bounds, layers, pieces)


def project_back(bounds, counts, cot, ups, layers, ranks, per_micro):
    tokens, features = cot.shape
    return pl.pallas_call(
        functools.partial(project_back_kernel, layers, ranks, per_micro),
        in_specs=[in_smem] * 2 + [in_vmem] * 2,
        out_specs=in_vmem,
        out_shape=jax.ShapeDtypeStruct((tokens, layers * ranks), f32),
        compiler_params=limited,
        cost_estimate=pl.CostEstimate(
            flops=2 * tokens * ups.shape[0] * features,
            bytes_accessed=2 * (tokens + ups.shape[0]) * features,
            transcendentals=0,
        ),
        name="project_back",
    )(bounds, counts, cot, ups)


def gram_kernel(sections, *refs):
    around = refs[:sections]
    gram_ref, right_ref = refs[sections:]
    section_at = lax.axis_index("section")
    ranks = around[0].shape[0] // 2
    layers = []
    for layer in range(sections):
        distance = lax.rem(layer - section_at + sections, sections)
        chosen = around[0][...]
        for step in range(1, sections):
            chosen = jnp.where(distance == step, around[step][...], chosen)
        layers.append(chosen)
    lefts = [chosen[ranks:] for chosen in layers[:-1]]
    right = jnp.concatenate([chosen[:ranks] for chosen in layers[1:]] + lefts, axis=0)
    right_ref[...] = right
    gram_ref[...] = dot_last(jnp.concatenate(lefts, axis=0), right)


def gram(around):
    sections = len(around)
    ranks = around[0].shape[0] // 2
    columns = around[0].shape[1]
    before = (sections - 1) * ranks
    return pl.pallas_call(
        functools.partial(gram_kernel, sections),
        in_specs=[in_vmem] * sections,
        out_specs=[in_vmem] * 2,
        out_shape=[
            jax.ShapeDtypeStruct((before, 2 * before), f32),
            jax.ShapeDtypeStruct((2 * before, columns), bf16),
        ],
        compiler_params=limited,
        name="gram",
    )(*around)


def chain_kernel(sections, parts, features, per_micro, counts, *refs):
    on_hidden, on_cot, grams = refs[:sections], refs[sections : 2 * sections], refs[2 * sections :]
    sq_ref = grams[parts]
    factor_ref, mixed_ref = grams[parts + 1 :]
    layers = sections
    section_at = lax.axis_index("section")
    tokens = sq_ref.shape[0]

    def total(arrays):
        result = arrays[0][...]
        for other in arrays[1:]:
            result = result + other[...]
        return result

    by_hidden, by_cot, table = total(on_hidden), total(on_cot), total(grams[:parts])
    ranks = by_cot.shape[1] // layers
    scale_d = 1.0 / math.sqrt(features)
    scale_r = 1.0 / math.sqrt(ranks)

    def part(layer, which):
        source, block = (by_cot, layer) if which == 2 else (by_hidden, 2 * layer + which)
        return source[:, block * ranks : (block + 1) * ranks]

    def up_down(i, layer):
        return table[i * ranks : (i + 1) * ranks, (layer - 1) * ranks : layer * ranks]

    def up_up(i, j):
        at_column = (layers - 1 + j) * ranks
        return table[i * ranks : (i + 1) * ranks, at_column : at_column + ranks]

    def times(x, y):
        return jnp.dot(x, y, preferred_element_type=f32, precision=exact)

    square = sq_ref[:, 0:1]
    inverses, inners, actives, sigmoids = [], [], [], []
    on_up = [[part(l, 1) for l in range(layers - 1)]]
    for layer in range(layers):
        inverse = lax.rsqrt(jnp.maximum(square, 0.0) * (1.0 / features) + norm_eps)
        on_down = part(layer, 0)
        for i in range(layer):
            on_down = on_down + scale_r * times(actives[i], up_down(i, layer))
        inner = on_down * (inverse * scale_d)
        sigmoid = jax.nn.sigmoid(inner)
        active = (inner * sigmoid).astype(bf16).astype(f32)
        inverses.append(inverse)
        inners.append(inner)
        sigmoids.append(sigmoid)
        actives.append(active)
        if layer < layers - 1:
            now = on_up[-1]
            grown = [now[l] + scale_r * times(active, up_up(layer, l)) for l in range(layers - 1)]
            square = square + scale_r * row_sum(active * (now[layer] + grown[layer]))
            on_up.append(grown)
    scaled = [None] * layers
    kappas = [None] * layers
    for layer in reversed(range(layers)):
        incoming = part(layer, 2)
        for k in range(layer + 1, layers):
            incoming = incoming + scale_d * dot_last(scaled[k], up_down(layer, k), exact)
            incoming = incoming - kappas[k] * on_up[k][layer]
        sigmoid, inner = sigmoids[layer], inners[layer]
        slope = sigmoid * (1.0 + inner * (1.0 - sigmoid))
        error = incoming * scale_r * slope
        scaled[layer] = error * inverses[layer]
        kappas[layer] = (
            inverses[layer] * inverses[layer] * (row_sum(error * inner) * (1.0 / features))
        )

    def owned(values):
        chosen = values[0]
        for layer in range(1, layers):
            chosen = jnp.where(section_at == layer, values[layer], chosen)
        return chosen

    own_error = owned(scaled)
    own_active = owned(actives)
    counted = counted_rows(counts, tokens, per_micro)
    later = jnp.zeros_like(square)
    for k in range(1, layers):
        later = later + jnp.where(k > section_at, kappas[k], 0.0)
    on_hidden = jnp.concatenate([own_error * scale_d, -scale_r * later * own_active], axis=1)
    on_cot = jnp.concatenate(
        [jnp.zeros_like(own_active), jnp.where(counted, own_active * scale_r, 0.0)], axis=1
    )
    factor_ref[...] = jnp.concatenate([on_hidden.T, on_cot.T], axis=1).astype(bf16)
    both = scale_d * scale_r
    for k in range(1, layers):
        cut = slice((k - 1) * ranks, k * ranks)
        across = dot_first(own_active, scaled[k], exact) * both
        mixed_ref[:ranks, cut] = jnp.zeros_like(across)
        mixed_ref[ranks:, cut] = jnp.where(k > section_at, across, 0.0)
    for i in range(layers - 1):
        cut = slice((layers - 1 + i) * ranks, (layers + i) * ranks)
        after = jnp.zeros_like(square)
        for k in range(i + 1, layers):
            after = after + jnp.where(k > section_at, kappas[k], 0.0)
        across = dot_first(own_error, actives[i], exact) * both
        mixed_ref[:ranks, cut] = jnp.where(i < section_at, across, 0.0)
        across = dot_first(own_active, after * actives[i], exact)
        mixed_ref[ranks:, cut] = across * (-scale_r * scale_r)


def chain(counts, on_hidden, on_cot, grams, square, features, per_micro):
    sections = len(on_cot)
    tokens, wide = on_cot[0].shape
    ranks = wide // sections
    inputs = [*on_hidden, *on_cot, *grams, square]
    kernel = functools.partial(chain_kernel, sections, len(grams), features, per_micro)
    return pl.pallas_call(
        kernel,
        in_specs=[in_smem] + [in_vmem] * len(inputs),
        out_specs=[in_vmem] * 2,
        out_shape=[
            jax.ShapeDtypeStruct((2 * ranks, 2 * tokens), bf16),
            jax.ShapeDtypeStruct((2 * ranks, 2 * (sections - 1) * ranks), f32),
        ],
        compiler_params=limited,
        name="chain",
    )(counts, *inputs)


def gradient_kernel(first, factor_ref, h_ref, g_ref, out_ref):
    groups, tensors, _, columns = out_ref.shape
    replica_at = lax.axis_index("replica")
    tensor_at = lax.axis_index("tensor")
    factors = factor_ref[...]
    for group in range(groups):
        for hop in range(tensors):
            owner = (replica_at ^ (first + 2 * group)) * tensors + (tensor_at ^ hop)
            cut = pl.ds(pl.multiple_of(owner * columns, columns), columns)
            stacked = jnp.concatenate([h_ref[:, cut], g_ref[:, cut]], axis=0)
            block = jnp.dot(factors, stacked, preferred_element_type=f32)
            out_ref[group, hop] = block.astype(bf16)


def gradient(factors, hidden, cot, first, replicas, tensors):
    tokens, features = hidden.shape
    rows = factors.shape[0]
    shape = (replicas // 2, tensors, rows, features // (replicas * tensors))
    return pl.pallas_call(
        functools.partial(gradient_kernel, first),
        in_specs=[in_vmem] * 3,
        out_specs=in_vmem,
        out_shape=jax.ShapeDtypeStruct(shape, bf16),
        compiler_params=limited,
        cost_estimate=pl.CostEstimate(
            flops=2 * rows * tokens * features,
            bytes_accessed=(2 * tokens + rows) * features,
            transcendentals=0,
        ),
        name="gradient",
    )(factors, hidden, cot)


def update_kernel(count, *refs):
    pieces = refs[:count]
    mixed_ref, other_ref, right_ref = refs[count : count + 3]
    state = refs[count + 3 : count + 9]
    outs = refs[count + 9 : count + 15]
    share_ref = refs[count + 15]
    mixed = mixed_ref[...] + other_ref[...]
    grad = jnp.dot(mixed, right_ref[...].astype(f32), preferred_element_type=f32, precision=exact)
    for piece in pieces:
        block = piece[(0,) * (len(piece.shape) - 2)] if len(piece.shape) > 2 else piece[...]
        grad = grad + block.astype(f32)
    ranks = grad.shape[0] // 2
    for which in range(2):
        rows = slice(which * ranks, (which + 1) * ranks)
        own = grad[rows]
        master, moment, second = (state[2 * kind + which][0] for kind in range(3))
        moment = beta_one * moment + (1.0 - beta_one) * own
        second = beta_two * second + (1.0 - beta_two) * own * own
        master = master - learn_rate * (
            moment / first_fix / (jnp.sqrt(second / second_fix) + adam_eps) + decay_rate * master
        )
        share_ref[rows] = master.astype(bf16)
        outs[which][0] = master
        outs[2 + which][0] = moment
        outs[4 + which][0] = second


def update(pieces, mixed, other, right, state):
    _, ranks, columns = state[0].shape
    return pl.pallas_call(
        functools.partial(update_kernel, len(pieces)),
        in_specs=[in_vmem] * (len(pieces) + 9),
        out_specs=[in_vmem] * 7,
        out_shape=[jax.ShapeDtypeStruct(array.shape, f32) for array in state]
        + [jax.ShapeDtypeStruct((2 * ranks, columns), bf16)],
        compiler_params=limited,
        name="update",
    )(*pieces, mixed, other, right, *state)


def place_kernel(layout, start, bounds, *refs):
    sources = refs[: len(layout)]
    outs = refs[-4:-2]
    zeros, sem = refs[-2:]
    slots, ranks, features = outs[0].shape
    columns = zeros.shape[1]
    tensors = lax.axis_size("tensor")
    first, after = held_layers(bounds)
    replica_at = lax.axis_index("replica")
    section_at = lax.axis_index("section")
    tensor_at = lax.axis_index("tensor")
    zeros[...] = jnp.zeros_like(zeros)

    def fill(slot, distance, go):
        for (window, rows, owners), source in zip(layout, sources):
            if window != distance:
                continue
            for i, (order, hop) in enumerate(owners):
                owner = (replica_at ^ order) * tensors + (tensor_at ^ hop)
                cut = pl.ds(pl.multiple_of(owner * columns, columns), columns)
                for at, which in enumerate(rows):
                    block = source.at[i, pl.ds(at * ranks, ranks), :]
                    go(pltpu.make_async_copy(block, outs[which].at[slot, :, cut], sem))

    def clear(slot, go):
        for out in outs:
            for block in range(features // columns):
                cut = pl.ds(block * columns, columns)
                go(pltpu.make_async_copy(zeros, out.at[slot, :, cut], sem))

    for act in (lambda copy: copy.start(), lambda copy: copy.wait()):
        for slot in range(slots):
            layer = first + slot
            present = layer < after
            for distance in range(2):

                @pl.when(present & (layer - section_at == distance))
                def _():
                    fill(slot, distance, act)

            if start:

                @pl.when(jnp.logical_not(present))
                def _():
                    clear(slot, act)


def place(bounds, pieces, before, slots, ranks, features):
    layout = [piece[:3] for piece in pieces]
    arrays = [piece[3] for piece in pieces]
    columns = arrays[0].shape[-1]
    return pl.pallas_call(
        functools.partial(place_kernel, layout, not before),
        in_specs=[in_smem] + [in_vmem] * len(arrays) + [in_hbm] * len(before),
        out_specs=[in_hbm] * 2,
        out_shape=[jax.ShapeDtypeStruct((slots, ranks, features), bf16)] * 2,
        scratch_shapes=[pltpu.VMEM((ranks, columns), bf16), pltpu.SemaphoreType.DMA],
        input_output_aliases={1 + len(arrays) + i: i for i in range(len(before))},
        compiler_params=limited,
        cost_estimate=pl.CostEstimate(
            flops=0,
            bytes_accessed=4 * sum(array.size for array in arrays),
            transcendentals=0,
        ),
        name="place",
    )(bounds, *arrays, *before)


def swapped(block, axis, distance):
    route = [(i, i ^ distance) for i in range(lax.axis_size(axis))]
    return lax.ppermute(block, axis, route)


def swaps(block, axis):
    return [swapped(block, axis, k) for k in range(1, lax.axis_size(axis))]


def from_next(block, distance=1):
    size = lax.axis_size("section")
    route = [((i + distance) % size, i) for i in range(size)]
    return lax.ppermute(block, "section", route)


def following_layer(block):
    size = lax.axis_size("section")
    return lax.ppermute(block, "section", [(i + 1, i) for i in range(size - 1)])


def summed(*blocks):
    total = blocks[0].astype(f32)
    for block in blocks[1:]:
        total = total + block.astype(f32)
    return total.astype(bf16)


def reduced(factors, hidden, cot, replicas, tensors):
    sent = gradient(factors, hidden, cot, 1, replicas, tensors)
    near = swapped(sent, "replica", 1)
    kept = gradient(factors, hidden, cot, 0, replicas, tensors)
    across = swapped(summed(kept[1, 1:], near[1, 1:]), "replica", 2)
    across, last = lax.optimization_barrier((across, summed(kept[1, 0], near[1, 0])))
    last = swapped(last, "replica", 2)
    along = [
        swapped(summed(kept[0, k], near[0, k], across[k - 1]), "tensor", k)
        for k in range(1, tensors)
    ]
    return [kept, near, last, *along]


def spread(share, bounds, slots, features):
    ranks = share.shape[0] // 2
    along = swaps(share, "tensor")
    far_one = swapped(share, "replica", 2)
    next_one = following_layer(share)
    next_far_one = following_layer(far_one)
    along, far_one, next_one, next_far_one = lax.optimization_barrier(
        (along, far_one, next_one, next_far_one)
    )
    line = jnp.stack(along)
    far_line = swapped(line, "replica", 2)
    next_line = following_layer(line)
    near = jnp.concatenate([share[None], far_one[None], line])
    next_near = jnp.concatenate([next_one[None], next_far_one[None], next_line])
    next_far_down = following_layer(far_line[:, :ranks])
    next_far_up = swapped(next_line[:, ranks:], "replica", 2)
    hops = range(1, lax.axis_size("tensor"))
    near_owners = [(0, 0), (2, 0)] + [(0, hop) for hop in hops]
    far_owners = [(2, hop) for hop in hops]
    placed = []
    for group in (
        (
            (0, (0, 1), near_owners, near),
            (0, (0, 1), far_owners, far_line),
            (1, (0, 1), near_owners, next_near),
        ),
        ((1, (0,), far_owners, next_far_down), (1, (1,), far_owners, next_far_up)),
    ):
        pieces = []
        for window, rows, owners, block in group:
            other = [(order ^ 1, hop) for order, hop in owners]
            pieces.append((window, rows, owners, block))
            pieces.append((window, rows, other, swapped(block, "replica", 1)))
        placed = place(bounds, pieces, placed, slots, ranks, features)
    return placed


def on_device(
    inputs,
    cotangent,
    micro_counts,
    bounds,
    holder_down,
    holder_up,
    master_down,
    master_up,
    moment_down,
    moment_up,
    second_down,
    second_up,
):
    sections = lax.axis_size("section")
    replicas = lax.axis_size("replica")
    tensors = lax.axis_size("tensor")
    assert replicas == 4 and tensors == 4
    _, micros, per_micro, features = inputs.shape
    slots = holder_down.shape[2]
    hidden = inputs.reshape(micros * per_micro, features)
    cot = cotangent.reshape(micros * per_micro, features)

    owned = jnp.concatenate([master_down[0], master_up[0]], axis=0).astype(bf16)
    around = [from_next(owned, d) for d in range(1, sections)]
    by_hidden, square, hidden, ups = project(
        bounds, hidden, holder_down[0, 0], holder_up[0, 0], sections
    )
    around, by_hidden = lax.optimization_barrier((around, by_hidden))
    table, right = gram([owned, *around])
    on_hidden = [by_hidden] + [from_next(by_hidden, d) for d in range(1, sections)]
    table, ups = lax.optimization_barrier((table, ups))
    by_cot = project_back(
        bounds, micro_counts, cot, ups, sections, holder_down.shape[3], per_micro
    )
    on_cot = [by_cot] + [from_next(by_cot, d) for d in range(1, sections)]
    table = table + sum(swaps(table, "replica"))
    tables = [table] + swaps(table, "tensor")
    factors, mixed = chain(micro_counts, on_hidden, on_cot, tables, square, features, per_micro)

    pieces = reduced(factors, hidden, cot, replicas, tensors)
    for axis, distance in (("tensor", 1), ("tensor", 2), ("replica", 1)):
        mixed = mixed + swapped(mixed, axis, distance)
    other = swapped(mixed, "replica", 2)
    state = [master_down, master_up, moment_down, moment_up, second_down, second_up]
    updated = update(pieces, mixed, other, right, state)
    placed = spread(updated[6], bounds, slots, features)
    return (placed[0][None, None], placed[1][None, None], *updated[:6])


def solution(mesh):
    held = P("replica", "section", None, None, None)
    owned = P("section", None, ("replica", "tensor"))
    tokens = P("replica", None, "tensor", None)
    return jax.shard_map(
        on_device,
        mesh=mesh,
        in_specs=(tokens, tokens, P(), P(), held, held) + (owned,) * 6,
        out_specs=(held, held) + (owned,) * 6,
        check_vma=False,
    )
```

```python
import functools
import math

import jax
import jax.numpy as jnp
from jax import lax
from jax.experimental import pallas as pl
from jax.experimental.pallas import tpu as pltpu
from jax.sharding import PartitionSpec as P

norm_eps = 1e-06
learn_rate = 0.01
beta_one = 0.9
beta_two = 0.95
decay_rate = 0.1
adam_eps = 1e-08
first_fix = 0.9999734386011124
second_fix = 0.9940794707796659

f32 = jnp.float32
bf16 = jnp.bfloat16
exact = lax.Precision.HIGHEST
in_smem = pl.BlockSpec(memory_space=pltpu.SMEM)
in_vmem = pl.BlockSpec(memory_space=pltpu.VMEM)
in_hbm = pl.BlockSpec(memory_space=pltpu.HBM)
limited = pltpu.CompilerParams(vmem_limit_bytes=16 * 1024 * 1024)


def held_layers(bounds):
    at_row = lax.axis_index("replica")
    at_column = lax.axis_index("section")
    return bounds[at_row, at_column], bounds[at_row, at_column + 1]


def counted_rows(counts, tokens, per_micro):
    rows = lax.broadcasted_iota(jnp.int32, (tokens, 1), 0)
    return rows < counts[lax.axis_index("replica")] * per_micro


def dot_last(x, y, precision=None):
    return lax.dot_general(
        x, y, (((1,), (1,)), ((), ())), preferred_element_type=f32, precision=precision
    )


def dot_first(x, y, precision=None):
    return lax.dot_general(
        x, y, (((0,), (0,)), ((), ())), preferred_element_type=f32, precision=precision
    )


def row_sum(x):
    return jnp.sum(x, axis=-1, keepdims=True)


def project_kernel(steps, h_in, down_in, up_in, *refs):
    out_ref, sq_ref, h_ref, up_ref, down_ref, sems = refs
    slots, ranks, features = down_in.shape
    tokens = h_ref.shape[0]
    width = features // steps
    copies = []
    for step in range(steps):
        cut = pl.ds(step * width, width)
        moves = [(h_in.at[:, cut], h_ref.at[:, cut])]
        for slot in range(slots):
            rows = pl.ds(slot * ranks, ranks)
            moves.append((down_in.at[slot, :, cut], down_ref.at[rows, cut]))
            moves.append((up_in.at[slot, :, cut], up_ref.at[rows, cut]))
        copies.append(
            [
                pltpu.make_async_copy(source, target, sems.at[step, i])
                for i, (source, target) in enumerate(moves)
            ]
        )
        for copy in copies[-1]:
            copy.start()
    ph = jnp.zeros((tokens, 2 * slots * ranks), f32)
    square = jnp.zeros((tokens, 128), f32)
    for step in range(steps):
        for copy in copies[step]:
            copy.wait()
        cut = pl.ds(step * width, width)
        h = h_ref[:, cut]
        ph = ph + dot_last(h, jnp.concatenate([down_ref[:, cut], up_ref[:, cut]], axis=0))
        wide = h.astype(f32)
        wide = wide * wide
        for lane in range(0, width, 128):
            square = square + wide[:, lane : lane + 128]
    sq_ref[...] = jnp.broadcast_to(row_sum(square), square.shape)
    out_ref[...] = ph


def project(hidden, downs, ups):
    tokens, features = hidden.shape
    slots, ranks, _ = downs.shape
    steps = 8
    sources = [pltpu.with_memory_space_constraint(x, pltpu.HBM) for x in (hidden, downs, ups)]
    return pl.pallas_call(
        functools.partial(project_kernel, steps),
        in_specs=[in_hbm] * 3,
        out_specs=[in_vmem] * 4,
        out_shape=[
            jax.ShapeDtypeStruct((tokens, 2 * slots * ranks), f32),
            jax.ShapeDtypeStruct((tokens, 128), f32),
            jax.ShapeDtypeStruct((tokens, features), bf16),
            jax.ShapeDtypeStruct((slots * ranks, features), bf16),
        ],
        scratch_shapes=[
            pltpu.VMEM((slots * ranks, features), bf16),
            pltpu.SemaphoreType.DMA((steps, 1 + 2 * slots)),
        ],
        compiler_params=limited,
        cost_estimate=pl.CostEstimate(
            flops=4 * tokens * slots * ranks * features,
            bytes_accessed=2 * (tokens + 2 * slots * ranks) * features,
            transcendentals=0,
        ),
        name="project",
    )(*sources)


def project_back_kernel(per_micro, counts, by_hidden, g_ref, up_ref, out_ref):
    pg = dot_last(g_ref[...], up_ref[...])
    pg = jnp.where(counted_rows(counts, pg.shape[0], per_micro), pg, 0.0)
    ahead = by_hidden.shape[1]
    out_ref[:, :ahead] = by_hidden[...]
    out_ref[:, ahead:] = pg


def project_back(counts, by_hidden, cot, ups, per_micro):
    tokens, features = cot.shape
    columns = by_hidden.shape[1] + ups.shape[0]
    return pl.pallas_call(
        functools.partial(project_back_kernel, per_micro),
        in_specs=[in_smem] + [in_vmem] * 3,
        out_specs=in_vmem,
        out_shape=jax.ShapeDtypeStruct((tokens, columns), f32),
        compiler_params=limited,
        cost_estimate=pl.CostEstimate(
            flops=2 * tokens * ups.shape[0] * features,
            bytes_accessed=2 * (tokens + ups.shape[0]) * features,
            transcendentals=0,
        ),
        name="project_back",
    )(counts, by_hidden, cot, ups)


def gram_kernel(sections, *refs):
    around = refs[:sections]
    gram_ref, right_ref = refs[sections:]
    section_at = lax.axis_index("section")
    ranks = around[0].shape[0] // 2
    layers = []
    for layer in range(sections):
        distance = lax.rem(layer - section_at + sections, sections)
        chosen = around[0][...]
        for step in range(1, sections):
            chosen = jnp.where(distance == step, around[step][...], chosen)
        layers.append(chosen)
    lefts = [chosen[ranks:] for chosen in layers[:-1]]
    right = jnp.concatenate([chosen[:ranks] for chosen in layers[1:]] + lefts, axis=0)
    right_ref[...] = right
    gram_ref[...] = dot_last(jnp.concatenate(lefts, axis=0), right)


def gram(around):
    sections = len(around)
    ranks = around[0].shape[0] // 2
    columns = around[0].shape[1]
    before = (sections - 1) * ranks
    return pl.pallas_call(
        functools.partial(gram_kernel, sections),
        in_specs=[in_vmem] * sections,
        out_specs=[in_vmem] * 2,
        out_shape=[
            jax.ShapeDtypeStruct((before, 2 * before), f32),
            jax.ShapeDtypeStruct((2 * before, columns), bf16),
        ],
        compiler_params=limited,
        name="gram",
    )(*around)


def chain_kernel(sections, slots, features, per_micro, bounds, counts, *refs):
    projections, grams = refs[:sections], refs[sections:-3]
    sq_ref, factor_ref, mixed_ref = refs[-3:]
    layers = sections
    replica_at = lax.axis_index("replica")
    section_at = lax.axis_index("section")
    tokens = sq_ref.shape[0]
    table = grams[0][...]
    for other in grams[1:]:
        table = table + other[...]
    ranks = projections[0].shape[1] // (3 * slots)
    parts = [[jnp.zeros((tokens, ranks), f32)] * 3 for _ in range(layers)]
    for distance, source in enumerate(projections):
        section = lax.rem(section_at + distance, sections)
        first, after = bounds[replica_at, section], bounds[replica_at, section + 1]
        for slot in range(slots):
            for which in range(3):
                block = which * slots + slot
                piece = source[:, block * ranks : (block + 1) * ranks]
                for layer in range(layers):
                    here = (first + slot == layer) & (layer < after)
                    parts[layer][which] = jnp.where(here, piece, parts[layer][which])
    scale_d = 1.0 / math.sqrt(features)
    scale_r = 1.0 / math.sqrt(ranks)

    def part(layer, which):
        return parts[layer][which]

    def up_down(i, layer):
        return table[i * ranks : (i + 1) * ranks, (layer - 1) * ranks : layer * ranks]

    def up_up(i, j):
        at_column = (layers - 1 + j) * ranks
        return table[i * ranks : (i + 1) * ranks, at_column : at_column + ranks]

    def times(x, y):
        return jnp.dot(x, y, preferred_element_type=f32, precision=exact)

    square = sq_ref[:, 0:1]
    inverses, inners, actives, sigmoids = [], [], [], []
    on_up = [[part(l, 1) for l in range(layers - 1)]]
    for layer in range(layers):
        inverse = lax.rsqrt(jnp.maximum(square, 0.0) * (1.0 / features) + norm_eps)
        on_down = part(layer, 0)
        for i in range(layer):
            on_down = on_down + scale_r * times(actives[i], up_down(i, layer))
        inner = on_down * (inverse * scale_d)
        sigmoid = jax.nn.sigmoid(inner)
        active = (inner * sigmoid).astype(bf16).astype(f32)
        inverses.append(inverse)
        inners.append(inner)
        sigmoids.append(sigmoid)
        actives.append(active)
        if layer < layers - 1:
            now = on_up[-1]
            grown = [now[l] + scale_r * times(active, up_up(layer, l)) for l in range(layers - 1)]
            square = square + scale_r * row_sum(active * (now[layer] + grown[layer]))
            on_up.append(grown)
    scaled = [None] * layers
    kappas = [None] * layers
    for layer in reversed(range(layers)):
        incoming = part(layer, 2)
        for k in range(layer + 1, layers):
            incoming = incoming + scale_d * dot_last(scaled[k], up_down(layer, k), exact)
            incoming = incoming - kappas[k] * on_up[k][layer]
        sigmoid, inner = sigmoids[layer], inners[layer]
        slope = sigmoid * (1.0 + inner * (1.0 - sigmoid))
        error = incoming * scale_r * slope
        scaled[layer] = error * inverses[layer]
        kappas[layer] = (
            inverses[layer] * inverses[layer] * (row_sum(error * inner) * (1.0 / features))
        )

    def owned(values):
        chosen = values[0]
        for layer in range(1, layers):
            chosen = jnp.where(section_at == layer, values[layer], chosen)
        return chosen

    own_error = owned(scaled)
    own_active = owned(actives)
    counted = counted_rows(counts, tokens, per_micro)
    later = jnp.zeros_like(square)
    for k in range(1, layers):
        later = later + jnp.where(k > section_at, kappas[k], 0.0)
    on_hidden = jnp.concatenate([own_error * scale_d, -scale_r * later * own_active], axis=1)
    on_cot = jnp.concatenate(
        [jnp.zeros_like(own_active), jnp.where(counted, own_active * scale_r, 0.0)], axis=1
    )
    factor_ref[...] = jnp.concatenate([on_hidden.T, on_cot.T], axis=1).astype(bf16)
    both = scale_d * scale_r
    for k in range(1, layers):
        cut = slice((k - 1) * ranks, k * ranks)
        across = dot_first(own_active, scaled[k], exact) * both
        mixed_ref[:ranks, cut] = jnp.zeros_like(across)
        mixed_ref[ranks:, cut] = jnp.where(k > section_at, across, 0.0)
    for i in range(layers - 1):
        cut = slice((layers - 1 + i) * ranks, (layers + i) * ranks)
        after = jnp.zeros_like(square)
        for k in range(i + 1, layers):
            after = after + jnp.where(k > section_at, kappas[k], 0.0)
        across = dot_first(own_error, actives[i], exact) * both
        mixed_ref[:ranks, cut] = jnp.where(i < section_at, across, 0.0)
        across = dot_first(own_active, after * actives[i], exact)
        mixed_ref[ranks:, cut] = across * (-scale_r * scale_r)


def chain(bounds, counts, projections, grams, square, slots, features, per_micro):
    sections = len(projections)
    tokens, wide = projections[0].shape
    ranks = wide // (3 * slots)
    inputs = [*projections, *grams, square]
    kernel = functools.partial(chain_kernel, sections, slots, features, per_micro)
    return pl.pallas_call(
        kernel,
        in_specs=[in_smem] * 2 + [in_vmem] * len(inputs),
        out_specs=[in_vmem] * 2,
        out_shape=[
            jax.ShapeDtypeStruct((2 * ranks, 2 * tokens), bf16),
            jax.ShapeDtypeStruct((2 * ranks, 2 * (sections - 1) * ranks), f32),
        ],
        compiler_params=limited,
        name="chain",
    )(bounds, counts, *inputs)


def gradient_kernel(first, factor_ref, h_ref, g_ref, out_ref):
    _, _, ranks, columns = out_ref.shape
    replica_at = lax.axis_index("replica")
    tensor_at = lax.axis_index("tensor")
    tensors = lax.axis_size("tensor")
    factors = factor_ref[...]
    for far in range(2):
        for hop in range(4):
            owner = (replica_at ^ (first + 2 * far)) * tensors + (tensor_at ^ hop)
            cut = pl.ds(pl.multiple_of(owner * columns, columns), columns)
            stacked = jnp.concatenate([h_ref[:, cut], g_ref[:, cut]], axis=0)
            block = jnp.dot(factors, stacked, preferred_element_type=f32).astype(bf16)
            low, high = hop % 2, hop // 2
            out_ref[0, 4 * far + 2 * low + high] = block[:ranks]
            out_ref[1, 4 * low + 2 * far + high] = block[ranks:]


def gradient(factors, hidden, cot, first, columns):
    tokens, features = hidden.shape
    rows = factors.shape[0]
    return pl.pallas_call(
        functools.partial(gradient_kernel, first),
        in_specs=[in_vmem] * 3,
        out_specs=in_vmem,
        out_shape=jax.ShapeDtypeStruct((2, 8, rows // 2, columns), bf16),
        compiler_params=limited,
        cost_estimate=pl.CostEstimate(
            flops=2 * rows * tokens * features,
            bytes_accessed=(2 * tokens + rows) * features,
            transcendentals=0,
        ),
        name="gradient",
    )(factors, hidden, cot)


def update_kernel(kept, near, downs, ups, *refs):
    last, mixed_ref, other_ref, right_ref = refs[:4]
    state, outs, share_ref = refs[4:10], refs[10:16], refs[16]
    mixed = mixed_ref[...] + other_ref[...]
    right = right_ref[...].astype(f32)
    small = jnp.dot(mixed, right, preferred_element_type=f32, precision=exact)
    ranks = small.shape[0] // 2
    for which, steps in enumerate((downs, ups)):
        own = small[which * ranks : (which + 1) * ranks]
        for block in (kept[which, 0], near[which, 0], *(step[0] for step in steps), last[which]):
            own = own + block.astype(f32)
        master, moment, second = (state[2 * kind + which][0] for kind in range(3))
        moment = beta_one * moment + (1.0 - beta_one) * own
        second = beta_two * second + (1.0 - beta_two) * own * own
        master = master - learn_rate * (
            moment / first_fix / (jnp.sqrt(second / second_fix) + adam_eps) + decay_rate * master
        )
        share_ref[which] = master.astype(bf16)
        outs[which][0] = master
        outs[2 + which][0] = moment
        outs[4 + which][0] = second


def update(kept, near, downs, ups, last, mixed, other, right, state):
    _, ranks, columns = state[0].shape

    def kernel(kept, near, down_one, down_two, up_one, up_two, *refs):
        update_kernel(kept, near, (down_one, down_two), (up_one, up_two), *refs)

    return pl.pallas_call(
        kernel,
        in_specs=[in_vmem] * 16,
        out_specs=[in_vmem] * 7,
        out_shape=[jax.ShapeDtypeStruct(array.shape, f32) for array in state]
        + [jax.ShapeDtypeStruct((2, ranks, columns), bf16)],
        compiler_params=limited,
        name="update",
    )(kept, near, *downs, *ups, last, mixed, other, right, *state)


def place_kernel(layout, start, bounds, *refs):
    sources = refs[: len(layout)]
    outs = refs[-4:-2]
    zeros, sem = refs[-2:]
    slots, ranks, features = outs[0].shape
    columns = zeros.shape[1]
    tensors = lax.axis_size("tensor")
    first, after = held_layers(bounds)
    replica_at = lax.axis_index("replica")
    section_at = lax.axis_index("section")
    tensor_at = lax.axis_index("tensor")
    zeros[...] = jnp.zeros_like(zeros)

    def fill(slot, distance, go):
        for (window, blocks), source in zip(layout, sources):
            if window != distance:
                continue
            for i, (which, order, hop) in enumerate(blocks):
                owner = (replica_at ^ order) * tensors + (tensor_at ^ hop)
                cut = pl.ds(pl.multiple_of(owner * columns, columns), columns)
                go(pltpu.make_async_copy(source.at[i], outs[which].at[slot, :, cut], sem))

    def clear(slot, go):
        for out in outs:
            for block in range(features // columns):
                cut = pl.ds(block * columns, columns)
                go(pltpu.make_async_copy(zeros, out.at[slot, :, cut], sem))

    for act in (lambda copy: copy.start(), lambda copy: copy.wait()):
        for slot in range(slots):
            layer = first + slot
            present = layer < after
            for distance in range(2):

                @pl.when(present & (layer - section_at == distance))
                def _():
                    fill(slot, distance, act)

            if start:

                @pl.when(jnp.logical_not(present))
                def _():
                    clear(slot, act)


def place(bounds, pieces, before, slots, ranks, features):
    layout = [piece[:2] for piece in pieces]
    arrays = [piece[2] for piece in pieces]
    columns = arrays[0].shape[-1]
    return pl.pallas_call(
        functools.partial(place_kernel, layout, not before),
        in_specs=[in_smem] + [in_vmem] * len(arrays) + [in_hbm] * len(before),
        out_specs=[in_hbm] * 2,
        out_shape=[jax.ShapeDtypeStruct((slots, ranks, features), bf16)] * 2,
        scratch_shapes=[pltpu.VMEM((ranks, columns), bf16), pltpu.SemaphoreType.DMA],
        input_output_aliases={1 + len(arrays) + i: i for i in range(len(before))},
        compiler_params=limited,
        cost_estimate=pl.CostEstimate(
            flops=0,
            bytes_accessed=4 * sum(array.size for array in arrays),
            transcendentals=0,
        ),
        name="place",
    )(bounds, *arrays, *before)


def swapped(block, axis, distance):
    route = [(i, i ^ distance) for i in range(lax.axis_size(axis))]
    return lax.ppermute(block, axis, route)


def swaps(block, axis):
    return [swapped(block, axis, k) for k in range(1, lax.axis_size(axis))]


def from_next(block, distance=1):
    size = lax.axis_size("section")
    route = [((i + distance) % size, i) for i in range(size)]
    return lax.ppermute(block, "section", route)


def following_layer(block):
    size = lax.axis_size("section")
    return lax.ppermute(block, "section", [(i + 1, i) for i in range(size - 1)])


def summed(*blocks):
    total = blocks[0].astype(f32)
    for block in blocks[1:]:
        total = total + block.astype(f32)
    return total.astype(bf16)


def reduced(factors, hidden, cot, columns, mixed):
    sent = gradient(factors, hidden, cot, 1, columns)
    near = swapped(sent, "replica", 1)
    kept = gradient(factors, hidden, cot, 0, columns)
    mixed = mixed + swapped(mixed, "tensor", 1)

    def part(which, cut, *steps):
        return summed(kept[which, cut], near[which, cut], *steps)

    high, low = slice(4, 8), slice(2, 4)
    down_one, up_one, mixed = lax.optimization_barrier((part(0, high), part(1, high), mixed))
    down_one = swapped(down_one, "replica", 2)
    up_one = swapped(up_one, "tensor", 1)
    down_two = swapped(part(0, low, down_one[2:]), "tensor", 1)
    up_two = swapped(part(1, low, up_one[2:]), "replica", 2)
    last = jnp.stack([part(0, 1, down_one[1], down_two[1]), part(1, 1, up_one[1], up_two[1])])
    last = swapped(last, "tensor", 2)
    return (kept, near, (down_one, down_two), (up_one, up_two), last), mixed


def crossed(piece, axis, distance):
    window, blocks, array = piece
    blocks = [
        (which, order ^ distance, hop) if axis == "replica" else (which, order, hop ^ distance)
        for which, order, hop in blocks
    ]
    return (window, blocks, swapped(array, axis, distance))


def fetched(piece):
    _, blocks, array = piece
    return (1, blocks, following_layer(array))


def picked(piece, cut):
    return (piece[0], piece[1][cut], piece[2][cut])


def joined(*pieces):
    blocks = [block for piece in pieces for block in piece[1]]
    return (pieces[0][0], blocks, jnp.concatenate([piece[2] for piece in pieces]))


def ordered(*pieces):
    arrays = lax.optimization_barrier(tuple(piece[2] for piece in pieces))
    return [(*piece[:2], array) for piece, array in zip(pieces, arrays)]


def spread(share, bounds, slots, features):
    ranks = share.shape[1]
    own = (0, [(0, 0, 0), (1, 0, 0)], share)
    one = crossed(own, "tensor", 2)
    next_own = fetched(own)
    both = joined(picked(own, slice(0, 1)), picked(one, slice(0, 1)))
    both_up = joined(picked(own, slice(1, 2)), picked(one, slice(1, 2)))
    down_two = crossed(both, "tensor", 1)
    up_two = crossed(both_up, "replica", 2)
    next_one = fetched(one)
    two = joined(down_two, up_two)
    down_three = crossed(joined(both, down_two), "replica", 2)
    up_three = crossed(joined(both_up, up_two), "tensor", 1)
    next_two = fetched(two)
    last, first = slice(3, 4), slice(0, 1)
    next_end = fetched(joined(picked(down_three, last), picked(up_three, last)))
    next_near = joined(next_own, next_one, next_two)
    down_end = crossed(
        joined(picked(next_own, first), picked(next_one, first), picked(next_two, first)),
        "replica",
        2,
    )
    second = slice(1, 2)
    up_end = crossed(
        joined(picked(next_own, second), picked(next_one, second), picked(next_two, slice(2, 3))),
        "tensor",
        1,
    )
    near = joined(own, one)
    early = [near, two, down_three, up_three, next_near]
    early += [crossed(piece, "replica", 1) for piece in early]
    placed = place(bounds, early, [], slots, ranks, features)
    end = joined(down_end, up_end, next_end)
    end_array, *placed = lax.optimization_barrier((end[2], *placed))
    end = (*end[:2], end_array)
    return place(bounds, [end, crossed(end, "replica", 1)], placed, slots, ranks, features)


def on_device(
    inputs,
    cotangent,
    micro_counts,
    bounds,
    holder_down,
    holder_up,
    master_down,
    master_up,
    moment_down,
    moment_up,
    second_down,
    second_up,
):
    sections = lax.axis_size("section")
    replicas = lax.axis_size("replica")
    tensors = lax.axis_size("tensor")
    assert replicas == 4 and tensors == 4
    _, micros, per_micro, features = inputs.shape
    slots = holder_down.shape[2]
    hidden = inputs.reshape(micros * per_micro, features)
    cot = cotangent.reshape(micros * per_micro, features)

    owned = jnp.concatenate([master_down[0], master_up[0]], axis=0).astype(bf16)
    around = [from_next(owned, d) for d in range(1, sections)]
    by_hidden, square, hidden, ups = project(hidden, holder_down[0, 0], holder_up[0, 0])
    around, by_hidden = lax.optimization_barrier((around, by_hidden))
    table, right = gram([owned, *around])
    table, ups = lax.optimization_barrier((table, ups))
    projected = project_back(micro_counts, by_hidden, cot, ups, per_micro)
    table = table + sum(swaps(table, "replica"))
    projections = [projected] + [from_next(projected, d) for d in range(1, sections)]
    table = table + swapped(table, "tensor", 1)
    tables = [table, swapped(table, "tensor", 2)]
    factors, mixed = chain(
        bounds, micro_counts, projections, tables, square, slots, features, per_micro
    )

    parts, mixed = reduced(factors, hidden, cot, master_down.shape[2], mixed)
    for axis, distance in (("tensor", 2), ("replica", 1)):
        mixed = mixed + swapped(mixed, axis, distance)
    other = swapped(mixed, "replica", 2)
    state = [master_down, master_up, moment_down, moment_up, second_down, second_up]
    updated = update(*parts, mixed, other, right, state)
    placed = spread(updated[6], bounds, slots, features)
    return (placed[0][None, None], placed[1][None, None], *updated[:6])


def solution(mesh):
    held = P("replica", "section", None, None, None)
    owned = P("section", None, ("replica", "tensor"))
    tokens = P("replica", None, "tensor", None)
    return jax.shard_map(
        on_device,
        mesh=mesh,
        in_specs=(tokens, tokens, P(), P(), held, held) + (owned,) * 6,
        out_specs=(held, held) + (owned,) * 6,
        check_vma=False,
    )
```

```python
import functools
import math

import jax
import jax.numpy as jnp
from jax import lax
from jax.experimental import pallas as pl
from jax.experimental.pallas import tpu as pltpu
from jax.sharding import PartitionSpec as P

norm_eps = 1e-06
learn_rate = 0.01
beta_one = 0.9
beta_two = 0.95
decay_rate = 0.1
adam_eps = 1e-08
first_fix = 0.9999734386011124
second_fix = 0.9940794707796659

f32 = jnp.float32
bf16 = jnp.bfloat16
exact = lax.Precision.HIGHEST
in_smem = pl.BlockSpec(memory_space=pltpu.SMEM)
in_vmem = pl.BlockSpec(memory_space=pltpu.VMEM)
in_hbm = pl.BlockSpec(memory_space=pltpu.HBM)
limited = pltpu.CompilerParams(vmem_limit_bytes=16 * 1024 * 1024)


def held_layers(bounds):
    at_row = lax.axis_index("replica")
    at_column = lax.axis_index("section")
    return bounds[at_row, at_column], bounds[at_row, at_column + 1]


def counted_rows(counts, tokens, per_micro):
    rows = lax.broadcasted_iota(jnp.int32, (tokens, 1), 0)
    return rows < counts[lax.axis_index("replica")] * per_micro


def dot_last(x, y, precision=None):
    return lax.dot_general(
        x, y, (((1,), (1,)), ((), ())), preferred_element_type=f32, precision=precision
    )


def dot_first(x, y, precision=None):
    return lax.dot_general(
        x, y, (((0,), (0,)), ((), ())), preferred_element_type=f32, precision=precision
    )


def row_sum(x):
    return jnp.sum(x, axis=-1, keepdims=True)


def project_kernel(steps, h_in, down_in, up_in, *refs):
    out_ref, sq_ref, h_ref, up_ref, down_ref, sems = refs
    slots, ranks, features = down_in.shape
    tokens = h_ref.shape[0]
    width = features // steps
    copies = []
    for step in range(steps):
        cut = pl.ds(step * width, width)
        moves = [(h_in.at[:, cut], h_ref.at[:, cut])]
        for slot in range(slots):
            rows = pl.ds(slot * ranks, ranks)
            moves.append((down_in.at[slot, :, cut], down_ref.at[rows, cut]))
            moves.append((up_in.at[slot, :, cut], up_ref.at[rows, cut]))
        copies.append(
            [
                pltpu.make_async_copy(source, target, sems.at[step, i])
                for i, (source, target) in enumerate(moves)
            ]
        )
        for copy in copies[-1]:
            copy.start()
    ph = jnp.zeros((tokens, 2 * slots * ranks), f32)
    square = jnp.zeros((tokens, 128), f32)
    for step in range(steps):
        for copy in copies[step]:
            copy.wait()
        cut = pl.ds(step * width, width)
        h = h_ref[:, cut]
        ph = ph + dot_last(h, jnp.concatenate([down_ref[:, cut], up_ref[:, cut]], axis=0))
        wide = h.astype(f32)
        wide = wide * wide
        for lane in range(0, width, 128):
            square = square + wide[:, lane : lane + 128]
    sq_ref[...] = jnp.broadcast_to(row_sum(square), square.shape)
    out_ref[...] = ph


def project(hidden, downs, ups):
    tokens, features = hidden.shape
    slots, ranks, _ = downs.shape
    steps = 8
    sources = [pltpu.with_memory_space_constraint(x, pltpu.HBM) for x in (hidden, downs, ups)]
    return pl.pallas_call(
        functools.partial(project_kernel, steps),
        in_specs=[in_hbm] * 3,
        out_specs=[in_vmem] * 4,
        out_shape=[
            jax.ShapeDtypeStruct((tokens, 2 * slots * ranks), f32),
            jax.ShapeDtypeStruct((tokens, 128), f32),
            jax.ShapeDtypeStruct((tokens, features), bf16),
            jax.ShapeDtypeStruct((slots * ranks, features), bf16),
        ],
        scratch_shapes=[
            pltpu.VMEM((slots * ranks, features), bf16),
            pltpu.SemaphoreType.DMA((steps, 1 + 2 * slots)),
        ],
        compiler_params=limited,
        cost_estimate=pl.CostEstimate(
            flops=4 * tokens * slots * ranks * features,
            bytes_accessed=2 * (tokens + 2 * slots * ranks) * features,
            transcendentals=0,
        ),
        name="project",
    )(*sources)


def project_back_kernel(per_micro, counts, by_hidden, g_ref, up_ref, out_ref):
    pg = dot_last(g_ref[...], up_ref[...])
    pg = jnp.where(counted_rows(counts, pg.shape[0], per_micro), pg, 0.0)
    ahead = by_hidden.shape[1]
    out_ref[:, :ahead] = by_hidden[...]
    out_ref[:, ahead:] = pg


def project_back(counts, by_hidden, cot, ups, per_micro):
    tokens, features = cot.shape
    columns = by_hidden.shape[1] + ups.shape[0]
    return pl.pallas_call(
        functools.partial(project_back_kernel, per_micro),
        in_specs=[in_smem] + [in_vmem] * 3,
        out_specs=in_vmem,
        out_shape=jax.ShapeDtypeStruct((tokens, columns), f32),
        compiler_params=limited,
        cost_estimate=pl.CostEstimate(
            flops=2 * tokens * ups.shape[0] * features,
            bytes_accessed=2 * (tokens + ups.shape[0]) * features,
            transcendentals=0,
        ),
        name="project_back",
    )(counts, by_hidden, cot, ups)


def gram_kernel(sections, *refs):
    around = refs[:sections]
    gram_ref, right_ref = refs[sections:]
    section_at = lax.axis_index("section")
    ranks = around[0].shape[0] // 2
    layers = []
    for layer in range(sections):
        distance = lax.rem(layer - section_at + sections, sections)
        chosen = around[0][...]
        for step in range(1, sections):
            chosen = jnp.where(distance == step, around[step][...], chosen)
        layers.append(chosen)
    lefts = [chosen[ranks:] for chosen in layers[:-1]]
    right = jnp.concatenate([chosen[:ranks] for chosen in layers[1:]] + lefts, axis=0)
    right_ref[...] = right
    gram_ref[...] = dot_last(jnp.concatenate(lefts, axis=0), right)


def gram(around):
    sections = len(around)
    ranks = around[0].shape[0] // 2
    columns = around[0].shape[1]
    before = (sections - 1) * ranks
    return pl.pallas_call(
        functools.partial(gram_kernel, sections),
        in_specs=[in_vmem] * sections,
        out_specs=[in_vmem] * 2,
        out_shape=[
            jax.ShapeDtypeStruct((before, 2 * before), f32),
            jax.ShapeDtypeStruct((2 * before, columns), bf16),
        ],
        compiler_params=limited,
        name="gram",
    )(*around)


def chain_kernel(sections, slots, features, per_micro, bounds, counts, *refs):
    projections, grams = refs[:sections], refs[sections:-3]
    sq_ref, factor_ref, mixed_ref = refs[-3:]
    layers = sections
    replica_at = lax.axis_index("replica")
    section_at = lax.axis_index("section")
    tokens = sq_ref.shape[0]
    table = grams[0][...]
    for other in grams[1:]:
        table = table + other[...]
    ranks = projections[0].shape[1] // (3 * slots)
    parts = [[jnp.zeros((tokens, ranks), f32)] * 3 for _ in range(layers)]
    for distance, source in enumerate(projections):
        section = lax.rem(section_at + distance, sections)
        first, after = bounds[replica_at, section], bounds[replica_at, section + 1]
        for slot in range(slots):
            for which in range(3):
                block = which * slots + slot
                piece = source[:, block * ranks : (block + 1) * ranks]
                for layer in range(layers):
                    here = (first + slot == layer) & (layer < after)
                    parts[layer][which] = jnp.where(here, piece, parts[layer][which])
    scale_d = 1.0 / math.sqrt(features)
    scale_r = 1.0 / math.sqrt(ranks)

    def part(layer, which):
        return parts[layer][which]

    def up_down(i, layer):
        return table[i * ranks : (i + 1) * ranks, (layer - 1) * ranks : layer * ranks]

    def up_up(i, j):
        at_column = (layers - 1 + j) * ranks
        return table[i * ranks : (i + 1) * ranks, at_column : at_column + ranks]

    def times(x, y):
        return jnp.dot(x, y, preferred_element_type=f32, precision=exact)

    square = sq_ref[:, 0:1]
    inverses, inners, actives, sigmoids = [], [], [], []
    on_up = [[part(l, 1) for l in range(layers - 1)]]
    for layer in range(layers):
        inverse = lax.rsqrt(jnp.maximum(square, 0.0) * (1.0 / features) + norm_eps)
        on_down = part(layer, 0)
        for i in range(layer):
            on_down = on_down + scale_r * times(actives[i], up_down(i, layer))
        inner = on_down * (inverse * scale_d)
        sigmoid = jax.nn.sigmoid(inner)
        active = (inner * sigmoid).astype(bf16).astype(f32)
        inverses.append(inverse)
        inners.append(inner)
        sigmoids.append(sigmoid)
        actives.append(active)
        if layer < layers - 1:
            now = on_up[-1]
            grown = [now[l] + scale_r * times(active, up_up(layer, l)) for l in range(layers - 1)]
            square = square + scale_r * row_sum(active * (now[layer] + grown[layer]))
            on_up.append(grown)
    scaled = [None] * layers
    kappas = [None] * layers
    for layer in reversed(range(layers)):
        incoming = part(layer, 2)
        for k in range(layer + 1, layers):
            incoming = incoming + scale_d * dot_last(scaled[k], up_down(layer, k), exact)
            incoming = incoming - kappas[k] * on_up[k][layer]
        sigmoid, inner = sigmoids[layer], inners[layer]
        slope = sigmoid * (1.0 + inner * (1.0 - sigmoid))
        error = incoming * scale_r * slope
        scaled[layer] = error * inverses[layer]
        kappas[layer] = (
            inverses[layer] * inverses[layer] * (row_sum(error * inner) * (1.0 / features))
        )

    def owned(values):
        chosen = values[0]
        for layer in range(1, layers):
            chosen = jnp.where(section_at == layer, values[layer], chosen)
        return chosen

    own_error = owned(scaled)
    own_active = owned(actives)
    counted = counted_rows(counts, tokens, per_micro)
    later = jnp.zeros_like(square)
    for k in range(1, layers):
        later = later + jnp.where(k > section_at, kappas[k], 0.0)
    on_hidden = jnp.concatenate([own_error * scale_d, -scale_r * later * own_active], axis=1)
    on_cot = jnp.concatenate(
        [jnp.zeros_like(own_active), jnp.where(counted, own_active * scale_r, 0.0)], axis=1
    )
    factor_ref[...] = jnp.concatenate([on_hidden.T, on_cot.T], axis=1).astype(bf16)
    both = scale_d * scale_r
    for k in range(1, layers):
        cut = slice((k - 1) * ranks, k * ranks)
        across = dot_first(own_active, scaled[k], exact) * both
        mixed_ref[:ranks, cut] = jnp.zeros_like(across)
        mixed_ref[ranks:, cut] = jnp.where(k > section_at, across, 0.0)
    for i in range(layers - 1):
        cut = slice((layers - 1 + i) * ranks, (layers + i) * ranks)
        after = jnp.zeros_like(square)
        for k in range(i + 1, layers):
            after = after + jnp.where(k > section_at, kappas[k], 0.0)
        across = dot_first(own_error, actives[i], exact) * both
        mixed_ref[:ranks, cut] = jnp.where(i < section_at, across, 0.0)
        across = dot_first(own_active, after * actives[i], exact)
        mixed_ref[ranks:, cut] = across * (-scale_r * scale_r)


def chain(bounds, counts, projections, grams, square, slots, features, per_micro):
    sections = len(projections)
    tokens, wide = projections[0].shape
    ranks = wide // (3 * slots)
    inputs = [*projections, *grams, square]
    kernel = functools.partial(chain_kernel, sections, slots, features, per_micro)
    return pl.pallas_call(
        kernel,
        in_specs=[in_smem] * 2 + [in_vmem] * len(inputs),
        out_specs=[in_vmem] * 2,
        out_shape=[
            jax.ShapeDtypeStruct((2 * ranks, 2 * tokens), bf16),
            jax.ShapeDtypeStruct((2 * ranks, 2 * (sections - 1) * ranks), f32),
        ],
        compiler_params=limited,
        name="chain",
    )(bounds, counts, *inputs)


def gradient_kernel(first, factor_ref, h_ref, g_ref, out_ref):
    _, _, ranks, columns = out_ref.shape
    replica_at = lax.axis_index("replica")
    tensor_at = lax.axis_index("tensor")
    tensors = lax.axis_size("tensor")
    factors = factor_ref[...]
    for far in range(2):
        for hop in range(4):
            owner = (replica_at ^ (first + 2 * far)) * tensors + (tensor_at ^ hop)
            cut = pl.ds(pl.multiple_of(owner * columns, columns), columns)
            stacked = jnp.concatenate([h_ref[:, cut], g_ref[:, cut]], axis=0)
            block = jnp.dot(factors, stacked, preferred_element_type=f32).astype(bf16)
            low, high = hop % 2, hop // 2
            out_ref[0, 4 * far + 2 * low + high] = block[:ranks]
            out_ref[1, 4 * low + 2 * far + high] = block[ranks:]


def gradient(factors, hidden, cot, first, columns):
    tokens, features = hidden.shape
    rows = factors.shape[0]
    return pl.pallas_call(
        functools.partial(gradient_kernel, first),
        in_specs=[in_vmem] * 3,
        out_specs=in_vmem,
        out_shape=jax.ShapeDtypeStruct((2, 8, rows // 2, columns), bf16),
        compiler_params=limited,
        cost_estimate=pl.CostEstimate(
            flops=2 * rows * tokens * features,
            bytes_accessed=(2 * tokens + rows) * features,
            transcendentals=0,
        ),
        name="gradient",
    )(factors, hidden, cot)


def update_kernel(kept, near, downs, ups, *refs):
    last, mixed_ref, other_ref, right_ref = refs[:4]
    state, outs, share_ref = refs[4:10], refs[10:16], refs[16]
    mixed = mixed_ref[...] + other_ref[...]
    right = right_ref[...].astype(f32)
    small = jnp.dot(mixed, right, preferred_element_type=f32, precision=exact)
    ranks = small.shape[0] // 2
    for which, steps in enumerate((downs, ups)):
        own = small[which * ranks : (which + 1) * ranks]
        for block in (kept[which, 0], near[which, 0], *(step[0] for step in steps), last[which]):
            own = own + block.astype(f32)
        master, moment, second = (state[2 * kind + which][0] for kind in range(3))
        moment = beta_one * moment + (1.0 - beta_one) * own
        second = beta_two * second + (1.0 - beta_two) * own * own
        master = master - learn_rate * (
            moment / first_fix / (jnp.sqrt(second / second_fix) + adam_eps) + decay_rate * master
        )
        share_ref[which] = master.astype(bf16)
        outs[which][0] = master
        outs[2 + which][0] = moment
        outs[4 + which][0] = second


def update(kept, near, downs, ups, last, mixed, other, right, state):
    _, ranks, columns = state[0].shape

    def kernel(kept, near, down_one, down_two, up_one, up_two, *refs):
        update_kernel(kept, near, (down_one, down_two), (up_one, up_two), *refs)

    return pl.pallas_call(
        kernel,
        in_specs=[in_vmem] * 16,
        out_specs=[in_vmem] * 7,
        out_shape=[jax.ShapeDtypeStruct(array.shape, f32) for array in state]
        + [jax.ShapeDtypeStruct((2, ranks, columns), bf16)],
        compiler_params=limited,
        name="update",
    )(kept, near, *downs, *ups, last, mixed, other, right, *state)


def place_kernel(layout, start, bounds, *refs):
    sources = refs[: len(layout)]
    outs = refs[-4:-2]
    zeros, sem = refs[-2:]
    slots, ranks, features = outs[0].shape
    columns = zeros.shape[1]
    tensors = lax.axis_size("tensor")
    first, after = held_layers(bounds)
    replica_at = lax.axis_index("replica")
    section_at = lax.axis_index("section")
    tensor_at = lax.axis_index("tensor")
    zeros[...] = jnp.zeros_like(zeros)

    def fill(slot, distance, go):
        for (window, blocks), source in zip(layout, sources):
            if window != distance:
                continue
            for i, (which, order, hop) in enumerate(blocks):
                owner = (replica_at ^ order) * tensors + (tensor_at ^ hop)
                cut = pl.ds(pl.multiple_of(owner * columns, columns), columns)
                go(pltpu.make_async_copy(source.at[i], outs[which].at[slot, :, cut], sem))

    def clear(slot, go):
        for out in outs:
            for block in range(features // columns):
                cut = pl.ds(block * columns, columns)
                go(pltpu.make_async_copy(zeros, out.at[slot, :, cut], sem))

    for act in (lambda copy: copy.start(), lambda copy: copy.wait()):
        for slot in range(slots):
            layer = first + slot
            present = layer < after
            for distance in range(2):

                @pl.when(present & (layer - section_at == distance))
                def _():
                    fill(slot, distance, act)

            if start:

                @pl.when(jnp.logical_not(present))
                def _():
                    clear(slot, act)


def place(bounds, pieces, before, slots, ranks, features):
    layout = [piece[:2] for piece in pieces]
    arrays = [piece[2] for piece in pieces]
    columns = arrays[0].shape[-1]
    return pl.pallas_call(
        functools.partial(place_kernel, layout, not before),
        in_specs=[in_smem] + [in_vmem] * len(arrays) + [in_hbm] * len(before),
        out_specs=[in_hbm] * 2,
        out_shape=[jax.ShapeDtypeStruct((slots, ranks, features), bf16)] * 2,
        scratch_shapes=[pltpu.VMEM((ranks, columns), bf16), pltpu.SemaphoreType.DMA],
        input_output_aliases={1 + len(arrays) + i: i for i in range(len(before))},
        compiler_params=limited,
        cost_estimate=pl.CostEstimate(
            flops=0,
            bytes_accessed=4 * sum(array.size for array in arrays),
            transcendentals=0,
        ),
        name="place",
    )(bounds, *arrays, *before)


def swapped(block, axis, distance):
    route = [(i, i ^ distance) for i in range(lax.axis_size(axis))]
    return lax.ppermute(block, axis, route)


def swaps(block, axis):
    return [swapped(block, axis, k) for k in range(1, lax.axis_size(axis))]


def from_next(block, distance=1):
    size = lax.axis_size("section")
    route = [((i + distance) % size, i) for i in range(size)]
    return lax.ppermute(block, "section", route)


def following_layer(block):
    size = lax.axis_size("section")
    return lax.ppermute(block, "section", [(i + 1, i) for i in range(size - 1)])


def summed(*blocks):
    total = blocks[0].astype(f32)
    for block in blocks[1:]:
        total = total + block.astype(f32)
    return total.astype(bf16)


def reduced(factors, hidden, cot, columns):
    sent = gradient(factors, hidden, cot, 1, columns)
    near = swapped(sent, "replica", 1)
    kept = gradient(factors, hidden, cot, 0, columns)

    def part(which, cut, *steps):
        return summed(kept[which, cut], near[which, cut], *steps)

    high, low = slice(4, 8), slice(2, 4)
    down_one = swapped(part(0, high), "replica", 2)
    up_one = swapped(part(1, high), "tensor", 1)
    down_two = swapped(part(0, low, down_one[2:]), "tensor", 1)
    up_two = swapped(part(1, low, up_one[2:]), "replica", 2)
    last = jnp.stack([part(0, 1, down_one[1], down_two[1]), part(1, 1, up_one[1], up_two[1])])
    last = swapped(last, "tensor", 2)
    return (kept, near, (down_one, down_two), (up_one, up_two), last)


def swapped_before_last(block, axis, distance):
    size, sections = lax.axis_size(axis), lax.axis_size("section")
    ahead = axis == "replica"
    axes = (axis, "section") if ahead else ("section", axis)

    def place_of(i, section):
        return i * sections + section if ahead else section * size + i

    route = [
        (place_of(i, section), place_of(i ^ distance, section))
        for i in range(size)
        for section in range(sections - 1)
    ]
    return lax.ppermute(block, axes, route)


def crossed(piece, axis, distance):
    window, blocks, array = piece
    blocks = [
        (which, order ^ distance, hop) if axis == "replica" else (which, order, hop ^ distance)
        for which, order, hop in blocks
    ]
    swap = swapped if window == 0 else swapped_before_last
    return (window, blocks, swap(array, axis, distance))


def fetched(piece):
    _, blocks, array = piece
    return (1, blocks, following_layer(array))


def picked(piece, cut):
    return (piece[0], piece[1][cut], piece[2][cut])


def joined(*pieces):
    blocks = [block for piece in pieces for block in piece[1]]
    return (pieces[0][0], blocks, jnp.concatenate([piece[2] for piece in pieces]))


def spread(share, bounds, slots, features):
    ranks = share.shape[1]
    own = (0, [(0, 0, 0), (1, 0, 0)], share)
    one = crossed(own, "tensor", 2)
    next_own = fetched(own)
    downs = joined(picked(own, slice(0, 1)), picked(one, slice(0, 1)))
    ups = joined(picked(own, slice(1, 2)), picked(one, slice(1, 2)))
    down_two = crossed(downs, "tensor", 1)
    up_two = crossed(ups, "replica", 2)
    next_one = fetched(one)
    two = joined(down_two, up_two)
    down_three = crossed(joined(downs, down_two), "replica", 2)
    up_three = crossed(joined(ups, up_two), "tensor", 1)
    next_two = fetched(two)
    near = joined(own, one, two)
    near_core = crossed(near, "replica", 1)
    last, first, second = slice(3, 4), slice(0, 1), slice(1, 2)
    next_end = fetched(joined(picked(down_three, last), picked(up_three, last)))
    next_near = joined(next_own, next_one, next_two)
    down_end = joined(*(picked(piece, first) for piece in (next_own, next_one, next_two)))
    up_end = joined(
        picked(next_own, second), picked(next_one, second), picked(next_two, slice(2, 3))
    )
    end = joined(crossed(down_end, "replica", 2), crossed(up_end, "tensor", 1), next_end)
    placed = place(bounds, [near, near_core], [], slots, ranks, features)
    far = joined(down_three, up_three)
    far_array, *placed = lax.optimization_barrier((far[2], *placed))
    far = (*far[:2], far_array)
    for group in ((far, next_near), (end,)):
        pieces = [*group, *(crossed(piece, "replica", 1) for piece in group)]
        placed = place(bounds, pieces, placed, slots, ranks, features)
    return placed


def on_device(
    inputs,
    cotangent,
    micro_counts,
    bounds,
    holder_down,
    holder_up,
    master_down,
    master_up,
    moment_down,
    moment_up,
    second_down,
    second_up,
):
    sections = lax.axis_size("section")
    replicas = lax.axis_size("replica")
    tensors = lax.axis_size("tensor")
    assert replicas == 4 and tensors == 4
    _, micros, per_micro, features = inputs.shape
    slots = holder_down.shape[2]
    hidden = inputs.reshape(micros * per_micro, features)
    cot = cotangent.reshape(micros * per_micro, features)

    owned = jnp.concatenate([master_down[0], master_up[0]], axis=0).astype(bf16)
    around = [from_next(owned, d) for d in range(1, sections)]
    by_hidden, square, hidden, ups = project(hidden, holder_down[0, 0], holder_up[0, 0])
    around, by_hidden = lax.optimization_barrier((around, by_hidden))
    table, right = gram([owned, *around])
    table, ups = lax.optimization_barrier((table, ups))
    projected = project_back(micro_counts, by_hidden, cot, ups, per_micro)
    table = table + sum(swaps(table, "replica"))
    projections = [projected] + [from_next(projected, d) for d in range(1, sections)]
    table = table + swapped(table, "tensor", 1)
    tables = [table, swapped(table, "tensor", 2)]
    factors, mixed = chain(
        bounds, micro_counts, projections, tables, square, slots, features, per_micro
    )

    parts = reduced(factors, hidden, cot, master_down.shape[2])
    for axis, distance in (("replica", 1), ("tensor", 1), ("tensor", 2)):
        mixed = mixed + swapped(mixed, axis, distance)
    other = swapped(mixed, "replica", 2)
    state = [master_down, master_up, moment_down, moment_up, second_down, second_up]
    updated = update(*parts, mixed, other, right, state)
    placed = spread(updated[6], bounds, slots, features)
    return (placed[0][None, None], placed[1][None, None], *updated[:6])


def solution(mesh):
    held = P("replica", "section", None, None, None)
    owned = P("section", None, ("replica", "tensor"))
    tokens = P("replica", None, "tensor", None)
    return jax.shard_map(
        on_device,
        mesh=mesh,
        in_specs=(tokens, tokens, P(), P(), held, held) + (owned,) * 6,
        out_specs=(held, held) + (owned,) * 6,
        check_vma=False,
    )
```

```python
import functools
import math

import jax
import jax.numpy as jnp
from jax import lax
from jax.experimental import pallas as pl
from jax.experimental.pallas import tpu as pltpu
from jax.sharding import PartitionSpec as P

norm_eps = 1e-06
learn_rate = 0.01
beta_one = 0.9
beta_two = 0.95
decay_rate = 0.1
adam_eps = 1e-08
first_fix = 0.9999734386011124
second_fix = 0.9940794707796659

f32 = jnp.float32
bf16 = jnp.bfloat16
exact = lax.Precision.HIGHEST
in_smem = pl.BlockSpec(memory_space=pltpu.SMEM)
in_vmem = pl.BlockSpec(memory_space=pltpu.VMEM)
in_hbm = pl.BlockSpec(memory_space=pltpu.HBM)
limited = pltpu.CompilerParams(vmem_limit_bytes=16 * 1024 * 1024)


def held_layers(bounds):
    at_row = lax.axis_index("replica")
    at_column = lax.axis_index("section")
    return bounds[at_row, at_column], bounds[at_row, at_column + 1]


def counted_rows(counts, tokens, per_micro):
    rows = lax.broadcasted_iota(jnp.int32, (tokens, 1), 0)
    return rows < counts[lax.axis_index("replica")] * per_micro


def dot_last(x, y, precision=None):
    return lax.dot_general(
        x, y, (((1,), (1,)), ((), ())), preferred_element_type=f32, precision=precision
    )


def dot_first(x, y, precision=None):
    return lax.dot_general(
        x, y, (((0,), (0,)), ((), ())), preferred_element_type=f32, precision=precision
    )


def row_sum(x):
    return jnp.sum(x, axis=-1, keepdims=True)


def project_back_kernel(steps, g_in, up_in, out_ref, g_ref, up_ref, sems):
    slots, ranks, features = up_in.shape
    width = features // steps
    copies = []
    for step in range(steps):
        cut = pl.ds(step * width, width)
        moves = [(g_in.at[:, cut], g_ref.at[:, cut])]
        for slot in range(slots):
            rows = pl.ds(slot * ranks, ranks)
            moves.append((up_in.at[slot, :, cut], up_ref.at[rows, cut]))
        copies.append(
            [
                pltpu.make_async_copy(source, target, sems.at[step, i])
                for i, (source, target) in enumerate(moves)
            ]
        )
        for copy in copies[-1]:
            copy.start()
    total = jnp.zeros(out_ref.shape, f32)
    for step in range(steps):
        for copy in copies[step]:
            copy.wait()
        cut = pl.ds(step * width, width)
        total = total + dot_last(g_ref[:, cut], up_ref[:, cut])
    out_ref[...] = total


def project_back(cot, ups):
    tokens, features = cot.shape
    slots, ranks, _ = ups.shape
    steps = 8
    sources = [pltpu.with_memory_space_constraint(x, pltpu.HBM) for x in (cot, ups)]
    return pl.pallas_call(
        functools.partial(project_back_kernel, steps),
        in_specs=[in_hbm] * 2,
        out_specs=[in_vmem] * 3,
        out_shape=[
            jax.ShapeDtypeStruct((tokens, slots * ranks), f32),
            jax.ShapeDtypeStruct((tokens, features), bf16),
            jax.ShapeDtypeStruct((slots * ranks, features), bf16),
        ],
        scratch_shapes=[pltpu.SemaphoreType.DMA((steps, 1 + slots))],
        compiler_params=limited,
        cost_estimate=pl.CostEstimate(
            flops=2 * tokens * slots * ranks * features,
            bytes_accessed=2 * (tokens + slots * ranks) * features,
            transcendentals=0,
        ),
        name="project_back",
    )(*sources)


def project_down_kernel(h_ref, down_ref, out_ref, sq_ref):
    slots, ranks, features = down_ref.shape
    tokens = h_ref.shape[0]
    out_ref[...] = dot_last(h_ref[...], down_ref[...].reshape(slots * ranks, features))
    square = jnp.zeros((tokens, 128), f32)
    for lane in range(0, features, 128):
        wide = h_ref[:, lane : lane + 128].astype(f32)
        square = square + wide * wide
    sq_ref[...] = jnp.broadcast_to(row_sum(square), square.shape)


def project_down(hidden, downs):
    tokens, features = hidden.shape
    slots, ranks, _ = downs.shape
    return pl.pallas_call(
        project_down_kernel,
        in_specs=[in_vmem] * 2,
        out_specs=[in_vmem] * 2,
        out_shape=[
            jax.ShapeDtypeStruct((tokens, slots * ranks), f32),
            jax.ShapeDtypeStruct((tokens, 128), f32),
        ],
        compiler_params=limited,
        cost_estimate=pl.CostEstimate(
            flops=2 * tokens * slots * ranks * features,
            bytes_accessed=2 * (tokens + slots * ranks) * features,
            transcendentals=0,
        ),
        name="project_down",
    )(hidden, downs)


def project_up_kernel(per_micro, counts, h_ref, up_ref, by_down, by_cot, out_ref):
    tokens, columns = by_down.shape
    out_ref[:, :columns] = by_down[...]
    out_ref[:, columns : 2 * columns] = dot_last(h_ref[...], up_ref[...])
    counted = counted_rows(counts, tokens, per_micro)
    out_ref[:, 2 * columns :] = jnp.where(counted, by_cot[...], 0.0)


def project_up(counts, hidden, ups, by_down, by_cot, per_micro):
    tokens, features = hidden.shape
    columns = ups.shape[0]
    return pl.pallas_call(
        functools.partial(project_up_kernel, per_micro),
        in_specs=[in_smem] + [in_vmem] * 4,
        out_specs=in_vmem,
        out_shape=jax.ShapeDtypeStruct((tokens, 3 * columns), f32),
        compiler_params=limited,
        cost_estimate=pl.CostEstimate(
            flops=2 * tokens * columns * features,
            bytes_accessed=2 * (tokens + columns) * features,
            transcendentals=0,
        ),
        name="project_up",
    )(counts, hidden, ups, by_down, by_cot)


def gram_kernel(sections, *refs):
    around = refs[:sections]
    gram_ref, right_ref = refs[sections:]
    section_at = lax.axis_index("section")
    ranks = around[0].shape[0] // 2
    layers = []
    for layer in range(sections):
        distance = lax.rem(layer - section_at + sections, sections)
        chosen = around[0][...]
        for step in range(1, sections):
            chosen = jnp.where(distance == step, around[step][...], chosen)
        layers.append(chosen)
    lefts = [chosen[ranks:] for chosen in layers[:-1]]
    right = jnp.concatenate([chosen[:ranks] for chosen in layers[1:]] + lefts, axis=0)
    right_ref[...] = right
    gram_ref[...] = dot_last(jnp.concatenate(lefts, axis=0), right)


def gram(around):
    sections = len(around)
    ranks = around[0].shape[0] // 2
    columns = around[0].shape[1]
    before = (sections - 1) * ranks
    return pl.pallas_call(
        functools.partial(gram_kernel, sections),
        in_specs=[in_vmem] * sections,
        out_specs=[in_vmem] * 2,
        out_shape=[
            jax.ShapeDtypeStruct((before, 2 * before), f32),
            jax.ShapeDtypeStruct((2 * before, columns), bf16),
        ],
        compiler_params=limited,
        name="gram",
    )(*around)


def chain_kernel(sections, slots, features, per_micro, bounds, counts, *refs):
    projections, grams = refs[:sections], refs[sections:-3]
    sq_ref, factor_ref, mixed_ref = refs[-3:]
    layers = sections
    replica_at = lax.axis_index("replica")
    section_at = lax.axis_index("section")
    tokens = sq_ref.shape[0]
    table = grams[0][...]
    for other in grams[1:]:
        table = table + other[...]
    ranks = projections[0].shape[1] // (3 * slots)
    parts = [[jnp.zeros((tokens, ranks), f32)] * 3 for _ in range(layers)]
    for distance, source in enumerate(projections):
        section = lax.rem(section_at + distance, sections)
        first, after = bounds[replica_at, section], bounds[replica_at, section + 1]
        for slot in range(slots):
            for which in range(3):
                block = which * slots + slot
                piece = source[:, block * ranks : (block + 1) * ranks]
                for layer in range(layers):
                    here = (first + slot == layer) & (layer < after)
                    parts[layer][which] = jnp.where(here, piece, parts[layer][which])
    scale_d = 1.0 / math.sqrt(features)
    scale_r = 1.0 / math.sqrt(ranks)

    def part(layer, which):
        return parts[layer][which]

    def up_down(i, layer):
        return table[i * ranks : (i + 1) * ranks, (layer - 1) * ranks : layer * ranks]

    def up_up(i, j):
        at_column = (layers - 1 + j) * ranks
        return table[i * ranks : (i + 1) * ranks, at_column : at_column + ranks]

    def times(x, y):
        return jnp.dot(x, y, preferred_element_type=f32, precision=exact)

    square = sq_ref[:, 0:1]
    inverses, inners, actives, sigmoids = [], [], [], []
    on_up = [[part(l, 1) for l in range(layers - 1)]]
    for layer in range(layers):
        inverse = lax.rsqrt(jnp.maximum(square, 0.0) * (1.0 / features) + norm_eps)
        on_down = part(layer, 0)
        for i in range(layer):
            on_down = on_down + scale_r * times(actives[i], up_down(i, layer))
        inner = on_down * (inverse * scale_d)
        sigmoid = jax.nn.sigmoid(inner)
        active = (inner * sigmoid).astype(bf16).astype(f32)
        inverses.append(inverse)
        inners.append(inner)
        sigmoids.append(sigmoid)
        actives.append(active)
        if layer < layers - 1:
            now = on_up[-1]
            grown = [now[l] + scale_r * times(active, up_up(layer, l)) for l in range(layers - 1)]
            square = square + scale_r * row_sum(active * (now[layer] + grown[layer]))
            on_up.append(grown)
    scaled = [None] * layers
    kappas = [None] * layers
    for layer in reversed(range(layers)):
        incoming = part(layer, 2)
        for k in range(layer + 1, layers):
            incoming = incoming + scale_d * dot_last(scaled[k], up_down(layer, k), exact)
            incoming = incoming - kappas[k] * on_up[k][layer]
        sigmoid, inner = sigmoids[layer], inners[layer]
        slope = sigmoid * (1.0 + inner * (1.0 - sigmoid))
        error = incoming * scale_r * slope
        scaled[layer] = error * inverses[layer]
        kappas[layer] = (
            inverses[layer] * inverses[layer] * (row_sum(error * inner) * (1.0 / features))
        )

    def owned(values):
        chosen = values[0]
        for layer in range(1, layers):
            chosen = jnp.where(section_at == layer, values[layer], chosen)
        return chosen

    own_error = owned(scaled)
    own_active = owned(actives)
    counted = counted_rows(counts, tokens, per_micro)
    later = jnp.zeros_like(square)
    for k in range(1, layers):
        later = later + jnp.where(k > section_at, kappas[k], 0.0)
    on_hidden = jnp.concatenate([own_error * scale_d, -scale_r * later * own_active], axis=1)
    on_cot = jnp.concatenate(
        [jnp.zeros_like(own_active), jnp.where(counted, own_active * scale_r, 0.0)], axis=1
    )
    factor_ref[...] = jnp.concatenate([on_hidden.T, on_cot.T], axis=1).astype(bf16)
    both = scale_d * scale_r
    for k in range(1, layers):
        cut = slice((k - 1) * ranks, k * ranks)
        across = dot_first(own_active, scaled[k], exact) * both
        mixed_ref[:ranks, cut] = jnp.zeros_like(across)
        mixed_ref[ranks:, cut] = jnp.where(k > section_at, across, 0.0)
    for i in range(layers - 1):
        cut = slice((layers - 1 + i) * ranks, (layers + i) * ranks)
        after = jnp.zeros_like(square)
        for k in range(i + 1, layers):
            after = after + jnp.where(k > section_at, kappas[k], 0.0)
        across = dot_first(own_error, actives[i], exact) * both
        mixed_ref[:ranks, cut] = jnp.where(i < section_at, across, 0.0)
        across = dot_first(own_active, after * actives[i], exact)
        mixed_ref[ranks:, cut] = across * (-scale_r * scale_r)


def chain(bounds, counts, projections, grams, square, slots, features, per_micro):
    sections = len(projections)
    tokens, wide = projections[0].shape
    ranks = wide // (3 * slots)
    inputs = [*projections, *grams, square]
    kernel = functools.partial(chain_kernel, sections, slots, features, per_micro)
    return pl.pallas_call(
        kernel,
        in_specs=[in_smem] * 2 + [in_vmem] * len(inputs),
        out_specs=[in_vmem] * 2,
        out_shape=[
            jax.ShapeDtypeStruct((2 * ranks, 2 * tokens), bf16),
            jax.ShapeDtypeStruct((2 * ranks, 2 * (sections - 1) * ranks), f32),
        ],
        compiler_params=limited,
        name="chain",
    )(bounds, counts, *inputs)


def gradient_kernel(first, factor_ref, h_ref, g_ref, out_ref):
    _, _, ranks, columns = out_ref.shape
    replica_at = lax.axis_index("replica")
    tensor_at = lax.axis_index("tensor")
    tensors = lax.axis_size("tensor")
    factors = factor_ref[...]
    for far in range(2):
        for hop in range(4):
            owner = (replica_at ^ (first + 2 * far)) * tensors + (tensor_at ^ hop)
            cut = pl.ds(pl.multiple_of(owner * columns, columns), columns)
            stacked = jnp.concatenate([h_ref[:, cut], g_ref[:, cut]], axis=0)
            block = jnp.dot(factors, stacked, preferred_element_type=f32).astype(bf16)
            low, high = hop % 2, hop // 2
            out_ref[0, 4 * far + 2 * low + high] = block[:ranks]
            out_ref[1, 4 * low + 2 * far + high] = block[ranks:]


def gradient(factors, hidden, cot, first, columns):
    tokens, features = hidden.shape
    rows = factors.shape[0]
    return pl.pallas_call(
        functools.partial(gradient_kernel, first),
        in_specs=[in_vmem] * 3,
        out_specs=in_vmem,
        out_shape=jax.ShapeDtypeStruct((2, 8, rows // 2, columns), bf16),
        compiler_params=limited,
        cost_estimate=pl.CostEstimate(
            flops=2 * rows * tokens * features,
            bytes_accessed=(2 * tokens + rows) * features,
            transcendentals=0,
        ),
        name="gradient",
    )(factors, hidden, cot)


def update_kernel(kept, near, downs, ups, *refs):
    last, mixed_ref, other_ref, right_ref = refs[:4]
    state, outs, share_ref = refs[4:10], refs[10:16], refs[16]
    mixed = mixed_ref[...] + other_ref[...]
    right = right_ref[...].astype(f32)
    small = jnp.dot(mixed, right, preferred_element_type=f32, precision=exact)
    ranks = small.shape[0] // 2
    for which, steps in enumerate((downs, ups)):
        own = small[which * ranks : (which + 1) * ranks]
        for block in (kept[which, 0], near[which, 0], *(step[0] for step in steps), last[which]):
            own = own + block.astype(f32)
        master, moment, second = (state[2 * kind + which][0] for kind in range(3))
        moment = beta_one * moment + (1.0 - beta_one) * own
        second = beta_two * second + (1.0 - beta_two) * own * own
        master = master - learn_rate * (
            moment / first_fix / (jnp.sqrt(second / second_fix) + adam_eps) + decay_rate * master
        )
        share_ref[which] = master.astype(bf16)
        outs[which][0] = master
        outs[2 + which][0] = moment
        outs[4 + which][0] = second


def update(kept, near, downs, ups, last, mixed, other, right, state):
    _, ranks, columns = state[0].shape

    def kernel(kept, near, down_one, down_two, up_one, up_two, *refs):
        update_kernel(kept, near, (down_one, down_two), (up_one, up_two), *refs)

    return pl.pallas_call(
        kernel,
        in_specs=[in_vmem] * 16,
        out_specs=[in_vmem] * 7,
        out_shape=[jax.ShapeDtypeStruct(array.shape, f32) for array in state]
        + [jax.ShapeDtypeStruct((2, ranks, columns), bf16)],
        compiler_params=limited,
        name="update",
    )(kept, near, *downs, *ups, last, mixed, other, right, *state)


def place_kernel(layout, start, bounds, *refs):
    sources = refs[: len(layout)]
    outs = refs[-4:-2]
    zeros, sem = refs[-2:]
    slots, ranks, features = outs[0].shape
    columns = zeros.shape[1]
    tensors = lax.axis_size("tensor")
    first, after = held_layers(bounds)
    replica_at = lax.axis_index("replica")
    section_at = lax.axis_index("section")
    tensor_at = lax.axis_index("tensor")
    zeros[...] = jnp.zeros_like(zeros)

    def fill(slot, distance, go):
        for (window, blocks), source in zip(layout, sources):
            if window != distance:
                continue
            for i, (which, order, hop) in enumerate(blocks):
                owner = (replica_at ^ order) * tensors + (tensor_at ^ hop)
                cut = pl.ds(pl.multiple_of(owner * columns, columns), columns)
                go(pltpu.make_async_copy(source.at[i], outs[which].at[slot, :, cut], sem))

    def clear(slot, go):
        for out in outs:
            for block in range(features // columns):
                cut = pl.ds(block * columns, columns)
                go(pltpu.make_async_copy(zeros, out.at[slot, :, cut], sem))

    for act in (lambda copy: copy.start(), lambda copy: copy.wait()):
        for slot in range(slots):
            layer = first + slot
            present = layer < after
            for distance in range(2):

                @pl.when(present & (layer - section_at == distance))
                def _():
                    fill(slot, distance, act)

            if start:

                @pl.when(jnp.logical_not(present))
                def _():
                    clear(slot, act)


def place(bounds, pieces, before, slots, ranks, features):
    layout = [piece[:2] for piece in pieces]
    arrays = [piece[2] for piece in pieces]
    columns = arrays[0].shape[-1]
    return pl.pallas_call(
        functools.partial(place_kernel, layout, not before),
        in_specs=[in_smem] + [in_vmem] * len(arrays) + [in_hbm] * len(before),
        out_specs=[in_hbm] * 2,
        out_shape=[jax.ShapeDtypeStruct((slots, ranks, features), bf16)] * 2,
        scratch_shapes=[pltpu.VMEM((ranks, columns), bf16), pltpu.SemaphoreType.DMA],
        input_output_aliases={1 + len(arrays) + i: i for i in range(len(before))},
        compiler_params=limited,
        cost_estimate=pl.CostEstimate(
            flops=0,
            bytes_accessed=4 * sum(array.size for array in arrays),
            transcendentals=0,
        ),
        name="place",
    )(bounds, *arrays, *before)


def swapped(block, axis, distance):
    route = [(i, i ^ distance) for i in range(lax.axis_size(axis))]
    return lax.ppermute(block, axis, route)


def swaps(block, axis):
    return [swapped(block, axis, k) for k in range(1, lax.axis_size(axis))]


def from_next(block, distance=1):
    size = lax.axis_size("section")
    route = [((i + distance) % size, i) for i in range(size)]
    return lax.ppermute(block, "section", route)


def following_layer(block):
    size = lax.axis_size("section")
    return lax.ppermute(block, "section", [(i + 1, i) for i in range(size - 1)])


def summed(*blocks):
    total = blocks[0].astype(f32)
    for block in blocks[1:]:
        total = total + block.astype(f32)
    return total.astype(bf16)


def reduced(factors, hidden, cot, columns, mixed):
    sent = gradient(factors, hidden, cot, 1, columns)
    near = swapped(sent, "replica", 1)
    kept = gradient(factors, hidden, cot, 0, columns)

    def part(which, cut, *steps):
        return summed(kept[which, cut], near[which, cut], *steps)

    high, low = slice(4, 8), slice(2, 4)
    def added(axis, distance):
        return mixed + swapped(mixed, axis, distance)

    down_one = swapped(part(0, high), "replica", 2)
    up_one = swapped(part(1, high), "tensor", 1)
    mixed = added("replica", 1)
    mixed = added("tensor", 2)
    down_one, up_one, mixed = lax.optimization_barrier((down_one, up_one, mixed))
    down_two = swapped(part(0, low, down_one[2:]), "tensor", 1)
    up_two = swapped(part(1, low, up_one[2:]), "replica", 2)
    mixed = added("tensor", 1)
    down_two, up_two, mixed = lax.optimization_barrier((down_two, up_two, mixed))
    last = jnp.stack([part(0, 1, down_one[1], down_two[1]), part(1, 1, up_one[1], up_two[1])])
    last = swapped(last, "tensor", 2)
    other = swapped(mixed, "replica", 2)
    return (kept, near, (down_one, down_two), (up_one, up_two), last, mixed, other)


def crossed(piece, axis, distance):
    window, blocks, array = piece
    blocks = [
        (which, order ^ distance, hop) if axis == "replica" else (which, order, hop ^ distance)
        for which, order, hop in blocks
    ]
    return (window, blocks, swapped(array, axis, distance))


def fetched(piece):
    _, blocks, array = piece
    return (1, blocks, following_layer(array))


def picked(piece, cut):
    return (piece[0], piece[1][cut], piece[2][cut])


def joined(*pieces):
    blocks = [block for piece in pieces for block in piece[1]]
    return (pieces[0][0], blocks, jnp.concatenate([piece[2] for piece in pieces]))


def spread(share, bounds, slots, features):
    ranks = share.shape[1]
    own = (0, [(0, 0, 0), (1, 0, 0)], share)
    one = crossed(own, "tensor", 2)
    next_own = fetched(own)
    downs = joined(picked(own, slice(0, 1)), picked(one, slice(0, 1)))
    ups = joined(picked(own, slice(1, 2)), picked(one, slice(1, 2)))
    down_two = crossed(downs, "tensor", 1)
    up_two = crossed(ups, "replica", 2)
    next_one = fetched(one)
    two = joined(down_two, up_two)
    down_three = crossed(joined(downs, down_two), "replica", 2)
    up_three = crossed(joined(ups, up_two), "tensor", 1)
    next_two = fetched(two)
    down_far, up_far, next_far = lax.optimization_barrier(
        (down_three[2], up_three[2], next_two[2])
    )
    down_three, up_three = (*down_three[:2], down_far), (*up_three[:2], up_far)
    next_two = (*next_two[:2], next_far)
    near = joined(own, one, two)
    near_core = crossed(near, "replica", 1)
    last, first, second = slice(3, 4), slice(0, 1), slice(1, 2)
    next_end = fetched(joined(picked(down_three, last), picked(up_three, last)))
    next_near = joined(next_own, next_one, next_two)
    down_end = joined(*(picked(piece, first) for piece in (next_own, next_one, next_two)))
    up_end = joined(
        picked(next_own, second), picked(next_one, second), picked(next_two, slice(2, 3))
    )
    end = joined(crossed(down_end, "replica", 2), crossed(up_end, "tensor", 1), next_end)
    placed = place(bounds, [near, near_core], [], slots, ranks, features)
    far = joined(down_three, up_three)
    far_array, *placed = lax.optimization_barrier((far[2], *placed))
    far = (*far[:2], far_array)
    for group in ((far, next_near), (end,)):
        pieces = [*group, *(crossed(piece, "replica", 1) for piece in group)]
        placed = place(bounds, pieces, placed, slots, ranks, features)
    return placed


def on_device(
    inputs,
    cotangent,
    micro_counts,
    bounds,
    holder_down,
    holder_up,
    master_down,
    master_up,
    moment_down,
    moment_up,
    second_down,
    second_up,
):
    sections = lax.axis_size("section")
    replicas = lax.axis_size("replica")
    tensors = lax.axis_size("tensor")
    assert replicas == 4 and tensors == 4
    _, micros, per_micro, features = inputs.shape
    slots = holder_down.shape[2]
    hidden = inputs.reshape(micros * per_micro, features)
    cot = cotangent.reshape(micros * per_micro, features)

    owned = jnp.concatenate([master_down[0], master_up[0]], axis=0).astype(bf16)
    around = [from_next(owned, d) for d in range(1, sections)]
    by_cot, cot, ups = project_back(cot, holder_up[0, 0])
    around, by_cot = lax.optimization_barrier((around, by_cot))
    table, right = gram([owned, *around])
    table, hidden = lax.optimization_barrier((table, hidden))
    by_down, square = project_down(hidden, holder_down[0, 0])
    table = table + sum(swaps(table, "replica"))
    table, by_down = lax.optimization_barrier((table, by_down))
    projected = project_up(micro_counts, hidden, ups, by_down, by_cot, per_micro)
    projections = [projected] + [from_next(projected, d) for d in range(1, sections)]
    table = table + swapped(table, "tensor", 1)
    tables = [table, swapped(table, "tensor", 2)]
    factors, mixed = chain(
        bounds, micro_counts, projections, tables, square, slots, features, per_micro
    )

    parts = reduced(factors, hidden, cot, master_down.shape[2], mixed)
    state = [master_down, master_up, moment_down, moment_up, second_down, second_up]
    updated = update(*parts, right, state)
    placed = spread(updated[6], bounds, slots, features)
    return (placed[0][None, None], placed[1][None, None], *updated[:6])


def solution(mesh):
    held = P("replica", "section", None, None, None)
    owned = P("section", None, ("replica", "tensor"))
    tokens = P("replica", None, "tensor", None)
    return jax.shard_map(
        on_device,
        mesh=mesh,
        in_specs=(tokens, tokens, P(), P(), held, held) + (owned,) * 6,
        out_specs=(held, held) + (owned,) * 6,
        check_vma=False,
    )
```

```python
import functools
import math

import jax
import jax.numpy as jnp
from jax import lax
from jax.experimental import pallas as pl
from jax.experimental.pallas import tpu as pltpu
from jax.sharding import PartitionSpec as P

norm_eps = 1e-06
learn_rate = 0.01
beta_one = 0.9
beta_two = 0.95
decay_rate = 0.1
adam_eps = 1e-08
first_fix = 0.9999734386011124
second_fix = 0.9940794707796659

f32 = jnp.float32
bf16 = jnp.bfloat16
exact = lax.Precision.HIGHEST
in_smem = pl.BlockSpec(memory_space=pltpu.SMEM)
in_vmem = pl.BlockSpec(memory_space=pltpu.VMEM)
in_hbm = pl.BlockSpec(memory_space=pltpu.HBM)
limited = pltpu.CompilerParams(vmem_limit_bytes=16 * 1024 * 1024)


def held_layers(bounds):
    at_row = lax.axis_index("replica")
    at_column = lax.axis_index("section")
    return bounds[at_row, at_column], bounds[at_row, at_column + 1]


def counted_rows(counts, tokens, per_micro):
    rows = lax.broadcasted_iota(jnp.int32, (tokens, 1), 0)
    return rows < counts[lax.axis_index("replica")] * per_micro


def dot_last(x, y, precision=None):
    return lax.dot_general(
        x, y, (((1,), (1,)), ((), ())), preferred_element_type=f32, precision=precision
    )


def dot_first(x, y, precision=None):
    return lax.dot_general(
        x, y, (((0,), (0,)), ((), ())), preferred_element_type=f32, precision=precision
    )


def row_sum(x):
    return jnp.sum(x, axis=-1, keepdims=True)


def project_kernel(steps, h_in, down_in, up_in, *refs):
    out_ref, sq_ref, h_ref, up_ref, down_ref, sems = refs
    slots, ranks, features = down_in.shape
    tokens = h_ref.shape[0]
    width = features // steps
    copies = []
    for step in range(steps):
        cut = pl.ds(step * width, width)
        moves = [(h_in.at[:, cut], h_ref.at[:, cut])]
        for slot in range(slots):
            rows = pl.ds(slot * ranks, ranks)
            moves.append((down_in.at[slot, :, cut], down_ref.at[rows, cut]))
            moves.append((up_in.at[slot, :, cut], up_ref.at[rows, cut]))
        copies.append(
            [
                pltpu.make_async_copy(source, target, sems.at[step, i])
                for i, (source, target) in enumerate(moves)
            ]
        )
        for copy in copies[-1]:
            copy.start()
    ph = jnp.zeros((tokens, 2 * slots * ranks), f32)
    square = jnp.zeros((tokens, 128), f32)
    for step in range(steps):
        for copy in copies[step]:
            copy.wait()
        cut = pl.ds(step * width, width)
        h = h_ref[:, cut]
        ph = ph + dot_last(h, jnp.concatenate([down_ref[:, cut], up_ref[:, cut]], axis=0))
        wide = h.astype(f32)
        wide = wide * wide
        for lane in range(0, width, 128):
            square = square + wide[:, lane : lane + 128]
    sq_ref[...] = jnp.broadcast_to(row_sum(square), square.shape)
    out_ref[...] = ph


def project(hidden, downs, ups):
    tokens, features = hidden.shape
    slots, ranks, _ = downs.shape
    steps = 8
    sources = [pltpu.with_memory_space_constraint(x, pltpu.HBM) for x in (hidden, downs, ups)]
    return pl.pallas_call(
        functools.partial(project_kernel, steps),
        in_specs=[in_hbm] * 3,
        out_specs=[in_vmem] * 4,
        out_shape=[
            jax.ShapeDtypeStruct((tokens, 2 * slots * ranks), f32),
            jax.ShapeDtypeStruct((tokens, 128), f32),
            jax.ShapeDtypeStruct((tokens, features), bf16),
            jax.ShapeDtypeStruct((slots * ranks, features), bf16),
        ],
        scratch_shapes=[
            pltpu.VMEM((slots * ranks, features), bf16),
            pltpu.SemaphoreType.DMA((steps, 1 + 2 * slots)),
        ],
        compiler_params=limited,
        cost_estimate=pl.CostEstimate(
            flops=4 * tokens * slots * ranks * features,
            bytes_accessed=2 * (tokens + 2 * slots * ranks) * features,
            transcendentals=0,
        ),
        name="project",
    )(*sources)


def project_back_kernel(per_micro, counts, by_hidden, g_ref, up_ref, out_ref):
    pg = dot_last(g_ref[...], up_ref[...])
    pg = jnp.where(counted_rows(counts, pg.shape[0], per_micro), pg, 0.0)
    ahead = by_hidden.shape[1]
    out_ref[:, :ahead] = by_hidden[...]
    out_ref[:, ahead:] = pg


def project_back(counts, by_hidden, cot, ups, per_micro):
    tokens, features = cot.shape
    columns = by_hidden.shape[1] + ups.shape[0]
    return pl.pallas_call(
        functools.partial(project_back_kernel, per_micro),
        in_specs=[in_smem] + [in_vmem] * 3,
        out_specs=in_vmem,
        out_shape=jax.ShapeDtypeStruct((tokens, columns), f32),
        compiler_params=limited,
        cost_estimate=pl.CostEstimate(
            flops=2 * tokens * ups.shape[0] * features,
            bytes_accessed=2 * (tokens + ups.shape[0]) * features,
            transcendentals=0,
        ),
        name="project_back",
    )(counts, by_hidden, cot, ups)


def gram_kernel(sections, *refs):
    around = refs[:sections]
    gram_ref, right_ref = refs[sections:]
    section_at = lax.axis_index("section")
    ranks = around[0].shape[0] // 2
    layers = []
    for layer in range(sections):
        distance = lax.rem(layer - section_at + sections, sections)
        chosen = around[0][...]
        for step in range(1, sections):
            chosen = jnp.where(distance == step, around[step][...], chosen)
        layers.append(chosen)
    lefts = [chosen[ranks:] for chosen in layers[:-1]]
    right = jnp.concatenate([chosen[:ranks] for chosen in layers[1:]] + lefts, axis=0)
    right_ref[...] = right
    gram_ref[...] = dot_last(jnp.concatenate(lefts, axis=0), right)


def gram(around):
    sections = len(around)
    ranks = around[0].shape[0] // 2
    columns = around[0].shape[1]
    before = (sections - 1) * ranks
    return pl.pallas_call(
        functools.partial(gram_kernel, sections),
        in_specs=[in_vmem] * sections,
        out_specs=[in_vmem] * 2,
        out_shape=[
            jax.ShapeDtypeStruct((before, 2 * before), f32),
            jax.ShapeDtypeStruct((2 * before, columns), bf16),
        ],
        compiler_params=limited,
        name="gram",
    )(*around)


def chain_kernel(sections, slots, features, per_micro, bounds, counts, *refs):
    projections, grams = refs[:sections], refs[sections:-3]
    sq_ref, factor_ref, mixed_ref = refs[-3:]
    layers = sections
    replica_at = lax.axis_index("replica")
    section_at = lax.axis_index("section")
    tokens = sq_ref.shape[0]
    table = grams[0][...]
    for other in grams[1:]:
        table = table + other[...]
    ranks = projections[0].shape[1] // (3 * slots)
    parts = [[jnp.zeros((tokens, ranks), f32)] * 3 for _ in range(layers)]
    for distance, source in enumerate(projections):
        section = lax.rem(section_at + distance, sections)
        first, after = bounds[replica_at, section], bounds[replica_at, section + 1]
        for slot in range(slots):
            for which in range(3):
                block = which * slots + slot
                piece = source[:, block * ranks : (block + 1) * ranks]
                for layer in range(layers):
                    here = (first + slot == layer) & (layer < after)
                    parts[layer][which] = jnp.where(here, piece, parts[layer][which])
    scale_d = 1.0 / math.sqrt(features)
    scale_r = 1.0 / math.sqrt(ranks)

    def part(layer, which):
        return parts[layer][which]

    def up_down(i, layer):
        return table[i * ranks : (i + 1) * ranks, (layer - 1) * ranks : layer * ranks]

    def up_up(i, j):
        at_column = (layers - 1 + j) * ranks
        return table[i * ranks : (i + 1) * ranks, at_column : at_column + ranks]

    def times(x, y):
        return jnp.dot(x, y, preferred_element_type=f32, precision=exact)

    square = sq_ref[:, 0:1]
    inverses, inners, actives, sigmoids = [], [], [], []
    on_up = [[part(l, 1) for l in range(layers - 1)]]
    for layer in range(layers):
        inverse = lax.rsqrt(jnp.maximum(square, 0.0) * (1.0 / features) + norm_eps)
        on_down = part(layer, 0)
        for i in range(layer):
            on_down = on_down + scale_r * times(actives[i], up_down(i, layer))
        inner = on_down * (inverse * scale_d)
        sigmoid = jax.nn.sigmoid(inner)
        active = (inner * sigmoid).astype(bf16).astype(f32)
        inverses.append(inverse)
        inners.append(inner)
        sigmoids.append(sigmoid)
        actives.append(active)
        if layer < layers - 1:
            now = on_up[-1]
            grown = [now[l] + scale_r * times(active, up_up(layer, l)) for l in range(layers - 1)]
            square = square + scale_r * row_sum(active * (now[layer] + grown[layer]))
            on_up.append(grown)
    scaled = [None] * layers
    kappas = [None] * layers
    for layer in reversed(range(layers)):
        incoming = part(layer, 2)
        for k in range(layer + 1, layers):
            incoming = incoming + scale_d * dot_last(scaled[k], up_down(layer, k), exact)
            incoming = incoming - kappas[k] * on_up[k][layer]
        sigmoid, inner = sigmoids[layer], inners[layer]
        slope = sigmoid * (1.0 + inner * (1.0 - sigmoid))
        error = incoming * scale_r * slope
        scaled[layer] = error * inverses[layer]
        kappas[layer] = (
            inverses[layer] * inverses[layer] * (row_sum(error * inner) * (1.0 / features))
        )

    def owned(values):
        chosen = values[0]
        for layer in range(1, layers):
            chosen = jnp.where(section_at == layer, values[layer], chosen)
        return chosen

    own_error = owned(scaled)
    own_active = owned(actives)
    counted = counted_rows(counts, tokens, per_micro)
    later = jnp.zeros_like(square)
    for k in range(1, layers):
        later = later + jnp.where(k > section_at, kappas[k], 0.0)
    on_hidden = jnp.concatenate([own_error * scale_d, -scale_r * later * own_active], axis=1)
    on_cot = jnp.concatenate(
        [jnp.zeros_like(own_active), jnp.where(counted, own_active * scale_r, 0.0)], axis=1
    )
    factor_ref[...] = jnp.concatenate([on_hidden.T, on_cot.T], axis=1).astype(bf16)
    both = scale_d * scale_r
    for k in range(1, layers):
        cut = slice((k - 1) * ranks, k * ranks)
        across = dot_first(own_active, scaled[k], exact) * both
        mixed_ref[:ranks, cut] = jnp.zeros_like(across)
        mixed_ref[ranks:, cut] = jnp.where(k > section_at, across, 0.0)
    for i in range(layers - 1):
        cut = slice((layers - 1 + i) * ranks, (layers + i) * ranks)
        after = jnp.zeros_like(square)
        for k in range(i + 1, layers):
            after = after + jnp.where(k > section_at, kappas[k], 0.0)
        across = dot_first(own_error, actives[i], exact) * both
        mixed_ref[:ranks, cut] = jnp.where(i < section_at, across, 0.0)
        across = dot_first(own_active, after * actives[i], exact)
        mixed_ref[ranks:, cut] = across * (-scale_r * scale_r)


def chain(bounds, counts, projections, grams, square, slots, features, per_micro):
    sections = len(projections)
    tokens, wide = projections[0].shape
    ranks = wide // (3 * slots)
    inputs = [*projections, *grams, square]
    kernel = functools.partial(chain_kernel, sections, slots, features, per_micro)
    return pl.pallas_call(
        kernel,
        in_specs=[in_smem] * 2 + [in_vmem] * len(inputs),
        out_specs=[in_vmem] * 2,
        out_shape=[
            jax.ShapeDtypeStruct((2 * ranks, 2 * tokens), bf16),
            jax.ShapeDtypeStruct((2 * ranks, 2 * (sections - 1) * ranks), f32),
        ],
        compiler_params=limited,
        name="chain",
    )(bounds, counts, *inputs)


def gradient_kernel(first, lead, factor_ref, h_ref, g_ref, out_ref):
    _, _, ranks, columns = out_ref.shape
    tokens = h_ref.shape[0]
    replica_at = lax.axis_index("replica")
    tensor_at = lax.axis_index("tensor")
    tensors = lax.axis_size("tensor")
    down = factor_ref[:ranks, :tokens]
    up = factor_ref[ranks:]
    for middle in range(2):
        for high in range(2):
            for which, (far, low) in enumerate(((lead, middle), (middle, lead))):
                hop = low + 2 * high
                owner = (replica_at ^ (first + 2 * far)) * tensors + (tensor_at ^ hop)
                cut = pl.ds(pl.multiple_of(owner * columns, columns), columns)
                if which == 0:
                    block = jnp.dot(down, h_ref[:, cut], preferred_element_type=f32)
                else:
                    stacked = jnp.concatenate([h_ref[:, cut], g_ref[:, cut]], axis=0)
                    block = jnp.dot(up, stacked, preferred_element_type=f32)
                out_ref[which, 2 * middle + high] = block.astype(bf16)


def gradient(factors, hidden, cot, first, lead, columns):
    tokens, features = hidden.shape
    rows = factors.shape[0]
    return pl.pallas_call(
        functools.partial(gradient_kernel, first, lead),
        in_specs=[in_vmem] * 3,
        out_specs=in_vmem,
        out_shape=jax.ShapeDtypeStruct((2, 4, rows // 2, columns), bf16),
        compiler_params=limited,
        cost_estimate=pl.CostEstimate(
            flops=rows * tokens * features,
            bytes_accessed=(tokens + rows // 2) * features,
            transcendentals=0,
        ),
        name="gradient",
    )(factors, hidden, cot)


def update_kernel(kept, near, downs, ups, *refs):
    last, mixed_ref, other_ref, right_ref = refs[:4]
    state, outs, share_ref = refs[4:10], refs[10:16], refs[16]
    mixed = mixed_ref[...] + other_ref[...]
    right = right_ref[...].astype(f32)
    small = jnp.dot(mixed, right, preferred_element_type=f32, precision=exact)
    ranks = small.shape[0] // 2
    for which, steps in enumerate((downs, ups)):
        own = small[which * ranks : (which + 1) * ranks]
        for block in (kept[which, 0], near[which, 0], *(step[0] for step in steps), last[which]):
            own = own + block.astype(f32)
        master, moment, second = (state[2 * kind + which][0] for kind in range(3))
        moment = beta_one * moment + (1.0 - beta_one) * own
        second = beta_two * second + (1.0 - beta_two) * own * own
        master = master - learn_rate * (
            moment / first_fix / (jnp.sqrt(second / second_fix) + adam_eps) + decay_rate * master
        )
        share_ref[which] = master.astype(bf16)
        outs[which][0] = master
        outs[2 + which][0] = moment
        outs[4 + which][0] = second


def update(kept, near, downs, ups, last, mixed, other, right, state):
    _, ranks, columns = state[0].shape

    def kernel(kept, near, down_one, down_two, up_one, up_two, *refs):
        update_kernel(kept, near, (down_one, down_two), (up_one, up_two), *refs)

    return pl.pallas_call(
        kernel,
        in_specs=[in_vmem] * 16,
        out_specs=[in_vmem] * 7,
        out_shape=[jax.ShapeDtypeStruct(array.shape, f32) for array in state]
        + [jax.ShapeDtypeStruct((2, ranks, columns), bf16)],
        compiler_params=limited,
        name="update",
    )(kept, near, *downs, *ups, last, mixed, other, right, *state)


def place_kernel(layout, start, bounds, *refs):
    sources = refs[: len(layout)]
    outs = refs[-4:-2]
    zeros, sem = refs[-2:]
    slots, ranks, features = outs[0].shape
    columns = zeros.shape[1]
    tensors = lax.axis_size("tensor")
    first, after = held_layers(bounds)
    replica_at = lax.axis_index("replica")
    section_at = lax.axis_index("section")
    tensor_at = lax.axis_index("tensor")
    zeros[...] = jnp.zeros_like(zeros)

    def fill(slot, distance, go):
        for blocks, source in zip(layout, sources):
            for i, (window, which, order, hop) in enumerate(blocks):
                if window != distance:
                    continue
                owner = (replica_at ^ order) * tensors + (tensor_at ^ hop)
                cut = pl.ds(pl.multiple_of(owner * columns, columns), columns)
                go(pltpu.make_async_copy(source.at[i], outs[which].at[slot, :, cut], sem))

    def clear(slot, go):
        for out in outs:
            for block in range(features // columns):
                cut = pl.ds(block * columns, columns)
                go(pltpu.make_async_copy(zeros, out.at[slot, :, cut], sem))

    for act in (lambda copy: copy.start(), lambda copy: copy.wait()):
        for slot in range(slots):
            layer = first + slot
            present = layer < after
            for distance in range(2):

                @pl.when(present & (layer - section_at == distance))
                def _():
                    fill(slot, distance, act)

            if start:

                @pl.when(jnp.logical_not(present))
                def _():
                    clear(slot, act)


def place(bounds, pieces, before, slots, ranks, features):
    layout = [blocks for blocks, _ in pieces]
    arrays = [array for _, array in pieces]
    columns = arrays[0].shape[-1]
    return pl.pallas_call(
        functools.partial(place_kernel, layout, not before),
        in_specs=[in_smem] + [in_vmem] * len(arrays) + [in_hbm] * len(before),
        out_specs=[in_hbm] * 2,
        out_shape=[jax.ShapeDtypeStruct((slots, ranks, features), bf16)] * 2,
        scratch_shapes=[pltpu.VMEM((ranks, columns), bf16), pltpu.SemaphoreType.DMA],
        input_output_aliases={1 + len(arrays) + i: i for i in range(len(before))},
        compiler_params=limited,
        cost_estimate=pl.CostEstimate(
            flops=0,
            bytes_accessed=4 * sum(array.size for array in arrays),
            transcendentals=0,
        ),
        name="place",
    )(bounds, *arrays, *before)


def swapped(block, axis, distance):
    route = [(i, i ^ distance) for i in range(lax.axis_size(axis))]
    return lax.ppermute(block, axis, route)


def swaps(block, axis):
    return [swapped(block, axis, k) for k in range(1, lax.axis_size(axis))]


def from_next(block, distance=1):
    size = lax.axis_size("section")
    route = [((i + distance) % size, i) for i in range(size)]
    return lax.ppermute(block, "section", route)


def following_layer(block):
    size = lax.axis_size("section")
    return lax.ppermute(block, "section", [(i + 1, i) for i in range(size - 1)])


def summed(*blocks):
    total = blocks[0].astype(f32)
    for block in blocks[1:]:
        total = total + block.astype(f32)
    return total.astype(bf16)


def reduced(factors, hidden, cot, columns, mixed):
    def halves(lead, factors):
        sent = gradient(factors, hidden, cot, 1, lead, columns)
        return swapped(sent, "replica", 1), gradient(factors, hidden, cot, 0, lead, columns)

    near, kept = halves(1, factors)
    mixed = mixed + swapped(mixed, "tensor", 1)
    down_one = summed(kept[0], near[0])
    up_one = summed(kept[1], near[1])
    down_one, up_one, mixed, factors = lax.optimization_barrier(
        (down_one, up_one, mixed, factors)
    )
    down_one = swapped(down_one, "replica", 2)
    up_one = swapped(up_one, "tensor", 1)
    near, kept = halves(0, factors)

    def part(which, cut, *steps):
        return summed(kept[which, cut], near[which, cut], *steps)

    low = slice(2, 4)
    down_two = swapped(part(0, low, down_one[2:]), "tensor", 1)
    up_two = swapped(part(1, low, up_one[2:]), "replica", 2)
    last = jnp.stack([part(0, 1, down_one[1], down_two[1]), part(1, 1, up_one[1], up_two[1])])
    last = swapped(last, "tensor", 2)
    for axis, distance in (("tensor", 2), ("replica", 1)):
        mixed = mixed + swapped(mixed, axis, distance)
    other = swapped(mixed, "replica", 2)
    return (kept, near, (down_one, down_two), (up_one, up_two), last, mixed, other)


def crossed(piece, axis, distance):
    blocks, array = piece
    blocks = [
        (window, which, order ^ distance, hop)
        if axis == "replica"
        else (window, which, order, hop ^ distance)
        for window, which, order, hop in blocks
    ]
    return blocks, swapped(array, axis, distance)


def fetched(piece):
    blocks, array = piece
    return [(1, *block[1:]) for block in blocks], following_layer(array)


def picked(piece, at):
    return piece[0][at : at + 1], piece[1][at : at + 1]


def joined(*pieces):
    blocks = [block for piece in pieces for block in piece[0]]
    return blocks, jnp.concatenate([array for _, array in pieces])


def spread(share, bounds, slots, features):
    ranks = share.shape[1]
    own = ([(0, 0, 0, 0), (0, 1, 0, 0)], share)
    one = crossed(own, "tensor", 2)
    next_own = fetched(own)
    downs = joined(picked(own, 0), picked(one, 0))
    ups = joined(picked(own, 1), picked(one, 1))
    down_two = crossed(downs, "tensor", 1)
    up_two = crossed(ups, "replica", 2)
    next_one = fetched(one)
    two = joined(down_two, up_two)
    down_three = crossed(joined(downs, down_two), "replica", 2)
    up_three = crossed(joined(ups, up_two), "tensor", 1)
    next_two = fetched(two)
    next_end = fetched(joined(picked(down_three, 3), picked(up_three, 3)))
    _, _, next_array = lax.optimization_barrier((down_three[1], up_three[1], next_two[1]))
    next_two = (next_two[0], next_array)
    down_end = joined(picked(next_own, 0), picked(next_one, 0), picked(next_two, 0))
    up_end = joined(picked(next_own, 1), picked(next_one, 1), picked(next_two, 2))
    end = joined(crossed(down_end, "replica", 2), crossed(up_end, "tensor", 1), next_end)
    near = joined(own, one, two)
    far = joined(down_three, up_three)
    next_near = joined(next_own, next_one, next_two)
    near_core, far_core, next_core, end_core = (
        crossed(piece, "replica", 1) for piece in (near, far, next_near, end)
    )
    placed = place(
        bounds, [near, near_core, far, far_core, next_near, next_core], [], slots, ranks, features
    )
    placed = place(bounds, [end, end_core], placed, slots, ranks, features)
    return placed


def on_device(
    inputs,
    cotangent,
    micro_counts,
    bounds,
    holder_down,
    holder_up,
    master_down,
    master_up,
    moment_down,
    moment_up,
    second_down,
    second_up,
):
    sections = lax.axis_size("section")
    replicas = lax.axis_size("replica")
    tensors = lax.axis_size("tensor")
    assert replicas == 4 and tensors == 4
    _, micros, per_micro, features = inputs.shape
    slots = holder_down.shape[2]
    hidden = inputs.reshape(micros * per_micro, features)
    cot = cotangent.reshape(micros * per_micro, features)

    owned = jnp.concatenate([master_down[0], master_up[0]], axis=0).astype(bf16)
    around = [from_next(owned, d) for d in range(1, sections)]
    by_hidden, square, hidden, ups = project(hidden, holder_down[0, 0], holder_up[0, 0])
    around, by_hidden = lax.optimization_barrier((around, by_hidden))
    table, right = gram([owned, *around])
    table, ups = lax.optimization_barrier((table, ups))
    projected = project_back(micro_counts, by_hidden, cot, ups, per_micro)
    table = table + sum(swaps(table, "replica"))
    projections = [projected] + [from_next(projected, d) for d in range(1, sections)]
    table = table + swapped(table, "tensor", 1)
    tables = [table, swapped(table, "tensor", 2)]
    factors, mixed = chain(
        bounds, micro_counts, projections, tables, square, slots, features, per_micro
    )

    parts = reduced(factors, hidden, cot, master_down.shape[2], mixed)
    state = [master_down, master_up, moment_down, moment_up, second_down, second_up]
    updated = update(*parts, right, state)
    placed = spread(updated[6], bounds, slots, features)
    return (placed[0][None, None], placed[1][None, None], *updated[:6])


def solution(mesh):
    held = P("replica", "section", None, None, None)
    owned = P("section", None, ("replica", "tensor"))
    tokens = P("replica", None, "tensor", None)
    return jax.shard_map(
        on_device,
        mesh=mesh,
        in_specs=(tokens, tokens, P(), P(), held, held) + (owned,) * 6,
        out_specs=(held, held) + (owned,) * 6,
        check_vma=False,
    )
```

```python
import functools
import math

import jax
import jax.numpy as jnp
from jax import lax
from jax.experimental import pallas as pl
from jax.experimental.pallas import tpu as pltpu
from jax.sharding import PartitionSpec as P

norm_eps = 1e-06
learn_rate = 0.01
beta_one = 0.9
beta_two = 0.95
decay_rate = 0.1
adam_eps = 1e-08
first_fix = 0.9999734386011124
second_fix = 0.9940794707796659

f32 = jnp.float32
bf16 = jnp.bfloat16
exact = lax.Precision.HIGHEST
in_smem = pl.BlockSpec(memory_space=pltpu.SMEM)
in_vmem = pl.BlockSpec(memory_space=pltpu.VMEM)
in_hbm = pl.BlockSpec(memory_space=pltpu.HBM)
limited = pltpu.CompilerParams(vmem_limit_bytes=16 * 1024 * 1024)


def held_layers(bounds):
    at_row = lax.axis_index("replica")
    at_column = lax.axis_index("section")
    return bounds[at_row, at_column], bounds[at_row, at_column + 1]


def counted_rows(counts, tokens, per_micro):
    rows = lax.broadcasted_iota(jnp.int32, (tokens, 1), 0)
    return rows < counts[lax.axis_index("replica")] * per_micro


def dot_last(x, y, precision=None):
    return lax.dot_general(
        x, y, (((1,), (1,)), ((), ())), preferred_element_type=f32, precision=precision
    )


def dot_first(x, y, precision=None):
    return lax.dot_general(
        x, y, (((0,), (0,)), ((), ())), preferred_element_type=f32, precision=precision
    )


def row_sum(x):
    return jnp.sum(x, axis=-1, keepdims=True)


def project_kernel(steps, h_in, down_in, up_in, *refs):
    out_ref, sq_ref, h_ref, up_ref, down_ref, sems = refs
    slots, ranks, features = down_in.shape
    tokens = h_ref.shape[0]
    width = features // steps
    copies = []
    for step in range(steps):
        cut = pl.ds(step * width, width)
        moves = [(h_in.at[:, cut], h_ref.at[:, cut])]
        for slot in range(slots):
            rows = pl.ds(slot * ranks, ranks)
            moves.append((down_in.at[slot, :, cut], down_ref.at[rows, cut]))
            moves.append((up_in.at[slot, :, cut], up_ref.at[rows, cut]))
        copies.append(
            [
                pltpu.make_async_copy(source, target, sems.at[step, i])
                for i, (source, target) in enumerate(moves)
            ]
        )
        for copy in copies[-1]:
            copy.start()
    ph = jnp.zeros((tokens, 2 * slots * ranks), f32)
    square = jnp.zeros((tokens, 128), f32)
    for step in range(steps):
        for copy in copies[step]:
            copy.wait()
        cut = pl.ds(step * width, width)
        h = h_ref[:, cut]
        ph = ph + dot_last(h, jnp.concatenate([down_ref[:, cut], up_ref[:, cut]], axis=0))
        wide = h.astype(f32)
        wide = wide * wide
        for lane in range(0, width, 128):
            square = square + wide[:, lane : lane + 128]
    sq_ref[...] = jnp.broadcast_to(row_sum(square), square.shape)
    out_ref[...] = ph


def project(hidden, downs, ups):
    tokens, features = hidden.shape
    slots, ranks, _ = downs.shape
    steps = 8
    sources = [pltpu.with_memory_space_constraint(x, pltpu.HBM) for x in (hidden, downs, ups)]
    return pl.pallas_call(
        functools.partial(project_kernel, steps),
        in_specs=[in_hbm] * 3,
        out_specs=[in_vmem] * 4,
        out_shape=[
            jax.ShapeDtypeStruct((tokens, 2 * slots * ranks), f32),
            jax.ShapeDtypeStruct((tokens, 128), f32),
            jax.ShapeDtypeStruct((tokens, features), bf16),
            jax.ShapeDtypeStruct((slots * ranks, features), bf16),
        ],
        scratch_shapes=[
            pltpu.VMEM((slots * ranks, features), bf16),
            pltpu.SemaphoreType.DMA((steps, 1 + 2 * slots)),
        ],
        compiler_params=limited,
        cost_estimate=pl.CostEstimate(
            flops=4 * tokens * slots * ranks * features,
            bytes_accessed=2 * (tokens + 2 * slots * ranks) * features,
            transcendentals=0,
        ),
        name="project",
    )(*sources)


def project_back_kernel(per_micro, counts, by_hidden, g_ref, up_ref, out_ref):
    pg = dot_last(g_ref[...], up_ref[...])
    pg = jnp.where(counted_rows(counts, pg.shape[0], per_micro), pg, 0.0)
    ahead = by_hidden.shape[1]
    out_ref[:, :ahead] = by_hidden[...]
    out_ref[:, ahead:] = pg


def project_back(counts, by_hidden, cot, ups, per_micro):
    tokens, features = cot.shape
    columns = by_hidden.shape[1] + ups.shape[0]
    return pl.pallas_call(
        functools.partial(project_back_kernel, per_micro),
        in_specs=[in_smem] + [in_vmem] * 3,
        out_specs=in_vmem,
        out_shape=jax.ShapeDtypeStruct((tokens, columns), f32),
        compiler_params=limited,
        cost_estimate=pl.CostEstimate(
            flops=2 * tokens * ups.shape[0] * features,
            bytes_accessed=2 * (tokens + ups.shape[0]) * features,
            transcendentals=0,
        ),
        name="project_back",
    )(counts, by_hidden, cot, ups)


def gram_kernel(sections, *refs):
    around = refs[:sections]
    gram_ref, right_ref = refs[sections:]
    section_at = lax.axis_index("section")
    ranks = around[0].shape[0] // 2
    layers = []
    for layer in range(sections):
        distance = lax.rem(layer - section_at + sections, sections)
        chosen = around[0][...]
        for step in range(1, sections):
            chosen = jnp.where(distance == step, around[step][...], chosen)
        layers.append(chosen)
    lefts = [chosen[ranks:] for chosen in layers[:-1]]
    right = jnp.concatenate([chosen[:ranks] for chosen in layers[1:]] + lefts, axis=0)
    right_ref[...] = right
    gram_ref[...] = dot_last(jnp.concatenate(lefts, axis=0), right)


def gram(around):
    sections = len(around)
    ranks = around[0].shape[0] // 2
    columns = around[0].shape[1]
    before = (sections - 1) * ranks
    return pl.pallas_call(
        functools.partial(gram_kernel, sections),
        in_specs=[in_vmem] * sections,
        out_specs=[in_vmem] * 2,
        out_shape=[
            jax.ShapeDtypeStruct((before, 2 * before), f32),
            jax.ShapeDtypeStruct((2 * before, columns), bf16),
        ],
        compiler_params=limited,
        name="gram",
    )(*around)


def chain_kernel(sections, slots, features, per_micro, bounds, counts, *refs):
    projections, grams = refs[:sections], refs[sections:-3]
    sq_ref, factor_ref, mixed_ref = refs[-3:]
    layers = sections
    replica_at = lax.axis_index("replica")
    section_at = lax.axis_index("section")
    tokens = sq_ref.shape[0]
    table = grams[0][...]
    for other in grams[1:]:
        table = table + other[...]
    ranks = projections[0].shape[1] // (3 * slots)
    parts = [[jnp.zeros((tokens, ranks), f32)] * 3 for _ in range(layers)]
    for distance, source in enumerate(projections):
        section = lax.rem(section_at + distance, sections)
        first, after = bounds[replica_at, section], bounds[replica_at, section + 1]
        for slot in range(slots):
            for which in range(3):
                block = which * slots + slot
                piece = source[:, block * ranks : (block + 1) * ranks]
                for layer in range(layers):
                    here = (first + slot == layer) & (layer < after)
                    parts[layer][which] = jnp.where(here, piece, parts[layer][which])
    scale_d = 1.0 / math.sqrt(features)
    scale_r = 1.0 / math.sqrt(ranks)

    def part(layer, which):
        return parts[layer][which]

    def up_down(i, layer):
        return table[i * ranks : (i + 1) * ranks, (layer - 1) * ranks : layer * ranks]

    def up_up(i, j):
        at_column = (layers - 1 + j) * ranks
        return table[i * ranks : (i + 1) * ranks, at_column : at_column + ranks]

    def times(x, y):
        return jnp.dot(x, y, preferred_element_type=f32, precision=exact)

    square = sq_ref[:, 0:1]
    inverses, inners, actives, sigmoids = [], [], [], []
    on_up = [[part(l, 1) for l in range(layers - 1)]]
    for layer in range(layers):
        inverse = lax.rsqrt(jnp.maximum(square, 0.0) * (1.0 / features) + norm_eps)
        on_down = part(layer, 0)
        for i in range(layer):
            on_down = on_down + scale_r * times(actives[i], up_down(i, layer))
        inner = on_down * (inverse * scale_d)
        sigmoid = jax.nn.sigmoid(inner)
        active = (inner * sigmoid).astype(bf16).astype(f32)
        inverses.append(inverse)
        inners.append(inner)
        sigmoids.append(sigmoid)
        actives.append(active)
        if layer < layers - 1:
            now = on_up[-1]
            grown = [now[l] + scale_r * times(active, up_up(layer, l)) for l in range(layers - 1)]
            square = square + scale_r * row_sum(active * (now[layer] + grown[layer]))
            on_up.append(grown)
    scaled = [None] * layers
    kappas = [None] * layers
    for layer in reversed(range(layers)):
        incoming = part(layer, 2)
        for k in range(layer + 1, layers):
            incoming = incoming + scale_d * dot_last(scaled[k], up_down(layer, k), exact)
            incoming = incoming - kappas[k] * on_up[k][layer]
        sigmoid, inner = sigmoids[layer], inners[layer]
        slope = sigmoid * (1.0 + inner * (1.0 - sigmoid))
        error = incoming * scale_r * slope
        scaled[layer] = error * inverses[layer]
        kappas[layer] = (
            inverses[layer] * inverses[layer] * (row_sum(error * inner) * (1.0 / features))
        )

    def owned(values):
        chosen = values[0]
        for layer in range(1, layers):
            chosen = jnp.where(section_at == layer, values[layer], chosen)
        return chosen

    own_error = owned(scaled)
    own_active = owned(actives)
    counted = counted_rows(counts, tokens, per_micro)
    later = jnp.zeros_like(square)
    for k in range(1, layers):
        later = later + jnp.where(k > section_at, kappas[k], 0.0)
    on_hidden = jnp.concatenate([own_error * scale_d, -scale_r * later * own_active], axis=1)
    on_cot = jnp.concatenate(
        [jnp.zeros_like(own_active), jnp.where(counted, own_active * scale_r, 0.0)], axis=1
    )
    factor_ref[...] = jnp.concatenate([on_hidden.T, on_cot.T], axis=1).astype(bf16)
    both = scale_d * scale_r
    for k in range(1, layers):
        cut = slice((k - 1) * ranks, k * ranks)
        across = dot_first(own_active.astype(bf16), scaled[k].astype(bf16)) * both
        mixed_ref[:ranks, cut] = jnp.zeros_like(across)
        mixed_ref[ranks:, cut] = jnp.where(k > section_at, across, 0.0)
    for i in range(layers - 1):
        cut = slice((layers - 1 + i) * ranks, (layers + i) * ranks)
        after = jnp.zeros_like(square)
        for k in range(i + 1, layers):
            after = after + jnp.where(k > section_at, kappas[k], 0.0)
        across = dot_first(own_error.astype(bf16), actives[i].astype(bf16)) * both
        mixed_ref[:ranks, cut] = jnp.where(i < section_at, across, 0.0)
        across = dot_first(own_active.astype(bf16), (after * actives[i]).astype(bf16))
        mixed_ref[ranks:, cut] = across * (-scale_r * scale_r)


def chain(bounds, counts, projections, grams, square, slots, features, per_micro):
    sections = len(projections)
    tokens, wide = projections[0].shape
    ranks = wide // (3 * slots)
    inputs = [*projections, *grams, square]
    kernel = functools.partial(chain_kernel, sections, slots, features, per_micro)
    return pl.pallas_call(
        kernel,
        in_specs=[in_smem] * 2 + [in_vmem] * len(inputs),
        out_specs=[in_vmem] * 2,
        out_shape=[
            jax.ShapeDtypeStruct((2 * ranks, 2 * tokens), bf16),
            jax.ShapeDtypeStruct((2 * ranks, 2 * (sections - 1) * ranks), f32),
        ],
        compiler_params=limited,
        name="chain",
    )(bounds, counts, *inputs)


def gradient_kernel(first, lead, factor_ref, h_ref, g_ref, out_ref):
    _, _, ranks, columns = out_ref.shape
    tokens = h_ref.shape[0]
    replica_at = lax.axis_index("replica")
    tensor_at = lax.axis_index("tensor")
    tensors = lax.axis_size("tensor")
    down = factor_ref[:ranks, :tokens]
    up = factor_ref[ranks:]
    for middle in range(2):
        for high in range(2):
            for which, (far, low) in enumerate(((lead, middle), (middle, lead))):
                hop = low + 2 * high
                owner = (replica_at ^ (first + 2 * far)) * tensors + (tensor_at ^ hop)
                cut = pl.ds(pl.multiple_of(owner * columns, columns), columns)
                if which == 0:
                    block = jnp.dot(down, h_ref[:, cut], preferred_element_type=f32)
                else:
                    stacked = jnp.concatenate([h_ref[:, cut], g_ref[:, cut]], axis=0)
                    block = jnp.dot(up, stacked, preferred_element_type=f32)
                out_ref[which, 2 * middle + high] = block.astype(bf16)


def gradient(factors, hidden, cot, first, lead, columns):
    tokens, features = hidden.shape
    rows = factors.shape[0]
    return pl.pallas_call(
        functools.partial(gradient_kernel, first, lead),
        in_specs=[in_vmem] * 3,
        out_specs=in_vmem,
        out_shape=jax.ShapeDtypeStruct((2, 4, rows // 2, columns), bf16),
        compiler_params=limited,
        cost_estimate=pl.CostEstimate(
            flops=rows * tokens * features,
            bytes_accessed=(tokens + rows // 2) * features,
            transcendentals=0,
        ),
        name="gradient",
    )(factors, hidden, cot)


def update_kernel(kept, near, downs, ups, *refs):
    last, mixed_ref, other_ref, right_ref = refs[:4]
    state, outs, share_ref = refs[4:10], refs[10:16], refs[16]
    mixed = mixed_ref[...] + other_ref[...].astype(f32)
    right = right_ref[...].astype(f32)
    small = jnp.dot(mixed, right, preferred_element_type=f32, precision=exact)
    ranks = small.shape[0] // 2
    for which, steps in enumerate((downs, ups)):
        own = small[which * ranks : (which + 1) * ranks]
        for block in (kept[which, 0], near[which, 0], *(step[0] for step in steps), last[which]):
            own = own + block.astype(f32)
        master, moment, second = (state[2 * kind + which][0] for kind in range(3))
        moment = beta_one * moment + (1.0 - beta_one) * own
        second = beta_two * second + (1.0 - beta_two) * own * own
        master = master - learn_rate * (
            moment / first_fix / (jnp.sqrt(second / second_fix) + adam_eps) + decay_rate * master
        )
        share_ref[which] = master.astype(bf16)
        outs[which][0] = master
        outs[2 + which][0] = moment
        outs[4 + which][0] = second


def update(kept, near, downs, ups, last, mixed, other, right, state):
    _, ranks, columns = state[0].shape

    def kernel(kept, near, down_one, down_two, up_one, up_two, *refs):
        update_kernel(kept, near, (down_one, down_two), (up_one, up_two), *refs)

    return pl.pallas_call(
        kernel,
        in_specs=[in_vmem] * 16,
        out_specs=[in_vmem] * 7,
        out_shape=[jax.ShapeDtypeStruct(array.shape, f32) for array in state]
        + [jax.ShapeDtypeStruct((2, ranks, columns), bf16)],
        compiler_params=limited,
        name="update",
    )(kept, near, *downs, *ups, last, mixed, other, right, *state)


def place_kernel(layout, start, bounds, *refs):
    sources = refs[: len(layout)]
    outs = refs[-4:-2]
    zeros, sem = refs[-2:]
    slots, ranks, features = outs[0].shape
    columns = zeros.shape[1]
    tensors = lax.axis_size("tensor")
    first, after = held_layers(bounds)
    replica_at = lax.axis_index("replica")
    section_at = lax.axis_index("section")
    tensor_at = lax.axis_index("tensor")
    zeros[...] = jnp.zeros_like(zeros)

    def fill(slot, distance, go):
        for blocks, source in zip(layout, sources):
            for i, (window, which, order, hop) in enumerate(blocks):
                if window != distance:
                    continue
                owner = (replica_at ^ order) * tensors + (tensor_at ^ hop)
                cut = pl.ds(pl.multiple_of(owner * columns, columns), columns)
                go(pltpu.make_async_copy(source.at[i], outs[which].at[slot, :, cut], sem))

    def clear(slot, go):
        for out in outs:
            for block in range(features // columns):
                cut = pl.ds(block * columns, columns)
                go(pltpu.make_async_copy(zeros, out.at[slot, :, cut], sem))

    for act in (lambda copy: copy.start(), lambda copy: copy.wait()):
        for slot in range(slots):
            layer = first + slot
            present = layer < after
            for distance in range(2):

                @pl.when(present & (layer - section_at == distance))
                def _():
                    fill(slot, distance, act)

            if start:

                @pl.when(jnp.logical_not(present))
                def _():
                    clear(slot, act)


def place(bounds, pieces, before, slots, ranks, features):
    layout = [blocks for blocks, _ in pieces]
    arrays = [array for _, array in pieces]
    columns = arrays[0].shape[-1]
    return pl.pallas_call(
        functools.partial(place_kernel, layout, not before),
        in_specs=[in_smem] + [in_vmem] * len(arrays) + [in_hbm] * len(before),
        out_specs=[in_hbm] * 2,
        out_shape=[jax.ShapeDtypeStruct((slots, ranks, features), bf16)] * 2,
        scratch_shapes=[pltpu.VMEM((ranks, columns), bf16), pltpu.SemaphoreType.DMA],
        input_output_aliases={1 + len(arrays) + i: i for i in range(len(before))},
        compiler_params=limited,
        cost_estimate=pl.CostEstimate(
            flops=0,
            bytes_accessed=4 * sum(array.size for array in arrays),
            transcendentals=0,
        ),
        name="place",
    )(bounds, *arrays, *before)


def swapped(block, axis, distance):
    route = [(i, i ^ distance) for i in range(lax.axis_size(axis))]
    return lax.ppermute(block, axis, route)


def swaps(block, axis):
    return [swapped(block, axis, k) for k in range(1, lax.axis_size(axis))]


def from_next(block, distance=1):
    size = lax.axis_size("section")
    route = [((i + distance) % size, i) for i in range(size)]
    return lax.ppermute(block, "section", route)


def following_layer(block):
    size = lax.axis_size("section")
    return lax.ppermute(block, "section", [(i + 1, i) for i in range(size - 1)])


def summed(*blocks):
    total = blocks[0].astype(f32)
    for block in blocks[1:]:
        total = total + block.astype(f32)
    return total.astype(bf16)


def reduced(factors, hidden, cot, columns, mixed):
    def halves(lead):
        sent = gradient(factors, hidden, cot, 1, lead, columns)
        return swapped(sent, "replica", 1), gradient(factors, hidden, cot, 0, lead, columns)

    def part(which, cut, *steps):
        return summed(kept[which, cut], near[which, cut], *steps)

    def added(axis, distance):
        return mixed + swapped(mixed.astype(bf16), axis, distance).astype(f32)

    near, kept = halves(1)
    whole, low = slice(0, 4), slice(2, 4)
    down_one = swapped(part(0, whole), "replica", 2)
    up_one = swapped(part(1, whole), "tensor", 1)
    near, kept = halves(0)
    mixed = added("replica", 1)
    mixed = added("tensor", 1)
    down_one, up_one, mixed = lax.optimization_barrier((down_one, up_one, mixed))
    down_two = swapped(part(0, low, down_one[2:]), "tensor", 1)
    up_two = swapped(part(1, low, up_one[2:]), "replica", 2)
    last = jnp.stack([part(0, 1, down_one[1], down_two[1]), part(1, 1, up_one[1], up_two[1])])
    last = swapped(last, "tensor", 2)
    mixed = added("tensor", 2)
    other = swapped(mixed.astype(bf16), "replica", 2)
    return (kept, near, (down_one, down_two), (up_one, up_two), last, mixed, other)


def crossed(piece, axis, distance):
    blocks, array = piece
    blocks = [
        (window, which, order ^ distance, hop)
        if axis == "replica"
        else (window, which, order, hop ^ distance)
        for window, which, order, hop in blocks
    ]
    return blocks, swapped(array, axis, distance)


def fetched(piece):
    blocks, array = piece
    return [(1, *block[1:]) for block in blocks], following_layer(array)


def picked(piece, at):
    return piece[0][at : at + 1], piece[1][at : at + 1]


def joined(*pieces):
    blocks = [block for piece in pieces for block in piece[0]]
    return blocks, jnp.concatenate([array for _, array in pieces])


def spread(share, bounds, slots, features):
    ranks = share.shape[1]
    own = ([(0, 0, 0, 0), (0, 1, 0, 0)], share)
    one = crossed(own, "tensor", 2)
    next_own = fetched(own)
    downs = joined(picked(own, 0), picked(one, 0))
    ups = joined(picked(own, 1), picked(one, 1))
    down_two = crossed(downs, "tensor", 1)
    up_two = crossed(ups, "replica", 2)
    next_one = fetched(one)
    two = joined(down_two, up_two)
    down_three = crossed(joined(downs, down_two), "replica", 2)
    up_three = crossed(joined(ups, up_two), "tensor", 1)
    next_two = fetched(two)
    next_end = fetched(joined(picked(down_three, 3), picked(up_three, 3)))
    _, _, next_array = lax.optimization_barrier((down_three[1], up_three[1], next_two[1]))
    next_two = (next_two[0], next_array)
    down_end = joined(picked(next_own, 0), picked(next_one, 0), picked(next_two, 0))
    up_end = joined(picked(next_own, 1), picked(next_one, 1), picked(next_two, 2))
    end = joined(crossed(down_end, "replica", 2), crossed(up_end, "tensor", 1), next_end)
    near = joined(own, one, two)
    far = joined(down_three, up_three)
    next_near = joined(next_own, next_one, next_two)
    near_core, far_core, next_core, end_core = (
        crossed(piece, "replica", 1) for piece in (near, far, next_near, end)
    )
    placed = place(
        bounds, [near, near_core, far, far_core, next_near, next_core], [], slots, ranks, features
    )
    placed = place(bounds, [end, end_core], placed, slots, ranks, features)
    return placed


def on_device(
    inputs,
    cotangent,
    micro_counts,
    bounds,
    holder_down,
    holder_up,
    master_down,
    master_up,
    moment_down,
    moment_up,
    second_down,
    second_up,
):
    sections = lax.axis_size("section")
    replicas = lax.axis_size("replica")
    tensors = lax.axis_size("tensor")
    assert replicas == 4 and tensors == 4
    _, micros, per_micro, features = inputs.shape
    slots = holder_down.shape[2]
    hidden = inputs.reshape(micros * per_micro, features)
    cot = cotangent.reshape(micros * per_micro, features)

    owned = jnp.concatenate([master_down[0], master_up[0]], axis=0).astype(bf16)
    around = [from_next(owned, d) for d in range(1, sections)]
    by_hidden, square, hidden, ups = project(hidden, holder_down[0, 0], holder_up[0, 0])
    around, by_hidden = lax.optimization_barrier((around, by_hidden))
    table, right = gram([owned, *around])
    table, ups = lax.optimization_barrier((table, ups))
    projected = project_back(micro_counts, by_hidden, cot, ups, per_micro)
    table = table + sum(swaps(table, "replica"))
    projections = [projected] + [from_next(projected, d) for d in range(1, sections)]
    table = table + swapped(table, "tensor", 1)
    tables = [table, swapped(table, "tensor", 2)]
    factors, mixed = chain(
        bounds, micro_counts, projections, tables, square, slots, features, per_micro
    )

    parts = reduced(factors, hidden, cot, master_down.shape[2], mixed)
    state = [master_down, master_up, moment_down, moment_up, second_down, second_up]
    updated = update(*parts, right, state)
    placed = spread(updated[6], bounds, slots, features)
    return (placed[0][None, None], placed[1][None, None], *updated[:6])


def solution(mesh):
    held = P("replica", "section", None, None, None)
    owned = P("section", None, ("replica", "tensor"))
    tokens = P("replica", None, "tensor", None)
    return jax.shard_map(
        on_device,
        mesh=mesh,
        in_specs=(tokens, tokens, P(), P(), held, held) + (owned,) * 6,
        out_specs=(held, held) + (owned,) * 6,
        check_vma=False,
    )
```

```python
import functools
import math

import jax
import jax.numpy as jnp
from jax import lax
from jax.experimental import pallas as pl
from jax.experimental.pallas import tpu as pltpu
from jax.sharding import PartitionSpec as P

norm_eps = 1e-06
learn_rate = 0.01
beta_one = 0.9
beta_two = 0.95
decay_rate = 0.1
adam_eps = 1e-08
first_fix = 0.9999734386011124
second_fix = 0.9940794707796659

f32 = jnp.float32
bf16 = jnp.bfloat16
exact = lax.Precision.HIGHEST
in_vmem = pl.BlockSpec(memory_space=pltpu.VMEM)
in_hbm = pl.BlockSpec(memory_space=pltpu.HBM)
limited = pltpu.CompilerParams(vmem_limit_bytes=16 * 1024 * 1024)


def entry(ref, row, column):
    values = ref[...].astype(f32)
    rows = lax.broadcasted_iota(jnp.int32, values.shape, 0)
    columns = lax.broadcasted_iota(jnp.int32, values.shape, 1)
    return jnp.sum(jnp.where((rows == row) & (columns == column), values, 0.0)).astype(jnp.int32)


def counted_rows(counts, tokens, per_micro):
    rows = lax.broadcasted_iota(jnp.int32, (tokens, 1), 0)
    return rows < entry(counts, 0, lax.axis_index("replica")) * per_micro


def dot_last(x, y, precision=None):
    return lax.dot_general(
        x, y, (((1,), (1,)), ((), ())), preferred_element_type=f32, precision=precision
    )


def dot_first(x, y, precision=None):
    return lax.dot_general(
        x, y, (((0,), (0,)), ((), ())), preferred_element_type=f32, precision=precision
    )


def row_sum(x):
    return jnp.sum(x, axis=-1, keepdims=True)


def project_kernel(steps, h_in, down_in, up_in, *refs):
    out_ref, sq_ref, h_ref, up_ref, down_ref, sems = refs
    slots, ranks, features = down_in.shape
    tokens = h_ref.shape[0]
    width = features // steps
    copies = []
    for step in range(steps):
        cut = pl.ds(step * width, width)
        moves = [(h_in.at[:, cut], h_ref.at[:, cut])]
        for slot in range(slots):
            rows = pl.ds(slot * ranks, ranks)
            moves.append((down_in.at[slot, :, cut], down_ref.at[rows, cut]))
            moves.append((up_in.at[slot, :, cut], up_ref.at[rows, cut]))
        copies.append(
            [
                pltpu.make_async_copy(source, target, sems.at[step, i])
                for i, (source, target) in enumerate(moves)
            ]
        )
        for copy in copies[-1]:
            copy.start()
    ph = jnp.zeros((tokens, 2 * slots * ranks), f32)
    square = jnp.zeros((tokens, 128), f32)
    for step in range(steps):
        for copy in copies[step]:
            copy.wait()
        cut = pl.ds(step * width, width)
        h = h_ref[:, cut]
        ph = ph + dot_last(h, jnp.concatenate([down_ref[:, cut], up_ref[:, cut]], axis=0))
        wide = h.astype(f32)
        wide = wide * wide
        for lane in range(0, width, 128):
            square = square + wide[:, lane : lane + 128]
    sq_ref[...] = jnp.broadcast_to(row_sum(square), square.shape)
    out_ref[...] = ph


def project(hidden, downs, ups):
    tokens, features = hidden.shape
    slots, ranks, _ = downs.shape
    steps = 8
    sources = [pltpu.with_memory_space_constraint(x, pltpu.HBM) for x in (hidden, downs, ups)]
    return pl.pallas_call(
        functools.partial(project_kernel, steps),
        in_specs=[in_hbm] * 3,
        out_specs=[in_vmem] * 4,
        out_shape=[
            jax.ShapeDtypeStruct((tokens, 2 * slots * ranks), f32),
            jax.ShapeDtypeStruct((tokens, 128), f32),
            jax.ShapeDtypeStruct((tokens, features), bf16),
            jax.ShapeDtypeStruct((slots * ranks, features), bf16),
        ],
        scratch_shapes=[
            pltpu.VMEM((slots * ranks, features), bf16),
            pltpu.SemaphoreType.DMA((steps, 1 + 2 * slots)),
        ],
        compiler_params=limited,
        cost_estimate=pl.CostEstimate(
            flops=4 * tokens * slots * ranks * features,
            bytes_accessed=2 * (tokens + 2 * slots * ranks) * features,
            transcendentals=0,
        ),
        name="project",
    )(*sources)


def project_back_kernel(per_micro, counts, by_hidden, g_ref, up_ref, out_ref):
    pg = dot_last(g_ref[...], up_ref[...])
    pg = jnp.where(counted_rows(counts, pg.shape[0], per_micro), pg, 0.0)
    ahead = by_hidden.shape[1]
    out_ref[:, :ahead] = by_hidden[...]
    out_ref[:, ahead:] = pg


def project_back(counts, by_hidden, cot, ups, per_micro):
    tokens, features = cot.shape
    columns = by_hidden.shape[1] + ups.shape[0]
    return pl.pallas_call(
        functools.partial(project_back_kernel, per_micro),
        in_specs=[in_vmem] * 4,
        out_specs=in_vmem,
        out_shape=jax.ShapeDtypeStruct((tokens, columns), f32),
        compiler_params=limited,
        cost_estimate=pl.CostEstimate(
            flops=2 * tokens * ups.shape[0] * features,
            bytes_accessed=2 * (tokens + ups.shape[0]) * features,
            transcendentals=0,
        ),
        name="project_back",
    )(counts, by_hidden, cot, ups)


def gram_kernel(sections, *refs):
    around = refs[:sections]
    gram_ref, right_ref = refs[sections:]
    section_at = lax.axis_index("section")
    ranks = around[0].shape[0] // 2
    layers = []
    for layer in range(sections):
        distance = lax.rem(layer - section_at + sections, sections)
        chosen = around[0][...]
        for step in range(1, sections):
            chosen = jnp.where(distance == step, around[step][...], chosen)
        layers.append(chosen)
    lefts = [chosen[ranks:] for chosen in layers[:-1]]
    right = jnp.concatenate([chosen[:ranks] for chosen in layers[1:]] + lefts, axis=0)
    right_ref[...] = right
    gram_ref[...] = dot_last(jnp.concatenate(lefts, axis=0), right)


def gram(around):
    sections = len(around)
    ranks = around[0].shape[0] // 2
    columns = around[0].shape[1]
    before = (sections - 1) * ranks
    return pl.pallas_call(
        functools.partial(gram_kernel, sections),
        in_specs=[in_vmem] * sections,
        out_specs=[in_vmem] * 2,
        out_shape=[
            jax.ShapeDtypeStruct((before, 2 * before), f32),
            jax.ShapeDtypeStruct((2 * before, columns), bf16),
        ],
        compiler_params=limited,
        name="gram",
    )(*around)


def chain_kernel(sections, slots, features, per_micro, bounds, counts, *refs):
    projections, grams = refs[:sections], refs[sections:-3]
    sq_ref, factor_ref, mixed_ref = refs[-3:]
    layers = sections
    replica_at = lax.axis_index("replica")
    section_at = lax.axis_index("section")
    tokens = sq_ref.shape[0]
    table = grams[0][...]
    for other in grams[1:]:
        table = table + other[...]
    ranks = projections[0].shape[1] // (3 * slots)
    parts = [[jnp.zeros((tokens, ranks), f32)] * 3 for _ in range(layers)]
    for distance, source in enumerate(projections):
        section = lax.rem(section_at + distance, sections)
        first = entry(bounds, replica_at, section)
        after = entry(bounds, replica_at, section + 1)
        for slot in range(slots):
            for which in range(3):
                block = which * slots + slot
                piece = source[:, block * ranks : (block + 1) * ranks]
                for layer in range(layers):
                    here = (first + slot == layer) & (layer < after)
                    parts[layer][which] = jnp.where(here, piece, parts[layer][which])
    scale_d = 1.0 / math.sqrt(features)
    scale_r = 1.0 / math.sqrt(ranks)

    def part(layer, which):
        return parts[layer][which]

    def up_down(i, layer):
        return table[i * ranks : (i + 1) * ranks, (layer - 1) * ranks : layer * ranks]

    def up_up(i, j):
        at_column = (layers - 1 + j) * ranks
        return table[i * ranks : (i + 1) * ranks, at_column : at_column + ranks]

    def times(x, y):
        return jnp.dot(x, y, preferred_element_type=f32, precision=exact)

    square = sq_ref[:, 0:1]
    inverses, inners, actives, sigmoids = [], [], [], []
    on_up = [[part(l, 1) for l in range(layers - 1)]]
    for layer in range(layers):
        inverse = lax.rsqrt(jnp.maximum(square, 0.0) * (1.0 / features) + norm_eps)
        on_down = part(layer, 0)
        for i in range(layer):
            on_down = on_down + scale_r * times(actives[i], up_down(i, layer))
        inner = on_down * (inverse * scale_d)
        sigmoid = jax.nn.sigmoid(inner)
        active = (inner * sigmoid).astype(bf16).astype(f32)
        inverses.append(inverse)
        inners.append(inner)
        sigmoids.append(sigmoid)
        actives.append(active)
        if layer < layers - 1:
            now = on_up[-1]
            grown = [now[l] + scale_r * times(active, up_up(layer, l)) for l in range(layers - 1)]
            square = square + scale_r * row_sum(active * (now[layer] + grown[layer]))
            on_up.append(grown)
    scaled = [None] * layers
    kappas = [None] * layers
    for layer in reversed(range(layers)):
        incoming = part(layer, 2)
        for k in range(layer + 1, layers):
            incoming = incoming + scale_d * dot_last(scaled[k], up_down(layer, k), exact)
            incoming = incoming - kappas[k] * on_up[k][layer]
        sigmoid, inner = sigmoids[layer], inners[layer]
        slope = sigmoid * (1.0 + inner * (1.0 - sigmoid))
        error = incoming * scale_r * slope
        scaled[layer] = error * inverses[layer]
        kappas[layer] = (
            inverses[layer] * inverses[layer] * (row_sum(error * inner) * (1.0 / features))
        )

    def owned(values):
        chosen = values[0]
        for layer in range(1, layers):
            chosen = jnp.where(section_at == layer, values[layer], chosen)
        return chosen

    own_error = owned(scaled)
    own_active = owned(actives)
    counted = counted_rows(counts, tokens, per_micro)
    later = jnp.zeros_like(square)
    for k in range(1, layers):
        later = later + jnp.where(k > section_at, kappas[k], 0.0)
    on_hidden = jnp.concatenate([own_error * scale_d, -scale_r * later * own_active], axis=1)
    on_cot = jnp.concatenate(
        [jnp.zeros_like(own_active), jnp.where(counted, own_active * scale_r, 0.0)], axis=1
    )
    factor_ref[...] = jnp.concatenate([on_hidden.T, on_cot.T], axis=1).astype(bf16)
    both = scale_d * scale_r
    for k in range(1, layers):
        cut = slice((k - 1) * ranks, k * ranks)
        across = dot_first(own_active.astype(bf16), scaled[k].astype(bf16)) * both
        mixed_ref[:ranks, cut] = jnp.zeros_like(across)
        mixed_ref[ranks:, cut] = jnp.where(k > section_at, across, 0.0)
    for i in range(layers - 1):
        cut = slice((layers - 1 + i) * ranks, (layers + i) * ranks)
        after = jnp.zeros_like(square)
        for k in range(i + 1, layers):
            after = after + jnp.where(k > section_at, kappas[k], 0.0)
        across = dot_first(own_error.astype(bf16), actives[i].astype(bf16)) * both
        mixed_ref[:ranks, cut] = jnp.where(i < section_at, across, 0.0)
        across = dot_first(own_active.astype(bf16), (after * actives[i]).astype(bf16))
        mixed_ref[ranks:, cut] = across * (-scale_r * scale_r)


def chain(bounds, counts, projections, grams, square, slots, features, per_micro):
    sections = len(projections)
    tokens, wide = projections[0].shape
    ranks = wide // (3 * slots)
    inputs = [*projections, *grams, square]
    kernel = functools.partial(chain_kernel, sections, slots, features, per_micro)
    return pl.pallas_call(
        kernel,
        in_specs=[in_vmem] * (2 + len(inputs)),
        out_specs=[in_vmem] * 2,
        out_shape=[
            jax.ShapeDtypeStruct((2 * ranks, 2 * tokens), bf16),
            jax.ShapeDtypeStruct((2 * ranks, 2 * (sections - 1) * ranks), f32),
        ],
        compiler_params=limited,
        name="chain",
    )(bounds, counts, *inputs)


def gradient_kernel(first, lead, factor_ref, h_ref, g_ref, out_ref):
    _, _, ranks, columns = out_ref.shape
    tokens = h_ref.shape[0]
    replica_at = lax.axis_index("replica")
    tensor_at = lax.axis_index("tensor")
    tensors = lax.axis_size("tensor")
    down = factor_ref[:ranks, :tokens]
    up = factor_ref[ranks:]
    for middle in range(2):
        for high in range(2):
            for which, (far, low) in enumerate(((lead, middle), (middle, lead))):
                hop = low + 2 * high
                owner = (replica_at ^ (first + 2 * far)) * tensors + (tensor_at ^ hop)
                cut = pl.ds(pl.multiple_of(owner * columns, columns), columns)
                if which == 0:
                    block = jnp.dot(down, h_ref[:, cut], preferred_element_type=f32)
                else:
                    stacked = jnp.concatenate([h_ref[:, cut], g_ref[:, cut]], axis=0)
                    block = jnp.dot(up, stacked, preferred_element_type=f32)
                out_ref[which, 2 * middle + high] = block.astype(bf16)


def gradient(factors, hidden, cot, first, lead, columns):
    tokens, features = hidden.shape
    rows = factors.shape[0]
    return pl.pallas_call(
        functools.partial(gradient_kernel, first, lead),
        in_specs=[in_vmem] * 3,
        out_specs=in_vmem,
        out_shape=jax.ShapeDtypeStruct((2, 4, rows // 2, columns), bf16),
        compiler_params=limited,
        cost_estimate=pl.CostEstimate(
            flops=rows * tokens * features,
            bytes_accessed=(tokens + rows // 2) * features,
            transcendentals=0,
        ),
        name="gradient",
    )(factors, hidden, cot)


def update_kernel(which, kept, near, one, two, last, mixed_ref, other_ref, right_ref, *refs):
    master_ref, moment_ref, second_ref, new_master, new_moment, new_second, share_ref = refs
    ranks = last.shape[0]
    rows = slice(which * ranks, (which + 1) * ranks)
    mixed = mixed_ref[rows] + other_ref[rows].astype(f32)
    right = right_ref[...].astype(f32)
    own = jnp.dot(mixed, right, preferred_element_type=f32, precision=exact)
    for block in (kept[which, 0], near[which, 0], one[0], two[0], last[...]):
        own = own + block.astype(f32)
    moment = beta_one * moment_ref[0] + (1.0 - beta_one) * own
    second = beta_two * second_ref[0] + (1.0 - beta_two) * own * own
    master = master_ref[0]
    master = master - learn_rate * (
        moment / first_fix / (jnp.sqrt(second / second_fix) + adam_eps) + decay_rate * master
    )
    share_ref[0] = master.astype(bf16)
    new_master[0] = master
    new_moment[0] = moment
    new_second[0] = second


def update(which, parts, right, state):
    inputs = [*parts, right, *state]
    return pl.pallas_call(
        functools.partial(update_kernel, which),
        in_specs=[in_vmem] * len(inputs),
        out_specs=[in_vmem] * 4,
        out_shape=[jax.ShapeDtypeStruct(array.shape, f32) for array in state]
        + [jax.ShapeDtypeStruct(state[0].shape, bf16)],
        compiler_params=limited,
        name="update",
    )(*inputs)


def place_kernel(layout, start, bounds, *refs):
    sources = refs[: len(layout)]
    outs = refs[-4:-2]
    zeros, sem = refs[-2:]
    slots, ranks, features = outs[0].shape
    columns = zeros.shape[1]
    tensors = lax.axis_size("tensor")
    replica_at = lax.axis_index("replica")
    section_at = lax.axis_index("section")
    tensor_at = lax.axis_index("tensor")
    first = entry(bounds, replica_at, section_at)
    after = entry(bounds, replica_at, section_at + 1)
    zeros[...] = jnp.zeros_like(zeros)

    def fill(slot, distance, go):
        for blocks, source in zip(layout, sources):
            for i, (window, which, order, hop) in enumerate(blocks):
                if window != distance:
                    continue
                owner = (replica_at ^ order) * tensors + (tensor_at ^ hop)
                cut = pl.ds(pl.multiple_of(owner * columns, columns), columns)
                go(pltpu.make_async_copy(source.at[i], outs[which].at[slot, :, cut], sem))

    def clear(slot, go):
        for out in outs:
            for block in range(features // columns):
                cut = pl.ds(block * columns, columns)
                go(pltpu.make_async_copy(zeros, out.at[slot, :, cut], sem))

    for act in (lambda copy: copy.start(), lambda copy: copy.wait()):
        for slot in range(slots):
            layer = first + slot
            present = layer < after
            for distance in range(2):

                @pl.when(present & (layer - section_at == distance))
                def _():
                    fill(slot, distance, act)

            if start:

                @pl.when(jnp.logical_not(present))
                def _():
                    clear(slot, act)


def place(bounds, pieces, before, slots, ranks, features):
    layout = [blocks for blocks, _ in pieces]
    arrays = [array for _, array in pieces]
    columns = arrays[0].shape[-1]
    return pl.pallas_call(
        functools.partial(place_kernel, layout, not before),
        in_specs=[in_vmem] * (1 + len(arrays)) + [in_hbm] * len(before),
        out_specs=[in_hbm] * 2,
        out_shape=[jax.ShapeDtypeStruct((slots, ranks, features), bf16)] * 2,
        scratch_shapes=[pltpu.VMEM((ranks, columns), bf16), pltpu.SemaphoreType.DMA],
        input_output_aliases={1 + len(arrays) + i: i for i in range(len(before))},
        compiler_params=limited,
        cost_estimate=pl.CostEstimate(
            flops=0,
            bytes_accessed=4 * sum(array.size for array in arrays),
            transcendentals=0,
        ),
        name="place",
    )(bounds, *arrays, *before)


def swapped(block, axis, distance):
    route = [(i, i ^ distance) for i in range(lax.axis_size(axis))]
    return lax.ppermute(block, axis, route)


def swaps(block, axis):
    return [swapped(block, axis, k) for k in range(1, lax.axis_size(axis))]


def from_next(block, distance=1):
    size = lax.axis_size("section")
    route = [((i + distance) % size, i) for i in range(size)]
    return lax.ppermute(block, "section", route)


def following_layer(block):
    size = lax.axis_size("section")
    return lax.ppermute(block, "section", [(i + 1, i) for i in range(size - 1)])


def summed(*blocks):
    total = blocks[0].astype(f32)
    for block in blocks[1:]:
        total = total + block.astype(f32)
    return total.astype(bf16)


def reduced(factors, hidden, cot, columns, mixed):
    def halves(lead):
        sent = gradient(factors, hidden, cot, 1, lead, columns)
        return swapped(sent, "replica", 1), gradient(factors, hidden, cot, 0, lead, columns)

    def part(which, cut, *steps):
        return summed(kept[which, cut], near[which, cut], *steps)

    def added(axis, distance):
        return mixed + swapped(mixed.astype(bf16), axis, distance).astype(f32)

    near, kept = halves(1)
    whole, low = slice(0, 4), slice(2, 4)
    down_one = swapped(part(0, whole), "replica", 2)
    up_one = swapped(part(1, whole), "tensor", 1)
    near, kept = halves(0)
    mixed = added("replica", 1)
    mixed = added("tensor", 1)
    down_one, up_one, mixed = lax.optimization_barrier((down_one, up_one, mixed))
    down_two = swapped(part(0, low, down_one[2:]), "tensor", 1)
    up_two = swapped(part(1, low, up_one[2:]), "replica", 2)
    down_last = swapped(part(0, 1, down_one[1], down_two[1]), "tensor", 2)
    kept, near = lax.optimization_barrier((kept, near))
    up_last = swapped(part(1, 1, up_one[1], up_two[1]), "tensor", 2)
    mixed = added("tensor", 2)
    other = swapped(mixed.astype(bf16), "replica", 2)
    down = (kept, near, down_one, down_two, down_last, mixed, other)
    return down, (kept, near, up_one, up_two, up_last, mixed, other)


def crossed(piece, axis, distance):
    blocks, array = piece
    blocks = [
        (window, which, order ^ distance, hop)
        if axis == "replica"
        else (window, which, order, hop ^ distance)
        for window, which, order, hop in blocks
    ]
    return blocks, swapped(array, axis, distance)


def fetched(piece):
    blocks, array = piece
    return [(1, *block[1:]) for block in blocks], following_layer(array)


def picked(piece, at):
    return piece[0][at : at + 1], piece[1][at : at + 1]


def joined(*pieces):
    blocks = [block for piece in pieces for block in piece[0]]
    return blocks, jnp.concatenate([array for _, array in pieces])


def spread(down, up, bounds, slots, features):
    ranks = down.shape[1]
    down_own, up_own = ([(0, 0, 0, 0)], down), ([(0, 1, 0, 0)], up)
    down_one = crossed(down_own, "tensor", 2)
    up_one = crossed(up_own, "tensor", 2)
    downs, ups = joined(down_own, down_one), joined(up_own, up_one)
    owns = lax.optimization_barrier((down, up))
    own = joined((down_own[0], owns[0]), (up_own[0], owns[1]))
    next_own = fetched(own)
    *ones, next_array = lax.optimization_barrier((down_one[1], up_one[1], next_own[1]))
    one = joined((down_one[0], ones[0]), (up_one[0], ones[1]))
    next_own = (next_own[0], next_array)
    down_two = crossed(downs, "tensor", 1)
    up_two = crossed(ups, "replica", 2)
    next_one = fetched(one)
    twos = lax.optimization_barrier((down_two[1], up_two[1]))
    two = joined((down_two[0], twos[0]), (up_two[0], twos[1]))
    down_three = crossed(joined(downs, down_two), "replica", 2)
    up_three = crossed(joined(ups, up_two), "tensor", 1)
    next_two = fetched(two)
    next_end = fetched(joined(picked(down_three, 3), picked(up_three, 3)))
    _, _, next_array = lax.optimization_barrier((down_three[1], up_three[1], next_two[1]))
    next_two = (next_two[0], next_array)
    down_end = joined(picked(next_own, 0), picked(next_one, 0), picked(next_two, 0))
    up_end = joined(picked(next_own, 1), picked(next_one, 1), picked(next_two, 2))
    end = joined(crossed(down_end, "replica", 2), crossed(up_end, "tensor", 1), next_end)
    near = joined(own, one, two)
    far = joined(down_three, up_three)
    next_near = joined(next_own, next_one, next_two)
    near_core, far_core, next_core, end_core = (
        crossed(piece, "replica", 1) for piece in (near, far, next_near, end)
    )
    placed = place(
        bounds, [near, near_core, far, far_core, next_near, next_core], [], slots, ranks, features
    )
    placed = place(bounds, [end, end_core], placed, slots, ranks, features)
    return placed


def on_device(
    inputs,
    cotangent,
    micro_counts,
    bounds,
    holder_down,
    holder_up,
    master_down,
    master_up,
    moment_down,
    moment_up,
    second_down,
    second_up,
):
    sections = lax.axis_size("section")
    replicas = lax.axis_size("replica")
    tensors = lax.axis_size("tensor")
    assert replicas == 4 and tensors == 4
    _, micros, per_micro, features = inputs.shape
    micro_counts = micro_counts[None]
    slots = holder_down.shape[2]
    hidden = inputs.reshape(micros * per_micro, features)
    cot = cotangent.reshape(micros * per_micro, features)

    owned = jnp.concatenate([master_down[0], master_up[0]], axis=0).astype(bf16)
    around = [from_next(owned, d) for d in range(1, sections)]
    by_hidden, square, hidden, ups = project(hidden, holder_down[0, 0], holder_up[0, 0])
    around, by_hidden = lax.optimization_barrier((around, by_hidden))
    table, right = gram([owned, *around])
    table, ups = lax.optimization_barrier((table, ups))
    projected = project_back(micro_counts, by_hidden, cot, ups, per_micro)
    table = table + sum(swaps(table, "replica"))
    projections = [projected] + [from_next(projected, d) for d in range(1, sections)]
    table = table + swapped(table, "tensor", 1)
    tables = [table, swapped(table, "tensor", 2)]
    factors, mixed = chain(
        bounds, micro_counts, projections, tables, square, slots, features, per_micro
    )

    down_parts, up_parts = reduced(factors, hidden, cot, master_down.shape[2], mixed)
    down = update(0, down_parts, right, [master_down, moment_down, second_down])
    up = update(1, up_parts, right, [master_up, moment_up, second_up])
    placed = spread(down[3], up[3], bounds, slots, features)
    return (
        placed[0][None, None],
        placed[1][None, None],
        down[0],
        up[0],
        down[1],
        up[1],
        down[2],
        up[2],
    )


def solution(mesh):
    held = P("replica", "section", None, None, None)
    owned = P("section", None, ("replica", "tensor"))
    tokens = P("replica", None, "tensor", None)
    return jax.shard_map(
        on_device,
        mesh=mesh,
        in_specs=(tokens, tokens, P(), P(), held, held) + (owned,) * 6,
        out_specs=(held, held) + (owned,) * 6,
        check_vma=False,
    )
```

```python
import functools
import math

import jax
import jax.numpy as jnp
from jax import lax
from jax.experimental import pallas as pl
from jax.experimental.pallas import tpu as pltpu
from jax.sharding import PartitionSpec as P

norm_eps = 1e-06
learn_rate = 0.01
beta_one = 0.9
beta_two = 0.95
decay_rate = 0.1
adam_eps = 1e-08
first_fix = 0.9999734386011124
second_fix = 0.9940794707796659

f32 = jnp.float32
bf16 = jnp.bfloat16
exact = lax.Precision.HIGHEST
in_vmem = pl.BlockSpec(memory_space=pltpu.VMEM)
in_hbm = pl.BlockSpec(memory_space=pltpu.HBM)
limited = pltpu.CompilerParams(vmem_limit_bytes=16 * 1024 * 1024)


def entry(ref, row, column):
    values = ref[...].astype(f32)
    rows = lax.broadcasted_iota(jnp.int32, values.shape, 0)
    columns = lax.broadcasted_iota(jnp.int32, values.shape, 1)
    return jnp.sum(jnp.where((rows == row) & (columns == column), values, 0.0)).astype(jnp.int32)


def counted_rows(counts, tokens, per_micro):
    rows = lax.broadcasted_iota(jnp.int32, (tokens, 1), 0)
    return rows < entry(counts, 0, lax.axis_index("replica")) * per_micro


def dot_last(x, y, precision=None):
    return lax.dot_general(
        x, y, (((1,), (1,)), ((), ())), preferred_element_type=f32, precision=precision
    )


def dot_first(x, y, precision=None):
    return lax.dot_general(
        x, y, (((0,), (0,)), ((), ())), preferred_element_type=f32, precision=precision
    )


def row_sum(x):
    return jnp.sum(x, axis=-1, keepdims=True)


def project_kernel(steps, h_in, down_in, up_in, *refs):
    out_ref, sq_ref, h_ref, up_ref, down_ref, sems = refs
    slots, ranks, features = down_in.shape
    tokens = h_ref.shape[0]
    width = features // steps
    copies = []
    for step in range(steps):
        cut = pl.ds(step * width, width)
        moves = [(h_in.at[:, cut], h_ref.at[:, cut])]
        for slot in range(slots):
            rows = pl.ds(slot * ranks, ranks)
            moves.append((down_in.at[slot, :, cut], down_ref.at[rows, cut]))
            moves.append((up_in.at[slot, :, cut], up_ref.at[rows, cut]))
        copies.append(
            [
                pltpu.make_async_copy(source, target, sems.at[step, i])
                for i, (source, target) in enumerate(moves)
            ]
        )
        for copy in copies[-1]:
            copy.start()
    ph = jnp.zeros((tokens, 2 * slots * ranks), f32)
    square = jnp.zeros((tokens, 128), f32)
    for step in range(steps):
        for copy in copies[step]:
            copy.wait()
        cut = pl.ds(step * width, width)
        h = h_ref[:, cut]
        ph = ph + dot_last(h, jnp.concatenate([down_ref[:, cut], up_ref[:, cut]], axis=0))
        wide = h.astype(f32)
        wide = wide * wide
        for lane in range(0, width, 128):
            square = square + wide[:, lane : lane + 128]
    sq_ref[...] = jnp.broadcast_to(row_sum(square), square.shape)
    out_ref[...] = ph


def project(hidden, downs, ups):
    tokens, features = hidden.shape
    slots, ranks, _ = downs.shape
    steps = 8
    sources = [pltpu.with_memory_space_constraint(x, pltpu.HBM) for x in (hidden, downs, ups)]
    return pl.pallas_call(
        functools.partial(project_kernel, steps),
        in_specs=[in_hbm] * 3,
        out_specs=[in_vmem] * 4,
        out_shape=[
            jax.ShapeDtypeStruct((tokens, 2 * slots * ranks), f32),
            jax.ShapeDtypeStruct((tokens, 128), f32),
            jax.ShapeDtypeStruct((tokens, features), bf16),
            jax.ShapeDtypeStruct((slots * ranks, features), bf16),
        ],
        scratch_shapes=[
            pltpu.VMEM((slots * ranks, features), bf16),
            pltpu.SemaphoreType.DMA((steps, 1 + 2 * slots)),
        ],
        compiler_params=limited,
        cost_estimate=pl.CostEstimate(
            flops=4 * tokens * slots * ranks * features,
            bytes_accessed=2 * (tokens + 2 * slots * ranks) * features,
            transcendentals=0,
        ),
        name="project",
    )(*sources)


def project_back_kernel(per_micro, counts, by_hidden, g_ref, up_ref, out_ref):
    pg = dot_last(g_ref[...], up_ref[...])
    pg = jnp.where(counted_rows(counts, pg.shape[0], per_micro), pg, 0.0)
    ahead = by_hidden.shape[1]
    out_ref[:, :ahead] = by_hidden[...]
    out_ref[:, ahead:] = pg


def project_back(counts, by_hidden, cot, ups, per_micro):
    tokens, features = cot.shape
    columns = by_hidden.shape[1] + ups.shape[0]
    return pl.pallas_call(
        functools.partial(project_back_kernel, per_micro),
        in_specs=[in_vmem] * 4,
        out_specs=in_vmem,
        out_shape=jax.ShapeDtypeStruct((tokens, columns), f32),
        compiler_params=limited,
        cost_estimate=pl.CostEstimate(
            flops=2 * tokens * ups.shape[0] * features,
            bytes_accessed=2 * (tokens + ups.shape[0]) * features,
            transcendentals=0,
        ),
        name="project_back",
    )(counts, by_hidden, cot, ups)


def gram_kernel(sections, *refs):
    around = refs[:sections]
    gram_ref, right_ref = refs[sections:]
    section_at = lax.axis_index("section")
    ranks = around[0].shape[0] // 2
    layers = []
    for layer in range(sections):
        distance = lax.rem(layer - section_at + sections, sections)
        chosen = around[0][...]
        for step in range(1, sections):
            chosen = jnp.where(distance == step, around[step][...], chosen)
        layers.append(chosen)
    lefts = [chosen[ranks:] for chosen in layers[:-1]]
    right = jnp.concatenate([chosen[:ranks] for chosen in layers[1:]] + lefts, axis=0)
    right_ref[...] = right
    gram_ref[...] = dot_last(jnp.concatenate(lefts, axis=0), right)


def gram(around):
    sections = len(around)
    ranks = around[0].shape[0] // 2
    columns = around[0].shape[1]
    before = (sections - 1) * ranks
    return pl.pallas_call(
        functools.partial(gram_kernel, sections),
        in_specs=[in_vmem] * sections,
        out_specs=[in_vmem] * 2,
        out_shape=[
            jax.ShapeDtypeStruct((before, 2 * before), f32),
            jax.ShapeDtypeStruct((2 * before, columns), bf16),
        ],
        compiler_params=limited,
        name="gram",
    )(*around)


def chain_kernel(sections, slots, features, per_micro, bounds, counts, *refs):
    projections, grams = refs[:sections], refs[sections:-3]
    sq_ref, factor_ref, mixed_ref = refs[-3:]
    layers = sections
    replica_at = lax.axis_index("replica")
    section_at = lax.axis_index("section")
    tokens = sq_ref.shape[0]
    table = grams[0][...]
    for other in grams[1:]:
        table = table + other[...]
    ranks = projections[0].shape[1] // (3 * slots)
    parts = [[jnp.zeros((tokens, ranks), f32)] * 3 for _ in range(layers)]
    for distance, source in enumerate(projections):
        section = lax.rem(section_at + distance, sections)
        first = entry(bounds, replica_at, section)
        after = entry(bounds, replica_at, section + 1)
        for slot in range(slots):
            for which in range(3):
                block = which * slots + slot
                piece = source[:, block * ranks : (block + 1) * ranks]
                for layer in range(layers):
                    here = (first + slot == layer) & (layer < after)
                    parts[layer][which] = jnp.where(here, piece, parts[layer][which])
    scale_d = 1.0 / math.sqrt(features)
    scale_r = 1.0 / math.sqrt(ranks)

    def part(layer, which):
        return parts[layer][which]

    def up_down(i, layer):
        return table[i * ranks : (i + 1) * ranks, (layer - 1) * ranks : layer * ranks]

    def up_up(i, j):
        at_column = (layers - 1 + j) * ranks
        return table[i * ranks : (i + 1) * ranks, at_column : at_column + ranks]

    def times(x, y):
        return jnp.dot(x, y, preferred_element_type=f32, precision=exact)

    square = sq_ref[:, 0:1]
    inverses, inners, actives, sigmoids = [], [], [], []
    on_up = [[part(l, 1) for l in range(layers - 1)]]
    for layer in range(layers):
        inverse = lax.rsqrt(jnp.maximum(square, 0.0) * (1.0 / features) + norm_eps)
        on_down = part(layer, 0)
        for i in range(layer):
            on_down = on_down + scale_r * times(actives[i], up_down(i, layer))
        inner = on_down * (inverse * scale_d)
        sigmoid = jax.nn.sigmoid(inner)
        active = (inner * sigmoid).astype(bf16).astype(f32)
        inverses.append(inverse)
        inners.append(inner)
        sigmoids.append(sigmoid)
        actives.append(active)
        if layer < layers - 1:
            now = on_up[-1]
            grown = [now[l] + scale_r * times(active, up_up(layer, l)) for l in range(layers - 1)]
            square = square + scale_r * row_sum(active * (now[layer] + grown[layer]))
            on_up.append(grown)
    scaled = [None] * layers
    kappas = [None] * layers
    for layer in reversed(range(layers)):
        incoming = part(layer, 2)
        for k in range(layer + 1, layers):
            incoming = incoming + scale_d * dot_last(scaled[k], up_down(layer, k), exact)
            incoming = incoming - kappas[k] * on_up[k][layer]
        sigmoid, inner = sigmoids[layer], inners[layer]
        slope = sigmoid * (1.0 + inner * (1.0 - sigmoid))
        error = incoming * scale_r * slope
        scaled[layer] = error * inverses[layer]
        kappas[layer] = (
            inverses[layer] * inverses[layer] * (row_sum(error * inner) * (1.0 / features))
        )

    def owned(values):
        chosen = values[0]
        for layer in range(1, layers):
            chosen = jnp.where(section_at == layer, values[layer], chosen)
        return chosen

    own_error = owned(scaled)
    own_active = owned(actives)
    counted = counted_rows(counts, tokens, per_micro)
    later = jnp.zeros_like(square)
    for k in range(1, layers):
        later = later + jnp.where(k > section_at, kappas[k], 0.0)
    on_hidden = jnp.concatenate([own_error * scale_d, -scale_r * later * own_active], axis=1)
    on_cot = jnp.concatenate(
        [jnp.zeros_like(own_active), jnp.where(counted, own_active * scale_r, 0.0)], axis=1
    )
    factor_ref[...] = jnp.concatenate([on_hidden.T, on_cot.T], axis=1).astype(bf16)
    both = scale_d * scale_r
    for k in range(1, layers):
        cut = slice((k - 1) * ranks, k * ranks)
        across = dot_first(own_active.astype(bf16), scaled[k].astype(bf16)) * both
        mixed_ref[:ranks, cut] = jnp.zeros_like(across)
        mixed_ref[ranks:, cut] = jnp.where(k > section_at, across, 0.0)
    for i in range(layers - 1):
        cut = slice((layers - 1 + i) * ranks, (layers + i) * ranks)
        after = jnp.zeros_like(square)
        for k in range(i + 1, layers):
            after = after + jnp.where(k > section_at, kappas[k], 0.0)
        across = dot_first(own_error.astype(bf16), actives[i].astype(bf16)) * both
        mixed_ref[:ranks, cut] = jnp.where(i < section_at, across, 0.0)
        across = dot_first(own_active.astype(bf16), (after * actives[i]).astype(bf16))
        mixed_ref[ranks:, cut] = across * (-scale_r * scale_r)


def chain(bounds, counts, projections, grams, square, slots, features, per_micro):
    sections = len(projections)
    tokens, wide = projections[0].shape
    ranks = wide // (3 * slots)
    inputs = [*projections, *grams, square]
    kernel = functools.partial(chain_kernel, sections, slots, features, per_micro)
    return pl.pallas_call(
        kernel,
        in_specs=[in_vmem] * (2 + len(inputs)),
        out_specs=[in_vmem] * 2,
        out_shape=[
            jax.ShapeDtypeStruct((2 * ranks, 2 * tokens), bf16),
            jax.ShapeDtypeStruct((2 * ranks, 2 * (sections - 1) * ranks), f32),
        ],
        compiler_params=limited,
        name="chain",
    )(bounds, counts, *inputs)


def gradient_kernel(first, lead, factor_ref, h_ref, g_ref, out_ref):
    _, _, ranks, columns = out_ref.shape
    tokens = h_ref.shape[0]
    replica_at = lax.axis_index("replica")
    tensor_at = lax.axis_index("tensor")
    tensors = lax.axis_size("tensor")
    down = factor_ref[:ranks, :tokens]
    up = factor_ref[ranks:]
    for middle in range(2):
        for high in range(2):
            for which, (far, low) in enumerate(((lead, middle), (middle, lead))):
                hop = low + 2 * high
                owner = (replica_at ^ (first + 2 * far)) * tensors + (tensor_at ^ hop)
                cut = pl.ds(pl.multiple_of(owner * columns, columns), columns)
                if which == 0:
                    block = jnp.dot(down, h_ref[:, cut], preferred_element_type=f32)
                else:
                    stacked = jnp.concatenate([h_ref[:, cut], g_ref[:, cut]], axis=0)
                    block = jnp.dot(up, stacked, preferred_element_type=f32)
                out_ref[which, 2 * middle + high] = block.astype(bf16)


def gradient(factors, hidden, cot, first, lead, columns):
    tokens, features = hidden.shape
    rows = factors.shape[0]
    return pl.pallas_call(
        functools.partial(gradient_kernel, first, lead),
        in_specs=[in_vmem] * 3,
        out_specs=in_vmem,
        out_shape=jax.ShapeDtypeStruct((2, 4, rows // 2, columns), bf16),
        compiler_params=limited,
        cost_estimate=pl.CostEstimate(
            flops=rows * tokens * features,
            bytes_accessed=(tokens + rows // 2) * features,
            transcendentals=0,
        ),
        name="gradient",
    )(factors, hidden, cot)


def update_kernel(which, kept, near, one, two, last, mixed_ref, other_ref, right_ref, *refs):
    master_ref, moment_ref, second_ref, new_master, new_moment, new_second, share_ref = refs
    ranks = last.shape[0]
    rows = slice(which * ranks, (which + 1) * ranks)
    mixed = mixed_ref[rows] + other_ref[rows].astype(f32)
    right = right_ref[...].astype(f32)
    own = jnp.dot(mixed, right, preferred_element_type=f32, precision=exact)
    for block in (kept[which, 0], near[which, 0], one[0], two[0], last[...]):
        own = own + block.astype(f32)
    moment = beta_one * moment_ref[0] + (1.0 - beta_one) * own
    second = beta_two * second_ref[0] + (1.0 - beta_two) * own * own
    master = master_ref[0]
    master = master - learn_rate * (
        moment / first_fix / (jnp.sqrt(second / second_fix) + adam_eps) + decay_rate * master
    )
    share_ref[0] = master.astype(bf16)
    new_master[0] = master
    new_moment[0] = moment
    new_second[0] = second


def update(which, parts, right, state):
    inputs = [*parts, right, *state]
    return pl.pallas_call(
        functools.partial(update_kernel, which),
        in_specs=[in_vmem] * len(inputs),
        out_specs=[in_vmem] * 4,
        out_shape=[jax.ShapeDtypeStruct(array.shape, f32) for array in state]
        + [jax.ShapeDtypeStruct(state[0].shape, bf16)],
        compiler_params=limited,
        name="update",
    )(*inputs)


def place_kernel(layout, start, bounds, *refs):
    sources = refs[: len(layout)]
    outs = refs[-4:-2]
    zeros, sem = refs[-2:]
    slots, ranks, features = outs[0].shape
    columns = zeros.shape[1]
    tensors = lax.axis_size("tensor")
    replica_at = lax.axis_index("replica")
    section_at = lax.axis_index("section")
    tensor_at = lax.axis_index("tensor")
    first = entry(bounds, replica_at, section_at)
    after = entry(bounds, replica_at, section_at + 1)
    zeros[...] = jnp.zeros_like(zeros)

    def fill(slot, distance, go):
        for blocks, source in zip(layout, sources):
            for i, (window, which, order, hop) in enumerate(blocks):
                if window != distance:
                    continue
                owner = (replica_at ^ order) * tensors + (tensor_at ^ hop)
                cut = pl.ds(pl.multiple_of(owner * columns, columns), columns)
                go(pltpu.make_async_copy(source.at[i], outs[which].at[slot, :, cut], sem))

    def clear(slot, go):
        for out in outs:
            for block in range(features // columns):
                cut = pl.ds(block * columns, columns)
                go(pltpu.make_async_copy(zeros, out.at[slot, :, cut], sem))

    for act in (lambda copy: copy.start(), lambda copy: copy.wait()):
        for slot in range(slots):
            layer = first + slot
            present = layer < after
            for distance in range(2):

                @pl.when(present & (layer - section_at == distance))
                def _():
                    fill(slot, distance, act)

            if start:

                @pl.when(jnp.logical_not(present))
                def _():
                    clear(slot, act)


def place(bounds, pieces, before, slots, ranks, features):
    layout = [blocks for blocks, _ in pieces]
    arrays = [array for _, array in pieces]
    columns = arrays[0].shape[-1]
    return pl.pallas_call(
        functools.partial(place_kernel, layout, not before),
        in_specs=[in_vmem] * (1 + len(arrays)) + [in_hbm] * len(before),
        out_specs=[in_hbm] * 2,
        out_shape=[jax.ShapeDtypeStruct((slots, ranks, features), bf16)] * 2,
        scratch_shapes=[pltpu.VMEM((ranks, columns), bf16), pltpu.SemaphoreType.DMA],
        input_output_aliases={1 + len(arrays) + i: i for i in range(len(before))},
        compiler_params=limited,
        cost_estimate=pl.CostEstimate(
            flops=0,
            bytes_accessed=4 * sum(array.size for array in arrays),
            transcendentals=0,
        ),
        name="place",
    )(bounds, *arrays, *before)


def swapped(block, axis, distance):
    route = [(i, i ^ distance) for i in range(lax.axis_size(axis))]
    return lax.ppermute(block, axis, route)


def swaps(block, axis):
    return [swapped(block, axis, k) for k in range(1, lax.axis_size(axis))]


def from_next(block, distance=1):
    size = lax.axis_size("section")
    route = [((i + distance) % size, i) for i in range(size)]
    return lax.ppermute(block, "section", route)


def following_layer(block):
    size = lax.axis_size("section")
    return lax.ppermute(block, "section", [(i + 1, i) for i in range(size - 1)])


def summed(*blocks):
    total = blocks[0].astype(f32)
    for block in blocks[1:]:
        total = total + block.astype(f32)
    return total.astype(bf16)


def reduced(factors, hidden, cot, columns, mixed):
    def halves(lead):
        sent = gradient(factors, hidden, cot, 1, lead, columns)
        return swapped(sent, "replica", 1), gradient(factors, hidden, cot, 0, lead, columns)

    def part(which, cut, *steps):
        return summed(kept[which, cut], near[which, cut], *steps)

    def added(axis, distance):
        return mixed + swapped(mixed.astype(bf16), axis, distance).astype(f32)

    near, kept = halves(1)
    whole, low = slice(0, 4), slice(2, 4)
    down_one = swapped(part(0, whole), "replica", 2)
    up_one = swapped(part(1, whole), "tensor", 1)
    near, kept = halves(0)
    mixed = added("tensor", 1)
    mixed = added("replica", 1)
    mixed = added("tensor", 2)
    down_one, up_one, mixed = lax.optimization_barrier((down_one, up_one, mixed))
    down_two = swapped(part(0, low, down_one[2:]), "tensor", 1)
    up_two = swapped(part(1, low, up_one[2:]), "replica", 2)
    down_last = swapped(part(0, 1, down_one[1], down_two[1]), "tensor", 2)
    kept, near = lax.optimization_barrier((kept, near))
    up_last = swapped(part(1, 1, up_one[1], up_two[1]), "tensor", 2)
    other = swapped(mixed.astype(bf16), "replica", 2)
    down = (kept, near, down_one, down_two, down_last, mixed, other)
    return down, (kept, near, up_one, up_two, up_last, mixed, other)


def crossed(piece, axis, distance):
    blocks, array = piece
    blocks = [
        (window, which, order ^ distance, hop)
        if axis == "replica"
        else (window, which, order, hop ^ distance)
        for window, which, order, hop in blocks
    ]
    return blocks, swapped(array, axis, distance)


def fetched(piece):
    blocks, array = piece
    return [(1, *block[1:]) for block in blocks], following_layer(array)


def picked(piece, at):
    return piece[0][at : at + 1], piece[1][at : at + 1]


def joined(*pieces):
    blocks = [block for piece in pieces for block in piece[0]]
    return blocks, jnp.concatenate([array for _, array in pieces])


def spread(down, up, bounds, slots, features):
    ranks = down.shape[1]
    down_own, up_own = ([(0, 0, 0, 0)], down), ([(0, 1, 0, 0)], up)
    down_one = crossed(down_own, "tensor", 2)
    up_one = crossed(up_own, "tensor", 2)
    downs, ups = joined(down_own, down_one), joined(up_own, up_one)
    owns = lax.optimization_barrier((down, up))
    own = joined((down_own[0], owns[0]), (up_own[0], owns[1]))
    next_own = fetched(own)
    *ones, next_array = lax.optimization_barrier((down_one[1], up_one[1], next_own[1]))
    one = joined((down_one[0], ones[0]), (up_one[0], ones[1]))
    next_own = (next_own[0], next_array)
    down_two = crossed(downs, "tensor", 1)
    up_two = crossed(ups, "replica", 2)
    next_one = fetched(one)
    two = joined(down_two, up_two)
    down_three = crossed(joined(downs, down_two), "replica", 2)
    up_three = crossed(joined(ups, up_two), "tensor", 1)
    next_two = fetched(two)
    next_end = fetched(joined(picked(down_three, 3), picked(up_three, 3)))
    _, _, next_array = lax.optimization_barrier((down_three[1], up_three[1], next_two[1]))
    next_two = (next_two[0], next_array)
    down_end = joined(picked(next_own, 0), picked(next_one, 0), picked(next_two, 0))
    up_end = joined(picked(next_own, 1), picked(next_one, 1), picked(next_two, 2))
    end = joined(crossed(down_end, "replica", 2), crossed(up_end, "tensor", 1), next_end)
    near = joined(own, one, two)
    far = joined(down_three, up_three)
    next_near = joined(next_own, next_one, next_two)
    near_core, far_core, next_core, end_core = (
        crossed(piece, "replica", 1) for piece in (near, far, next_near, end)
    )
    placed = place(
        bounds, [near, near_core, far, far_core, next_near, next_core], [], slots, ranks, features
    )
    placed = place(bounds, [end, end_core], placed, slots, ranks, features)
    return placed


def on_device(
    inputs,
    cotangent,
    micro_counts,
    bounds,
    holder_down,
    holder_up,
    master_down,
    master_up,
    moment_down,
    moment_up,
    second_down,
    second_up,
):
    sections = lax.axis_size("section")
    replicas = lax.axis_size("replica")
    tensors = lax.axis_size("tensor")
    assert replicas == 4 and tensors == 4
    _, micros, per_micro, features = inputs.shape
    micro_counts = micro_counts[None]
    slots = holder_down.shape[2]
    hidden = inputs.reshape(micros * per_micro, features)
    cot = cotangent.reshape(micros * per_micro, features)

    owned = jnp.concatenate([master_down[0], master_up[0]], axis=0).astype(bf16)
    around = [from_next(owned, d) for d in range(1, sections)]
    by_hidden, square, hidden, ups = project(hidden, holder_down[0, 0], holder_up[0, 0])
    around, by_hidden = lax.optimization_barrier((around, by_hidden))
    table, right = gram([owned, *around])
    table, ups = lax.optimization_barrier((table, ups))
    projected = project_back(micro_counts, by_hidden, cot, ups, per_micro)
    table = table + sum(swaps(table, "replica"))
    projections = [projected] + [from_next(projected, d) for d in range(1, sections)]
    table = table + swapped(table, "tensor", 1)
    tables = [table, swapped(table, "tensor", 2)]
    factors, mixed = chain(
        bounds, micro_counts, projections, tables, square, slots, features, per_micro
    )

    down_parts, up_parts = reduced(factors, hidden, cot, master_down.shape[2], mixed)
    down = update(0, down_parts, right, [master_down, moment_down, second_down])
    up = update(1, up_parts, right, [master_up, moment_up, second_up])
    placed = spread(down[3], up[3], bounds, slots, features)
    return (
        placed[0][None, None],
        placed[1][None, None],
        down[0],
        up[0],
        down[1],
        up[1],
        down[2],
        up[2],
    )


def solution(mesh):
    held = P("replica", "section", None, None, None)
    owned = P("section", None, ("replica", "tensor"))
    tokens = P("replica", None, "tensor", None)
    return jax.shard_map(
        on_device,
        mesh=mesh,
        in_specs=(tokens, tokens, P(), P(), held, held) + (owned,) * 6,
        out_specs=(held, held) + (owned,) * 6,
        check_vma=False,
    )
```

```python
import functools
import math

import jax
import jax.numpy as jnp
from jax import lax
from jax.experimental import pallas as pl
from jax.experimental.pallas import tpu as pltpu
from jax.sharding import PartitionSpec as P

norm_eps = 1e-06
learn_rate = 0.01
beta_one = 0.9
beta_two = 0.95
decay_rate = 0.1
adam_eps = 1e-08
first_fix = 0.9999734386011124
second_fix = 0.9940794707796659

f32 = jnp.float32
bf16 = jnp.bfloat16
exact = lax.Precision.HIGHEST
in_vmem = pl.BlockSpec(memory_space=pltpu.VMEM)
in_hbm = pl.BlockSpec(memory_space=pltpu.HBM)
limited = pltpu.CompilerParams(vmem_limit_bytes=16 * 1024 * 1024)


def entry(ref, row, column):
    values = ref[...].astype(f32)
    rows = lax.broadcasted_iota(jnp.int32, values.shape, 0)
    columns = lax.broadcasted_iota(jnp.int32, values.shape, 1)
    return jnp.sum(jnp.where((rows == row) & (columns == column), values, 0.0)).astype(jnp.int32)


def counted_rows(counts, tokens, per_micro):
    rows = lax.broadcasted_iota(jnp.int32, (tokens, 1), 0)
    return rows < entry(counts, 0, lax.axis_index("replica")) * per_micro


def dot_last(x, y, precision=None):
    return lax.dot_general(
        x, y, (((1,), (1,)), ((), ())), preferred_element_type=f32, precision=precision
    )


def dot_first(x, y, precision=None):
    return lax.dot_general(
        x, y, (((0,), (0,)), ((), ())), preferred_element_type=f32, precision=precision
    )


def in_parts(product, wide, parts):
    total = None
    for _ in range(parts):
        piece = wide.astype(bf16)
        wide = wide - piece.astype(f32)
        term = product(piece)
        total = term if total is None else total + term
    return total


def row_sum(x):
    return jnp.sum(x, axis=-1, keepdims=True)


def project_kernel(steps, h_in, down_in, up_in, *refs):
    out_ref, sq_ref, h_ref, up_ref, down_ref, sems = refs
    slots, ranks, features = down_in.shape
    tokens = h_ref.shape[0]
    width = features // steps
    copies = []
    for step in range(steps):
        cut = pl.ds(step * width, width)
        moves = [(h_in.at[:, cut], h_ref.at[:, cut])]
        for slot in range(slots):
            rows = pl.ds(slot * ranks, ranks)
            moves.append((down_in.at[slot, :, cut], down_ref.at[rows, cut]))
            moves.append((up_in.at[slot, :, cut], up_ref.at[rows, cut]))
        copies.append(
            [
                pltpu.make_async_copy(source, target, sems.at[step, i])
                for i, (source, target) in enumerate(moves)
            ]
        )
        for copy in copies[-1]:
            copy.start()
    ph = jnp.zeros((tokens, 2 * slots * ranks), f32)
    square = jnp.zeros((tokens, 128), f32)
    for step in range(steps):
        for copy in copies[step]:
            copy.wait()
        cut = pl.ds(step * width, width)
        h = h_ref[:, cut]
        ph = ph + dot_last(h, jnp.concatenate([down_ref[:, cut], up_ref[:, cut]], axis=0))
        wide = h.astype(f32)
        wide = wide * wide
        for lane in range(0, width, 128):
            square = square + wide[:, lane : lane + 128]
    sq_ref[...] = jnp.broadcast_to(row_sum(square), square.shape)
    out_ref[...] = ph


def project(hidden, downs, ups):
    tokens, features = hidden.shape
    slots, ranks, _ = downs.shape
    steps = 8
    sources = [pltpu.with_memory_space_constraint(x, pltpu.HBM) for x in (hidden, downs, ups)]
    return pl.pallas_call(
        functools.partial(project_kernel, steps),
        in_specs=[in_hbm] * 3,
        out_specs=[in_vmem] * 4,
        out_shape=[
            jax.ShapeDtypeStruct((tokens, 2 * slots * ranks), f32),
            jax.ShapeDtypeStruct((tokens, 128), f32),
            jax.ShapeDtypeStruct((tokens, features), bf16),
            jax.ShapeDtypeStruct((slots * ranks, features), bf16),
        ],
        scratch_shapes=[
            pltpu.VMEM((slots * ranks, features), bf16),
            pltpu.SemaphoreType.DMA((steps, 1 + 2 * slots)),
        ],
        compiler_params=limited,
        cost_estimate=pl.CostEstimate(
            flops=4 * tokens * slots * ranks * features,
            bytes_accessed=2 * (tokens + 2 * slots * ranks) * features,
            transcendentals=0,
        ),
        name="project",
    )(*sources)


def project_back_kernel(per_micro, counts, by_hidden, g_ref, up_ref, out_ref):
    pg = dot_last(g_ref[...], up_ref[...])
    pg = jnp.where(counted_rows(counts, pg.shape[0], per_micro), pg, 0.0)
    ahead = by_hidden.shape[1]
    out_ref[:, :ahead] = by_hidden[...]
    out_ref[:, ahead:] = pg


def project_back(counts, by_hidden, cot, ups, per_micro):
    tokens, features = cot.shape
    columns = by_hidden.shape[1] + ups.shape[0]
    return pl.pallas_call(
        functools.partial(project_back_kernel, per_micro),
        in_specs=[in_vmem] * 4,
        out_specs=in_vmem,
        out_shape=jax.ShapeDtypeStruct((tokens, columns), f32),
        compiler_params=limited,
        cost_estimate=pl.CostEstimate(
            flops=2 * tokens * ups.shape[0] * features,
            bytes_accessed=2 * (tokens + ups.shape[0]) * features,
            transcendentals=0,
        ),
        name="project_back",
    )(counts, by_hidden, cot, ups)


def gram_kernel(sections, *refs):
    around = refs[:sections]
    gram_ref, right_ref = refs[sections:]
    section_at = lax.axis_index("section")
    ranks = around[0].shape[0] // 2
    layers = []
    for layer in range(sections):
        distance = lax.rem(layer - section_at + sections, sections)
        chosen = around[0][...]
        for step in range(1, sections):
            chosen = jnp.where(distance == step, around[step][...], chosen)
        layers.append(chosen)
    lefts = [chosen[ranks:] for chosen in layers[:-1]]
    right = jnp.concatenate([chosen[:ranks] for chosen in layers[1:]] + lefts, axis=0)
    right_ref[...] = right
    gram_ref[...] = dot_last(jnp.concatenate(lefts, axis=0), right)


def gram(around):
    sections = len(around)
    ranks = around[0].shape[0] // 2
    columns = around[0].shape[1]
    before = (sections - 1) * ranks
    return pl.pallas_call(
        functools.partial(gram_kernel, sections),
        in_specs=[in_vmem] * sections,
        out_specs=[in_vmem] * 2,
        out_shape=[
            jax.ShapeDtypeStruct((before, 2 * before), f32),
            jax.ShapeDtypeStruct((2 * before, columns), bf16),
        ],
        compiler_params=limited,
        name="gram",
    )(*around)


def chain_kernel(sections, slots, features, per_micro, bounds, counts, *refs):
    projections, grams = refs[:sections], refs[sections:-3]
    sq_ref, factor_ref, mixed_ref = refs[-3:]
    layers = sections
    replica_at = lax.axis_index("replica")
    section_at = lax.axis_index("section")
    tokens = sq_ref.shape[0]
    table = grams[0][...]
    for other in grams[1:]:
        table = table + other[...]
    ranks = projections[0].shape[1] // (3 * slots)
    parts = [[jnp.zeros((tokens, ranks), f32)] * 3 for _ in range(layers)]
    for distance, source in enumerate(projections):
        section = lax.rem(section_at + distance, sections)
        first = entry(bounds, replica_at, section)
        after = entry(bounds, replica_at, section + 1)
        for slot in range(slots):
            for which in range(3):
                block = which * slots + slot
                piece = source[:, block * ranks : (block + 1) * ranks]
                for layer in range(layers):
                    here = (first + slot == layer) & (layer < after)
                    parts[layer][which] = jnp.where(here, piece, parts[layer][which])
    scale_d = 1.0 / math.sqrt(features)
    scale_r = 1.0 / math.sqrt(ranks)

    def part(layer, which):
        return parts[layer][which]

    def up_down(i, layer):
        return table[i * ranks : (i + 1) * ranks, (layer - 1) * ranks : layer * ranks]

    square = sq_ref[:, 0:1]
    inverses, inners, actives, sigmoids, products = [], [], [], [], []
    on_up = [[part(l, 1) for l in range(layers - 1)]]
    for layer in range(layers):
        inverse = lax.rsqrt(jnp.maximum(square, 0.0) * (1.0 / features) + norm_eps)
        on_down = part(layer, 0)
        for i in range(layer):
            on_down = on_down + products[i][:, (layer - 1) * ranks : layer * ranks]
        inner = on_down * (inverse * scale_d)
        sigmoid = jax.nn.sigmoid(inner)
        active = (inner * sigmoid).astype(bf16).astype(f32)
        inverses.append(inverse)
        inners.append(inner)
        sigmoids.append(sigmoid)
        actives.append(active)
        if layer < layers - 1:
            now = on_up[-1]
            product = in_parts(
                lambda part: jnp.dot(active.astype(bf16), part, preferred_element_type=f32),
                table[layer * ranks : (layer + 1) * ranks],
                3,
            )
            products.append(scale_r * product)
            grown = [
                now[l] + products[layer][:, (layers - 1 + l) * ranks : (layers + l) * ranks]
                for l in range(layers - 1)
            ]
            square = square + scale_r * row_sum(active * (now[layer] + grown[layer]))
            on_up.append(grown)
    scaled = [None] * layers
    kappas = [None] * layers
    for layer in reversed(range(layers)):
        incoming = part(layer, 2)
        for k in range(layer + 1, layers):
            incoming = incoming + scale_d * dot_last(scaled[k], up_down(layer, k), exact)
            incoming = incoming - kappas[k] * on_up[k][layer]
        sigmoid, inner = sigmoids[layer], inners[layer]
        slope = sigmoid * (1.0 + inner * (1.0 - sigmoid))
        error = incoming * scale_r * slope
        scaled[layer] = error * inverses[layer]
        kappas[layer] = (
            inverses[layer] * inverses[layer] * (row_sum(error * inner) * (1.0 / features))
        )

    def owned(values):
        chosen = values[0]
        for layer in range(1, layers):
            chosen = jnp.where(section_at == layer, values[layer], chosen)
        return chosen

    own_error = owned(scaled)
    own_active = owned(actives)
    counted = counted_rows(counts, tokens, per_micro)
    later = jnp.zeros_like(square)
    for k in range(1, layers):
        later = later + jnp.where(k > section_at, kappas[k], 0.0)
    on_hidden = jnp.concatenate([own_error * scale_d, -scale_r * later * own_active], axis=1)
    on_cot = jnp.concatenate(
        [jnp.zeros_like(own_active), jnp.where(counted, own_active * scale_r, 0.0)], axis=1
    )
    factor_ref[...] = jnp.concatenate([on_hidden.T, on_cot.T], axis=1).astype(bf16)
    both = scale_d * scale_r
    for k in range(1, layers):
        cut = slice((k - 1) * ranks, k * ranks)
        across = dot_first(own_active.astype(bf16), scaled[k].astype(bf16)) * both
        mixed_ref[:ranks, cut] = jnp.zeros_like(across)
        mixed_ref[ranks:, cut] = jnp.where(k > section_at, across, 0.0)
    for i in range(layers - 1):
        cut = slice((layers - 1 + i) * ranks, (layers + i) * ranks)
        after = jnp.zeros_like(square)
        for k in range(i + 1, layers):
            after = after + jnp.where(k > section_at, kappas[k], 0.0)
        across = dot_first(own_error.astype(bf16), actives[i].astype(bf16)) * both
        mixed_ref[:ranks, cut] = jnp.where(i < section_at, across, 0.0)
        across = dot_first(own_active.astype(bf16), (after * actives[i]).astype(bf16))
        mixed_ref[ranks:, cut] = across * (-scale_r * scale_r)


def chain(bounds, counts, projections, grams, square, slots, features, per_micro):
    sections = len(projections)
    tokens, wide = projections[0].shape
    ranks = wide // (3 * slots)
    inputs = [*projections, *grams, square]
    kernel = functools.partial(chain_kernel, sections, slots, features, per_micro)
    return pl.pallas_call(
        kernel,
        in_specs=[in_vmem] * (2 + len(inputs)),
        out_specs=[in_vmem] * 2,
        out_shape=[
            jax.ShapeDtypeStruct((2 * ranks, 2 * tokens), bf16),
            jax.ShapeDtypeStruct((2 * ranks, 2 * (sections - 1) * ranks), f32),
        ],
        compiler_params=limited,
        name="chain",
    )(bounds, counts, *inputs)


def gradient_kernel(first, lead, factor_ref, h_ref, g_ref, out_ref):
    _, _, ranks, columns = out_ref.shape
    tokens = h_ref.shape[0]
    replica_at = lax.axis_index("replica")
    tensor_at = lax.axis_index("tensor")
    tensors = lax.axis_size("tensor")
    down = factor_ref[:ranks, :tokens]
    up = factor_ref[ranks:]
    for middle in range(2):
        for high in range(2):
            for which, (far, low) in enumerate(((lead, middle), (middle, lead))):
                hop = low + 2 * high
                owner = (replica_at ^ (first + 2 * far)) * tensors + (tensor_at ^ hop)
                cut = pl.ds(pl.multiple_of(owner * columns, columns), columns)
                if which == 0:
                    block = jnp.dot(down, h_ref[:, cut], preferred_element_type=f32)
                else:
                    stacked = jnp.concatenate([h_ref[:, cut], g_ref[:, cut]], axis=0)
                    block = jnp.dot(up, stacked, preferred_element_type=f32)
                out_ref[which, 2 * middle + high] = block.astype(bf16)


def gradient(factors, hidden, cot, first, lead, columns):
    tokens, features = hidden.shape
    rows = factors.shape[0]
    return pl.pallas_call(
        functools.partial(gradient_kernel, first, lead),
        in_specs=[in_vmem] * 3,
        out_specs=in_vmem,
        out_shape=jax.ShapeDtypeStruct((2, 4, rows // 2, columns), bf16),
        compiler_params=limited,
        cost_estimate=pl.CostEstimate(
            flops=rows * tokens * features,
            bytes_accessed=(tokens + rows // 2) * features,
            transcendentals=0,
        ),
        name="gradient",
    )(factors, hidden, cot)


def update_kernel(which, kept, near, one, two, last, mixed_ref, other_ref, right_ref, *refs):
    master_ref, moment_ref, second_ref, new_master, new_moment, new_second, share_ref = refs
    ranks = last.shape[0]
    rows = slice(which * ranks, (which + 1) * ranks)
    mixed = mixed_ref[rows] + other_ref[rows].astype(f32)
    right = right_ref[...]
    own = in_parts(lambda part: jnp.dot(part, right, preferred_element_type=f32), mixed, 3)
    for block in (kept[which, 0], near[which, 0], one[0], two[0], last[...]):
        own = own + block.astype(f32)
    moment = beta_one * moment_ref[0] + (1.0 - beta_one) * own
    second = beta_two * second_ref[0] + (1.0 - beta_two) * own * own
    master = master_ref[0]
    master = master - learn_rate * (
        moment / first_fix / (jnp.sqrt(second / second_fix) + adam_eps) + decay_rate * master
    )
    share_ref[0] = master.astype(bf16)
    new_master[0] = master
    new_moment[0] = moment
    new_second[0] = second


def update(which, parts, right, state):
    inputs = [*parts, right, *state]
    return pl.pallas_call(
        functools.partial(update_kernel, which),
        in_specs=[in_vmem] * len(inputs),
        out_specs=[in_vmem] * 4,
        out_shape=[jax.ShapeDtypeStruct(array.shape, f32) for array in state]
        + [jax.ShapeDtypeStruct(state[0].shape, bf16)],
        compiler_params=limited,
        name="update",
    )(*inputs)


def place_kernel(layout, start, bounds, *refs):
    sources = refs[: len(layout)]
    outs = refs[-4:-2]
    zeros, sem = refs[-2:]
    slots, ranks, features = outs[0].shape
    columns = zeros.shape[1]
    tensors = lax.axis_size("tensor")
    replica_at = lax.axis_index("replica")
    section_at = lax.axis_index("section")
    tensor_at = lax.axis_index("tensor")
    first = entry(bounds, replica_at, section_at)
    after = entry(bounds, replica_at, section_at + 1)
    zeros[...] = jnp.zeros_like(zeros)

    def fill(slot, distance, go):
        for blocks, source in zip(layout, sources):
            for i, (window, which, order, hop) in enumerate(blocks):
                if window != distance:
                    continue
                owner = (replica_at ^ order) * tensors + (tensor_at ^ hop)
                cut = pl.ds(pl.multiple_of(owner * columns, columns), columns)
                go(pltpu.make_async_copy(source.at[i], outs[which].at[slot, :, cut], sem))

    def clear(slot, go):
        for out in outs:
            for block in range(features // columns):
                cut = pl.ds(block * columns, columns)
                go(pltpu.make_async_copy(zeros, out.at[slot, :, cut], sem))

    for act in (lambda copy: copy.start(), lambda copy: copy.wait()):
        for slot in range(slots):
            layer = first + slot
            present = layer < after
            for distance in range(2):

                @pl.when(present & (layer - section_at == distance))
                def _():
                    fill(slot, distance, act)

            if start:

                @pl.when(jnp.logical_not(present))
                def _():
                    clear(slot, act)


def place(bounds, pieces, before, slots, ranks, features):
    layout = [blocks for blocks, _ in pieces]
    arrays = [array for _, array in pieces]
    columns = arrays[0].shape[-1]
    return pl.pallas_call(
        functools.partial(place_kernel, layout, not before),
        in_specs=[in_vmem] * (1 + len(arrays)) + [in_hbm] * len(before),
        out_specs=[in_hbm] * 2,
        out_shape=[jax.ShapeDtypeStruct((slots, ranks, features), bf16)] * 2,
        scratch_shapes=[pltpu.VMEM((ranks, columns), bf16), pltpu.SemaphoreType.DMA],
        input_output_aliases={1 + len(arrays) + i: i for i in range(len(before))},
        compiler_params=limited,
        cost_estimate=pl.CostEstimate(
            flops=0,
            bytes_accessed=4 * sum(array.size for array in arrays),
            transcendentals=0,
        ),
        name="place",
    )(bounds, *arrays, *before)


def swapped(block, axis, distance):
    route = [(i, i ^ distance) for i in range(lax.axis_size(axis))]
    return lax.ppermute(block, axis, route)


def swaps(block, axis):
    return [swapped(block, axis, k) for k in range(1, lax.axis_size(axis))]


def from_next(block, distance=1):
    size = lax.axis_size("section")
    route = [((i + distance) % size, i) for i in range(size)]
    return lax.ppermute(block, "section", route)


def following_layer(block):
    size = lax.axis_size("section")
    return lax.ppermute(block, "section", [(i + 1, i) for i in range(size - 1)])


def summed(*blocks):
    total = blocks[0].astype(f32)
    for block in blocks[1:]:
        total = total + block.astype(f32)
    return total.astype(bf16)


def reduced(factors, hidden, cot, columns, mixed):
    def halves(lead):
        sent = gradient(factors, hidden, cot, 1, lead, columns)
        return swapped(sent, "replica", 1), gradient(factors, hidden, cot, 0, lead, columns)

    def part(which, cut, *steps):
        return summed(kept[which, cut], near[which, cut], *steps)

    def added(axis, distance):
        return mixed + swapped(mixed.astype(bf16), axis, distance).astype(f32)

    near, kept = halves(1)
    whole, low = slice(0, 4), slice(2, 4)
    down_one = swapped(part(0, whole), "replica", 2)
    up_one = swapped(part(1, whole), "tensor", 1)
    near, kept = halves(0)
    mixed = added("replica", 1)
    mixed = added("tensor", 2)
    down_one, up_one, mixed = lax.optimization_barrier((down_one, up_one, mixed))
    down_two = swapped(part(0, low, down_one[2:]), "tensor", 1)
    up_two = swapped(part(1, low, up_one[2:]), "replica", 2)
    down_last = swapped(part(0, 1, down_one[1], down_two[1]), "tensor", 2)
    kept, near = lax.optimization_barrier((kept, near))
    up_last = swapped(part(1, 1, up_one[1], up_two[1]), "tensor", 2)
    mixed = added("tensor", 1)
    other = swapped(mixed.astype(bf16), "replica", 2)
    down = (kept, near, down_one, down_two, down_last, mixed, other)
    return down, (kept, near, up_one, up_two, up_last, mixed, other)


def crossed(piece, axis, distance):
    blocks, array = piece
    blocks = [
        (window, which, order ^ distance, hop)
        if axis == "replica"
        else (window, which, order, hop ^ distance)
        for window, which, order, hop in blocks
    ]
    return blocks, swapped(array, axis, distance)


def fetched(piece):
    blocks, array = piece
    return [(1, *block[1:]) for block in blocks], following_layer(array)


def picked(piece, at):
    return piece[0][at : at + 1], piece[1][at : at + 1]


def joined(*pieces):
    blocks = [block for piece in pieces for block in piece[0]]
    return blocks, jnp.concatenate([array for _, array in pieces])


def spread(down, up, bounds, slots, features):
    ranks = down.shape[1]
    down_own, up_own = ([(0, 0, 0, 0)], down), ([(0, 1, 0, 0)], up)
    down_one = crossed(down_own, "tensor", 2)
    up_one = crossed(up_own, "tensor", 2)
    downs, ups = joined(down_own, down_one), joined(up_own, up_one)
    owns = lax.optimization_barrier((down, up))
    own = joined((down_own[0], owns[0]), (up_own[0], owns[1]))
    next_own = fetched(own)
    *ones, next_array = lax.optimization_barrier((down_one[1], up_one[1], next_own[1]))
    one = joined((down_one[0], ones[0]), (up_one[0], ones[1]))
    next_own = (next_own[0], next_array)
    down_two = crossed(downs, "tensor", 1)
    up_two = crossed(ups, "replica", 2)
    next_one = fetched(one)
    two = joined(down_two, up_two)
    down_three = crossed(joined(downs, down_two), "replica", 2)
    up_three = crossed(joined(ups, up_two), "tensor", 1)
    next_two = fetched(two)
    next_end = fetched(joined(picked(down_three, 3), picked(up_three, 3)))
    _, _, next_array = lax.optimization_barrier((down_three[1], up_three[1], next_two[1]))
    next_two = (next_two[0], next_array)
    down_end = joined(picked(next_own, 0), picked(next_one, 0), picked(next_two, 0))
    up_end = joined(picked(next_own, 1), picked(next_one, 1), picked(next_two, 2))
    end = joined(crossed(down_end, "replica", 2), crossed(up_end, "tensor", 1), next_end)
    near = joined(own, one, two)
    far = joined(down_three, up_three)
    next_near = joined(next_own, next_one, next_two)
    near_core, far_core, next_core, end_core = (
        crossed(piece, "replica", 1) for piece in (near, far, next_near, end)
    )
    placed = place(
        bounds, [near, near_core, far, far_core, next_near, next_core], [], slots, ranks, features
    )
    placed = place(bounds, [end, end_core], placed, slots, ranks, features)
    return placed


def on_device(
    inputs,
    cotangent,
    micro_counts,
    bounds,
    holder_down,
    holder_up,
    master_down,
    master_up,
    moment_down,
    moment_up,
    second_down,
    second_up,
):
    sections = lax.axis_size("section")
    replicas = lax.axis_size("replica")
    tensors = lax.axis_size("tensor")
    assert replicas == 4 and tensors == 4
    _, micros, per_micro, features = inputs.shape
    micro_counts = micro_counts[None]
    slots = holder_down.shape[2]
    hidden = inputs.reshape(micros * per_micro, features)
    cot = cotangent.reshape(micros * per_micro, features)

    owned = jnp.concatenate([master_down[0], master_up[0]], axis=0).astype(bf16)
    around = [from_next(owned, d) for d in range(1, sections)]
    by_hidden, square, hidden, ups = project(hidden, holder_down[0, 0], holder_up[0, 0])
    around, by_hidden = lax.optimization_barrier((around, by_hidden))
    table, right = gram([owned, *around])
    table, ups = lax.optimization_barrier((table, ups))
    projected = project_back(micro_counts, by_hidden, cot, ups, per_micro)
    table = table + sum(swaps(table, "replica"))
    projections = [projected] + [from_next(projected, d) for d in range(1, sections)]
    table = table + swapped(table, "tensor", 1)
    tables = [table, swapped(table, "tensor", 2)]
    factors, mixed = chain(
        bounds, micro_counts, projections, tables, square, slots, features, per_micro
    )

    down_parts, up_parts = reduced(factors, hidden, cot, master_down.shape[2], mixed)
    down = update(0, down_parts, right, [master_down, moment_down, second_down])
    up = update(1, up_parts, right, [master_up, moment_up, second_up])
    placed = spread(down[3], up[3], bounds, slots, features)
    return (
        placed[0][None, None],
        placed[1][None, None],
        down[0],
        up[0],
        down[1],
        up[1],
        down[2],
        up[2],
    )


def solution(mesh):
    held = P("replica", "section", None, None, None)
    owned = P("section", None, ("replica", "tensor"))
    tokens = P("replica", None, "tensor", None)
    return jax.shard_map(
        on_device,
        mesh=mesh,
        in_specs=(tokens, tokens, P(), P(), held, held) + (owned,) * 6,
        out_specs=(held, held) + (owned,) * 6,
        check_vma=False,
    )
```

```python
import functools
import math

import jax
import jax.numpy as jnp
from jax import lax
from jax.experimental import pallas as pl
from jax.experimental.pallas import tpu as pltpu
from jax.sharding import PartitionSpec as P

norm_eps = 1e-06
learn_rate = 0.01
beta_one = 0.9
beta_two = 0.95
decay_rate = 0.1
adam_eps = 1e-08
first_fix = 0.9999734386011124
second_fix = 0.9940794707796659

f32 = jnp.float32
bf16 = jnp.bfloat16
exact = lax.Precision.HIGHEST
in_vmem = pl.BlockSpec(memory_space=pltpu.VMEM)
in_hbm = pl.BlockSpec(memory_space=pltpu.HBM)
limited = pltpu.CompilerParams(vmem_limit_bytes=16 * 1024 * 1024)


def entry(ref, row, column):
    values = ref[...].astype(f32)
    rows = lax.broadcasted_iota(jnp.int32, values.shape, 0)
    columns = lax.broadcasted_iota(jnp.int32, values.shape, 1)
    return jnp.sum(jnp.where((rows == row) & (columns == column), values, 0.0)).astype(jnp.int32)


def counted_rows(counts, tokens, per_micro):
    rows = lax.broadcasted_iota(jnp.int32, (tokens, 1), 0)
    return rows < entry(counts, 0, lax.axis_index("replica")) * per_micro


def dot_last(x, y, precision=None):
    return lax.dot_general(
        x, y, (((1,), (1,)), ((), ())), preferred_element_type=f32, precision=precision
    )


def dot_first(x, y, precision=None):
    return lax.dot_general(
        x, y, (((0,), (0,)), ((), ())), preferred_element_type=f32, precision=precision
    )


def in_parts(product, wide, parts):
    total = None
    for _ in range(parts):
        piece = wide.astype(bf16)
        wide = wide - piece.astype(f32)
        term = product(piece)
        total = term if total is None else total + term
    return total


def row_sum(x):
    return jnp.sum(x, axis=-1, keepdims=True)


def project_down_kernel(steps, h_in, down_in, out_ref, sq_ref, h_ref, down_ref, sems):
    slots, ranks, features = down_in.shape
    tokens = h_ref.shape[0]
    width = features // steps
    copies = []
    for step in range(steps):
        cut = pl.ds(step * width, width)
        moves = [(h_in.at[:, cut], h_ref.at[:, cut])]
        for slot in range(slots):
            rows = pl.ds(slot * ranks, ranks)
            moves.append((down_in.at[slot, :, cut], down_ref.at[rows, cut]))
        copies.append(
            [
                pltpu.make_async_copy(source, target, sems.at[step, i])
                for i, (source, target) in enumerate(moves)
            ]
        )
        for copy in copies[-1]:
            copy.start()
    total = jnp.zeros((tokens, slots * ranks), f32)
    square = jnp.zeros((tokens, 128), f32)
    for step in range(steps):
        for copy in copies[step]:
            copy.wait()
        cut = pl.ds(step * width, width)
        h = h_ref[:, cut]
        total = total + dot_last(h, down_ref[:, cut])
        wide = h.astype(f32)
        wide = wide * wide
        for lane in range(0, width, 128):
            square = square + wide[:, lane : lane + 128]
    sq_ref[...] = jnp.broadcast_to(row_sum(square), square.shape)
    out_ref[...] = total


def project_down(hidden, downs):
    tokens, features = hidden.shape
    slots, ranks, _ = downs.shape
    steps = 8
    sources = [pltpu.with_memory_space_constraint(x, pltpu.HBM) for x in (hidden, downs)]
    return pl.pallas_call(
        functools.partial(project_down_kernel, steps),
        in_specs=[in_hbm] * 2,
        out_specs=[in_vmem] * 3,
        out_shape=[
            jax.ShapeDtypeStruct((tokens, slots * ranks), f32),
            jax.ShapeDtypeStruct((tokens, 128), f32),
            jax.ShapeDtypeStruct((tokens, features), bf16),
        ],
        scratch_shapes=[
            pltpu.VMEM((slots * ranks, features), bf16),
            pltpu.SemaphoreType.DMA((steps, 1 + slots)),
        ],
        compiler_params=limited,
        cost_estimate=pl.CostEstimate(
            flops=2 * tokens * slots * ranks * features,
            bytes_accessed=2 * (tokens + slots * ranks) * features,
            transcendentals=0,
        ),
        name="project_down",
    )(*sources)


def project_up_kernel(per_micro, counts, by_down, h_ref, g_ref, up_ref, out_ref):
    tokens, columns = by_down.shape
    ups = up_ref[...].reshape(columns, up_ref.shape[2])
    out_ref[:, :columns] = by_down[...]
    out_ref[:, columns : 2 * columns] = dot_last(h_ref[...], ups)
    by_cot = dot_last(g_ref[...], ups)
    out_ref[:, 2 * columns :] = jnp.where(counted_rows(counts, tokens, per_micro), by_cot, 0.0)


def project_up(counts, by_down, hidden, cot, ups, per_micro):
    tokens, features = hidden.shape
    columns = by_down.shape[1]
    return pl.pallas_call(
        functools.partial(project_up_kernel, per_micro),
        in_specs=[in_vmem] * 5,
        out_specs=in_vmem,
        out_shape=jax.ShapeDtypeStruct((tokens, 3 * columns), f32),
        compiler_params=limited,
        cost_estimate=pl.CostEstimate(
            flops=4 * tokens * columns * features,
            bytes_accessed=2 * (2 * tokens + columns) * features,
            transcendentals=0,
        ),
        name="project_up",
    )(counts, by_down, hidden, cot, ups)


def gram_kernel(sections, *refs):
    around = refs[:sections]
    gram_ref, right_ref = refs[sections:]
    section_at = lax.axis_index("section")
    ranks = around[0].shape[0] // 2
    if sections == 2:
        own, other = around[0][...], around[1][...]
        downs = [jnp.where(section_at == 0, other, own[:ranks])]
        lefts = [jnp.where(section_at == 0, own[ranks:], other)]
    else:
        layers = []
        for layer in range(sections):
            distance = lax.rem(layer - section_at + sections, sections)
            chosen = around[0][...]
            for step in range(1, sections):
                chosen = jnp.where(distance == step, around[step][...], chosen)
            layers.append(chosen)
        downs = [chosen[:ranks] for chosen in layers[1:]]
        lefts = [chosen[ranks:] for chosen in layers[:-1]]
    right = jnp.concatenate(downs + lefts, axis=0)
    right_ref[...] = right
    gram_ref[...] = dot_last(jnp.concatenate(lefts, axis=0), right)


def gram(around):
    sections = len(around)
    ranks = around[0].shape[0] // 2
    columns = around[0].shape[1]
    before = (sections - 1) * ranks
    return pl.pallas_call(
        functools.partial(gram_kernel, sections),
        in_specs=[in_vmem] * sections,
        out_specs=[in_vmem] * 2,
        out_shape=[
            jax.ShapeDtypeStruct((before, 2 * before), f32),
            jax.ShapeDtypeStruct((2 * before, columns), bf16),
        ],
        compiler_params=limited,
        name="gram",
    )(*around)


def chain_kernel(sections, slots, features, per_micro, bounds, counts, *refs):
    projections, grams = refs[:sections], refs[sections:-3]
    sq_ref, factor_ref, mixed_ref = refs[-3:]
    layers = sections
    replica_at = lax.axis_index("replica")
    section_at = lax.axis_index("section")
    tokens = sq_ref.shape[0]
    table = grams[0][...]
    for other in grams[1:]:
        table = table + other[...]
    ranks = projections[0].shape[1] // (3 * slots)
    parts = [[jnp.zeros((tokens, ranks), f32)] * 3 for _ in range(layers)]
    for distance, source in enumerate(projections):
        section = lax.rem(section_at + distance, sections)
        first = entry(bounds, replica_at, section)
        after = entry(bounds, replica_at, section + 1)
        for slot in range(slots):
            for which in range(3):
                block = which * slots + slot
                piece = source[:, block * ranks : (block + 1) * ranks]
                for layer in range(layers):
                    here = (first + slot == layer) & (layer < after)
                    parts[layer][which] = jnp.where(here, piece, parts[layer][which])
    scale_d = 1.0 / math.sqrt(features)
    scale_r = 1.0 / math.sqrt(ranks)

    def part(layer, which):
        return parts[layer][which]

    def up_down(i, layer):
        return table[i * ranks : (i + 1) * ranks, (layer - 1) * ranks : layer * ranks]

    square = sq_ref[:, 0:1]
    inverses, inners, actives, sigmoids, products = [], [], [], [], []
    on_up = [[part(l, 1) for l in range(layers - 1)]]
    for layer in range(layers):
        inverse = lax.rsqrt(jnp.maximum(square, 0.0) * (1.0 / features) + norm_eps)
        on_down = part(layer, 0)
        for i in range(layer):
            on_down = on_down + products[i][:, (layer - 1) * ranks : layer * ranks]
        inner = on_down * (inverse * scale_d)
        sigmoid = jax.nn.sigmoid(inner)
        active = (inner * sigmoid).astype(bf16).astype(f32)
        inverses.append(inverse)
        inners.append(inner)
        sigmoids.append(sigmoid)
        actives.append(active)
        if layer < layers - 1:
            now = on_up[-1]
            product = in_parts(
                lambda part: jnp.dot(active.astype(bf16), part, preferred_element_type=f32),
                table[layer * ranks : (layer + 1) * ranks],
                3,
            )
            products.append(scale_r * product)
            grown = [
                now[l] + products[layer][:, (layers - 1 + l) * ranks : (layers + l) * ranks]
                for l in range(layers - 1)
            ]
            square = square + scale_r * row_sum(active * (now[layer] + grown[layer]))
            on_up.append(grown)
    scaled = [None] * layers
    kappas = [None] * layers
    for layer in reversed(range(layers)):
        incoming = part(layer, 2)
        for k in range(layer + 1, layers):
            incoming = incoming + scale_d * dot_last(scaled[k], up_down(layer, k), exact)
            incoming = incoming - kappas[k] * on_up[k][layer]
        sigmoid, inner = sigmoids[layer], inners[layer]
        slope = sigmoid * (1.0 + inner * (1.0 - sigmoid))
        error = incoming * scale_r * slope
        scaled[layer] = error * inverses[layer]
        kappas[layer] = (
            inverses[layer] * inverses[layer] * (row_sum(error * inner) * (1.0 / features))
        )

    def owned(values):
        chosen = values[0]
        for layer in range(1, layers):
            chosen = jnp.where(section_at == layer, values[layer], chosen)
        return chosen

    own_error = owned(scaled)
    own_active = owned(actives)
    counted = counted_rows(counts, tokens, per_micro)
    later = jnp.zeros_like(square)
    for k in range(1, layers):
        later = later + jnp.where(k > section_at, kappas[k], 0.0)
    on_hidden = jnp.concatenate([own_error * scale_d, -scale_r * later * own_active], axis=1)
    on_cot = jnp.concatenate(
        [jnp.zeros_like(own_active), jnp.where(counted, own_active * scale_r, 0.0)], axis=1
    )
    factor_ref[...] = jnp.concatenate([on_hidden.T, on_cot.T], axis=1).astype(bf16)
    both = scale_d * scale_r
    for k in range(1, layers):
        cut = slice((k - 1) * ranks, k * ranks)
        across = dot_first(own_active.astype(bf16), scaled[k].astype(bf16)) * both
        mixed_ref[:ranks, cut] = jnp.zeros_like(across)
        mixed_ref[ranks:, cut] = jnp.where(k > section_at, across, 0.0)
    for i in range(layers - 1):
        cut = slice((layers - 1 + i) * ranks, (layers + i) * ranks)
        after = jnp.zeros_like(square)
        for k in range(i + 1, layers):
            after = after + jnp.where(k > section_at, kappas[k], 0.0)
        across = dot_first(own_error.astype(bf16), actives[i].astype(bf16)) * both
        mixed_ref[:ranks, cut] = jnp.where(i < section_at, across, 0.0)
        across = dot_first(own_active.astype(bf16), (after * actives[i]).astype(bf16))
        mixed_ref[ranks:, cut] = across * (-scale_r * scale_r)


def chain(bounds, counts, projections, grams, square, slots, features, per_micro):
    sections = len(projections)
    tokens, wide = projections[0].shape
    ranks = wide // (3 * slots)
    inputs = [*projections, *grams, square]
    kernel = functools.partial(chain_kernel, sections, slots, features, per_micro)
    return pl.pallas_call(
        kernel,
        in_specs=[in_vmem] * (2 + len(inputs)),
        out_specs=[in_vmem] * 2,
        out_shape=[
            jax.ShapeDtypeStruct((2 * ranks, 2 * tokens), bf16),
            jax.ShapeDtypeStruct((2 * ranks, 2 * (sections - 1) * ranks), f32),
        ],
        compiler_params=limited,
        name="chain",
    )(bounds, counts, *inputs)


def gradient_kernel(first, lead, factor_ref, h_ref, g_ref, out_ref):
    _, _, ranks, columns = out_ref.shape
    tokens = h_ref.shape[0]
    replica_at = lax.axis_index("replica")
    tensor_at = lax.axis_index("tensor")
    tensors = lax.axis_size("tensor")
    down = factor_ref[:ranks, :tokens]
    up = factor_ref[ranks:]
    for middle in range(2):
        for high in range(2):
            for which, (far, low) in enumerate(((lead, middle), (middle, lead))):
                hop = low + 2 * high
                owner = (replica_at ^ (first + 2 * far)) * tensors + (tensor_at ^ hop)
                cut = pl.ds(pl.multiple_of(owner * columns, columns), columns)
                if which == 0:
                    block = jnp.dot(down, h_ref[:, cut], preferred_element_type=f32)
                else:
                    stacked = jnp.concatenate([h_ref[:, cut], g_ref[:, cut]], axis=0)
                    block = jnp.dot(up, stacked, preferred_element_type=f32)
                out_ref[which, 2 * middle + high] = block.astype(bf16)


def gradient(factors, hidden, cot, first, lead, columns):
    tokens, features = hidden.shape
    rows = factors.shape[0]
    return pl.pallas_call(
        functools.partial(gradient_kernel, first, lead),
        in_specs=[in_vmem] * 3,
        out_specs=in_vmem,
        out_shape=jax.ShapeDtypeStruct((2, 4, rows // 2, columns), bf16),
        compiler_params=limited,
        cost_estimate=pl.CostEstimate(
            flops=rows * tokens * features,
            bytes_accessed=(tokens + rows // 2) * features,
            transcendentals=0,
        ),
        name="gradient",
    )(factors, hidden, cot)


def update_kernel(which, kept, near, one, two, last, mixed_ref, other_ref, right_ref, *refs):
    master_ref, moment_ref, second_ref, new_master, new_moment, new_second, share_ref = refs
    ranks = last.shape[0]
    rows = slice(which * ranks, (which + 1) * ranks)
    mixed = mixed_ref[rows] + other_ref[rows].astype(f32)
    right = right_ref[...]
    own = in_parts(lambda part: jnp.dot(part, right, preferred_element_type=f32), mixed, 3)
    for block in (kept[which, 0], near[which, 0], one[0], two[0], last[...]):
        own = own + block.astype(f32)
    moment = beta_one * moment_ref[0] + (1.0 - beta_one) * own
    second = beta_two * second_ref[0] + (1.0 - beta_two) * own * own
    master = master_ref[0]
    master = master - learn_rate * (
        moment / first_fix / (jnp.sqrt(second / second_fix) + adam_eps) + decay_rate * master
    )
    share_ref[0] = master.astype(bf16)
    new_master[0] = master
    new_moment[0] = moment
    new_second[0] = second


def update(which, parts, right, state):
    inputs = [*parts, right, *state]
    return pl.pallas_call(
        functools.partial(update_kernel, which),
        in_specs=[in_vmem] * len(inputs),
        out_specs=[in_vmem] * 4,
        out_shape=[jax.ShapeDtypeStruct(array.shape, f32) for array in state]
        + [jax.ShapeDtypeStruct(state[0].shape, bf16)],
        compiler_params=limited,
        name="update",
    )(*inputs)


def place_kernel(layout, start, bounds, *refs):
    sources = refs[: len(layout)]
    outs = refs[-4:-2]
    zeros, sem = refs[-2:]
    slots, ranks, features = outs[0].shape
    columns = zeros.shape[1]
    tensors = lax.axis_size("tensor")
    replica_at = lax.axis_index("replica")
    section_at = lax.axis_index("section")
    tensor_at = lax.axis_index("tensor")
    first = entry(bounds, replica_at, section_at)
    after = entry(bounds, replica_at, section_at + 1)
    zeros[...] = jnp.zeros_like(zeros)

    def fill(slot, distance, go):
        for blocks, source in zip(layout, sources):
            for i, (window, which, order, hop) in enumerate(blocks):
                if window != distance:
                    continue
                owner = (replica_at ^ order) * tensors + (tensor_at ^ hop)
                cut = pl.ds(pl.multiple_of(owner * columns, columns), columns)
                go(pltpu.make_async_copy(source.at[i], outs[which].at[slot, :, cut], sem))

    def clear(slot, go):
        for out in outs:
            for block in range(features // columns):
                cut = pl.ds(block * columns, columns)
                go(pltpu.make_async_copy(zeros, out.at[slot, :, cut], sem))

    for act in (lambda copy: copy.start(), lambda copy: copy.wait()):
        for slot in range(slots):
            layer = first + slot
            present = layer < after
            for distance in range(2):

                @pl.when(present & (layer - section_at == distance))
                def _():
                    fill(slot, distance, act)

            if start:

                @pl.when(jnp.logical_not(present))
                def _():
                    clear(slot, act)


def place(bounds, pieces, before, slots, ranks, features):
    layout = [blocks for blocks, _ in pieces]
    arrays = [array for _, array in pieces]
    columns = arrays[0].shape[-1]
    return pl.pallas_call(
        functools.partial(place_kernel, layout, not before),
        in_specs=[in_vmem] * (1 + len(arrays)) + [in_hbm] * len(before),
        out_specs=[in_hbm] * 2,
        out_shape=[jax.ShapeDtypeStruct((slots, ranks, features), bf16)] * 2,
        scratch_shapes=[pltpu.VMEM((ranks, columns), bf16), pltpu.SemaphoreType.DMA],
        input_output_aliases={1 + len(arrays) + i: i for i in range(len(before))},
        compiler_params=limited,
        cost_estimate=pl.CostEstimate(
            flops=0,
            bytes_accessed=4 * sum(array.size for array in arrays),
            transcendentals=0,
        ),
        name="place",
    )(bounds, *arrays, *before)


def swapped(block, axis, distance):
    route = [(i, i ^ distance) for i in range(lax.axis_size(axis))]
    return lax.ppermute(block, axis, route)


def swaps(block, axis):
    return [swapped(block, axis, k) for k in range(1, lax.axis_size(axis))]


def from_next(block, distance=1):
    size = lax.axis_size("section")
    route = [((i + distance) % size, i) for i in range(size)]
    return lax.ppermute(block, "section", route)


def following_layer(block):
    size = lax.axis_size("section")
    return lax.ppermute(block, "section", [(i + 1, i) for i in range(size - 1)])


def summed(*blocks):
    total = blocks[0].astype(f32)
    for block in blocks[1:]:
        total = total + block.astype(f32)
    return total.astype(bf16)


def reduced(factors, hidden, cot, columns, mixed):
    def halves(lead):
        sent = gradient(factors, hidden, cot, 1, lead, columns)
        return swapped(sent, "replica", 1), gradient(factors, hidden, cot, 0, lead, columns)

    def part(which, cut, *steps):
        return summed(kept[which, cut], near[which, cut], *steps)

    def added(axis, distance):
        return mixed + swapped(mixed.astype(bf16), axis, distance).astype(f32)

    near, kept = halves(1)
    whole, low = slice(0, 4), slice(2, 4)
    down_one = swapped(part(0, whole), "replica", 2)
    up_one = swapped(part(1, whole), "tensor", 1)
    near, kept = halves(0)
    mixed = added("replica", 1)
    mixed = added("tensor", 2)
    down_one, up_one, mixed = lax.optimization_barrier((down_one, up_one, mixed))
    down_two = swapped(part(0, low, down_one[2:]), "tensor", 1)
    up_two = swapped(part(1, low, up_one[2:]), "replica", 2)
    down_last = swapped(part(0, 1, down_one[1], down_two[1]), "tensor", 2)
    kept, near = lax.optimization_barrier((kept, near))
    up_last = swapped(part(1, 1, up_one[1], up_two[1]), "tensor", 2)
    mixed = added("tensor", 1)
    other = swapped(mixed.astype(bf16), "replica", 2)
    down = (kept, near, down_one, down_two, down_last, mixed, other)
    return down, (kept, near, up_one, up_two, up_last, mixed, other)


def crossed(piece, axis, distance):
    blocks, array = piece
    blocks = [
        (window, which, order ^ distance, hop)
        if axis == "replica"
        else (window, which, order, hop ^ distance)
        for window, which, order, hop in blocks
    ]
    return blocks, swapped(array, axis, distance)


def fetched(piece):
    blocks, array = piece
    return [(1, *block[1:]) for block in blocks], following_layer(array)


def picked(piece, at):
    return piece[0][at : at + 1], piece[1][at : at + 1]


def joined(*pieces):
    blocks = [block for piece in pieces for block in piece[0]]
    return blocks, jnp.concatenate([array for _, array in pieces])


def spread(down, up, bounds, slots, features):
    ranks = down.shape[1]
    down_own, up_own = ([(0, 0, 0, 0)], down), ([(0, 1, 0, 0)], up)
    down_one = crossed(down_own, "tensor", 2)
    up_one = crossed(up_own, "tensor", 2)
    downs, ups = joined(down_own, down_one), joined(up_own, up_one)
    owns = lax.optimization_barrier((down, up))
    own = joined((down_own[0], owns[0]), (up_own[0], owns[1]))
    next_own = fetched(own)
    *ones, next_array = lax.optimization_barrier((down_one[1], up_one[1], next_own[1]))
    one = joined((down_one[0], ones[0]), (up_one[0], ones[1]))
    next_own = (next_own[0], next_array)
    down_two = crossed(downs, "tensor", 1)
    up_two = crossed(ups, "replica", 2)
    next_one = fetched(one)
    two = joined(down_two, up_two)
    down_three = crossed(joined(downs, down_two), "replica", 2)
    up_three = crossed(joined(ups, up_two), "tensor", 1)
    next_two = fetched(two)
    next_end = fetched(joined(picked(down_three, 3), picked(up_three, 3)))
    _, _, next_array = lax.optimization_barrier((down_three[1], up_three[1], next_two[1]))
    next_two = (next_two[0], next_array)
    down_end = joined(picked(next_own, 0), picked(next_one, 0), picked(next_two, 0))
    up_end = joined(picked(next_own, 1), picked(next_one, 1), picked(next_two, 2))
    end = joined(crossed(down_end, "replica", 2), crossed(up_end, "tensor", 1), next_end)
    near = joined(own, one, two)
    far = joined(down_three, up_three)
    next_near = joined(next_own, next_one, next_two)
    near_core, far_core, next_core, end_core = (
        crossed(piece, "replica", 1) for piece in (near, far, next_near, end)
    )
    placed = place(
        bounds, [near, near_core, far, far_core, next_near, next_core], [], slots, ranks, features
    )
    placed = place(bounds, [end, end_core], placed, slots, ranks, features)
    return placed


def on_device(
    inputs,
    cotangent,
    micro_counts,
    bounds,
    holder_down,
    holder_up,
    master_down,
    master_up,
    moment_down,
    moment_up,
    second_down,
    second_up,
):
    sections = lax.axis_size("section")
    replicas = lax.axis_size("replica")
    tensors = lax.axis_size("tensor")
    assert replicas == 4 and tensors == 4
    _, micros, per_micro, features = inputs.shape
    micro_counts = micro_counts[None]
    slots = holder_down.shape[2]
    hidden = inputs.reshape(micros * per_micro, features)
    cot = cotangent.reshape(micros * per_micro, features)

    owned = jnp.concatenate([master_down[0], master_up[0]], axis=0).astype(bf16)
    if sections == 2:
        first = lax.axis_index("section") == 0
        needed = jnp.where(first, master_up[0], master_down[0]).astype(bf16)
    else:
        needed = owned
    around = [from_next(needed, d) for d in range(1, sections)]
    by_down, square, hidden = project_down(hidden, holder_down[0, 0])
    around, by_down = lax.optimization_barrier((around, by_down))
    table, right = gram([owned, *around])
    table, hidden = lax.optimization_barrier((table, hidden))
    projected = project_up(micro_counts, by_down, hidden, cot, holder_up[0, 0], per_micro)
    table = table + sum(swaps(table, "replica"))
    projections = [projected] + [from_next(projected, d) for d in range(1, sections)]
    table = table + swapped(table, "tensor", 1)
    tables = [table, swapped(table, "tensor", 2)]
    factors, mixed = chain(
        bounds, micro_counts, projections, tables, square, slots, features, per_micro
    )

    down_parts, up_parts = reduced(factors, hidden, cot, master_down.shape[2], mixed)
    down = update(0, down_parts, right, [master_down, moment_down, second_down])
    up = update(1, up_parts, right, [master_up, moment_up, second_up])
    placed = spread(down[3], up[3], bounds, slots, features)
    return (
        placed[0][None, None],
        placed[1][None, None],
        down[0],
        up[0],
        down[1],
        up[1],
        down[2],
        up[2],
    )


def solution(mesh):
    held = P("replica", "section", None, None, None)
    owned = P("section", None, ("replica", "tensor"))
    tokens = P("replica", None, "tensor", None)
    return jax.shard_map(
        on_device,
        mesh=mesh,
        in_specs=(tokens, tokens, P(), P(), held, held) + (owned,) * 6,
        out_specs=(held, held) + (owned,) * 6,
        check_vma=False,
    )
```

```python
import functools
import math

import jax
import jax.numpy as jnp
from jax import lax
from jax.experimental import pallas as pl
from jax.experimental.pallas import tpu as pltpu
from jax.sharding import PartitionSpec as P

norm_eps = 1e-06
learn_rate = 0.01
beta_one = 0.9
beta_two = 0.95
decay_rate = 0.1
adam_eps = 1e-08
first_fix = 0.9999734386011124
second_fix = 0.9940794707796659

f32 = jnp.float32
bf16 = jnp.bfloat16
exact = lax.Precision.HIGHEST
in_vmem = pl.BlockSpec(memory_space=pltpu.VMEM)
in_hbm = pl.BlockSpec(memory_space=pltpu.HBM)
limited = pltpu.CompilerParams(vmem_limit_bytes=16 * 1024 * 1024)


def entry(ref, row, column):
    values = ref[...].astype(f32)
    rows = lax.broadcasted_iota(jnp.int32, values.shape, 0)
    columns = lax.broadcasted_iota(jnp.int32, values.shape, 1)
    return jnp.sum(jnp.where((rows == row) & (columns == column), values, 0.0)).astype(jnp.int32)


def counted_rows(counts, tokens, per_micro):
    rows = lax.broadcasted_iota(jnp.int32, (tokens, 1), 0)
    return rows < entry(counts, 0, lax.axis_index("replica")) * per_micro


def dot_last(x, y, precision=None):
    return lax.dot_general(
        x, y, (((1,), (1,)), ((), ())), preferred_element_type=f32, precision=precision
    )


def dot_first(x, y, precision=None):
    return lax.dot_general(
        x, y, (((0,), (0,)), ((), ())), preferred_element_type=f32, precision=precision
    )


def in_parts(product, wide, parts):
    total = None
    for _ in range(parts):
        piece = wide.astype(bf16)
        wide = wide - piece.astype(f32)
        term = product(piece)
        total = term if total is None else total + term
    return total


def row_sum(x):
    return jnp.sum(x, axis=-1, keepdims=True)


def project_down_kernel(steps, h_in, down_in, out_ref, sq_ref, h_ref, down_ref, sems):
    slots, ranks, features = down_in.shape
    tokens = h_ref.shape[0]
    width = features // steps
    copies = []
    for step in range(steps):
        cut = pl.ds(step * width, width)
        moves = [(h_in.at[:, cut], h_ref.at[:, cut])]
        for slot in range(slots):
            rows = pl.ds(slot * ranks, ranks)
            moves.append((down_in.at[slot, :, cut], down_ref.at[rows, cut]))
        copies.append(
            [
                pltpu.make_async_copy(source, target, sems.at[step, i])
                for i, (source, target) in enumerate(moves)
            ]
        )
        for copy in copies[-1]:
            copy.start()
    total = jnp.zeros((tokens, slots * ranks), f32)
    square = jnp.zeros((tokens, 128), f32)
    for step in range(steps):
        for copy in copies[step]:
            copy.wait()
        cut = pl.ds(step * width, width)
        h = h_ref[:, cut]
        total = total + dot_last(h, down_ref[:, cut])
        wide = h.astype(f32)
        wide = wide * wide
        for lane in range(0, width, 128):
            square = square + wide[:, lane : lane + 128]
    sq_ref[...] = jnp.broadcast_to(row_sum(square), square.shape)
    out_ref[...] = total


def project_down(hidden, downs):
    tokens, features = hidden.shape
    slots, ranks, _ = downs.shape
    steps = 8
    sources = [pltpu.with_memory_space_constraint(x, pltpu.HBM) for x in (hidden, downs)]
    return pl.pallas_call(
        functools.partial(project_down_kernel, steps),
        in_specs=[in_hbm] * 2,
        out_specs=[in_vmem] * 3,
        out_shape=[
            jax.ShapeDtypeStruct((tokens, slots * ranks), f32),
            jax.ShapeDtypeStruct((tokens, 128), f32),
            jax.ShapeDtypeStruct((tokens, features), bf16),
        ],
        scratch_shapes=[
            pltpu.VMEM((slots * ranks, features), bf16),
            pltpu.SemaphoreType.DMA((steps, 1 + slots)),
        ],
        compiler_params=limited,
        cost_estimate=pl.CostEstimate(
            flops=2 * tokens * slots * ranks * features,
            bytes_accessed=2 * (tokens + slots * ranks) * features,
            transcendentals=0,
        ),
        name="project_down",
    )(*sources)


def project_up_kernel(per_micro, counts, by_down, h_ref, g_ref, up_ref, out_ref):
    tokens, columns = by_down.shape
    ups = up_ref[...].reshape(columns, up_ref.shape[2])
    out_ref[:, :columns] = by_down[...]
    out_ref[:, columns : 2 * columns] = dot_last(h_ref[...], ups)
    by_cot = dot_last(g_ref[...], ups)
    out_ref[:, 2 * columns :] = jnp.where(counted_rows(counts, tokens, per_micro), by_cot, 0.0)


def project_up(counts, by_down, hidden, cot, ups, per_micro):
    tokens, features = hidden.shape
    columns = by_down.shape[1]
    return pl.pallas_call(
        functools.partial(project_up_kernel, per_micro),
        in_specs=[in_vmem] * 5,
        out_specs=in_vmem,
        out_shape=jax.ShapeDtypeStruct((tokens, 3 * columns), f32),
        compiler_params=limited,
        cost_estimate=pl.CostEstimate(
            flops=4 * tokens * columns * features,
            bytes_accessed=2 * (2 * tokens + columns) * features,
            transcendentals=0,
        ),
        name="project_up",
    )(counts, by_down, hidden, cot, ups)


def gram_kernel(sections, *refs):
    around = refs[:sections]
    gram_ref, right_ref = refs[sections:]
    section_at = lax.axis_index("section")
    ranks = around[0].shape[0] // 2
    if sections == 2:
        own, other = around[0][...], around[1][...]
        downs = [jnp.where(section_at == 0, other, own[:ranks])]
        lefts = [jnp.where(section_at == 0, own[ranks:], other)]
    else:
        layers = []
        for layer in range(sections):
            distance = lax.rem(layer - section_at + sections, sections)
            chosen = around[0][...]
            for step in range(1, sections):
                chosen = jnp.where(distance == step, around[step][...], chosen)
            layers.append(chosen)
        downs = [chosen[:ranks] for chosen in layers[1:]]
        lefts = [chosen[ranks:] for chosen in layers[:-1]]
    right = jnp.concatenate(downs + lefts, axis=0)
    right_ref[...] = right
    gram_ref[...] = dot_last(jnp.concatenate(lefts, axis=0), right)


def gram(around):
    sections = len(around)
    ranks = around[0].shape[0] // 2
    columns = around[0].shape[1]
    before = (sections - 1) * ranks
    return pl.pallas_call(
        functools.partial(gram_kernel, sections),
        in_specs=[in_vmem] * sections,
        out_specs=[in_vmem] * 2,
        out_shape=[
            jax.ShapeDtypeStruct((before, 2 * before), f32),
            jax.ShapeDtypeStruct((2 * before, columns), bf16),
        ],
        compiler_params=limited,
        name="gram",
    )(*around)


def chain_kernel(sections, slots, features, per_micro, bounds, counts, *refs):
    projections, grams = refs[:sections], refs[sections:-3]
    sq_ref, factor_ref, mixed_ref = refs[-3:]
    layers = sections
    replica_at = lax.axis_index("replica")
    section_at = lax.axis_index("section")
    tokens = sq_ref.shape[0]
    table = grams[0][...]
    for other in grams[1:]:
        table = table + other[...]
    ranks = projections[0].shape[1] // (3 * slots)
    parts = [[jnp.zeros((tokens, ranks), f32)] * 3 for _ in range(layers)]
    for distance, source in enumerate(projections):
        section = lax.rem(section_at + distance, sections)
        first = entry(bounds, replica_at, section)
        after = entry(bounds, replica_at, section + 1)
        for slot in range(slots):
            for which in range(3):
                block = which * slots + slot
                piece = source[:, block * ranks : (block + 1) * ranks]
                for layer in range(layers):
                    here = (first + slot == layer) & (layer < after)
                    parts[layer][which] = jnp.where(here, piece, parts[layer][which])
    scale_d = 1.0 / math.sqrt(features)
    scale_r = 1.0 / math.sqrt(ranks)

    def part(layer, which):
        return parts[layer][which]

    def up_down(i, layer):
        return table[i * ranks : (i + 1) * ranks, (layer - 1) * ranks : layer * ranks]

    square = sq_ref[:, 0:1]
    inverses, inners, actives, sigmoids, products = [], [], [], [], []
    on_up = [[part(l, 1) for l in range(layers - 1)]]
    for layer in range(layers):
        inverse = lax.rsqrt(jnp.maximum(square, 0.0) * (1.0 / features) + norm_eps)
        on_down = part(layer, 0)
        for i in range(layer):
            on_down = on_down + products[i][:, (layer - 1) * ranks : layer * ranks]
        inner = on_down * (inverse * scale_d)
        sigmoid = jax.nn.sigmoid(inner)
        active = (inner * sigmoid).astype(bf16).astype(f32)
        inverses.append(inverse)
        inners.append(inner)
        sigmoids.append(sigmoid)
        actives.append(active)
        if layer < layers - 1:
            now = on_up[-1]
            product = in_parts(
                lambda part: jnp.dot(active.astype(bf16), part, preferred_element_type=f32),
                table[layer * ranks : (layer + 1) * ranks],
                3,
            )
            products.append(scale_r * product)
            grown = [
                now[l] + products[layer][:, (layers - 1 + l) * ranks : (layers + l) * ranks]
                for l in range(layers - 1)
            ]
            square = square + scale_r * row_sum(active * (now[layer] + grown[layer]))
            on_up.append(grown)
    scaled = [None] * layers
    kappas = [None] * layers
    for layer in reversed(range(layers)):
        incoming = part(layer, 2)
        for k in range(layer + 1, layers):
            incoming = incoming + scale_d * dot_last(scaled[k], up_down(layer, k), exact)
            incoming = incoming - kappas[k] * on_up[k][layer]
        sigmoid, inner = sigmoids[layer], inners[layer]
        slope = sigmoid * (1.0 + inner * (1.0 - sigmoid))
        error = incoming * scale_r * slope
        scaled[layer] = error * inverses[layer]
        kappas[layer] = (
            inverses[layer] * inverses[layer] * (row_sum(error * inner) * (1.0 / features))
        )

    def owned(values):
        chosen = values[0]
        for layer in range(1, layers):
            chosen = jnp.where(section_at == layer, values[layer], chosen)
        return chosen

    own_error = owned(scaled)
    own_active = owned(actives)
    counted = counted_rows(counts, tokens, per_micro)
    later = jnp.zeros_like(square)
    for k in range(1, layers):
        later = later + jnp.where(k > section_at, kappas[k], 0.0)
    on_hidden = jnp.concatenate([own_error * scale_d, -scale_r * later * own_active], axis=1)
    on_cot = jnp.concatenate(
        [jnp.zeros_like(own_active), jnp.where(counted, own_active * scale_r, 0.0)], axis=1
    )
    factor_ref[...] = jnp.concatenate([on_hidden.T, on_cot.T], axis=1).astype(bf16)
    both = scale_d * scale_r
    for k in range(1, layers):
        cut = slice((k - 1) * ranks, k * ranks)
        across = dot_first(own_active.astype(bf16), scaled[k].astype(bf16)) * both
        mixed_ref[:ranks, cut] = jnp.zeros_like(across)
        mixed_ref[ranks:, cut] = jnp.where(k > section_at, across, 0.0)
    for i in range(layers - 1):
        cut = slice((layers - 1 + i) * ranks, (layers + i) * ranks)
        after = jnp.zeros_like(square)
        for k in range(i + 1, layers):
            after = after + jnp.where(k > section_at, kappas[k], 0.0)
        across = dot_first(own_error.astype(bf16), actives[i].astype(bf16)) * both
        mixed_ref[:ranks, cut] = jnp.where(i < section_at, across, 0.0)
        across = dot_first(own_active.astype(bf16), (after * actives[i]).astype(bf16))
        mixed_ref[ranks:, cut] = across * (-scale_r * scale_r)


def chain(bounds, counts, projections, grams, square, slots, features, per_micro):
    sections = len(projections)
    tokens, wide = projections[0].shape
    ranks = wide // (3 * slots)
    inputs = [*projections, *grams, square]
    kernel = functools.partial(chain_kernel, sections, slots, features, per_micro)
    return pl.pallas_call(
        kernel,
        in_specs=[in_vmem] * (2 + len(inputs)),
        out_specs=[in_vmem] * 2,
        out_shape=[
            jax.ShapeDtypeStruct((2 * ranks, 2 * tokens), bf16),
            jax.ShapeDtypeStruct((2 * ranks, 2 * (sections - 1) * ranks), f32),
        ],
        compiler_params=limited,
        name="chain",
    )(bounds, counts, *inputs)


def gradient_kernel(first, lead, factor_ref, h_ref, g_ref, out_ref):
    _, _, ranks, columns = out_ref.shape
    tokens = h_ref.shape[0]
    replica_at = lax.axis_index("replica")
    tensor_at = lax.axis_index("tensor")
    tensors = lax.axis_size("tensor")
    down = factor_ref[:ranks, :tokens]
    up = factor_ref[ranks:]
    for middle in range(2):
        for high in range(2):
            for which, (far, low) in enumerate(((lead, middle), (middle, lead))):
                hop = low + 2 * high
                owner = (replica_at ^ (first + 2 * far)) * tensors + (tensor_at ^ hop)
                cut = pl.ds(pl.multiple_of(owner * columns, columns), columns)
                if which == 0:
                    block = jnp.dot(down, h_ref[:, cut], preferred_element_type=f32)
                else:
                    stacked = jnp.concatenate([h_ref[:, cut], g_ref[:, cut]], axis=0)
                    block = jnp.dot(up, stacked, preferred_element_type=f32)
                out_ref[which, 2 * middle + high] = block.astype(bf16)


def gradient(factors, hidden, cot, first, lead, columns):
    tokens, features = hidden.shape
    rows = factors.shape[0]
    return pl.pallas_call(
        functools.partial(gradient_kernel, first, lead),
        in_specs=[in_vmem] * 3,
        out_specs=in_vmem,
        out_shape=jax.ShapeDtypeStruct((2, 4, rows // 2, columns), bf16),
        compiler_params=limited,
        cost_estimate=pl.CostEstimate(
            flops=rows * tokens * features,
            bytes_accessed=(tokens + rows // 2) * features,
            transcendentals=0,
        ),
        name="gradient",
    )(factors, hidden, cot)


def update_kernel(which, kept, near, one, two, last, mixed_ref, other_ref, right_ref, *refs):
    master_ref, moment_ref, second_ref, new_master, new_moment, new_second, share_ref = refs
    ranks = last.shape[0]
    rows = slice(which * ranks, (which + 1) * ranks)
    mixed = mixed_ref[rows] + other_ref[rows].astype(f32)
    right = right_ref[...]
    own = in_parts(lambda part: jnp.dot(part, right, preferred_element_type=f32), mixed, 3)
    for block in (kept[which, 0], near[which, 0], one[0], two[0], last[...]):
        own = own + block.astype(f32)
    moment = beta_one * moment_ref[0] + (1.0 - beta_one) * own
    second = beta_two * second_ref[0] + (1.0 - beta_two) * own * own
    master = master_ref[0]
    master = master - learn_rate * (
        moment / first_fix / (jnp.sqrt(second / second_fix) + adam_eps) + decay_rate * master
    )
    share_ref[0] = master.astype(bf16)
    new_master[0] = master
    new_moment[0] = moment
    new_second[0] = second


def update(which, parts, right, state):
    inputs = [*parts, right, *state]
    return pl.pallas_call(
        functools.partial(update_kernel, which),
        in_specs=[in_vmem] * len(inputs),
        out_specs=[in_vmem] * 4,
        out_shape=[jax.ShapeDtypeStruct(array.shape, f32) for array in state]
        + [jax.ShapeDtypeStruct(state[0].shape, bf16)],
        compiler_params=limited,
        name="update",
    )(*inputs)


def place_kernel(layout, start, bounds, *refs):
    sources = refs[: len(layout)]
    outs = refs[-4:-2]
    zeros, sem = refs[-2:]
    slots, ranks, features = outs[0].shape
    columns = zeros.shape[1]
    tensors = lax.axis_size("tensor")
    replica_at = lax.axis_index("replica")
    section_at = lax.axis_index("section")
    tensor_at = lax.axis_index("tensor")
    first = entry(bounds, replica_at, section_at)
    after = entry(bounds, replica_at, section_at + 1)
    zeros[...] = jnp.zeros_like(zeros)

    def fill(slot, distance, go):
        for blocks, source in zip(layout, sources):
            for i, (window, which, order, hop) in enumerate(blocks):
                if window != distance:
                    continue
                owner = (replica_at ^ order) * tensors + (tensor_at ^ hop)
                cut = pl.ds(pl.multiple_of(owner * columns, columns), columns)
                go(pltpu.make_async_copy(source.at[i], outs[which].at[slot, :, cut], sem))

    def clear(slot, go):
        for out in outs:
            for block in range(features // columns):
                cut = pl.ds(block * columns, columns)
                go(pltpu.make_async_copy(zeros, out.at[slot, :, cut], sem))

    for act in (lambda copy: copy.start(), lambda copy: copy.wait()):
        for slot in range(slots):
            layer = first + slot
            present = layer < after
            for distance in range(2):

                @pl.when(present & (layer - section_at == distance))
                def _():
                    fill(slot, distance, act)

            if start:

                @pl.when(jnp.logical_not(present))
                def _():
                    clear(slot, act)


def place(bounds, pieces, before, slots, ranks, features):
    layout = [blocks for blocks, _ in pieces]
    arrays = [array for _, array in pieces]
    columns = arrays[0].shape[-1]
    return pl.pallas_call(
        functools.partial(place_kernel, layout, not before),
        in_specs=[in_vmem] * (1 + len(arrays)) + [in_hbm] * len(before),
        out_specs=[in_hbm] * 2,
        out_shape=[jax.ShapeDtypeStruct((slots, ranks, features), bf16)] * 2,
        scratch_shapes=[pltpu.VMEM((ranks, columns), bf16), pltpu.SemaphoreType.DMA],
        input_output_aliases={1 + len(arrays) + i: i for i in range(len(before))},
        compiler_params=limited,
        cost_estimate=pl.CostEstimate(
            flops=0,
            bytes_accessed=4 * sum(array.size for array in arrays),
            transcendentals=0,
        ),
        name="place",
    )(bounds, *arrays, *before)


def swapped(block, axis, distance):
    route = [(i, i ^ distance) for i in range(lax.axis_size(axis))]
    return lax.ppermute(block, axis, route)


def swaps(block, axis):
    return [swapped(block, axis, k) for k in range(1, lax.axis_size(axis))]


def from_next(block, distance=1):
    size = lax.axis_size("section")
    route = [((i + distance) % size, i) for i in range(size)]
    return lax.ppermute(block, "section", route)


def summed(*blocks):
    total = blocks[0].astype(f32)
    for block in blocks[1:]:
        total = total + block.astype(f32)
    return total.astype(bf16)


def reduced(factors, hidden, cot, columns, mixed):
    def halves(lead):
        sent = gradient(factors, hidden, cot, 1, lead, columns)
        return swapped(sent, "replica", 1), gradient(factors, hidden, cot, 0, lead, columns)

    def part(which, cut, *steps):
        return summed(kept[which, cut], near[which, cut], *steps)

    def added(axis, distance):
        return mixed + swapped(mixed.astype(bf16), axis, distance).astype(f32)

    near, kept = halves(1)
    whole, low = slice(0, 4), slice(2, 4)
    down_one = swapped(part(0, whole), "replica", 2)
    up_one = swapped(part(1, whole), "tensor", 1)
    near, kept = halves(0)
    mixed = added("replica", 1)
    mixed = added("tensor", 2)
    down_one, up_one, mixed = lax.optimization_barrier((down_one, up_one, mixed))
    down_two = swapped(part(0, low, down_one[2:]), "tensor", 1)
    up_two = swapped(part(1, low, up_one[2:]), "replica", 2)
    down_last = swapped(part(0, 1, down_one[1], down_two[1]), "tensor", 2)
    kept, near = lax.optimization_barrier((kept, near))
    up_last = swapped(part(1, 1, up_one[1], up_two[1]), "tensor", 2)
    mixed = added("tensor", 1)
    other = swapped(mixed.astype(bf16), "replica", 2)
    down = (kept, near, down_one, down_two, down_last, mixed, other)
    return down, (kept, near, up_one, up_two, up_last, mixed, other)


def crossed(piece, axis, distance):
    blocks, array = piece
    blocks = [
        (window, which, order ^ distance, hop)
        if axis == "replica"
        else (window, which, order, hop ^ distance)
        for window, which, order, hop in blocks
    ]
    return blocks, swapped(array, axis, distance)


def fetched(piece):
    blocks, array = piece
    return [(1, *block[1:]) for block in blocks], from_next(array)


def picked(piece, at):
    return piece[0][at : at + 1], piece[1][at : at + 1]


def joined(*pieces):
    blocks = [block for piece in pieces for block in piece[0]]
    return blocks, jnp.concatenate([array for _, array in pieces])


def spread(down, up, bounds, slots, features):
    ranks = down.shape[1]
    down_own, up_own = ([(0, 0, 0, 0)], down), ([(0, 1, 0, 0)], up)
    down_one = crossed(down_own, "tensor", 2)
    up_one = crossed(up_own, "tensor", 2)
    downs, ups = joined(down_own, down_one), joined(up_own, up_one)
    owns = lax.optimization_barrier((down, up))
    own = joined((down_own[0], owns[0]), (up_own[0], owns[1]))
    next_own = fetched(own)
    *ones, next_array = lax.optimization_barrier((down_one[1], up_one[1], next_own[1]))
    one = joined((down_one[0], ones[0]), (up_one[0], ones[1]))
    next_own = (next_own[0], next_array)
    down_two = crossed(downs, "tensor", 1)
    up_two = crossed(ups, "replica", 2)
    next_one = fetched(one)
    two = joined(down_two, up_two)
    down_three = crossed(joined(downs, down_two), "replica", 2)
    up_three = crossed(joined(ups, up_two), "tensor", 1)
    next_two = fetched(two)
    next_end = fetched(joined(picked(down_three, 3), picked(up_three, 3)))
    _, _, next_array = lax.optimization_barrier((down_three[1], up_three[1], next_two[1]))
    next_two = (next_two[0], next_array)
    down_end = joined(picked(next_own, 0), picked(next_one, 0), picked(next_two, 0))
    up_end = joined(picked(next_own, 1), picked(next_one, 1), picked(next_two, 2))
    end = joined(crossed(down_end, "replica", 2), crossed(up_end, "tensor", 1), next_end)
    near = joined(own, one, two)
    far = joined(down_three, up_three)
    next_near = joined(next_own, next_one, next_two)
    near_core, far_core, next_core, end_core = (
        crossed(piece, "replica", 1) for piece in (near, far, next_near, end)
    )
    placed = place(
        bounds, [near, near_core, far, far_core, next_near, next_core], [], slots, ranks, features
    )
    placed = place(bounds, [end, end_core], placed, slots, ranks, features)
    return placed


def on_device(
    inputs,
    cotangent,
    micro_counts,
    bounds,
    holder_down,
    holder_up,
    master_down,
    master_up,
    moment_down,
    moment_up,
    second_down,
    second_up,
):
    sections = lax.axis_size("section")
    replicas = lax.axis_size("replica")
    tensors = lax.axis_size("tensor")
    assert replicas == 4 and tensors == 4
    _, micros, per_micro, features = inputs.shape
    micro_counts = micro_counts[None]
    slots = holder_down.shape[2]
    hidden = inputs.reshape(micros * per_micro, features)
    cot = cotangent.reshape(micros * per_micro, features)

    owned = jnp.concatenate([master_down[0], master_up[0]], axis=0).astype(bf16)
    if sections == 2:
        first = lax.axis_index("section") == 0
        needed = jnp.where(first, master_up[0], master_down[0]).astype(bf16)
    else:
        needed = owned
    around = [from_next(needed, d) for d in range(1, sections)]
    by_down, square, hidden = project_down(hidden, holder_down[0, 0])
    around, by_down = lax.optimization_barrier((around, by_down))
    table, right = gram([owned, *around])
    table, hidden = lax.optimization_barrier((table, hidden))
    projected = project_up(micro_counts, by_down, hidden, cot, holder_up[0, 0], per_micro)
    table = table + sum(swaps(table, "replica"))
    projections = [projected] + [from_next(projected, d) for d in range(1, sections)]
    table = table + swapped(table, "tensor", 1)
    tables = [table, swapped(table, "tensor", 2)]
    factors, mixed = chain(
        bounds, micro_counts, projections, tables, square, slots, features, per_micro
    )

    down_parts, up_parts = reduced(factors, hidden, cot, master_down.shape[2], mixed)
    down = update(0, down_parts, right, [master_down, moment_down, second_down])
    up = update(1, up_parts, right, [master_up, moment_up, second_up])
    placed = spread(down[3], up[3], bounds, slots, features)
    return (
        placed[0][None, None],
        placed[1][None, None],
        down[0],
        up[0],
        down[1],
        up[1],
        down[2],
        up[2],
    )


def solution(mesh):
    held = P("replica", "section", None, None, None)
    owned = P("section", None, ("replica", "tensor"))
    tokens = P("replica", None, "tensor", None)
    return jax.shard_map(
        on_device,
        mesh=mesh,
        in_specs=(tokens, tokens, P(), P(), held, held) + (owned,) * 6,
        out_specs=(held, held) + (owned,) * 6,
        check_vma=False,
    )
```

```python
import functools
import math

import jax
import jax.numpy as jnp
from jax import lax
from jax.experimental import pallas as pl
from jax.experimental.pallas import tpu as pltpu
from jax.sharding import PartitionSpec as P

norm_eps = 1e-06
learn_rate = 0.01
beta_one = 0.9
beta_two = 0.95
decay_rate = 0.1
adam_eps = 1e-08
first_fix = 0.9999734386011124
second_fix = 0.9940794707796659

f32 = jnp.float32
bf16 = jnp.bfloat16
exact = lax.Precision.HIGHEST
in_vmem = pl.BlockSpec(memory_space=pltpu.VMEM)
in_hbm = pl.BlockSpec(memory_space=pltpu.HBM)
limited = pltpu.CompilerParams(vmem_limit_bytes=16 * 1024 * 1024)


def entry(ref, row, column):
    values = ref[...].astype(f32)
    rows = lax.broadcasted_iota(jnp.int32, values.shape, 0)
    columns = lax.broadcasted_iota(jnp.int32, values.shape, 1)
    return jnp.sum(jnp.where((rows == row) & (columns == column), values, 0.0)).astype(jnp.int32)


def counted_rows(counts, tokens, per_micro):
    rows = lax.broadcasted_iota(jnp.int32, (tokens, 1), 0)
    return rows < entry(counts, 0, lax.axis_index("replica")) * per_micro


def dot_last(x, y, precision=None):
    return lax.dot_general(
        x, y, (((1,), (1,)), ((), ())), preferred_element_type=f32, precision=precision
    )


def dot_first(x, y, precision=None):
    return lax.dot_general(
        x, y, (((0,), (0,)), ((), ())), preferred_element_type=f32, precision=precision
    )


def in_parts(product, wide, parts):
    total = None
    for _ in range(parts):
        piece = wide.astype(bf16)
        wide = wide - piece.astype(f32)
        term = product(piece)
        total = term if total is None else total + term
    return total


def row_sum(x):
    return jnp.sum(x, axis=-1, keepdims=True)


def project_down_kernel(steps, h_in, down_in, out_ref, sq_ref, h_ref, down_ref, sems):
    slots, ranks, features = down_in.shape
    tokens = h_ref.shape[0]
    width = features // steps
    copies = []
    for step in range(steps):
        cut = pl.ds(step * width, width)
        moves = [(h_in.at[:, cut], h_ref.at[:, cut])]
        for slot in range(slots):
            rows = pl.ds(slot * ranks, ranks)
            moves.append((down_in.at[slot, :, cut], down_ref.at[rows, cut]))
        copies.append(
            [
                pltpu.make_async_copy(source, target, sems.at[step, i])
                for i, (source, target) in enumerate(moves)
            ]
        )
        for copy in copies[-1]:
            copy.start()
    total = jnp.zeros((tokens, slots * ranks), f32)
    square = jnp.zeros((tokens, 128), f32)
    for step in range(steps):
        for copy in copies[step]:
            copy.wait()
        cut = pl.ds(step * width, width)
        h = h_ref[:, cut]
        total = total + dot_last(h, down_ref[:, cut])
        wide = h.astype(f32)
        wide = wide * wide
        for lane in range(0, width, 128):
            square = square + wide[:, lane : lane + 128]
    sq_ref[...] = jnp.broadcast_to(row_sum(square), square.shape)
    out_ref[...] = total


def project_down(hidden, downs):
    tokens, features = hidden.shape
    slots, ranks, _ = downs.shape
    steps = 8
    sources = [pltpu.with_memory_space_constraint(x, pltpu.HBM) for x in (hidden, downs)]
    return pl.pallas_call(
        functools.partial(project_down_kernel, steps),
        in_specs=[in_hbm] * 2,
        out_specs=[in_vmem] * 3,
        out_shape=[
            jax.ShapeDtypeStruct((tokens, slots * ranks), f32),
            jax.ShapeDtypeStruct((tokens, 128), f32),
            jax.ShapeDtypeStruct((tokens, features), bf16),
        ],
        scratch_shapes=[
            pltpu.VMEM((slots * ranks, features), bf16),
            pltpu.SemaphoreType.DMA((steps, 1 + slots)),
        ],
        compiler_params=limited,
        cost_estimate=pl.CostEstimate(
            flops=2 * tokens * slots * ranks * features,
            bytes_accessed=2 * (tokens + slots * ranks) * features,
            transcendentals=0,
        ),
        name="project_down",
    )(*sources)


def project_up_kernel(per_micro, counts, by_down, h_ref, g_ref, up_ref, out_ref):
    tokens, columns = by_down.shape
    ups = up_ref[...].reshape(columns, up_ref.shape[2])
    out_ref[:, :columns] = by_down[...]
    out_ref[:, columns : 2 * columns] = dot_last(h_ref[...], ups)
    by_cot = dot_last(g_ref[...], ups)
    out_ref[:, 2 * columns :] = jnp.where(counted_rows(counts, tokens, per_micro), by_cot, 0.0)


def project_up(counts, by_down, hidden, cot, ups, per_micro):
    tokens, features = hidden.shape
    columns = by_down.shape[1]
    return pl.pallas_call(
        functools.partial(project_up_kernel, per_micro),
        in_specs=[in_vmem] * 5,
        out_specs=in_vmem,
        out_shape=jax.ShapeDtypeStruct((tokens, 3 * columns), f32),
        compiler_params=limited,
        cost_estimate=pl.CostEstimate(
            flops=4 * tokens * columns * features,
            bytes_accessed=2 * (2 * tokens + columns) * features,
            transcendentals=0,
        ),
        name="project_up",
    )(counts, by_down, hidden, cot, ups)


def gram_kernel(sections, *refs):
    around = refs[:sections]
    gram_ref, right_ref = refs[sections:]
    section_at = lax.axis_index("section")
    ranks = around[0].shape[0] // 2
    if sections == 2:
        own, other = around[0][...], around[1][...]
        downs = [jnp.where(section_at == 0, other, own[:ranks])]
        lefts = [jnp.where(section_at == 0, own[ranks:], other)]
    else:
        layers = []
        for layer in range(sections):
            distance = lax.rem(layer - section_at + sections, sections)
            chosen = around[0][...]
            for step in range(1, sections):
                chosen = jnp.where(distance == step, around[step][...], chosen)
            layers.append(chosen)
        downs = [chosen[:ranks] for chosen in layers[1:]]
        lefts = [chosen[ranks:] for chosen in layers[:-1]]
    right = jnp.concatenate(downs + lefts, axis=0)
    right_ref[...] = right
    gram_ref[...] = dot_last(jnp.concatenate(lefts, axis=0), right)


def gram(around):
    sections = len(around)
    ranks = around[0].shape[0] // 2
    columns = around[0].shape[1]
    before = (sections - 1) * ranks
    return pl.pallas_call(
        functools.partial(gram_kernel, sections),
        in_specs=[in_vmem] * sections,
        out_specs=[in_vmem] * 2,
        out_shape=[
            jax.ShapeDtypeStruct((before, 2 * before), f32),
            jax.ShapeDtypeStruct((2 * before, columns), bf16),
        ],
        compiler_params=limited,
        name="gram",
    )(*around)


def chain_kernel(sections, slots, features, per_micro, bounds, counts, *refs):
    projections, grams = refs[:sections], refs[sections:-3]
    sq_ref, factor_ref, mixed_ref = refs[-3:]
    layers = sections
    replica_at = lax.axis_index("replica")
    section_at = lax.axis_index("section")
    tokens = sq_ref.shape[0]
    table = grams[0][...]
    for other in grams[1:]:
        table = table + other[...]
    ranks = projections[0].shape[1] // (3 * slots)
    parts = [[jnp.zeros((tokens, ranks), f32)] * 3 for _ in range(layers)]
    for distance, source in enumerate(projections):
        section = lax.rem(section_at + distance, sections)
        first = entry(bounds, replica_at, section)
        after = entry(bounds, replica_at, section + 1)
        for slot in range(slots):
            for which in range(3):
                block = which * slots + slot
                piece = source[:, block * ranks : (block + 1) * ranks]
                for layer in range(layers):
                    here = (first + slot == layer) & (layer < after)
                    parts[layer][which] = jnp.where(here, piece, parts[layer][which])
    scale_d = 1.0 / math.sqrt(features)
    scale_r = 1.0 / math.sqrt(ranks)

    def part(layer, which):
        return parts[layer][which]

    def up_down(i, layer):
        return table[i * ranks : (i + 1) * ranks, (layer - 1) * ranks : layer * ranks]

    square = sq_ref[:, 0:1]
    inverses, inners, actives, sigmoids, products = [], [], [], [], []
    on_up = [[part(l, 1) for l in range(layers - 1)]]
    for layer in range(layers):
        inverse = lax.rsqrt(jnp.maximum(square, 0.0) * (1.0 / features) + norm_eps)
        on_down = part(layer, 0)
        for i in range(layer):
            on_down = on_down + products[i][:, (layer - 1) * ranks : layer * ranks]
        inner = on_down * (inverse * scale_d)
        sigmoid = jax.nn.sigmoid(inner)
        active = (inner * sigmoid).astype(bf16).astype(f32)
        inverses.append(inverse)
        inners.append(inner)
        sigmoids.append(sigmoid)
        actives.append(active)
        if layer < layers - 1:
            now = on_up[-1]
            product = in_parts(
                lambda part: jnp.dot(active.astype(bf16), part, preferred_element_type=f32),
                table[layer * ranks : (layer + 1) * ranks],
                3,
            )
            products.append(scale_r * product)
            grown = [
                now[l] + products[layer][:, (layers - 1 + l) * ranks : (layers + l) * ranks]
                for l in range(layers - 1)
            ]
            square = square + scale_r * row_sum(active * (now[layer] + grown[layer]))
            on_up.append(grown)
    scaled = [None] * layers
    kappas = [None] * layers
    for layer in reversed(range(layers)):
        incoming = part(layer, 2)
        for k in range(layer + 1, layers):
            incoming = incoming + scale_d * dot_last(scaled[k], up_down(layer, k), exact)
            incoming = incoming - kappas[k] * on_up[k][layer]
        sigmoid, inner = sigmoids[layer], inners[layer]
        slope = sigmoid * (1.0 + inner * (1.0 - sigmoid))
        error = incoming * scale_r * slope
        scaled[layer] = error * inverses[layer]
        kappas[layer] = (
            inverses[layer] * inverses[layer] * (row_sum(error * inner) * (1.0 / features))
        )

    def owned(values):
        chosen = values[0]
        for layer in range(1, layers):
            chosen = jnp.where(section_at == layer, values[layer], chosen)
        return chosen

    own_error = owned(scaled)
    own_active = owned(actives)
    counted = counted_rows(counts, tokens, per_micro)
    later = jnp.zeros_like(square)
    for k in range(1, layers):
        later = later + jnp.where(k > section_at, kappas[k], 0.0)
    on_hidden = jnp.concatenate([own_error * scale_d, -scale_r * later * own_active], axis=1)
    on_cot = jnp.concatenate(
        [jnp.zeros_like(own_active), jnp.where(counted, own_active * scale_r, 0.0)], axis=1
    )
    factor_ref[...] = jnp.concatenate([on_hidden.T, on_cot.T], axis=1).astype(bf16)
    both = scale_d * scale_r
    for k in range(1, layers):
        cut = slice((k - 1) * ranks, k * ranks)
        across = dot_first(own_active.astype(bf16), scaled[k].astype(bf16)) * both
        mixed_ref[:ranks, cut] = jnp.zeros_like(across)
        mixed_ref[ranks:, cut] = jnp.where(k > section_at, across, 0.0)
    for i in range(layers - 1):
        cut = slice((layers - 1 + i) * ranks, (layers + i) * ranks)
        after = jnp.zeros_like(square)
        for k in range(i + 1, layers):
            after = after + jnp.where(k > section_at, kappas[k], 0.0)
        across = dot_first(own_error.astype(bf16), actives[i].astype(bf16)) * both
        mixed_ref[:ranks, cut] = jnp.where(i < section_at, across, 0.0)
        across = dot_first(own_active.astype(bf16), (after * actives[i]).astype(bf16))
        mixed_ref[ranks:, cut] = across * (-scale_r * scale_r)


def chain(bounds, counts, projections, grams, square, slots, features, per_micro):
    sections = len(projections)
    tokens, wide = projections[0].shape
    ranks = wide // (3 * slots)
    inputs = [*projections, *grams, square]
    kernel = functools.partial(chain_kernel, sections, slots, features, per_micro)
    return pl.pallas_call(
        kernel,
        in_specs=[in_vmem] * (2 + len(inputs)),
        out_specs=[in_vmem] * 2,
        out_shape=[
            jax.ShapeDtypeStruct((2 * ranks, 2 * tokens), bf16),
            jax.ShapeDtypeStruct((2 * ranks, 2 * (sections - 1) * ranks), f32),
        ],
        compiler_params=limited,
        name="chain",
    )(bounds, counts, *inputs)


def gradient_kernel(first, lead, factor_ref, h_ref, g_ref, out_ref):
    _, _, ranks, columns = out_ref.shape
    tokens = h_ref.shape[0]
    replica_at = lax.axis_index("replica")
    tensor_at = lax.axis_index("tensor")
    tensors = lax.axis_size("tensor")
    down = factor_ref[:ranks, :tokens]
    up = factor_ref[ranks:]
    for middle in range(2):
        for high in range(2):
            for which, (far, low) in enumerate(((lead, middle), (middle, lead))):
                hop = low + 2 * high
                owner = (replica_at ^ (first + 2 * far)) * tensors + (tensor_at ^ hop)
                cut = pl.ds(pl.multiple_of(owner * columns, columns), columns)
                if which == 0:
                    block = jnp.dot(down, h_ref[:, cut], preferred_element_type=f32)
                else:
                    stacked = jnp.concatenate([h_ref[:, cut], g_ref[:, cut]], axis=0)
                    block = jnp.dot(up, stacked, preferred_element_type=f32)
                out_ref[which, 2 * middle + high] = block.astype(bf16)


def gradient(factors, hidden, cot, first, lead, columns):
    tokens, features = hidden.shape
    rows = factors.shape[0]
    return pl.pallas_call(
        functools.partial(gradient_kernel, first, lead),
        in_specs=[in_vmem] * 3,
        out_specs=in_vmem,
        out_shape=jax.ShapeDtypeStruct((2, 4, rows // 2, columns), bf16),
        compiler_params=limited,
        cost_estimate=pl.CostEstimate(
            flops=rows * tokens * features,
            bytes_accessed=(tokens + rows // 2) * features,
            transcendentals=0,
        ),
        name="gradient",
    )(factors, hidden, cot)


def update_kernel(which, kept, near, one, two, last, mixed_ref, other_ref, right_ref, *refs):
    master_ref, moment_ref, second_ref, new_master, new_moment, new_second, share_ref = refs
    ranks = last.shape[0]
    rows = slice(which * ranks, (which + 1) * ranks)
    mixed = mixed_ref[rows] + other_ref[rows].astype(f32)
    right = right_ref[...]
    own = in_parts(lambda part: jnp.dot(part, right, preferred_element_type=f32), mixed, 3)
    for block in (kept[which, 0], near[which, 0], one[0], two[0], last[...]):
        own = own + block.astype(f32)
    moment = beta_one * moment_ref[0] + (1.0 - beta_one) * own
    second = beta_two * second_ref[0] + (1.0 - beta_two) * own * own
    master = master_ref[0]
    master = master - learn_rate * (
        moment / first_fix / (jnp.sqrt(second / second_fix) + adam_eps) + decay_rate * master
    )
    share_ref[0] = master.astype(bf16)
    new_master[0] = master
    new_moment[0] = moment
    new_second[0] = second


def update(which, parts, right, state):
    inputs = [*parts, right, *state]
    return pl.pallas_call(
        functools.partial(update_kernel, which),
        in_specs=[in_vmem] * len(inputs),
        out_specs=[in_vmem] * 4,
        out_shape=[jax.ShapeDtypeStruct(array.shape, f32) for array in state]
        + [jax.ShapeDtypeStruct(state[0].shape, bf16)],
        compiler_params=limited,
        name="update",
    )(*inputs)


def place_kernel(layout, start, bounds, *refs):
    sources = refs[: len(layout)]
    outs = refs[-4:-2]
    zeros, sem = refs[-2:]
    slots, ranks, features = outs[0].shape
    columns = zeros.shape[1]
    tensors = lax.axis_size("tensor")
    replica_at = lax.axis_index("replica")
    section_at = lax.axis_index("section")
    tensor_at = lax.axis_index("tensor")
    first = entry(bounds, replica_at, section_at)
    after = entry(bounds, replica_at, section_at + 1)
    zeros[...] = jnp.zeros_like(zeros)

    def fill(slot, distance, go):
        for blocks, source in zip(layout, sources):
            for i, (window, which, order, hop) in enumerate(blocks):
                if window != distance:
                    continue
                owner = (replica_at ^ order) * tensors + (tensor_at ^ hop)
                cut = pl.ds(pl.multiple_of(owner * columns, columns), columns)
                go(pltpu.make_async_copy(source.at[i], outs[which].at[slot, :, cut], sem))

    def clear(slot, go):
        for out in outs:
            for block in range(features // columns):
                cut = pl.ds(block * columns, columns)
                go(pltpu.make_async_copy(zeros, out.at[slot, :, cut], sem))

    for act in (lambda copy: copy.start(), lambda copy: copy.wait()):
        for slot in range(slots):
            layer = first + slot
            present = layer < after
            for distance in range(2):

                @pl.when(present & (layer - section_at == distance))
                def _():
                    fill(slot, distance, act)

            if start:

                @pl.when(jnp.logical_not(present))
                def _():
                    clear(slot, act)


def place(bounds, pieces, before, slots, ranks, features):
    layout = [blocks for blocks, _ in pieces]
    arrays = [array for _, array in pieces]
    columns = arrays[0].shape[-1]
    return pl.pallas_call(
        functools.partial(place_kernel, layout, not before),
        in_specs=[in_vmem] * (1 + len(arrays)) + [in_hbm] * len(before),
        out_specs=[in_hbm] * 2,
        out_shape=[jax.ShapeDtypeStruct((slots, ranks, features), bf16)] * 2,
        scratch_shapes=[pltpu.VMEM((ranks, columns), bf16), pltpu.SemaphoreType.DMA],
        input_output_aliases={1 + len(arrays) + i: i for i in range(len(before))},
        compiler_params=limited,
        cost_estimate=pl.CostEstimate(
            flops=0,
            bytes_accessed=4 * sum(array.size for array in arrays),
            transcendentals=0,
        ),
        name="place",
    )(bounds, *arrays, *before)


def swapped(block, axis, distance):
    route = [(i, i ^ distance) for i in range(lax.axis_size(axis))]
    return lax.ppermute(block, axis, route)


def swaps(block, axis):
    return [swapped(block, axis, k) for k in range(1, lax.axis_size(axis))]


def from_next(block, distance=1):
    size = lax.axis_size("section")
    route = [((i + distance) % size, i) for i in range(size)]
    return lax.ppermute(block, "section", route)


def following_layer(block):
    size = lax.axis_size("section")
    return lax.ppermute(block, "section", [(i + 1, i) for i in range(size - 1)])


def summed(*blocks):
    total = blocks[0].astype(f32)
    for block in blocks[1:]:
        total = total + block.astype(f32)
    return total.astype(bf16)


def reduced(factors, hidden, cot, columns, mixed):
    def halves(lead):
        sent = gradient(factors, hidden, cot, 1, lead, columns)
        return swapped(sent, "replica", 1), gradient(factors, hidden, cot, 0, lead, columns)

    def part(which, cut, *steps):
        return summed(kept[which, cut], near[which, cut], *steps)

    def added(axis, distance):
        return mixed + swapped(mixed.astype(bf16), axis, distance).astype(f32)

    near, kept = halves(1)
    whole, low = slice(0, 4), slice(2, 4)
    down_one = swapped(part(0, whole), "replica", 2)
    up_one = swapped(part(1, whole), "tensor", 1)
    near, kept = halves(0)
    mixed = added("replica", 1)
    mixed = added("tensor", 2)
    down_one, up_one, mixed = lax.optimization_barrier((down_one, up_one, mixed))
    down_two = swapped(part(0, low, down_one[2:]), "tensor", 1)
    up_two = swapped(part(1, low, up_one[2:]), "replica", 2)
    down_last = swapped(part(0, 1, down_one[1], down_two[1]), "tensor", 2)
    kept, near = lax.optimization_barrier((kept, near))
    up_last = swapped(part(1, 1, up_one[1], up_two[1]), "tensor", 2)
    mixed = added("tensor", 1)
    other = swapped(mixed.astype(bf16), "replica", 2)
    down = (kept, near, down_one, down_two, down_last, mixed, other)
    return down, (kept, near, up_one, up_two, up_last, mixed, other)


def crossed(piece, axis, distance):
    blocks, array = piece
    blocks = [
        (window, which, order ^ distance, hop)
        if axis == "replica"
        else (window, which, order, hop ^ distance)
        for window, which, order, hop in blocks
    ]
    return blocks, swapped(array, axis, distance)


def fetched(piece, fetch):
    blocks, array = piece
    return [(1, *block[1:]) for block in blocks], fetch(array)


def picked(piece, at):
    return piece[0][at : at + 1], piece[1][at : at + 1]


def joined(*pieces):
    blocks = [block for piece in pieces for block in piece[0]]
    return blocks, jnp.concatenate([array for _, array in pieces])


def spread(down, up, bounds, slots, features):
    ranks = down.shape[1]
    down_own, up_own = ([(0, 0, 0, 0)], down), ([(0, 1, 0, 0)], up)
    down_one = crossed(down_own, "tensor", 2)
    up_one = crossed(up_own, "tensor", 2)
    downs, ups = joined(down_own, down_one), joined(up_own, up_one)
    owns = lax.optimization_barrier((down, up))
    own = joined((down_own[0], owns[0]), (up_own[0], owns[1]))
    next_own = fetched(own, from_next)
    *ones, next_array = lax.optimization_barrier((down_one[1], up_one[1], next_own[1]))
    one = joined((down_one[0], ones[0]), (up_one[0], ones[1]))
    next_own = (next_own[0], next_array)
    down_two = crossed(downs, "tensor", 1)
    up_two = crossed(ups, "replica", 2)
    next_one = fetched(one, from_next)
    two = joined(down_two, up_two)
    down_three = crossed(joined(downs, down_two), "replica", 2)
    up_three = crossed(joined(ups, up_two), "tensor", 1)
    next_two = fetched(two, from_next)
    ends = joined(picked(down_three, 3), picked(up_three, 3))
    next_end = fetched(ends, following_layer)
    _, _, next_array = lax.optimization_barrier((down_three[1], up_three[1], next_two[1]))
    next_two = (next_two[0], next_array)
    down_end = joined(picked(next_own, 0), picked(next_one, 0), picked(next_two, 0))
    up_end = joined(picked(next_own, 1), picked(next_one, 1), picked(next_two, 2))
    end = joined(crossed(down_end, "replica", 2), crossed(up_end, "tensor", 1), next_end)
    near = joined(own, one, two)
    far = joined(down_three, up_three)
    next_near = joined(next_own, next_one, next_two)
    near_core, far_core, next_core, end_core = (
        crossed(piece, "replica", 1) for piece in (near, far, next_near, end)
    )
    placed = place(
        bounds, [near, near_core, far, far_core, next_near, next_core], [], slots, ranks, features
    )
    placed = place(bounds, [end, end_core], placed, slots, ranks, features)
    return placed


def on_device(
    inputs,
    cotangent,
    micro_counts,
    bounds,
    holder_down,
    holder_up,
    master_down,
    master_up,
    moment_down,
    moment_up,
    second_down,
    second_up,
):
    sections = lax.axis_size("section")
    replicas = lax.axis_size("replica")
    tensors = lax.axis_size("tensor")
    assert replicas == 4 and tensors == 4
    _, micros, per_micro, features = inputs.shape
    micro_counts = micro_counts[None]
    slots = holder_down.shape[2]
    hidden = inputs.reshape(micros * per_micro, features)
    cot = cotangent.reshape(micros * per_micro, features)

    owned = jnp.concatenate([master_down[0], master_up[0]], axis=0).astype(bf16)
    if sections == 2:
        first = lax.axis_index("section") == 0
        needed = jnp.where(first, master_up[0], master_down[0]).astype(bf16)
    else:
        needed = owned
    around = [from_next(needed, d) for d in range(1, sections)]
    by_down, square, hidden = project_down(hidden, holder_down[0, 0])
    around, by_down = lax.optimization_barrier((around, by_down))
    table, right = gram([owned, *around])
    table, hidden = lax.optimization_barrier((table, hidden))
    projected = project_up(micro_counts, by_down, hidden, cot, holder_up[0, 0], per_micro)
    table = table + sum(swaps(table, "replica"))
    projections = [projected] + [from_next(projected, d) for d in range(1, sections)]
    table = table + swapped(table, "tensor", 1)
    tables = [table, swapped(table, "tensor", 2)]
    factors, mixed = chain(
        bounds, micro_counts, projections, tables, square, slots, features, per_micro
    )

    down_parts, up_parts = reduced(factors, hidden, cot, master_down.shape[2], mixed)
    down = update(0, down_parts, right, [master_down, moment_down, second_down])
    up = update(1, up_parts, right, [master_up, moment_up, second_up])
    placed = spread(down[3], up[3], bounds, slots, features)
    return (
        placed[0][None, None],
        placed[1][None, None],
        down[0],
        up[0],
        down[1],
        up[1],
        down[2],
        up[2],
    )


def solution(mesh):
    held = P("replica", "section", None, None, None)
    owned = P("section", None, ("replica", "tensor"))
    tokens = P("replica", None, "tensor", None)
    return jax.shard_map(
        on_device,
        mesh=mesh,
        in_specs=(tokens, tokens, P(), P(), held, held) + (owned,) * 6,
        out_specs=(held, held) + (owned,) * 6,
        check_vma=False,
    )
```

```python
import functools
import math

import jax
import jax.numpy as jnp
from jax import lax
from jax.experimental import pallas as pl
from jax.experimental.pallas import tpu as pltpu
from jax.sharding import PartitionSpec as P

norm_eps = 1e-06
learn_rate = 0.01
beta_one = 0.9
beta_two = 0.95
decay_rate = 0.1
adam_eps = 1e-08
first_fix = 0.9999734386011124
second_fix = 0.9940794707796659

f32 = jnp.float32
bf16 = jnp.bfloat16
exact = lax.Precision.HIGHEST
in_vmem = pl.BlockSpec(memory_space=pltpu.VMEM)
in_hbm = pl.BlockSpec(memory_space=pltpu.HBM)
limited = pltpu.CompilerParams(vmem_limit_bytes=16 * 1024 * 1024)


def entry(ref, row, column):
    values = ref[...].astype(f32)
    rows = lax.broadcasted_iota(jnp.int32, values.shape, 0)
    columns = lax.broadcasted_iota(jnp.int32, values.shape, 1)
    return jnp.sum(jnp.where((rows == row) & (columns == column), values, 0.0)).astype(jnp.int32)


def counted_rows(counts, tokens, per_micro):
    rows = lax.broadcasted_iota(jnp.int32, (tokens, 1), 0)
    return rows < entry(counts, 0, lax.axis_index("replica")) * per_micro


def dot_last(x, y, precision=None):
    return lax.dot_general(
        x, y, (((1,), (1,)), ((), ())), preferred_element_type=f32, precision=precision
    )


def dot_first(x, y, precision=None):
    return lax.dot_general(
        x, y, (((0,), (0,)), ((), ())), preferred_element_type=f32, precision=precision
    )


def in_parts(product, wide, parts):
    total = None
    for _ in range(parts):
        piece = wide.astype(bf16)
        wide = wide - piece.astype(f32)
        term = product(piece)
        total = term if total is None else total + term
    return total


def row_sum(x):
    return jnp.sum(x, axis=-1, keepdims=True)


def project_down_kernel(steps, h_in, down_in, out_ref, sq_ref, h_ref, down_ref, sems):
    slots, ranks, features = down_in.shape
    tokens = h_ref.shape[0]
    width = features // steps
    copies = []
    for step in range(steps):
        cut = pl.ds(step * width, width)
        moves = [(h_in.at[:, cut], h_ref.at[:, cut])]
        for slot in range(slots):
            rows = pl.ds(slot * ranks, ranks)
            moves.append((down_in.at[slot, :, cut], down_ref.at[rows, cut]))
        copies.append(
            [
                pltpu.make_async_copy(source, target, sems.at[step, i])
                for i, (source, target) in enumerate(moves)
            ]
        )
        for copy in copies[-1]:
            copy.start()
    total = jnp.zeros((tokens, slots * ranks), f32)
    square = jnp.zeros((tokens, 128), f32)
    for step in range(steps):
        for copy in copies[step]:
            copy.wait()
        cut = pl.ds(step * width, width)
        h = h_ref[:, cut]
        total = total + dot_last(h, down_ref[:, cut])
        wide = h.astype(f32)
        wide = wide * wide
        for lane in range(0, width, 128):
            square = square + wide[:, lane : lane + 128]
    sq_ref[...] = jnp.broadcast_to(row_sum(square), square.shape)
    out_ref[...] = total


def project_down(hidden, downs):
    tokens, features = hidden.shape
    slots, ranks, _ = downs.shape
    steps = 8
    sources = [pltpu.with_memory_space_constraint(x, pltpu.HBM) for x in (hidden, downs)]
    return pl.pallas_call(
        functools.partial(project_down_kernel, steps),
        in_specs=[in_hbm] * 2,
        out_specs=[in_vmem] * 3,
        out_shape=[
            jax.ShapeDtypeStruct((tokens, slots * ranks), f32),
            jax.ShapeDtypeStruct((tokens, 128), f32),
            jax.ShapeDtypeStruct((tokens, features), bf16),
        ],
        scratch_shapes=[
            pltpu.VMEM((slots * ranks, features), bf16),
            pltpu.SemaphoreType.DMA((steps, 1 + slots)),
        ],
        compiler_params=limited,
        cost_estimate=pl.CostEstimate(
            flops=2 * tokens * slots * ranks * features,
            bytes_accessed=2 * (tokens + slots * ranks) * features,
            transcendentals=0,
        ),
        name="project_down",
    )(*sources)


def project_up_kernel(per_micro, counts, by_down, h_ref, g_ref, up_ref, out_ref):
    tokens, columns = by_down.shape
    ups = up_ref[...].reshape(columns, up_ref.shape[2])
    out_ref[:, :columns] = by_down[...]
    out_ref[:, columns : 2 * columns] = dot_last(h_ref[...], ups)
    by_cot = dot_last(g_ref[...], ups)
    out_ref[:, 2 * columns :] = jnp.where(counted_rows(counts, tokens, per_micro), by_cot, 0.0)


def project_up(counts, by_down, hidden, cot, ups, per_micro):
    tokens, features = hidden.shape
    columns = by_down.shape[1]
    return pl.pallas_call(
        functools.partial(project_up_kernel, per_micro),
        in_specs=[in_vmem] * 5,
        out_specs=in_vmem,
        out_shape=jax.ShapeDtypeStruct((tokens, 3 * columns), f32),
        compiler_params=limited,
        cost_estimate=pl.CostEstimate(
            flops=4 * tokens * columns * features,
            bytes_accessed=2 * (2 * tokens + columns) * features,
            transcendentals=0,
        ),
        name="project_up",
    )(counts, by_down, hidden, cot, ups)


def gram_kernel(sections, *refs):
    around = refs[:sections]
    gram_ref, right_ref = refs[sections:]
    section_at = lax.axis_index("section")
    ranks = around[0].shape[0] // 2
    if sections == 2:
        own, other = around[0][...], around[1][...]
        downs = [jnp.where(section_at == 0, other, own[:ranks])]
        lefts = [jnp.where(section_at == 0, own[ranks:], other)]
    else:
        layers = []
        for layer in range(sections):
            distance = lax.rem(layer - section_at + sections, sections)
            chosen = around[0][...]
            for step in range(1, sections):
                chosen = jnp.where(distance == step, around[step][...], chosen)
            layers.append(chosen)
        downs = [chosen[:ranks] for chosen in layers[1:]]
        lefts = [chosen[ranks:] for chosen in layers[:-1]]
    right = jnp.concatenate(downs + lefts, axis=0)
    right_ref[...] = right
    gram_ref[...] = dot_last(jnp.concatenate(lefts, axis=0), right)


def gram(around):
    sections = len(around)
    ranks = around[0].shape[0] // 2
    columns = around[0].shape[1]
    before = (sections - 1) * ranks
    return pl.pallas_call(
        functools.partial(gram_kernel, sections),
        in_specs=[in_vmem] * sections,
        out_specs=[in_vmem] * 2,
        out_shape=[
            jax.ShapeDtypeStruct((before, 2 * before), f32),
            jax.ShapeDtypeStruct((2 * before, columns), bf16),
        ],
        compiler_params=limited,
        name="gram",
    )(*around)


def chain_kernel(sections, slots, features, per_micro, bounds, counts, *refs):
    projections, grams = refs[:sections], refs[sections:-3]
    sq_ref, factor_ref, mixed_ref = refs[-3:]
    layers = sections
    replica_at = lax.axis_index("replica")
    section_at = lax.axis_index("section")
    tokens = sq_ref.shape[0]
    table = grams[0][...]
    for other in grams[1:]:
        table = table + other[...]
    ranks = projections[0].shape[1] // (3 * slots)
    parts = [[jnp.zeros((tokens, ranks), f32)] * 3 for _ in range(layers)]
    for distance, source in enumerate(projections):
        section = lax.rem(section_at + distance, sections)
        first = entry(bounds, replica_at, section)
        after = entry(bounds, replica_at, section + 1)
        for slot in range(slots):
            for which in range(3):
                block = which * slots + slot
                piece = source[:, block * ranks : (block + 1) * ranks]
                for layer in range(layers):
                    here = (first + slot == layer) & (layer < after)
                    parts[layer][which] = jnp.where(here, piece, parts[layer][which])
    scale_d = 1.0 / math.sqrt(features)
    scale_r = 1.0 / math.sqrt(ranks)

    def part(layer, which):
        return parts[layer][which]

    def up_down(i, layer):
        return table[i * ranks : (i + 1) * ranks, (layer - 1) * ranks : layer * ranks]

    square = sq_ref[:, 0:1]
    inverses, inners, actives, sigmoids, products = [], [], [], [], []
    on_up = [[part(l, 1) for l in range(layers - 1)]]
    for layer in range(layers):
        inverse = lax.rsqrt(jnp.maximum(square, 0.0) * (1.0 / features) + norm_eps)
        on_down = part(layer, 0)
        for i in range(layer):
            on_down = on_down + products[i][:, (layer - 1) * ranks : layer * ranks]
        inner = on_down * (inverse * scale_d)
        sigmoid = jax.nn.sigmoid(inner)
        active = (inner * sigmoid).astype(bf16).astype(f32)
        inverses.append(inverse)
        inners.append(inner)
        sigmoids.append(sigmoid)
        actives.append(active)
        if layer < layers - 1:
            now = on_up[-1]
            product = in_parts(
                lambda part: jnp.dot(active.astype(bf16), part, preferred_element_type=f32),
                table[layer * ranks : (layer + 1) * ranks],
                3,
            )
            products.append(scale_r * product)
            grown = [
                now[l] + products[layer][:, (layers - 1 + l) * ranks : (layers + l) * ranks]
                for l in range(layers - 1)
            ]
            square = square + scale_r * row_sum(active * (now[layer] + grown[layer]))
            on_up.append(grown)
    scaled = [None] * layers
    kappas = [None] * layers
    for layer in reversed(range(layers)):
        incoming = part(layer, 2)
        for k in range(layer + 1, layers):
            incoming = incoming + scale_d * dot_last(scaled[k], up_down(layer, k), exact)
            incoming = incoming - kappas[k] * on_up[k][layer]
        sigmoid, inner = sigmoids[layer], inners[layer]
        slope = sigmoid * (1.0 + inner * (1.0 - sigmoid))
        error = incoming * scale_r * slope
        scaled[layer] = error * inverses[layer]
        kappas[layer] = (
            inverses[layer] * inverses[layer] * (row_sum(error * inner) * (1.0 / features))
        )

    def owned(values):
        chosen = values[0]
        for layer in range(1, layers):
            chosen = jnp.where(section_at == layer, values[layer], chosen)
        return chosen

    own_error = owned(scaled)
    own_active = owned(actives)
    counted = counted_rows(counts, tokens, per_micro)
    later = jnp.zeros_like(square)
    for k in range(1, layers):
        later = later + jnp.where(k > section_at, kappas[k], 0.0)
    on_hidden = jnp.concatenate([own_error * scale_d, -scale_r * later * own_active], axis=1)
    on_cot = jnp.concatenate(
        [jnp.zeros_like(own_active), jnp.where(counted, own_active * scale_r, 0.0)], axis=1
    )
    factor_ref[...] = jnp.concatenate([on_hidden.T, on_cot.T], axis=1).astype(bf16)
    both = scale_d * scale_r
    for k in range(1, layers):
        cut = slice((k - 1) * ranks, k * ranks)
        across = dot_first(own_active.astype(bf16), scaled[k].astype(bf16)) * both
        mixed_ref[:ranks, cut] = jnp.zeros_like(across)
        mixed_ref[ranks:, cut] = jnp.where(k > section_at, across, 0.0)
    for i in range(layers - 1):
        cut = slice((layers - 1 + i) * ranks, (layers + i) * ranks)
        after = jnp.zeros_like(square)
        for k in range(i + 1, layers):
            after = after + jnp.where(k > section_at, kappas[k], 0.0)
        across = dot_first(own_error.astype(bf16), actives[i].astype(bf16)) * both
        mixed_ref[:ranks, cut] = jnp.where(i < section_at, across, 0.0)
        across = dot_first(own_active.astype(bf16), (after * actives[i]).astype(bf16))
        mixed_ref[ranks:, cut] = across * (-scale_r * scale_r)


def chain(bounds, counts, projections, grams, square, slots, features, per_micro):
    sections = len(projections)
    tokens, wide = projections[0].shape
    ranks = wide // (3 * slots)
    inputs = [*projections, *grams, square]
    kernel = functools.partial(chain_kernel, sections, slots, features, per_micro)
    return pl.pallas_call(
        kernel,
        in_specs=[in_vmem] * (2 + len(inputs)),
        out_specs=[in_vmem] * 2,
        out_shape=[
            jax.ShapeDtypeStruct((2 * ranks, 2 * tokens), bf16),
            jax.ShapeDtypeStruct((2 * ranks, 2 * (sections - 1) * ranks), f32),
        ],
        compiler_params=limited,
        name="chain",
    )(bounds, counts, *inputs)


def gradient_kernel(first, lead, factor_ref, h_ref, g_ref, out_ref):
    _, _, ranks, columns = out_ref.shape
    tokens = h_ref.shape[0]
    replica_at = lax.axis_index("replica")
    tensor_at = lax.axis_index("tensor")
    tensors = lax.axis_size("tensor")
    down = factor_ref[:ranks, :tokens]
    up = factor_ref[ranks:]
    for middle in range(2):
        for high in range(2):
            for which, (far, low) in enumerate(((lead, middle), (middle, lead))):
                hop = low + 2 * high
                owner = (replica_at ^ (first + 2 * far)) * tensors + (tensor_at ^ hop)
                cut = pl.ds(pl.multiple_of(owner * columns, columns), columns)
                if which == 0:
                    block = jnp.dot(down, h_ref[:, cut], preferred_element_type=f32)
                else:
                    stacked = jnp.concatenate([h_ref[:, cut], g_ref[:, cut]], axis=0)
                    block = jnp.dot(up, stacked, preferred_element_type=f32)
                out_ref[which, 2 * middle + high] = block.astype(bf16)


def gradient(factors, hidden, cot, first, lead, columns):
    tokens, features = hidden.shape
    rows = factors.shape[0]
    return pl.pallas_call(
        functools.partial(gradient_kernel, first, lead),
        in_specs=[in_vmem] * 3,
        out_specs=in_vmem,
        out_shape=jax.ShapeDtypeStruct((2, 4, rows // 2, columns), bf16),
        compiler_params=limited,
        cost_estimate=pl.CostEstimate(
            flops=rows * tokens * features,
            bytes_accessed=(tokens + rows // 2) * features,
            transcendentals=0,
        ),
        name="gradient",
    )(factors, hidden, cot)


def update_kernel(which, kept, near, one, two, last, mixed_ref, other_ref, right_ref, *refs):
    master_ref, moment_ref, second_ref, new_master, new_moment, new_second, share_ref = refs
    ranks = last.shape[0]
    rows = slice(which * ranks, (which + 1) * ranks)
    mixed = mixed_ref[rows] + other_ref[rows].astype(f32)
    right = right_ref[...]
    own = in_parts(lambda part: jnp.dot(part, right, preferred_element_type=f32), mixed, 3)
    for block in (kept[which, 0], near[which, 0], one[0], two[0], last[...]):
        own = own + block.astype(f32)
    moment = beta_one * moment_ref[0] + (1.0 - beta_one) * own
    second = beta_two * second_ref[0] + (1.0 - beta_two) * own * own
    master = master_ref[0]
    master = master - learn_rate * (
        moment / first_fix / (jnp.sqrt(second / second_fix) + adam_eps) + decay_rate * master
    )
    share_ref[0] = master.astype(bf16)
    new_master[0] = master
    new_moment[0] = moment
    new_second[0] = second


def update(which, parts, right, state):
    inputs = [*parts, right, *state]
    return pl.pallas_call(
        functools.partial(update_kernel, which),
        in_specs=[in_vmem] * len(inputs),
        out_specs=[in_vmem] * 4,
        out_shape=[jax.ShapeDtypeStruct(array.shape, f32) for array in state]
        + [jax.ShapeDtypeStruct(state[0].shape, bf16)],
        compiler_params=limited,
        name="update",
    )(*inputs)


def place_kernel(layout, start, bounds, *refs):
    sources = refs[: len(layout)]
    outs = refs[-4:-2]
    zeros, sem = refs[-2:]
    slots, ranks, features = outs[0].shape
    columns = zeros.shape[1]
    tensors = lax.axis_size("tensor")
    replica_at = lax.axis_index("replica")
    section_at = lax.axis_index("section")
    tensor_at = lax.axis_index("tensor")
    first = entry(bounds, replica_at, section_at)
    after = entry(bounds, replica_at, section_at + 1)
    zeros[...] = jnp.zeros_like(zeros)

    def fill(slot, distance, go):
        for blocks, source in zip(layout, sources):
            for i, (window, which, order, hop) in enumerate(blocks):
                if window != distance:
                    continue
                owner = (replica_at ^ order) * tensors + (tensor_at ^ hop)
                cut = pl.ds(pl.multiple_of(owner * columns, columns), columns)
                go(pltpu.make_async_copy(source.at[i], outs[which].at[slot, :, cut], sem))

    def clear(slot, go):
        for out in outs:
            for block in range(features // columns):
                cut = pl.ds(block * columns, columns)
                go(pltpu.make_async_copy(zeros, out.at[slot, :, cut], sem))

    for act in (lambda copy: copy.start(), lambda copy: copy.wait()):
        for slot in range(slots):
            layer = first + slot
            present = layer < after
            for distance in range(2):

                @pl.when(present & (layer - section_at == distance))
                def _():
                    fill(slot, distance, act)

            if start:

                @pl.when(jnp.logical_not(present))
                def _():
                    clear(slot, act)


def place(bounds, pieces, before, slots, ranks, features):
    layout = [blocks for blocks, _ in pieces]
    arrays = [array for _, array in pieces]
    columns = arrays[0].shape[-1]
    return pl.pallas_call(
        functools.partial(place_kernel, layout, not before),
        in_specs=[in_vmem] * (1 + len(arrays)) + [in_hbm] * len(before),
        out_specs=[in_hbm] * 2,
        out_shape=[jax.ShapeDtypeStruct((slots, ranks, features), bf16)] * 2,
        scratch_shapes=[pltpu.VMEM((ranks, columns), bf16), pltpu.SemaphoreType.DMA],
        input_output_aliases={1 + len(arrays) + i: i for i in range(len(before))},
        compiler_params=limited,
        cost_estimate=pl.CostEstimate(
            flops=0,
            bytes_accessed=4 * sum(array.size for array in arrays),
            transcendentals=0,
        ),
        name="place",
    )(bounds, *arrays, *before)


def swapped(block, axis, distance):
    route = [(i, i ^ distance) for i in range(lax.axis_size(axis))]
    return lax.ppermute(block, axis, route)


def swaps(block, axis):
    return [swapped(block, axis, k) for k in range(1, lax.axis_size(axis))]


def from_next(block, distance=1):
    size = lax.axis_size("section")
    route = [((i + distance) % size, i) for i in range(size)]
    return lax.ppermute(block, "section", route)


def following_layer(block):
    size = lax.axis_size("section")
    return lax.ppermute(block, "section", [(i + 1, i) for i in range(size - 1)])


def summed(*blocks):
    total = blocks[0].astype(f32)
    for block in blocks[1:]:
        total = total + block.astype(f32)
    return total.astype(bf16)


def reduced(factors, hidden, cot, columns, mixed):
    def halves(lead):
        sent = gradient(factors, hidden, cot, 1, lead, columns)
        return swapped(sent, "replica", 1), gradient(factors, hidden, cot, 0, lead, columns)

    def part(which, cut, *steps):
        return summed(kept[which, cut], near[which, cut], *steps)

    def added(axis, distance):
        return mixed + swapped(mixed.astype(bf16), axis, distance).astype(f32)

    near, kept = halves(1)
    whole, low = slice(0, 4), slice(2, 4)
    down_one = swapped(part(0, whole), "replica", 2)
    up_one = swapped(part(1, whole), "tensor", 1)
    near, kept = halves(0)
    mixed = added("replica", 1)
    mixed = added("tensor", 2)
    down_one, up_one, mixed = lax.optimization_barrier((down_one, up_one, mixed))
    down_two = swapped(part(0, low, down_one[2:]), "tensor", 1)
    up_two = swapped(part(1, low, up_one[2:]), "replica", 2)
    down_last = swapped(part(0, 1, down_one[1], down_two[1]), "tensor", 2)
    kept, near = lax.optimization_barrier((kept, near))
    up_last = swapped(part(1, 1, up_one[1], up_two[1]), "tensor", 2)
    mixed = added("tensor", 1)
    other = swapped(mixed.astype(bf16), "replica", 2)
    down = (kept, near, down_one, down_two, down_last, mixed, other)
    return down, (kept, near, up_one, up_two, up_last, mixed, other)


def crossed(piece, axis, distance):
    blocks, array = piece
    blocks = [
        (window, which, order ^ distance, hop)
        if axis == "replica"
        else (window, which, order, hop ^ distance)
        for window, which, order, hop in blocks
    ]
    return blocks, swapped(array, axis, distance)


def fetched(piece, fetch):
    blocks, array = piece
    return [(1, *block[1:]) for block in blocks], fetch(array)


def picked(piece, at):
    return piece[0][at : at + 1], piece[1][at : at + 1]


def joined(*pieces):
    blocks = [block for piece in pieces for block in piece[0]]
    return blocks, jnp.concatenate([array for _, array in pieces])


def spread(down, up, bounds, slots, features):
    ranks = down.shape[1]
    down_own, up_own = ([(0, 0, 0, 0)], down), ([(0, 1, 0, 0)], up)
    down_one = crossed(down_own, "tensor", 2)
    up_one = crossed(up_own, "tensor", 2)
    downs, ups = joined(down_own, down_one), joined(up_own, up_one)
    owns = lax.optimization_barrier((down, up))
    own = joined((down_own[0], owns[0]), (up_own[0], owns[1]))
    next_own = fetched(own, from_next)
    *ones, next_array = lax.optimization_barrier((down_one[1], up_one[1], next_own[1]))
    one = joined((down_one[0], ones[0]), (up_one[0], ones[1]))
    next_own = (next_own[0], next_array)
    down_two = crossed(downs, "tensor", 1)
    up_two = crossed(ups, "replica", 2)
    next_one = fetched(one, from_next)
    two = joined(down_two, up_two)
    down_three = crossed(joined(downs, down_two), "replica", 2)
    up_three = crossed(joined(ups, up_two), "tensor", 1)
    next_two = fetched(two, from_next)
    ends = joined(picked(down_three, 3), picked(up_three, 3))
    next_end = fetched(ends, following_layer)
    near = joined(own, one, two)
    core_blocks, core_array = crossed(near, "replica", 1)
    _, _, next_array, core_array = lax.optimization_barrier(
        (down_three[1], up_three[1], next_two[1], core_array)
    )
    next_two, near_core = (next_two[0], next_array), (core_blocks, core_array)
    down_end = joined(picked(next_own, 0), picked(next_one, 0), picked(next_two, 0))
    up_end = joined(picked(next_own, 1), picked(next_one, 1), picked(next_two, 2))
    end = joined(crossed(down_end, "replica", 2), crossed(up_end, "tensor", 1), next_end)
    far = joined(down_three, up_three)
    next_near = joined(next_own, next_one, next_two)
    far_core, next_core, end_core = (
        crossed(piece, "replica", 1) for piece in (far, next_near, end)
    )
    placed = place(
        bounds, [near, near_core, far, far_core, next_near, next_core], [], slots, ranks, features
    )
    placed = place(bounds, [end, end_core], placed, slots, ranks, features)
    return placed


def on_device(
    inputs,
    cotangent,
    micro_counts,
    bounds,
    holder_down,
    holder_up,
    master_down,
    master_up,
    moment_down,
    moment_up,
    second_down,
    second_up,
):
    sections = lax.axis_size("section")
    replicas = lax.axis_size("replica")
    tensors = lax.axis_size("tensor")
    assert replicas == 4 and tensors == 4
    _, micros, per_micro, features = inputs.shape
    micro_counts = micro_counts[None]
    slots = holder_down.shape[2]
    hidden = inputs.reshape(micros * per_micro, features)
    cot = cotangent.reshape(micros * per_micro, features)

    owned = jnp.concatenate([master_down[0], master_up[0]], axis=0).astype(bf16)
    if sections == 2:
        first = lax.axis_index("section") == 0
        needed = jnp.where(first, master_up[0], master_down[0]).astype(bf16)
    else:
        needed = owned
    around = [from_next(needed, d) for d in range(1, sections)]
    by_down, square, hidden = project_down(hidden, holder_down[0, 0])
    around, by_down = lax.optimization_barrier((around, by_down))
    table, right = gram([owned, *around])
    table, hidden = lax.optimization_barrier((table, hidden))
    projected = project_up(micro_counts, by_down, hidden, cot, holder_up[0, 0], per_micro)
    table = table + sum(swaps(table, "replica"))
    projections = [projected] + [from_next(projected, d) for d in range(1, sections)]
    table = table + swapped(table, "tensor", 1)
    tables = [table, swapped(table, "tensor", 2)]
    factors, mixed = chain(
        bounds, micro_counts, projections, tables, square, slots, features, per_micro
    )

    down_parts, up_parts = reduced(factors, hidden, cot, master_down.shape[2], mixed)
    down = update(0, down_parts, right, [master_down, moment_down, second_down])
    up = update(1, up_parts, right, [master_up, moment_up, second_up])
    placed = spread(down[3], up[3], bounds, slots, features)
    return (
        placed[0][None, None],
        placed[1][None, None],
        down[0],
        up[0],
        down[1],
        up[1],
        down[2],
        up[2],
    )


def solution(mesh):
    held = P("replica", "section", None, None, None)
    owned = P("section", None, ("replica", "tensor"))
    tokens = P("replica", None, "tensor", None)
    return jax.shard_map(
        on_device,
        mesh=mesh,
        in_specs=(tokens, tokens, P(), P(), held, held) + (owned,) * 6,
        out_specs=(held, held) + (owned,) * 6,
        check_vma=False,
    )
```

```python
import functools
import math

import jax
import jax.numpy as jnp
from jax import lax
from jax.experimental import pallas as pl
from jax.experimental.pallas import tpu as pltpu
from jax.sharding import PartitionSpec as P

norm_eps = 1e-06
learn_rate = 0.01
beta_one = 0.9
beta_two = 0.95
decay_rate = 0.1
adam_eps = 1e-08
first_fix = 0.9999734386011124
second_fix = 0.9940794707796659

f32 = jnp.float32
bf16 = jnp.bfloat16
exact = lax.Precision.HIGHEST
in_vmem = pl.BlockSpec(memory_space=pltpu.VMEM)
in_hbm = pl.BlockSpec(memory_space=pltpu.HBM)
limited = pltpu.CompilerParams(vmem_limit_bytes=16 * 1024 * 1024)


def entry(ref, row, column):
    values = ref[...].astype(f32)
    rows = lax.broadcasted_iota(jnp.int32, values.shape, 0)
    columns = lax.broadcasted_iota(jnp.int32, values.shape, 1)
    return jnp.sum(jnp.where((rows == row) & (columns == column), values, 0.0)).astype(jnp.int32)


def counted_rows(counts, tokens, per_micro):
    rows = lax.broadcasted_iota(jnp.int32, (tokens, 1), 0)
    return rows < entry(counts, 0, lax.axis_index("replica")) * per_micro


def dot_last(x, y, precision=None):
    return lax.dot_general(
        x, y, (((1,), (1,)), ((), ())), preferred_element_type=f32, precision=precision
    )


def dot_first(x, y, precision=None):
    return lax.dot_general(
        x, y, (((0,), (0,)), ((), ())), preferred_element_type=f32, precision=precision
    )


def in_parts(product, wide, parts):
    total = None
    for _ in range(parts):
        piece = wide.astype(bf16)
        wide = wide - piece.astype(f32)
        term = product(piece)
        total = term if total is None else total + term
    return total


def row_sum(x):
    return jnp.sum(x, axis=-1, keepdims=True)


def project_down_kernel(steps, h_in, down_in, out_ref, sq_ref, h_ref, down_ref, sems):
    slots, ranks, features = down_in.shape
    tokens = h_ref.shape[0]
    width = features // steps
    copies = []
    for step in range(steps):
        cut = pl.ds(step * width, width)
        moves = [(h_in.at[:, cut], h_ref.at[:, cut])]
        for slot in range(slots):
            rows = pl.ds(slot * ranks, ranks)
            moves.append((down_in.at[slot, :, cut], down_ref.at[rows, cut]))
        copies.append(
            [
                pltpu.make_async_copy(source, target, sems.at[step, i])
                for i, (source, target) in enumerate(moves)
            ]
        )
        for copy in copies[-1]:
            copy.start()
    total = jnp.zeros((tokens, slots * ranks), f32)
    square = jnp.zeros((tokens, 128), f32)
    for step in range(steps):
        for copy in copies[step]:
            copy.wait()
        cut = pl.ds(step * width, width)
        h = h_ref[:, cut]
        total = total + dot_last(h, down_ref[:, cut])
        wide = h.astype(f32)
        wide = wide * wide
        for lane in range(0, width, 128):
            square = square + wide[:, lane : lane + 128]
    sq_ref[...] = jnp.broadcast_to(row_sum(square), square.shape)
    out_ref[...] = total


def project_down(hidden, downs):
    tokens, features = hidden.shape
    slots, ranks, _ = downs.shape
    steps = 8
    sources = [pltpu.with_memory_space_constraint(x, pltpu.HBM) for x in (hidden, downs)]
    return pl.pallas_call(
        functools.partial(project_down_kernel, steps),
        in_specs=[in_hbm] * 2,
        out_specs=[in_vmem] * 3,
        out_shape=[
            jax.ShapeDtypeStruct((tokens, slots * ranks), f32),
            jax.ShapeDtypeStruct((tokens, 128), f32),
            jax.ShapeDtypeStruct((tokens, features), bf16),
        ],
        scratch_shapes=[
            pltpu.VMEM((slots * ranks, features), bf16),
            pltpu.SemaphoreType.DMA((steps, 1 + slots)),
        ],
        compiler_params=limited,
        cost_estimate=pl.CostEstimate(
            flops=2 * tokens * slots * ranks * features,
            bytes_accessed=2 * (tokens + slots * ranks) * features,
            transcendentals=0,
        ),
        name="project_down",
    )(*sources)


def project_up_kernel(per_micro, counts, by_down, h_ref, g_ref, up_ref, out_ref):
    tokens, columns = by_down.shape
    ups = up_ref[...].reshape(columns, up_ref.shape[2])
    out_ref[:, :columns] = by_down[...]
    out_ref[:, columns : 2 * columns] = dot_last(h_ref[...], ups)
    by_cot = dot_last(g_ref[...], ups)
    out_ref[:, 2 * columns :] = jnp.where(counted_rows(counts, tokens, per_micro), by_cot, 0.0)


def project_up(counts, by_down, hidden, cot, ups, per_micro):
    tokens, features = hidden.shape
    columns = by_down.shape[1]
    return pl.pallas_call(
        functools.partial(project_up_kernel, per_micro),
        in_specs=[in_vmem] * 5,
        out_specs=in_vmem,
        out_shape=jax.ShapeDtypeStruct((tokens, 3 * columns), f32),
        compiler_params=limited,
        cost_estimate=pl.CostEstimate(
            flops=4 * tokens * columns * features,
            bytes_accessed=2 * (2 * tokens + columns) * features,
            transcendentals=0,
        ),
        name="project_up",
    )(counts, by_down, hidden, cot, ups)


def gram_kernel(sections, *refs):
    around = refs[:sections]
    gram_ref, right_ref = refs[sections:]
    section_at = lax.axis_index("section")
    ranks = around[0].shape[0] // 2
    if sections == 2:
        own, other = around[0][...], around[1][...]
        downs = [jnp.where(section_at == 0, other, own[:ranks])]
        lefts = [jnp.where(section_at == 0, own[ranks:], other)]
    else:
        layers = []
        for layer in range(sections):
            distance = lax.rem(layer - section_at + sections, sections)
            chosen = around[0][...]
            for step in range(1, sections):
                chosen = jnp.where(distance == step, around[step][...], chosen)
            layers.append(chosen)
        downs = [chosen[:ranks] for chosen in layers[1:]]
        lefts = [chosen[ranks:] for chosen in layers[:-1]]
    right = jnp.concatenate(downs + lefts, axis=0)
    right_ref[...] = right
    gram_ref[...] = dot_last(jnp.concatenate(lefts, axis=0), right)


def gram(around):
    sections = len(around)
    ranks = around[0].shape[0] // 2
    columns = around[0].shape[1]
    before = (sections - 1) * ranks
    return pl.pallas_call(
        functools.partial(gram_kernel, sections),
        in_specs=[in_vmem] * sections,
        out_specs=[in_vmem] * 2,
        out_shape=[
            jax.ShapeDtypeStruct((before, 2 * before), f32),
            jax.ShapeDtypeStruct((2 * before, columns), bf16),
        ],
        compiler_params=limited,
        name="gram",
    )(*around)


def chain_kernel(sections, slots, features, per_micro, bounds, counts, *refs):
    projections, grams = refs[:sections], refs[sections:-3]
    sq_ref, factor_ref, mixed_ref = refs[-3:]
    layers = sections
    replica_at = lax.axis_index("replica")
    section_at = lax.axis_index("section")
    tokens = sq_ref.shape[0]
    table = grams[0][...]
    for other in grams[1:]:
        table = table + other[...]
    ranks = projections[0].shape[1] // (3 * slots)
    parts = [[jnp.zeros((tokens, ranks), f32)] * 3 for _ in range(layers)]
    for distance, source in enumerate(projections):
        section = lax.rem(section_at + distance, sections)
        first = entry(bounds, replica_at, section)
        after = entry(bounds, replica_at, section + 1)
        for slot in range(slots):
            for which in range(3):
                block = which * slots + slot
                piece = source[:, block * ranks : (block + 1) * ranks]
                for layer in range(layers):
                    here = (first + slot == layer) & (layer < after)
                    parts[layer][which] = jnp.where(here, piece, parts[layer][which])
    scale_d = 1.0 / math.sqrt(features)
    scale_r = 1.0 / math.sqrt(ranks)

    def part(layer, which):
        return parts[layer][which]

    def up_down(i, layer):
        return table[i * ranks : (i + 1) * ranks, (layer - 1) * ranks : layer * ranks]

    square = sq_ref[:, 0:1]
    inverses, inners, actives, sigmoids, products = [], [], [], [], []
    on_up = [[part(l, 1) for l in range(layers - 1)]]
    for layer in range(layers):
        inverse = lax.rsqrt(jnp.maximum(square, 0.0) * (1.0 / features) + norm_eps)
        on_down = part(layer, 0)
        for i in range(layer):
            on_down = on_down + products[i][:, (layer - 1) * ranks : layer * ranks]
        inner = on_down * (inverse * scale_d)
        sigmoid = jax.nn.sigmoid(inner)
        active = (inner * sigmoid).astype(bf16).astype(f32)
        inverses.append(inverse)
        inners.append(inner)
        sigmoids.append(sigmoid)
        actives.append(active)
        if layer < layers - 1:
            now = on_up[-1]
            product = in_parts(
                lambda part: jnp.dot(active.astype(bf16), part, preferred_element_type=f32),
                table[layer * ranks : (layer + 1) * ranks],
                3,
            )
            products.append(scale_r * product)
            grown = [
                now[l] + products[layer][:, (layers - 1 + l) * ranks : (layers + l) * ranks]
                for l in range(layers - 1)
            ]
            square = square + scale_r * row_sum(active * (now[layer] + grown[layer]))
            on_up.append(grown)
    scaled = [None] * layers
    kappas = [None] * layers
    for layer in reversed(range(layers)):
        incoming = part(layer, 2)
        for k in range(layer + 1, layers):
            incoming = incoming + scale_d * dot_last(scaled[k], up_down(layer, k), exact)
            incoming = incoming - kappas[k] * on_up[k][layer]
        sigmoid, inner = sigmoids[layer], inners[layer]
        slope = sigmoid * (1.0 + inner * (1.0 - sigmoid))
        error = incoming * scale_r * slope
        scaled[layer] = error * inverses[layer]
        kappas[layer] = (
            inverses[layer] * inverses[layer] * (row_sum(error * inner) * (1.0 / features))
        )

    def owned(values):
        chosen = values[0]
        for layer in range(1, layers):
            chosen = jnp.where(section_at == layer, values[layer], chosen)
        return chosen

    own_error = owned(scaled)
    own_active = owned(actives)
    counted = counted_rows(counts, tokens, per_micro)
    later = jnp.zeros_like(square)
    for k in range(1, layers):
        later = later + jnp.where(k > section_at, kappas[k], 0.0)
    on_hidden = jnp.concatenate([own_error * scale_d, -scale_r * later * own_active], axis=1)
    on_cot = jnp.concatenate(
        [jnp.zeros_like(own_active), jnp.where(counted, own_active * scale_r, 0.0)], axis=1
    )
    factor_ref[...] = jnp.concatenate([on_hidden.T, on_cot.T], axis=1).astype(bf16)
    both = scale_d * scale_r
    for k in range(1, layers):
        cut = slice((k - 1) * ranks, k * ranks)
        across = dot_first(own_active.astype(bf16), scaled[k].astype(bf16)) * both
        mixed_ref[:ranks, cut] = jnp.zeros_like(across)
        mixed_ref[ranks:, cut] = jnp.where(k > section_at, across, 0.0)
    for i in range(layers - 1):
        cut = slice((layers - 1 + i) * ranks, (layers + i) * ranks)
        after = jnp.zeros_like(square)
        for k in range(i + 1, layers):
            after = after + jnp.where(k > section_at, kappas[k], 0.0)
        across = dot_first(own_error.astype(bf16), actives[i].astype(bf16)) * both
        mixed_ref[:ranks, cut] = jnp.where(i < section_at, across, 0.0)
        across = dot_first(own_active.astype(bf16), (after * actives[i]).astype(bf16))
        mixed_ref[ranks:, cut] = across * (-scale_r * scale_r)


def chain(bounds, counts, projections, grams, square, slots, features, per_micro):
    sections = len(projections)
    tokens, wide = projections[0].shape
    ranks = wide // (3 * slots)
    inputs = [*projections, *grams, square]
    kernel = functools.partial(chain_kernel, sections, slots, features, per_micro)
    return pl.pallas_call(
        kernel,
        in_specs=[in_vmem] * (2 + len(inputs)),
        out_specs=[in_vmem] * 2,
        out_shape=[
            jax.ShapeDtypeStruct((2 * ranks, 2 * tokens), bf16),
            jax.ShapeDtypeStruct((2 * ranks, 2 * (sections - 1) * ranks), f32),
        ],
        compiler_params=limited,
        name="chain",
    )(bounds, counts, *inputs)


def gradient_kernel(first, lead, factor_ref, h_ref, g_ref, out_ref):
    _, _, ranks, columns = out_ref.shape
    tokens = h_ref.shape[0]
    replica_at = lax.axis_index("replica")
    tensor_at = lax.axis_index("tensor")
    tensors = lax.axis_size("tensor")
    down = factor_ref[:ranks, :tokens]
    up = factor_ref[ranks:]
    for middle in range(2):
        for high in range(2):
            for which, (far, low) in enumerate(((lead, middle), (middle, lead))):
                hop = low + 2 * high
                owner = (replica_at ^ (first + 2 * far)) * tensors + (tensor_at ^ hop)
                cut = pl.ds(pl.multiple_of(owner * columns, columns), columns)
                if which == 0:
                    block = jnp.dot(down, h_ref[:, cut], preferred_element_type=f32)
                else:
                    stacked = jnp.concatenate([h_ref[:, cut], g_ref[:, cut]], axis=0)
                    block = jnp.dot(up, stacked, preferred_element_type=f32)
                out_ref[which, 2 * middle + high] = block.astype(bf16)


def gradient(factors, hidden, cot, first, lead, columns):
    tokens, features = hidden.shape
    rows = factors.shape[0]
    return pl.pallas_call(
        functools.partial(gradient_kernel, first, lead),
        in_specs=[in_vmem] * 3,
        out_specs=in_vmem,
        out_shape=jax.ShapeDtypeStruct((2, 4, rows // 2, columns), bf16),
        compiler_params=limited,
        cost_estimate=pl.CostEstimate(
            flops=rows * tokens * features,
            bytes_accessed=(tokens + rows // 2) * features,
            transcendentals=0,
        ),
        name="gradient",
    )(factors, hidden, cot)


def update_kernel(which, kept, near, one, two, last, mixed_ref, other_ref, right_ref, *refs):
    master_ref, moment_ref, second_ref, new_master, new_moment, new_second, share_ref = refs
    ranks = last.shape[0]
    rows = slice(which * ranks, (which + 1) * ranks)
    mixed = mixed_ref[rows] + other_ref[rows].astype(f32)
    right = right_ref[...]
    own = in_parts(lambda part: jnp.dot(part, right, preferred_element_type=f32), mixed, 3)
    for block in (kept[which, 0], near[which, 0], one[0], two[0], last[...]):
        own = own + block.astype(f32)
    moment = beta_one * moment_ref[0] + (1.0 - beta_one) * own
    second = beta_two * second_ref[0] + (1.0 - beta_two) * own * own
    master = master_ref[0]
    master = master - learn_rate * (
        moment / first_fix / (jnp.sqrt(second / second_fix) + adam_eps) + decay_rate * master
    )
    share_ref[0] = master.astype(bf16)
    new_master[0] = master
    new_moment[0] = moment
    new_second[0] = second


def update(which, parts, right, state):
    inputs = [*parts, right, *state]
    return pl.pallas_call(
        functools.partial(update_kernel, which),
        in_specs=[in_vmem] * len(inputs),
        out_specs=[in_vmem] * 4,
        out_shape=[jax.ShapeDtypeStruct(array.shape, f32) for array in state]
        + [jax.ShapeDtypeStruct(state[0].shape, bf16)],
        compiler_params=limited,
        name="update",
    )(*inputs)


def place_kernel(layout, start, bounds, *refs):
    sources = refs[: len(layout)]
    outs = refs[-4:-2]
    zeros, sem = refs[-2:]
    slots, ranks, features = outs[0].shape
    columns = zeros.shape[1]
    tensors = lax.axis_size("tensor")
    replica_at = lax.axis_index("replica")
    section_at = lax.axis_index("section")
    tensor_at = lax.axis_index("tensor")
    first = entry(bounds, replica_at, section_at)
    after = entry(bounds, replica_at, section_at + 1)
    zeros[...] = jnp.zeros_like(zeros)

    def fill(slot, distance, go):
        for blocks, source in zip(layout, sources):
            for i, (window, which, order, hop) in enumerate(blocks):
                if window != distance:
                    continue
                owner = (replica_at ^ order) * tensors + (tensor_at ^ hop)
                cut = pl.ds(pl.multiple_of(owner * columns, columns), columns)
                go(pltpu.make_async_copy(source.at[i], outs[which].at[slot, :, cut], sem))

    def clear(slot, go):
        for out in outs:
            for block in range(features // columns):
                cut = pl.ds(block * columns, columns)
                go(pltpu.make_async_copy(zeros, out.at[slot, :, cut], sem))

    for act in (lambda copy: copy.start(), lambda copy: copy.wait()):
        for slot in range(slots):
            layer = first + slot
            present = layer < after
            for distance in range(2):

                @pl.when(present & (layer - section_at == distance))
                def _():
                    fill(slot, distance, act)

            if start:

                @pl.when(jnp.logical_not(present))
                def _():
                    clear(slot, act)


def place(bounds, pieces, before, slots, ranks, features):
    layout = [blocks for blocks, _ in pieces]
    arrays = [array for _, array in pieces]
    columns = arrays[0].shape[-1]
    return pl.pallas_call(
        functools.partial(place_kernel, layout, not before),
        in_specs=[in_vmem] * (1 + len(arrays)) + [in_hbm] * len(before),
        out_specs=[in_hbm] * 2,
        out_shape=[jax.ShapeDtypeStruct((slots, ranks, features), bf16)] * 2,
        scratch_shapes=[pltpu.VMEM((ranks, columns), bf16), pltpu.SemaphoreType.DMA],
        input_output_aliases={1 + len(arrays) + i: i for i in range(len(before))},
        compiler_params=limited,
        cost_estimate=pl.CostEstimate(
            flops=0,
            bytes_accessed=4 * sum(array.size for array in arrays),
            transcendentals=0,
        ),
        name="place",
    )(bounds, *arrays, *before)


def swapped(block, axis, distance):
    route = [(i, i ^ distance) for i in range(lax.axis_size(axis))]
    return lax.ppermute(block, axis, route)


def swaps(block, axis):
    return [swapped(block, axis, k) for k in range(1, lax.axis_size(axis))]


def from_next(block, distance=1):
    size = lax.axis_size("section")
    route = [((i + distance) % size, i) for i in range(size)]
    return lax.ppermute(block, "section", route)


def following_layer(block):
    size = lax.axis_size("section")
    return lax.ppermute(block, "section", [(i + 1, i) for i in range(size - 1)])


def summed(*blocks):
    total = blocks[0].astype(f32)
    for block in blocks[1:]:
        total = total + block.astype(f32)
    return total.astype(bf16)


def reduced(factors, hidden, cot, columns, mixed):
    def halves(lead):
        sent = gradient(factors, hidden, cot, 1, lead, columns)
        return swapped(sent, "replica", 1), gradient(factors, hidden, cot, 0, lead, columns)

    def part(which, cut, *steps):
        return summed(kept[which, cut], near[which, cut], *steps)

    def added(axis, distance):
        return mixed + swapped(mixed.astype(bf16), axis, distance).astype(f32)

    near, kept = halves(1)
    whole, low = slice(0, 4), slice(2, 4)
    down_one = swapped(part(0, whole), "replica", 2)
    up_one = swapped(part(1, whole), "tensor", 1)
    near, kept = halves(0)
    mixed = added("replica", 1)
    mixed = added("tensor", 2)
    down_one, up_one, mixed = lax.optimization_barrier((down_one, up_one, mixed))
    down_two = swapped(part(0, low, down_one[2:]), "tensor", 1)
    up_two = swapped(part(1, low, up_one[2:]), "replica", 2)
    down_last = swapped(part(0, 1, down_one[1], down_two[1]), "tensor", 2)
    kept, near = lax.optimization_barrier((kept, near))
    up_last = swapped(part(1, 1, up_one[1], up_two[1]), "tensor", 2)
    mixed = added("tensor", 1)
    other = swapped(mixed.astype(bf16), "replica", 2)
    down = (kept, near, down_one, down_two, down_last, mixed, other)
    return down, (kept, near, up_one, up_two, up_last, mixed, other)


def crossed(piece, axis, distance):
    blocks, array = piece
    blocks = [
        (window, which, order ^ distance, hop)
        if axis == "replica"
        else (window, which, order, hop ^ distance)
        for window, which, order, hop in blocks
    ]
    return blocks, swapped(array, axis, distance)


def fetched(piece, fetch):
    blocks, array = piece
    return [(1, *block[1:]) for block in blocks], fetch(array)


def picked(piece, at):
    return piece[0][at : at + 1], piece[1][at : at + 1]


def joined(*pieces):
    blocks = [block for piece in pieces for block in piece[0]]
    return blocks, jnp.concatenate([array for _, array in pieces])


def spread(down, up, bounds, slots, features):
    ranks = down.shape[1]
    down_own, up_own = ([(0, 0, 0, 0)], down), ([(0, 1, 0, 0)], up)
    down_one = crossed(down_own, "tensor", 2)
    up_one = crossed(up_own, "tensor", 2)
    downs, ups = joined(down_own, down_one), joined(up_own, up_one)
    owns = lax.optimization_barrier((down, up))
    own = joined((down_own[0], owns[0]), (up_own[0], owns[1]))
    next_own = fetched(own, from_next)
    *ones, next_array = lax.optimization_barrier((down_one[1], up_one[1], next_own[1]))
    one = joined((down_one[0], ones[0]), (up_one[0], ones[1]))
    next_own = (next_own[0], next_array)
    down_two = crossed(downs, "tensor", 1)
    up_two = crossed(ups, "replica", 2)
    next_one = fetched(one, from_next)
    two = joined(down_two, up_two)
    down_three = crossed(joined(downs, down_two), "replica", 2)
    up_three = crossed(joined(ups, up_two), "tensor", 1)
    next_two = fetched(two, from_next)
    ends = joined(picked(down_three, 3), picked(up_three, 3))
    next_end = fetched(ends, following_layer)
    _, _, next_array = lax.optimization_barrier((down_three[1], up_three[1], next_two[1]))
    next_two = (next_two[0], next_array)
    down_end = joined(picked(next_own, 0), picked(next_one, 0), picked(next_two, 0))
    up_end = joined(picked(next_own, 1), picked(next_one, 1), picked(next_two, 2))
    end = joined(crossed(down_end, "replica", 2), crossed(up_end, "tensor", 1), next_end)
    owned = joined(own, one, two, down_three, up_three)
    next_near = joined(next_own, next_one, next_two)
    owned_core, next_core, end_core = (
        crossed(piece, "replica", 1) for piece in (owned, next_near, end)
    )
    early = [owned, owned_core, next_near, next_core]
    placed = place(bounds, early, [], slots, ranks, features)
    placed = place(bounds, [end, end_core], placed, slots, ranks, features)
    return placed


def on_device(
    inputs,
    cotangent,
    micro_counts,
    bounds,
    holder_down,
    holder_up,
    master_down,
    master_up,
    moment_down,
    moment_up,
    second_down,
    second_up,
):
    sections = lax.axis_size("section")
    replicas = lax.axis_size("replica")
    tensors = lax.axis_size("tensor")
    assert replicas == 4 and tensors == 4
    _, micros, per_micro, features = inputs.shape
    micro_counts = micro_counts[None]
    slots = holder_down.shape[2]
    hidden = inputs.reshape(micros * per_micro, features)
    cot = cotangent.reshape(micros * per_micro, features)

    owned = jnp.concatenate([master_down[0], master_up[0]], axis=0).astype(bf16)
    if sections == 2:
        first = lax.axis_index("section") == 0
        needed = jnp.where(first, master_up[0], master_down[0]).astype(bf16)
    else:
        needed = owned
    around = [from_next(needed, d) for d in range(1, sections)]
    by_down, square, hidden = project_down(hidden, holder_down[0, 0])
    around, by_down = lax.optimization_barrier((around, by_down))
    table, right = gram([owned, *around])
    table, hidden = lax.optimization_barrier((table, hidden))
    projected = project_up(micro_counts, by_down, hidden, cot, holder_up[0, 0], per_micro)
    table = table + sum(swaps(table, "replica"))
    projections = [projected] + [from_next(projected, d) for d in range(1, sections)]
    table = table + swapped(table, "tensor", 1)
    tables = [table, swapped(table, "tensor", 2)]
    factors, mixed = chain(
        bounds, micro_counts, projections, tables, square, slots, features, per_micro
    )

    down_parts, up_parts = reduced(factors, hidden, cot, master_down.shape[2], mixed)
    down = update(0, down_parts, right, [master_down, moment_down, second_down])
    up = update(1, up_parts, right, [master_up, moment_up, second_up])
    placed = spread(down[3], up[3], bounds, slots, features)
    return (
        placed[0][None, None],
        placed[1][None, None],
        down[0],
        up[0],
        down[1],
        up[1],
        down[2],
        up[2],
    )


def solution(mesh):
    held = P("replica", "section", None, None, None)
    owned = P("section", None, ("replica", "tensor"))
    tokens = P("replica", None, "tensor", None)
    return jax.shard_map(
        on_device,
        mesh=mesh,
        in_specs=(tokens, tokens, P(), P(), held, held) + (owned,) * 6,
        out_specs=(held, held) + (owned,) * 6,
        check_vma=False,
    )
```
